32 devices in a mesh: gx: 4 (over x, core), gy: 8 (over z, y).
Axes of the slice: x: 2, y: 2, z: 4, core: 2. Of those that a mesh axis runs over, the one named last changes fastest.
Arguments:
- model_state: float32 [16, 256, 528], P('gx', 'gy'), may hold values from -6 to 6
- hyper_coef: float32 [528], replicated, may hold values from 0.0001 to 0.001
- point_mass: float32 [16, 256], P('gx', 'gy'), may hold values from 0.5 to 2
- inverse_mass: float32 [16, 256], P('gx', 'gy'), may hold values from 0.2 to 0.8
- span_slot: int32 [16, 256], P('gx', 'gy'), may hold values from 0 to 511, as said below
- vert_diff: float32 [8, 48, 512], P('gy', None, 'gx'), may hold values from 0.05 to 20
- fall_rate: float32 [8, 48, 512], P('gy', None, 'gx'), may hold values from 0.1 to 10
- cloud_frac: float32 [8, 48, 512], P('gy', None, 'gx'), may hold values from 0 to 1
Outputs:
- new_state: float32 [16, 256, 528], P('gx', 'gy')
The draws below stay inside these ranges and needn't reach their ends.
Inputs may be any that keep to these rules, and one draw needn't show every extreme that they name: `span_slot`: within the columns that share a block of 32 along the second dimension, the values form a permutation; each device's 128 columns hold exactly 32 values in each range from p * 128 to (p + 1) * 128 - 1.
All inputs are finite; a program needn't handle non-finite values.
Results may differ from the reference program's by a relative error of at most 0.0003.
Values sent between devices are 32-bit elements; how exact they have to be, the bound alone decides.
No kernel may reach another device: no remote copies, remote signals or barrier semaphores. Data moves between devices by JAX's collectives and lax.ppermute only.
A program may use at most 64 MiB of HBM per device.

```python
import math
import jax
import jax.numpy as jnp
import numpy as np
from jax import lax

NLEV = 48
FLD = 528
PTS_X = 4
PTS_Y = 32
COLS = 128
PER = 32
NXP = 16
NYP = 256
PHYS = 512
BLOCKS_Y = 8
N_GX = 4
N_GY = 8


def draw_span_slot(key, part):
    key_first, key_second = jax.random.split(jax.random.fold_in(key, 7))
    keys_first = jax.random.split(key_first, N_GY * N_GX)
    keys_second = jax.random.split(key_second, N_GY * N_GX)
    first_perm = jax.vmap(lambda one_key: jax.random.permutation(one_key, COLS))(keys_first).reshape(N_GY, N_GX, COLS)
    second_perm = jax.vmap(lambda one_key: jax.random.permutation(one_key, COLS))(keys_second).reshape(N_GY, N_GX, COLS)
    target = first_perm // PER
    incoming = jnp.arange(N_GX)[None, :, None] * PER + first_perm % PER
    group_index = jnp.arange(N_GY)[:, None, None]
    within = second_perm[group_index, target, incoming]
    position_labels = (target * COLS + within).astype(jnp.int32)
    grid = position_labels.reshape(N_GY, N_GX, PTS_X, PTS_Y)
    return jnp.transpose(grid, (1, 2, 0, 3)).reshape(NXP, NYP)


def block_levels(key, extent, pieces, smallest, largest):
    loudness = 1.0
    for dim, blocks in pieces:
        heights = jax.random.uniform(jax.random.fold_in(jax.random.fold_in(key, 6), dim), (blocks,), jnp.float32, smallest / len(pieces), largest / len(pieces))
        loudness = loudness * jnp.repeat(jnp.exp(heights), extent[dim] // blocks).reshape((-1,) + (1,) * (len(extent) - 1 - dim))
    return loudness


def bell_draw(own_key, extent, width, most, shards=(), dtype=jnp.bfloat16):
    result = width * jax.random.normal(own_key, extent, jnp.float32)
    if shards:
        result = result * block_levels(own_key, extent, shards, -0.22, 0.18)
    return jnp.clip(result, -most, most).astype(dtype)


def setup_inputs(seed: int = 0) -> dict:
    streams_of = jax.random.split(jax.random.key(seed), 9)
    model_state = bell_draw(streams_of[0], (NXP, NYP, FLD), 1.0, 6.0, ((0, 4), (1, 8)), jnp.float32)
    hyper_coef = jnp.clip(jnp.exp(jax.random.uniform(streams_of[1], (FLD,), jnp.float32, math.log(0.0001), math.log(0.001))), 0.0001, 0.001)
    point_mass = jnp.clip(jnp.exp(math.log(2.0) - 1.3862944 * jax.random.uniform(streams_of[2], (NXP, NYP), jnp.float32) ** block_levels(streams_of[2], (NXP, NYP), ((0, 4), (1, 8)), -0.2, 0.2)), 0.5, 2.0)
    inverse_mass = jnp.clip(jnp.exp(math.log(0.8) - 1.3862944 * jax.random.uniform(streams_of[3], (NXP, NYP), jnp.float32) ** block_levels(streams_of[3], (NXP, NYP), ((0, 4), (1, 8)), -0.2, 0.2)), 0.2, 0.8)
    span_slot = draw_span_slot(jax.random.fold_in(streams_of[8], 71), 0)
    vert_diff = jnp.clip(jnp.exp(math.log(20.0) - 5.9914645 * jax.random.uniform(streams_of[5], (BLOCKS_Y, NLEV, PHYS), jnp.float32) ** block_levels(streams_of[5], (BLOCKS_Y, NLEV, PHYS), ((0, 8), (2, 4)), -0.2, 0.2)), 0.05, 20.0)
    fall_rate = jnp.clip(jnp.exp(math.log(10.0) - 4.6051702 * jax.random.uniform(streams_of[6], (BLOCKS_Y, NLEV, PHYS), jnp.float32) ** block_levels(streams_of[6], (BLOCKS_Y, NLEV, PHYS), ((0, 8), (2, 4)), -0.2, 0.2)), 0.1, 10.0)
    cloud_frac = jnp.clip(1.0 * jax.random.uniform(streams_of[7], (BLOCKS_Y, NLEV, PHYS), jnp.float32) ** block_levels(streams_of[7], (BLOCKS_Y, NLEV, PHYS), ((0, 8), (2, 4)), -0.2, 0.2), 0.0, 1.0)
    return dict(model_state=model_state, hyper_coef=hyper_coef, point_mass=point_mass, inverse_mass=inverse_mass, span_slot=span_slot, vert_diff=vert_diff, fall_rate=fall_rate, cloud_frac=cloud_frac)


def second_table():
    nodes = np.array([-1.0, -1.0 / np.sqrt(5.0), 1.0 / np.sqrt(5.0), 1.0])
    deriv = np.zeros((4, 4))
    for row_index in range(4):
        for col_index in range(4):
            if row_index == col_index:
                deriv[row_index, col_index] = sum((1.0 / (nodes[row_index] - nodes[other]) for other in range(4) if other != row_index))
            else:
                upper_part = np.prod([nodes[row_index] - nodes[other] for other in range(4) if other != row_index])
                lower_part = np.prod([nodes[col_index] - nodes[other] for other in range(4) if other != col_index])
                deriv[row_index, col_index] = upper_part / (lower_part * (nodes[row_index] - nodes[col_index]))
    return deriv @ deriv

def harmonic_operator(field):
    second_deriv = jnp.asarray(second_table(), jnp.float32)
    size_x, size_y, row_width = field.shape
    along_x = jnp.einsum('ab,ebyf->eayf', second_deriv, field.reshape(size_x // 4, 4, size_y, row_width), precision=lax.Precision.HIGHEST).reshape(size_x, size_y, row_width)
    along_y = jnp.einsum('ab,xebf->xeaf', second_deriv, field.reshape(size_x, size_y // 4, 4, row_width), precision=lax.Precision.HIGHEST).reshape(size_x, size_y, row_width)
    return along_x + along_y

def assemble(values, point_mass, inverse_mass):
    weighted = point_mass[:, :, None] * values
    size_x, size_y = point_mass.shape
    first_x = (jnp.arange(size_x) % 4 == 0)[:, None, None]
    last_x = (jnp.arange(size_x) % 4 == 3)[:, None, None]
    first_y = (jnp.arange(size_y) % 4 == 0)[None, :, None]
    last_y = (jnp.arange(size_y) % 4 == 3)[None, :, None]
    total = weighted + jnp.where(first_x, jnp.roll(weighted, 1, 0), 0.0) + jnp.where(last_x, jnp.roll(weighted, -1, 0), 0.0)
    total = total + jnp.where(first_y, jnp.roll(weighted, 1, 1), 0.0) + jnp.where(last_y, jnp.roll(weighted, -1, 1), 0.0)
    total = total + jnp.where(first_x & first_y, jnp.roll(weighted, (1, 1), (0, 1)), 0.0)
    total = total + jnp.where(first_x & last_y, jnp.roll(weighted, (1, -1), (0, 1)), 0.0)
    total = total + jnp.where(last_x & first_y, jnp.roll(weighted, (-1, 1), (0, 1)), 0.0)
    total = total + jnp.where(last_x & last_y, jnp.roll(weighted, (-1, -1), (0, 1)), 0.0)
    return inverse_mass[:, :, None] * total

def physics(fields, diff_coef, fall_coef, overcast_fraction_weight):
    zero_row = jnp.zeros_like(diff_coef[:1])
    above = jnp.concatenate([zero_row, diff_coef[1:]], 0)
    below = jnp.concatenate([diff_coef[1:], zero_row], 0)
    surface = jnp.concatenate([jnp.zeros_like(diff_coef[1:]), diff_coef[:1]], 0)
    centre = 1.0 + above + below + surface

    def forward(state_carry, inputs):
        prev_gain, previous_value = state_carry
        sub_k, centre_k, sup_k, rhs_k = inputs
        divisor = centre_k - sub_k * prev_gain
        gain = sup_k / divisor
        value = (rhs_k + sub_k[None, :] * previous_value) / divisor[None, :]
        return ((gain, value), (gain, value))
    start = (jnp.zeros_like(diff_coef[0]), jnp.zeros_like(fields[0]))
    _, (gains, values) = lax.scan(forward, start, (above, centre, below, fields))

    def backward(next_solved, inputs):
        gain, value = inputs
        solved_line_entries = value + gain[None, :] * next_solved
        return (solved_line_entries, solved_line_entries)
    _, solved_line_entries = lax.scan(backward, jnp.zeros_like(fields[0]), (gains, values), reverse=True)
    thermal_state_kelvin = solved_line_entries[:, 0]
    humidity_mixing_ratio = solved_line_entries[:, 1]
    droplet_mixing_ratio = solved_line_entries[:, 2]
    condensed_mass_content = overcast_fraction_weight * 0.5 * jnp.maximum(humidity_mixing_ratio - 0.3 * thermal_state_kelvin, 0.0)
    humidity_mixing_ratio = humidity_mixing_ratio - condensed_mass_content
    droplet_mixing_ratio = droplet_mixing_ratio + condensed_mass_content
    thermal_state_kelvin = thermal_state_kelvin + 2.0 * condensed_mass_content

    def settle(inflow, inputs):
        liquid_k, fall_k = inputs
        settled = (liquid_k + inflow) / (1.0 + fall_k)
        return (fall_k * settled, settled)
    _, droplet_mixing_ratio = lax.scan(settle, jnp.zeros_like(droplet_mixing_ratio[0]), (droplet_mixing_ratio, fall_coef))
    return jnp.concatenate([thermal_state_kelvin[:, None], humidity_mixing_ratio[:, None], droplet_mixing_ratio[:, None], solved_line_entries[:, 3:]], 1)

def reference(model_state, hyper_coef, point_mass, inverse_mass, span_slot, vert_diff, fall_rate, cloud_frac):
    lap_once = assemble(harmonic_operator(model_state), point_mass, inverse_mass)
    lap_twice = assemble(harmonic_operator(lap_once), point_mass, inverse_mass)
    dynamic = model_state - hyper_coef[None, None, :] * lap_twice
    size_x, size_y, row_width = dynamic.shape
    levels = vert_diff.shape[1]
    variables = row_width // levels
    block_cols = size_x * PTS_Y
    dyn_blocks = dynamic.reshape(size_x, BLOCKS_Y, PTS_Y, row_width).transpose(1, 0, 2, 3)
    slot_blocks = span_slot.reshape(size_x, BLOCKS_Y, PTS_Y).transpose(1, 0, 2)

    def one_block(items):
        block_state, block_slot, diff_block, fall_block, cloud_block = items
        fields = block_state.reshape(block_cols, variables, levels).transpose(2, 1, 0)
        index = block_slot.reshape(block_cols).astype(jnp.int32)
        updated = physics(fields, jnp.take(diff_block, index, axis=1), jnp.take(fall_block, index, axis=1), jnp.take(cloud_block, index, axis=1))
        tendency = updated - fields
        return (fields + tendency).transpose(2, 1, 0).reshape(size_x, PTS_Y, row_width)
    blocks = lax.map(one_block, (dyn_blocks, slot_blocks, vert_diff, fall_rate, cloud_frac))
    return blocks.transpose(1, 0, 2, 3).reshape(size_x, size_y, row_width)
```

```python
import functools

import jax
import jax.numpy as jnp
import numpy as np
from jax import lax
from jax.experimental import pallas as pl
from jax.experimental.pallas import tpu as pltpu
from jax.sharding import PartitionSpec as P

VMEM = pl.BlockSpec(memory_space=pltpu.VMEM)
PARAMS = pltpu.CompilerParams(vmem_limit_bytes=16 * 1024 * 1024)


def second_table():
    nodes = np.array([-1.0, -1.0 / np.sqrt(5.0), 1.0 / np.sqrt(5.0), 1.0])
    deriv = np.zeros((4, 4))
    for i in range(4):
        for j in range(4):
            if i == j:
                deriv[i, j] = sum(1.0 / (nodes[i] - nodes[k]) for k in range(4) if k != i)
            else:
                upper = np.prod([nodes[i] - nodes[k] for k in range(4) if k != i])
                lower = np.prod([nodes[j] - nodes[k] for k in range(4) if k != j])
                deriv[i, j] = upper / (lower * (nodes[i] - nodes[j]))
    return deriv @ deriv


def laplacian_tables(size_x, size_y):
    second = second_table()
    lap = np.kron(np.kron(np.eye(size_x // 4), second), np.eye(size_y))
    lap = lap + np.kron(np.eye(size_x), np.kron(np.eye(size_y // 4), second))
    partner = np.zeros_like(lap)
    for x in range(size_x):
        for y in range(size_y):
            other = y - 1 if y % 4 == 0 else y + 1 if y % 4 == 3 else -1
            if 0 <= other < size_y:
                partner[x * size_y + y] = lap[x * size_y + other]
    return np.stack([lap, partner]).astype(np.float32)


def split(value):
    high = value.astype(jnp.bfloat16)
    return high, (value - high.astype(jnp.float32)).astype(jnp.bfloat16)


def product(left, right):
    left_high, left_low = left
    right_high, right_low = right
    dot = functools.partial(jnp.dot, preferred_element_type=jnp.float32)
    return dot(left_high, right_high) + (dot(left_high, right_low) + dot(left_low, right_high))


def to_column(plane, partner=False):
    size_x, size_y = plane.shape
    row = lax.broadcasted_iota(jnp.int32, (size_y, size_y), 0)
    lane = lax.broadcasted_iota(jnp.int32, (size_y, size_y), 1)
    if partner:
        row = jnp.where(row % 4 == 0, row - 1, jnp.where(row % 4 == 3, row + 1, -1))
    pick = row == lane
    parts = [
        jnp.sum(jnp.where(pick, plane[x : x + 1, :], 0.0), axis=1, keepdims=True)
        for x in range(size_x)
    ]
    return jnp.concatenate(parts, axis=0)


def operator(tables, mass):
    return split(to_column(mass) * tables[0] + to_column(mass, True) * tables[1])


def emit(total, size_x, size_y, refs):
    x_low, x_high, y_low, y_high, c_ll, c_lh, c_hl, c_hh = refs
    last = (size_x - 1) * size_y
    x_low[...] = total[:size_y]
    x_high[...] = total[last:]
    for x in range(size_x):
        y_low[x : x + 1, :] = total[x * size_y : x * size_y + 1]
        y_high[x : x + 1, :] = total[(x + 1) * size_y - 1 : (x + 1) * size_y]
    c_ll[...] = total[:1]
    c_lh[...] = total[size_y - 1 : size_y]
    c_hl[...] = total[last : last + 1]
    c_hh[...] = total[last + size_y - 1 :]


def absorb(total_ref, size_x, size_y, refs):
    x_low, x_high, y_low, y_high, c_ll, c_lh, c_hl, c_hh = refs
    last = (size_x - 1) * size_y
    total_ref[:size_y] += x_low[...]
    total_ref[last:] += x_high[...]
    for x in range(size_x):
        first, final = x * size_y, (x + 1) * size_y - 1
        total_ref[first : first + 1, :] += y_low[x : x + 1, :]
        total_ref[final : final + 1, :] += y_high[x : x + 1, :]
    total_ref[:1] += c_ll[...]
    total_ref[size_y - 1 : size_y] += c_lh[...]
    total_ref[last : last + 1] += c_hl[...]
    total_ref[last + size_y - 1 :] += c_hh[...]


def first_kernel(size_x, size_y, state, mass, tables, total, *messages):
    result = product(operator(tables, mass[...]), split(state[...]))
    total[...] = result
    emit(result, size_x, size_y, messages)


def second_kernel(size_x, size_y, total, mass, inverse, tables, *refs):
    halos, result_ref, messages, work = refs[:8], refs[8], refs[9:17], refs[17]
    work[...] = total[...]
    absorb(work, size_x, size_y, halos)
    once = to_column(inverse[...]) * work[...]
    result = product(operator(tables, mass[...]), split(once))
    result_ref[...] = result
    emit(result, size_x, size_y, messages)


def third_kernel(size_x, size_y, levels, state, hyper, total, inverse, factors, *refs):
    halos, out, work, turned, values = refs[:8], refs[8], refs[9], refs[10], refs[11]
    columns, width = state.shape
    variables = width // levels
    work[...] = total[...]
    absorb(work, size_x, size_y, halos)
    dynamic = state[...] - hyper[...] * (to_column(inverse[...]) * work[...])
    turned[...] = dynamic.T
    scale, down, up, keep, flow, cloud = (
        factors.at[i * levels : (i + 1) * levels] for i in range(6)
    )
    value = jnp.zeros((variables, columns), jnp.float32)
    for k in range(levels):
        rows = turned[pl.ds(k, variables, stride=levels), :]
        value = rows * scale[k : k + 1, :] + down[k : k + 1, :] * value
        values[k, :variables, :] = value
    solved = jnp.zeros((variables, columns), jnp.float32)
    for k in reversed(range(levels)):
        solved = values[k, :variables, :] + up[k : k + 1, :] * solved
        turned[pl.ds(k, variables, stride=levels), :] = solved
    heat, vapour, liquid = (turned.at[i * levels : (i + 1) * levels] for i in range(3))
    condensed = cloud[...] * 0.5 * jnp.maximum(vapour[...] - 0.3 * heat[...], 0.0)
    vapour[...] = vapour[...] - condensed
    heat[...] = heat[...] + 2.0 * condensed
    liquid[...] = (liquid[...] + condensed) * keep[...]
    settled = jnp.zeros((1, columns), jnp.float32)
    for k in range(levels):
        settled = liquid[k : k + 1, :] + flow[k : k + 1, :] * settled
        liquid[k : k + 1, :] = settled
    out[...] = turned[...].T


def factor_kernel(levels, slots, diff, fall, cloud, factors):
    peers, _, span = diff.shape
    size_x, size_y = slots.shape
    columns = size_x * size_y
    picked = [jnp.zeros((levels, columns), jnp.float32) for _ in range(3)]
    wanted = jnp.concatenate([slots[x : x + 1, :] for x in range(size_x)], axis=1)
    for peer in range(peers):
        entry = lax.broadcasted_iota(jnp.int32, (span, columns), 0) + peer * span
        choice = (entry == wanted).astype(jnp.float32).astype(jnp.bfloat16)
        for i, source in enumerate((diff, fall, cloud)):
            rest = source[peer]
            for _ in range(3):
                part = rest.astype(jnp.bfloat16)
                rest = rest - part.astype(jnp.float32)
                picked[i] = picked[i] + jnp.dot(part, choice, preferred_element_type=jnp.float32)
    mixing, falling, covered = picked
    scale, down, up, keep, flow, cover = (
        factors.at[i * levels : (i + 1) * levels] for i in range(6)
    )
    gain = jnp.zeros((1, columns), jnp.float32)
    for k in range(levels):
        above = mixing[k : k + 1] if k else jnp.zeros_like(gain)
        below = mixing[k + 1 : k + 2] if k + 1 < levels else jnp.zeros_like(gain)
        centre = 1.0 + above + (below if k + 1 < levels else mixing[:1])
        inverse = 1.0 / (centre - above * gain)
        gain = below * inverse
        scale[k : k + 1, :] = inverse
        down[k : k + 1, :] = above * inverse
        up[k : k + 1, :] = gain
    kept = 1.0 / (1.0 + falling)
    keep[...] = kept
    flow[:1, :] = jnp.zeros((1, columns), jnp.float32)
    flow[1:, :] = falling[:-1] * kept[1:]
    cover[...] = covered


def neighbours(messages):
    size_gx, size_gy = lax.axis_size("gx"), lax.axis_size("gy")
    x_low, x_high, y_low, y_high, c_ll, c_lh, c_hl, c_hh = messages

    def send(value, step_x, step_y):
        pairs = [
            (
                i * size_gy + j,
                (i + step_x) % size_gx * size_gy + (j + step_y) % size_gy,
            )
            for i in range(size_gx)
            for j in range(size_gy)
        ]
        return lax.ppermute(value, ("gx", "gy"), pairs)

    return (
        send(x_high, 1, 0),
        send(x_low, -1, 0),
        send(y_high, 0, 1),
        send(y_low, 0, -1),
        send(c_hh, 1, 1),
        send(c_hl, 1, -1),
        send(c_lh, -1, 1),
        send(c_ll, -1, -1),
    )


def local(
    model_state, hyper_coef, point_mass, inverse_mass, span_slot, vert_diff, fall_rate, cloud_frac
):
    size_x, size_y, width = model_state.shape
    levels = vert_diff.shape[1]
    columns = size_x * size_y
    state = model_state.reshape(columns, width)
    hyper = hyper_coef.reshape(1, width)
    tables = jnp.asarray(laplacian_tables(size_x, size_y))

    def array(*shape):
        return jax.ShapeDtypeStruct(shape, jnp.float32)

    whole = array(columns, width)
    messages = [array(size_y, width)] * 2 + [array(size_x, width)] * 2 + [array(1, width)] * 4

    diff, fall, cloud = (
        lax.all_gather(value[0], "gx") for value in (vert_diff, fall_rate, cloud_frac)
    )
    factors = pl.pallas_call(
        functools.partial(factor_kernel, levels),
        out_shape=array(6 * levels, columns),
        in_specs=[VMEM] * 4,
        out_specs=VMEM,
        compiler_params=PARAMS,
        name="factors",
    )(span_slot, diff, fall, cloud)

    total, *sent = pl.pallas_call(
        functools.partial(first_kernel, size_x, size_y),
        out_shape=[whole] + messages,
        in_specs=[VMEM] * 3,
        out_specs=[VMEM] * 9,
        compiler_params=PARAMS,
        name="first",
    )(state, point_mass, tables)
    arrived = neighbours(sent)
    total, *sent = pl.pallas_call(
        functools.partial(second_kernel, size_x, size_y),
        out_shape=[whole] + messages,
        in_specs=[VMEM] * 12,
        out_specs=[VMEM] * 9,
        scratch_shapes=[pltpu.VMEM((columns, width), jnp.float32)],
        compiler_params=PARAMS,
        name="second",
    )(total, point_mass, inverse_mass, tables, *arrived)
    arrived = neighbours(sent)
    result = pl.pallas_call(
        functools.partial(third_kernel, size_x, size_y, levels),
        out_shape=whole,
        in_specs=[VMEM] * 13,
        out_specs=VMEM,
        scratch_shapes=[
            pltpu.VMEM((columns, width), jnp.float32),
            pltpu.VMEM((width, columns), jnp.float32),
            pltpu.VMEM((levels, 16, columns), jnp.float32),
        ],
        compiler_params=PARAMS,
        name="third",
    )(state, hyper, total, inverse_mass, factors, *arrived)
    return result.reshape(size_x, size_y, width)


def solution(mesh):
    placed = (
        P("gx", "gy", None),
        P(),
        P("gx", "gy"),
        P("gx", "gy"),
        P("gx", "gy"),
        P("gy", None, "gx"),
        P("gy", None, "gx"),
        P("gy", None, "gx"),
    )
    return jax.shard_map(
        local, mesh=mesh, in_specs=placed, out_specs=P("gx", "gy", None), check_vma=False
    )
```

```python
import functools

import jax
import jax.numpy as jnp
import numpy as np
from jax import lax
from jax.experimental import pallas as pl
from jax.experimental.pallas import tpu as pltpu
from jax.sharding import PartitionSpec as P

VMEM = pl.BlockSpec(memory_space=pltpu.VMEM)
PARAMS = pltpu.CompilerParams(vmem_limit_bytes=16 * 1024 * 1024)


def second_table():
    nodes = np.array([-1.0, -1.0 / np.sqrt(5.0), 1.0 / np.sqrt(5.0), 1.0])
    deriv = np.zeros((4, 4))
    for i in range(4):
        for j in range(4):
            if i == j:
                deriv[i, j] = sum(1.0 / (nodes[i] - nodes[k]) for k in range(4) if k != i)
            else:
                upper = np.prod([nodes[i] - nodes[k] for k in range(4) if k != i])
                lower = np.prod([nodes[j] - nodes[k] for k in range(4) if k != j])
                deriv[i, j] = upper / (lower * (nodes[i] - nodes[j]))
    return deriv @ deriv


def laplacian_tables(size_x, rows, columns):
    second = second_table()
    count = len(columns)
    lap = np.kron(np.kron(np.eye(size_x // 4), second), np.eye(count))
    lap = lap + np.kron(np.eye(size_x), np.kron(np.eye(count // 4), second))
    lap = lap.reshape(size_x, count, size_x * count)
    own = [columns.index(y) for y in rows]
    partner = np.zeros((size_x, len(rows), size_x * count))
    for i, y in enumerate(rows):
        other = y - 1 if y % 4 == 0 else y + 1 if y % 4 == 3 else None
        if other in columns:
            partner[:, i] = lap[:, columns.index(other)]
    both = np.stack([lap[:, own], partner])
    return both.reshape(2, size_x * len(rows), size_x * count).astype(np.float32)


def split(value):
    high = value.astype(jnp.bfloat16)
    return high, (value - high.astype(jnp.float32)).astype(jnp.bfloat16)


def product(left, right):
    left_high, left_low = left
    right_high, right_low = right
    dot = functools.partial(jnp.dot, preferred_element_type=jnp.float32)
    return dot(left_high, right_high) + (dot(left_high, right_low) + dot(left_low, right_high))


def to_column(planes, low, count, partner=False):
    size_x, size_y = planes[0][0].shape
    row = lax.broadcasted_iota(jnp.int32, (count, size_y), 0) + low
    lane = lax.broadcasted_iota(jnp.int32, (count, size_y), 1)
    if partner:
        phase = (row + 4 * count) % 4
        row = jnp.where(phase == 0, row - 1, jnp.where(phase == 3, row + 1, 4 * size_y))
    parts = []
    for x in range(size_x):
        picked = jnp.zeros((count, size_y), jnp.float32)
        for plane, first in planes:
            picked = picked + jnp.where(row == lane + first, plane[x : x + 1, :], 0.0)
        parts.append(jnp.sum(picked, axis=1, keepdims=True))
    return jnp.concatenate(parts, axis=0)


def mass_planes(own, halo_low, halo_high, which):
    size_x, size_y = own.shape
    rows = slice(which * size_x, (which + 1) * size_x)
    return (
        (own[...], 0),
        (halo_low[size_x, rows, :size_y], -size_y),
        (halo_high[size_x, rows, :size_y], size_y),
    )


def operator(tables, planes, low, count):
    mass = to_column(planes, low, count)
    partner = to_column(planes, low, count, True)
    return split(mass * tables[0] + partner * tables[1])


def pack_kernel(
    state, mass, inverse, diff, fall, cloud, low, high, coefs, mass_here, inverse_here, sems
):
    size_x, size_y, _ = state.shape
    levels = diff.shape[1]
    depth = low.shape[1]
    pairs = [
        (mass, mass_here),
        (inverse, inverse_here),
        (state.at[:, :depth, :], low.at[:size_x]),
        (state.at[:, size_y - depth :, :], high.at[:size_x]),
    ]
    for i, source in enumerate((diff, fall, cloud)):
        pairs.append((source.at[0], coefs.at[i * levels : (i + 1) * levels]))
    copies = [
        pltpu.make_async_copy(source, target, sems.at[i])
        for i, (source, target) in enumerate(pairs)
    ]
    for copy in copies:
        copy.start()
    for message in (low, high):
        message[size_x] = jnp.zeros(message.shape[1:], jnp.float32)
    copies[0].wait()
    copies[1].wait()
    for message in (low, high):
        message[size_x, :size_x, :size_y] = mass_here[...]
        message[size_x, size_x : 2 * size_x, :size_y] = inverse_here[...]
    for copy in copies[2:]:
        copy.wait()


def first_kernel(state, mass, halo_low, halo_high, tables, total, x_low, x_high, work):
    size_x, size_y, _ = state.shape
    depth = halo_low.shape[1]
    count = size_y + 2 * depth
    for x in range(size_x):
        start = x * count
        work[start : start + depth] = halo_low[x]
        work[start + depth : start + depth + size_y] = state[x]
        work[start + depth + size_y : start + count] = halo_high[x]
    planes = mass_planes(mass, halo_low, halo_high, 0)
    rows = size_y + depth
    result = product(operator(tables, planes, -depth // 2, rows), split(work[...]))
    total[...] = result
    x_low[...] = result[:rows]
    x_high[...] = result[-rows:]


def second_kernel(
    total, mass, inverse, halo_low, halo_high, tables, from_low, from_high, out, x_low, x_high, work
):
    size_x, size_y = mass.shape
    depth = halo_low.shape[1]
    rows = size_y + depth
    work[...] = total[...]
    work[:rows] += from_low[...]
    work[-rows:] += from_high[...]
    inverses = mass_planes(inverse, halo_low, halo_high, 1)
    once = to_column(inverses, -depth // 2, rows) * work[...]
    planes = mass_planes(mass, halo_low, halo_high, 0)
    result = product(operator(tables, planes, 0, size_y), split(once))
    out[...] = result
    x_low[...] = result[:size_y]
    x_high[...] = result[-size_y:]


def third_kernel(
    levels, state, hyper, total, inverse, factors, from_low, from_high, out, work, turned, values
):
    columns, width = total.shape
    size_x, size_y = inverse.shape
    variables = width // levels
    work[...] = total[...]
    work[:size_y] += from_low[...]
    work[-size_y:] += from_high[...]
    twice = to_column([(inverse[...], 0)], 0, size_y) * work[...]
    turned[...] = (state[...].reshape(columns, width) - hyper[...] * twice).T
    scale, down, up, keep, flow, cloud = (
        factors.at[i * levels : (i + 1) * levels] for i in range(6)
    )
    value = jnp.zeros((variables, columns), jnp.float32)
    for k in range(levels):
        rows = turned[pl.ds(k, variables, stride=levels), :]
        value = rows * scale[k : k + 1, :] + down[k : k + 1, :] * value
        values[k, :variables, :] = value
    solved = jnp.zeros((variables, columns), jnp.float32)
    for k in reversed(range(levels)):
        solved = values[k, :variables, :] + up[k : k + 1, :] * solved
        turned[pl.ds(k, variables, stride=levels), :] = solved
    heat, vapour, liquid = (turned.at[i * levels : (i + 1) * levels] for i in range(3))
    condensed = cloud[...] * 0.5 * jnp.maximum(vapour[...] - 0.3 * heat[...], 0.0)
    vapour[...] = vapour[...] - condensed
    heat[...] = heat[...] + 2.0 * condensed
    liquid[...] = (liquid[...] + condensed) * keep[...]
    settled = jnp.zeros((1, columns), jnp.float32)
    for k in range(levels):
        settled = liquid[k : k + 1, :] + flow[k : k + 1, :] * settled
        liquid[k : k + 1, :] = settled
    out[...] = turned[...].T.reshape(out.shape)


def factor_kernel(levels, shifts, slots, *refs):
    pieces, factors = refs[:-1], refs[-1]
    span = pieces[0].shape[-1]
    size_x, size_y = slots.shape
    columns = size_x * size_y
    peers, here = lax.axis_size("gx"), lax.axis_index("gx")
    picked = jnp.zeros((3 * levels, columns), jnp.float32)
    wanted = jnp.concatenate([slots[x : x + 1, :] for x in range(size_x)], axis=1)
    for shift, piece in zip(shifts, pieces):
        peer = lax.rem(here + peers - shift, peers)
        entry = lax.broadcasted_iota(jnp.int32, (span, columns), 0) + peer * span
        choice = (entry == wanted).astype(jnp.float32).astype(jnp.bfloat16)
        rest = piece[...]
        for _ in range(3):
            part = rest.astype(jnp.bfloat16)
            rest = rest - part.astype(jnp.float32)
            picked = picked + jnp.dot(part, choice, preferred_element_type=jnp.float32)
    mixing, falling, covered = (picked[i * levels : (i + 1) * levels] for i in range(3))
    scale, down, up, keep, flow, cover = (
        factors.at[i * levels : (i + 1) * levels] for i in range(6)
    )
    gain = jnp.zeros((1, columns), jnp.float32)
    for k in range(levels):
        above = mixing[k : k + 1] if k else jnp.zeros_like(gain)
        below = mixing[k + 1 : k + 2] if k + 1 < levels else jnp.zeros_like(gain)
        centre = 1.0 + above + (below if k + 1 < levels else mixing[:1])
        inverse = 1.0 / (centre - above * gain)
        gain = below * inverse
        scale[k : k + 1, :] = inverse
        down[k : k + 1, :] = above * inverse
        up[k : k + 1, :] = gain
    kept = 1.0 / (1.0 + falling)
    keep[...] = kept
    flow[:1, :] = jnp.zeros((1, columns), jnp.float32)
    flow[1:, :] = falling[:-1] * kept[1:]
    cover[...] = covered


def shifted(value, axis, step):
    size = lax.axis_size(axis)
    return lax.ppermute(value, axis, [(i, (i + step) % size) for i in range(size)])


def local(
    model_state, hyper_coef, point_mass, inverse_mass, span_slot, vert_diff, fall_rate, cloud_frac
):
    size_x, size_y, width = model_state.shape
    levels, span = vert_diff.shape[1:]
    columns = size_x * size_y
    depth, half = 8, 4
    rows = size_y + depth
    hyper = hyper_coef.reshape(1, width)
    wide = list(range(-depth, size_y + depth))
    middle = list(range(-half, size_y + half))
    inner = list(range(size_y))
    first_tables = jnp.asarray(laplacian_tables(size_x, middle, wide))
    second_tables = jnp.asarray(laplacian_tables(size_x, inner, middle))

    def array(*shape):
        return jax.ShapeDtypeStruct(shape, jnp.float32)

    def scratch(*shape):
        return pltpu.VMEM(shape, jnp.float32)

    def call(kernel, name, outs, scratches, *operands, spec=VMEM):
        return pl.pallas_call(
            kernel,
            out_shape=outs,
            in_specs=[spec] * len(operands),
            out_specs=[VMEM] * len(outs),
            scratch_shapes=scratches,
            compiler_params=PARAMS,
            name=name,
        )(*operands)

    edge = array(size_x + 1, depth, width)
    low, high, coefs = call(
        pack_kernel,
        "pack",
        [edge, edge, array(3 * levels, span)],
        [scratch(size_x, size_y), scratch(size_x, size_y), pltpu.SemaphoreType.DMA((7,))],
        *(
            pltpu.with_memory_space_constraint(value, pltpu.HBM)
            for value in (
                model_state,
                point_mass,
                inverse_mass,
                vert_diff,
                fall_rate,
                cloud_frac,
            )
        ),
        spec=pl.BlockSpec(memory_space=pltpu.HBM),
    )
    halo_low, halo_high = shifted(high, "gy", 1), shifted(low, "gy", -1)
    shifts = range(lax.axis_size("gx"))
    if len(shifts) <= 4:
        pieces = [coefs] + [shifted(coefs, "gx", step) for step in shifts[1:]]
    else:
        gathered = lax.all_gather(coefs, "gx")
        here = lax.axis_index("gx")
        pieces = [gathered[(here - step) % len(shifts)] for step in shifts]
    (factors,) = call(
        functools.partial(factor_kernel, levels, shifts),
        "factors",
        [array(6 * levels, columns)],
        [],
        span_slot,
        *pieces,
    )

    total, x_low, x_high = call(
        first_kernel,
        "first",
        [array(size_x * rows, width), array(rows, width), array(rows, width)],
        [scratch(size_x * len(wide), width)],
        model_state,
        point_mass,
        halo_low,
        halo_high,
        first_tables,
    )
    total, x_low, x_high = call(
        second_kernel,
        "second",
        [array(columns, width), array(size_y, width), array(size_y, width)],
        [scratch(size_x * rows, width)],
        total,
        point_mass,
        inverse_mass,
        halo_low,
        halo_high,
        second_tables,
        shifted(x_high, "gx", 1),
        shifted(x_low, "gx", -1),
    )
    (result,) = call(
        functools.partial(third_kernel, levels),
        "third",
        [array(size_x, size_y, width)],
        [scratch(columns, width), scratch(width, columns), scratch(levels, 16, columns)],
        model_state,
        hyper,
        total,
        inverse_mass,
        factors,
        shifted(x_high, "gx", 1),
        shifted(x_low, "gx", -1),
    )
    return result


def solution(mesh):
    placed = (
        P("gx", "gy", None),
        P(),
        P("gx", "gy"),
        P("gx", "gy"),
        P("gx", "gy"),
        P("gy", None, "gx"),
        P("gy", None, "gx"),
        P("gy", None, "gx"),
    )
    return jax.shard_map(
        local, mesh=mesh, in_specs=placed, out_specs=P("gx", "gy", None), check_vma=False
    )
```

```python
import functools

import jax
import jax.numpy as jnp
import numpy as np
from jax import lax
from jax.experimental import pallas as pl
from jax.experimental.pallas import tpu as pltpu
from jax.sharding import PartitionSpec as P

VMEM = pl.BlockSpec(memory_space=pltpu.VMEM)
PARAMS = pltpu.CompilerParams(vmem_limit_bytes=16 * 1024 * 1024)


def second_table():
    nodes = np.array([-1.0, -1.0 / np.sqrt(5.0), 1.0 / np.sqrt(5.0), 1.0])
    deriv = np.zeros((4, 4))
    for i in range(4):
        for j in range(4):
            if i == j:
                deriv[i, j] = sum(1.0 / (nodes[i] - nodes[k]) for k in range(4) if k != i)
            else:
                upper = np.prod([nodes[i] - nodes[k] for k in range(4) if k != i])
                lower = np.prod([nodes[j] - nodes[k] for k in range(4) if k != j])
                deriv[i, j] = upper / (lower * (nodes[i] - nodes[j]))
    return deriv @ deriv


def laplacian_tables(size_x, size_y):
    second = second_table()
    lap = np.kron(np.kron(np.eye(size_x // 4), second), np.eye(size_y))
    lap = lap + np.kron(np.eye(size_x), np.kron(np.eye(size_y // 4), second))
    partner = np.zeros_like(lap)
    for x in range(size_x):
        for y in range(size_y):
            other = y - 1 if y % 4 == 0 else y + 1 if y % 4 == 3 else -1
            if 0 <= other < size_y:
                partner[x * size_y + y] = lap[x * size_y + other]
    return np.stack([lap, partner]).astype(np.float32)


def split(value):
    high = value.astype(jnp.bfloat16)
    return high, (value - high.astype(jnp.float32)).astype(jnp.bfloat16)


def product(left, right):
    left_high, left_low = left
    right_high, right_low = right
    dot = functools.partial(jnp.dot, preferred_element_type=jnp.float32)
    return dot(left_high, right_high) + (dot(left_high, right_low) + dot(left_low, right_high))


def to_column(plane, partner=False):
    size_x, size_y = plane.shape
    row = lax.broadcasted_iota(jnp.int32, (size_y, size_y), 0)
    lane = lax.broadcasted_iota(jnp.int32, (size_y, size_y), 1)
    if partner:
        row = jnp.where(row % 4 == 0, row - 1, jnp.where(row % 4 == 3, row + 1, -1))
    pick = row == lane
    parts = [
        jnp.sum(jnp.where(pick, plane[x : x + 1, :], 0.0), axis=1, keepdims=True)
        for x in range(size_x)
    ]
    return jnp.concatenate(parts, axis=0)


def start_kernel(
    state,
    mass,
    inverse,
    diff,
    fall,
    cloud,
    tables,
    here,
    total,
    x_low,
    x_high,
    operator,
    columns,
    coefs,
    mass_here,
    inverse_here,
    tables_here,
    sems,
):
    size_x, size_y, width = state.shape
    levels = diff.shape[1]
    pairs = [(mass, mass_here), (tables, tables_here), (inverse, inverse_here), (state, here)]
    for i, source in enumerate((diff, fall, cloud)):
        pairs.append((source.at[0], coefs.at[i * levels : (i + 1) * levels]))
    copies = [
        pltpu.make_async_copy(source, target, sems.at[i])
        for i, (source, target) in enumerate(pairs)
    ]
    for copy in copies:
        copy.start()
    for copy in copies[:3]:
        copy.wait()
    own = to_column(mass_here[...])
    lane = lax.broadcasted_iota(jnp.int32, columns.shape, 1)
    columns[...] = jnp.where(lane == 0, own, to_column(inverse_here[...]))
    matrix = own * tables_here[0] + to_column(mass_here[...], True) * tables_here[1]
    operator[...] = matrix
    copies[3].wait()
    result = product(split(matrix), split(here[...].reshape(size_x * size_y, width)))
    total[...] = result
    x_low[...] = result[:size_y]
    x_high[...] = result[-size_y:]
    for copy in copies[4:]:
        copy.wait()


def edge_rows(ref, y, size_x, size_y):
    return jnp.concatenate(
        [ref[x * size_y + y : x * size_y + y + 1, :] for x in range(size_x)], axis=0
    )


def turn_kernel(size_x, total, columns, operator, from_low, from_high, out, y_low, y_high):
    size_y = from_low.shape[0]
    width = total.shape[1]
    out[...] = total[...]
    out[:size_y] += from_low[...]
    out[-size_y:] += from_high[...]
    once = split(columns[:, 1:2] * out[...])
    for y, message in ((0, y_low), (size_y - 1, y_high)):
        rows = product(split(edge_rows(operator, y, size_x, size_y)), once)
        message[:size_x, :width] = edge_rows(out, y, size_x, size_y)
        message[size_x:, :width] = rows
        message[:size_x, width : width + 2] = edge_rows(columns, y, size_x, size_y)[:, :2]


def second_kernel(
    size_x, known, columns, operator, from_low, from_high, out, x_low, x_high, work
):
    size_y = x_low.shape[0]
    width = known.shape[1]
    second = second_table()
    work[...] = known[...]
    beyond = []
    for y, node, message in ((0, 3, from_low), (size_y - 1, 0, from_high)):
        mass = message[:size_x, width : width + 1]
        inverse = message[:size_x, width + 1 : width + 2]
        theirs = inverse * edge_rows(known, y, size_x, size_y)
        rows = []
        for x in range(size_x):
            row = message[size_x + x : size_x + x + 1, :width]
            line = sum(
                float(second[x, i] + second[node, node] * (x == i)) * theirs[i : i + 1]
                for i in range(size_x)
            )
            rows.append(row + mass[x : x + 1] * line)
            work[x * size_y + y : x * size_y + y + 1, :] += message[x : x + 1, :width]
        beyond.append(rows)
    result = product(split(operator[...]), split(columns[:, 1:2] * work[...]))
    out[...] = result
    for y, rows in zip((0, size_y - 1), beyond):
        for x in range(size_x):
            out[x * size_y + y : x * size_y + y + 1, :] += rows[x]
    x_low[...] = out[:size_y]
    x_high[...] = out[-size_y:]


def third_kernel(
    levels, state, hyper, total, masses, factors, from_low, from_high, out, work, turned, values
):
    columns, width = total.shape
    size_x, size_y, _ = state.shape
    variables = width // levels
    work[...] = total[...]
    work[:size_y] += from_low[...]
    work[-size_y:] += from_high[...]
    twice = masses[:, 1:2] * work[...]
    turned[...] = (state[...].reshape(columns, width) - hyper[...] * twice).T
    scale, down, up, keep, flow, cloud = (
        factors.at[i * levels : (i + 1) * levels] for i in range(6)
    )
    value = jnp.zeros((variables, columns), jnp.float32)
    for k in range(levels):
        rows = turned[pl.ds(k, variables, stride=levels), :]
        value = rows * scale[k : k + 1, :] + down[k : k + 1, :] * value
        values[k, :variables, :] = value
    solved = jnp.zeros((variables, columns), jnp.float32)
    for k in reversed(range(levels)):
        solved = values[k, :variables, :] + up[k : k + 1, :] * solved
        turned[pl.ds(k, variables, stride=levels), :] = solved
    heat, vapour, liquid = (turned.at[i * levels : (i + 1) * levels] for i in range(3))
    condensed = cloud[...] * 0.5 * jnp.maximum(vapour[...] - 0.3 * heat[...], 0.0)
    vapour[...] = vapour[...] - condensed
    heat[...] = heat[...] + 2.0 * condensed
    liquid[...] = (liquid[...] + condensed) * keep[...]
    settled = jnp.zeros((1, columns), jnp.float32)
    for k in range(levels):
        settled = liquid[k : k + 1, :] + flow[k : k + 1, :] * settled
        liquid[k : k + 1, :] = settled
    out[...] = turned[...].T.reshape(out.shape)


def factor_kernel(levels, shifts, slots, *refs):
    pieces, factors = refs[:-1], refs[-1]
    span = pieces[0].shape[-1]
    size_x, size_y = slots.shape
    columns = size_x * size_y
    peers, here = lax.axis_size("gx"), lax.axis_index("gx")
    picked = jnp.zeros((3 * levels, columns), jnp.float32)
    wanted = jnp.concatenate([slots[x : x + 1, :] for x in range(size_x)], axis=1)
    for shift, piece in zip(shifts, pieces):
        peer = lax.rem(here + peers - shift, peers)
        entry = lax.broadcasted_iota(jnp.int32, (span, columns), 0) + peer * span
        choice = (entry == wanted).astype(jnp.float32).astype(jnp.bfloat16)
        rest = piece[...]
        for _ in range(3):
            part = rest.astype(jnp.bfloat16)
            rest = rest - part.astype(jnp.float32)
            picked = picked + jnp.dot(part, choice, preferred_element_type=jnp.float32)
    mixing, falling, covered = (picked[i * levels : (i + 1) * levels] for i in range(3))
    scale, down, up, keep, flow, cover = (
        factors.at[i * levels : (i + 1) * levels] for i in range(6)
    )
    gain = jnp.zeros((1, columns), jnp.float32)
    for k in range(levels):
        above = mixing[k : k + 1] if k else jnp.zeros_like(gain)
        below = mixing[k + 1 : k + 2] if k + 1 < levels else jnp.zeros_like(gain)
        centre = 1.0 + above + (below if k + 1 < levels else mixing[:1])
        inverse = 1.0 / (centre - above * gain)
        gain = below * inverse
        scale[k : k + 1, :] = inverse
        down[k : k + 1, :] = above * inverse
        up[k : k + 1, :] = gain
    kept = 1.0 / (1.0 + falling)
    keep[...] = kept
    flow[:1, :] = jnp.zeros((1, columns), jnp.float32)
    flow[1:, :] = falling[:-1] * kept[1:]
    cover[...] = covered


def shifted(value, axis, step):
    size = lax.axis_size(axis)
    return lax.ppermute(value, axis, [(i, (i + step) % size) for i in range(size)])


def local(
    model_state, hyper_coef, point_mass, inverse_mass, span_slot, vert_diff, fall_rate, cloud_frac
):
    size_x, size_y, width = model_state.shape
    levels, span = vert_diff.shape[1:]
    columns = size_x * size_y
    hyper = hyper_coef.reshape(1, width)
    padded = -(-(width + 2) // 128) * 128
    tables = jnp.asarray(laplacian_tables(size_x, size_y))

    def array(*shape):
        return jax.ShapeDtypeStruct(shape, jnp.float32)

    def scratch(*shape):
        return pltpu.VMEM(shape, jnp.float32)

    def call(kernel, name, outs, scratches, *operands, spec=VMEM):
        return pl.pallas_call(
            kernel,
            out_shape=outs,
            in_specs=[spec] * len(operands),
            out_specs=[VMEM] * len(outs),
            scratch_shapes=scratches,
            compiler_params=PARAMS,
            name=name,
        )(*operands)

    whole, line, edge = array(columns, width), array(size_y, width), array(2 * size_x, padded)
    here, total, x_low, x_high, operator, masses, coefs = call(
        start_kernel,
        "start",
        [
            array(size_x, size_y, width),
            whole,
            line,
            line,
            array(columns, columns),
            array(columns, 128),
            array(3 * levels, span),
        ],
        [
            scratch(size_x, size_y),
            scratch(size_x, size_y),
            scratch(*tables.shape),
            pltpu.SemaphoreType.DMA((7,)),
        ],
        *(
            pltpu.with_memory_space_constraint(value, pltpu.HBM)
            for value in (
                model_state,
                point_mass,
                inverse_mass,
                vert_diff,
                fall_rate,
                cloud_frac,
                tables,
            )
        ),
        spec=pl.BlockSpec(memory_space=pltpu.HBM),
    )
    known, y_low, y_high = call(
        functools.partial(turn_kernel, size_x),
        "turn",
        [whole, edge, edge],
        [],
        total,
        masses,
        operator,
        shifted(x_high, "gx", 1),
        shifted(x_low, "gx", -1),
    )
    total, x_low, x_high = call(
        functools.partial(second_kernel, size_x),
        "second",
        [whole, line, line],
        [scratch(columns, width)],
        known,
        masses,
        operator,
        shifted(y_high, "gy", 1),
        shifted(y_low, "gy", -1),
    )
    coefs, _ = lax.optimization_barrier((coefs, y_low))
    shifts = range(lax.axis_size("gx"))
    if len(shifts) <= 4:
        pieces = [coefs] + [shifted(coefs, "gx", step) for step in shifts[1:]]
    else:
        gathered = lax.all_gather(coefs, "gx")
        place = lax.axis_index("gx")
        pieces = [gathered[(place - step) % len(shifts)] for step in shifts]
    (factors,) = call(
        functools.partial(factor_kernel, levels, shifts),
        "factors",
        [array(6 * levels, columns)],
        [],
        span_slot,
        *pieces,
    )

    (result,) = call(
        functools.partial(third_kernel, levels),
        "third",
        [array(size_x, size_y, width)],
        [scratch(columns, width), scratch(width, columns), scratch(levels, 16, columns)],
        here,
        hyper,
        total,
        masses,
        factors,
        shifted(x_high, "gx", 1),
        shifted(x_low, "gx", -1),
    )
    return result


def solution(mesh):
    placed = (
        P("gx", "gy", None),
        P(),
        P("gx", "gy"),
        P("gx", "gy"),
        P("gx", "gy"),
        P("gy", None, "gx"),
        P("gy", None, "gx"),
        P("gy", None, "gx"),
    )
    return jax.shard_map(
        local, mesh=mesh, in_specs=placed, out_specs=P("gx", "gy", None), check_vma=False
    )
```

```python
import functools

import jax
import jax.numpy as jnp
import numpy as np
from jax import lax
from jax.experimental import pallas as pl
from jax.experimental.pallas import tpu as pltpu
from jax.sharding import PartitionSpec as P

VMEM = pl.BlockSpec(memory_space=pltpu.VMEM)
PARAMS = pltpu.CompilerParams(vmem_limit_bytes=16 * 1024 * 1024)


def second_table():
    nodes = np.array([-1.0, -1.0 / np.sqrt(5.0), 1.0 / np.sqrt(5.0), 1.0])
    deriv = np.zeros((4, 4))
    for i in range(4):
        for j in range(4):
            if i == j:
                deriv[i, j] = sum(1.0 / (nodes[i] - nodes[k]) for k in range(4) if k != i)
            else:
                upper = np.prod([nodes[i] - nodes[k] for k in range(4) if k != i])
                lower = np.prod([nodes[j] - nodes[k] for k in range(4) if k != j])
                deriv[i, j] = upper / (lower * (nodes[i] - nodes[j]))
    return deriv @ deriv


def laplacian_tables(size_x, size_y):
    second = second_table()
    lap = np.kron(np.kron(np.eye(size_x // 4), second), np.eye(size_y))
    lap = lap + np.kron(np.eye(size_x), np.kron(np.eye(size_y // 4), second))
    partner = np.zeros_like(lap)
    for x in range(size_x):
        for y in range(size_y):
            other = y - 1 if y % 4 == 0 else y + 1 if y % 4 == 3 else -1
            if 0 <= other < size_y:
                partner[x * size_y + y] = lap[x * size_y + other]
    return np.stack([lap, partner]).astype(np.float32)


def split(value):
    high = value.astype(jnp.bfloat16)
    return high, (value - high.astype(jnp.float32)).astype(jnp.bfloat16)


def product(left, right):
    left_high, left_low = left
    right_high, right_low = right
    dot = functools.partial(jnp.dot, preferred_element_type=jnp.float32)
    return dot(left_high, right_high) + (dot(left_high, right_low) + dot(left_low, right_high))


def to_column(plane, partner=False):
    size_x, size_y = plane.shape
    row = lax.broadcasted_iota(jnp.int32, (size_y, size_y), 0)
    lane = lax.broadcasted_iota(jnp.int32, (size_y, size_y), 1)
    if partner:
        row = jnp.where(row % 4 == 0, row - 1, jnp.where(row % 4 == 3, row + 1, -1))
    pick = row == lane
    parts = [
        jnp.sum(jnp.where(pick, plane[x : x + 1, :], 0.0), axis=1, keepdims=True)
        for x in range(size_x)
    ]
    return jnp.concatenate(parts, axis=0)


def even(axis):
    return lax.rem(lax.axis_index(axis), 2) == 0


def x_rows(count, size_y):
    near = jnp.where(even("gx"), count - size_y, 0)
    far = count - size_y - near
    return tuple(pl.ds(pl.multiple_of(start, size_y), size_y) for start in (near, far))


def start_kernel(
    state,
    mass,
    inverse,
    diff,
    fall,
    cloud,
    tables,
    here,
    total,
    x_near,
    x_far,
    operator,
    columns,
    coefs,
    mass_here,
    inverse_here,
    tables_here,
    sems,
):
    size_x, size_y, width = state.shape
    levels = diff.shape[1]
    pairs = [(mass, mass_here), (tables, tables_here), (inverse, inverse_here), (state, here)]
    for i, source in enumerate((diff, fall, cloud)):
        pairs.append((source.at[0], coefs.at[i * levels : (i + 1) * levels]))
    copies = [
        pltpu.make_async_copy(source, target, sems.at[i])
        for i, (source, target) in enumerate(pairs)
    ]
    for copy in copies:
        copy.start()
    for copy in copies[:3]:
        copy.wait()
    own = to_column(mass_here[...])
    lane = lax.broadcasted_iota(jnp.int32, columns.shape, 1)
    columns[...] = jnp.where(lane == 0, own, to_column(inverse_here[...]))
    matrix = own * tables_here[0] + to_column(mass_here[...], True) * tables_here[1]
    operator[...] = matrix
    copies[3].wait()
    result = product(split(matrix), split(here[...].reshape(size_x * size_y, width)))
    total[...] = result
    near, far = x_rows(size_x * size_y, size_y)
    x_near[...] = total[near]
    x_far[...] = total[far]
    for copy in copies[4:]:
        copy.wait()


def edge_rows(ref, y, size_x, size_y):
    return jnp.concatenate(
        [ref[x * size_y + y : x * size_y + y + 1, :] for x in range(size_x)], axis=0
    )


def turn_kernel(
    size_x, total, columns, operator, from_far, from_near, out, y_near, y_far, y_low, y_high
):
    size_y = from_near.shape[0]
    width = total.shape[1]
    near, far = x_rows(size_x * size_y, size_y)
    out[...] = total[...]
    out[near] += from_near[...]
    out[far] += from_far[...]
    once = split(columns[:, 1:2] * out[...])
    for y, message in ((0, y_low), (size_y - 1, y_high)):
        rows = product(split(edge_rows(operator, y, size_x, size_y)), once)
        message[:size_x, :width] = edge_rows(out, y, size_x, size_y)
        message[size_x:, :width] = rows
        message[:size_x, width : width + 2] = edge_rows(columns, y, size_x, size_y)[:, :2]
    y_near[...] = jnp.where(even("gy"), y_high[...], y_low[...])
    y_far[...] = jnp.where(even("gy"), y_low[...], y_high[...])


def second_kernel(
    size_x, known, columns, operator, from_far, from_near, out, x_near, x_far, work, low, high
):
    size_y = x_near.shape[0]
    width = known.shape[1]
    second = second_table()
    work[...] = known[...]
    low[...] = jnp.where(even("gy"), from_far[...], from_near[...])
    high[...] = jnp.where(even("gy"), from_near[...], from_far[...])
    beyond = []
    for y, node, message in ((0, 3, low), (size_y - 1, 0, high)):
        mass = message[:size_x, width : width + 1]
        inverse = message[:size_x, width + 1 : width + 2]
        theirs = inverse * edge_rows(known, y, size_x, size_y)
        rows = []
        for x in range(size_x):
            row = message[size_x + x : size_x + x + 1, :width]
            line = sum(
                float(second[x, i] + second[node, node] * (x == i)) * theirs[i : i + 1]
                for i in range(size_x)
            )
            rows.append(row + mass[x : x + 1] * line)
            work[x * size_y + y : x * size_y + y + 1, :] += message[x : x + 1, :width]
        beyond.append(rows)
    result = product(split(operator[...]), split(columns[:, 1:2] * work[...]))
    out[...] = result
    for y, rows in zip((0, size_y - 1), beyond):
        for x in range(size_x):
            out[x * size_y + y : x * size_y + y + 1, :] += rows[x]
    near, far = x_rows(size_x * size_y, size_y)
    x_near[...] = out[near]
    x_far[...] = out[far]


def third_kernel(
    levels, state, hyper, total, masses, factors, from_far, from_near, out, work, turned, values
):
    columns, width = total.shape
    size_x, size_y, _ = state.shape
    variables = width // levels
    near, far = x_rows(columns, size_y)
    work[...] = total[...]
    work[near] += from_near[...]
    work[far] += from_far[...]
    twice = masses[:, 1:2] * work[...]
    turned[...] = (state[...].reshape(columns, width) - hyper[...] * twice).T
    scale, down, up, keep, flow, cloud = (
        factors.at[i * levels : (i + 1) * levels] for i in range(6)
    )
    value = jnp.zeros((variables, columns), jnp.float32)
    for k in range(levels):
        rows = turned[pl.ds(k, variables, stride=levels), :]
        value = rows * scale[k : k + 1, :] + down[k : k + 1, :] * value
        values[k, :variables, :] = value
    solved = jnp.zeros((variables, columns), jnp.float32)
    for k in reversed(range(levels)):
        solved = values[k, :variables, :] + up[k : k + 1, :] * solved
        turned[pl.ds(k, variables, stride=levels), :] = solved
    heat, vapour, liquid = (turned.at[i * levels : (i + 1) * levels] for i in range(3))
    condensed = cloud[...] * 0.5 * jnp.maximum(vapour[...] - 0.3 * heat[...], 0.0)
    vapour[...] = vapour[...] - condensed
    heat[...] = heat[...] + 2.0 * condensed
    liquid[...] = (liquid[...] + condensed) * keep[...]
    settled = jnp.zeros((1, columns), jnp.float32)
    for k in range(levels):
        settled = liquid[k : k + 1, :] + flow[k : k + 1, :] * settled
        liquid[k : k + 1, :] = settled
    out[...] = turned[...].T.reshape(out.shape)


def factor_kernel(levels, owners, slots, *refs):
    pieces, factors = refs[:-1], refs[-1]
    span = pieces[0].shape[-1]
    size_x, size_y = slots.shape
    columns = size_x * size_y
    picked = jnp.zeros((3 * levels, columns), jnp.float32)
    wanted = jnp.concatenate([slots[x : x + 1, :] for x in range(size_x)], axis=1)
    for owner, piece in zip(owners, pieces):
        entry = lax.broadcasted_iota(jnp.int32, (span, columns), 0) + owner() * span
        choice = (entry == wanted).astype(jnp.float32).astype(jnp.bfloat16)
        rest = piece[...]
        for _ in range(3):
            part = rest.astype(jnp.bfloat16)
            rest = rest - part.astype(jnp.float32)
            picked = picked + jnp.dot(part, choice, preferred_element_type=jnp.float32)
    mixing, falling, covered = (picked[i * levels : (i + 1) * levels] for i in range(3))
    scale, down, up, keep, flow, cover = (
        factors.at[i * levels : (i + 1) * levels] for i in range(6)
    )
    gain = jnp.zeros((1, columns), jnp.float32)
    for k in range(levels):
        above = mixing[k : k + 1] if k else jnp.zeros_like(gain)
        below = mixing[k + 1 : k + 2] if k + 1 < levels else jnp.zeros_like(gain)
        centre = 1.0 + above + (below if k + 1 < levels else mixing[:1])
        inverse = 1.0 / (centre - above * gain)
        gain = below * inverse
        scale[k : k + 1, :] = inverse
        down[k : k + 1, :] = above * inverse
        up[k : k + 1, :] = gain
    kept = 1.0 / (1.0 + falling)
    keep[...] = kept
    flow[:1, :] = jnp.zeros((1, columns), jnp.float32)
    flow[1:, :] = falling[:-1] * kept[1:]
    cover[...] = covered


def swapped(value, axis, partner):
    return lax.ppermute(value, axis, [(i, partner(i)) for i in range(lax.axis_size(axis))])


def exchanged(near, far, axis):
    size = lax.axis_size(axis)
    from_far = swapped(far, axis, lambda i: (i + (1 if i % 2 else -1)) % size)
    from_near = swapped(near, axis, lambda i: i ^ 1)
    return from_far, from_near


def local(
    model_state, hyper_coef, point_mass, inverse_mass, span_slot, vert_diff, fall_rate, cloud_frac
):
    size_x, size_y, width = model_state.shape
    levels, span = vert_diff.shape[1:]
    columns = size_x * size_y
    hyper = hyper_coef.reshape(1, width)
    padded = -(-(width + 2) // 128) * 128
    tables = jnp.asarray(laplacian_tables(size_x, size_y))

    def array(*shape):
        return jax.ShapeDtypeStruct(shape, jnp.float32)

    def scratch(*shape):
        return pltpu.VMEM(shape, jnp.float32)

    def call(kernel, name, outs, scratches, *operands, spec=VMEM):
        return pl.pallas_call(
            kernel,
            out_shape=outs,
            in_specs=[spec] * len(operands),
            out_specs=[VMEM] * len(outs),
            scratch_shapes=scratches,
            compiler_params=PARAMS,
            name=name,
        )(*operands)

    whole, line, edge = array(columns, width), array(size_y, width), array(2 * size_x, padded)
    here, total, x_near, x_far, operator, masses, coefs = call(
        start_kernel,
        "start",
        [
            array(size_x, size_y, width),
            whole,
            line,
            line,
            array(columns, columns),
            array(columns, 128),
            array(3 * levels, span),
        ],
        [
            scratch(size_x, size_y),
            scratch(size_x, size_y),
            scratch(*tables.shape),
            pltpu.SemaphoreType.DMA((7,)),
        ],
        *(
            pltpu.with_memory_space_constraint(value, pltpu.HBM)
            for value in (
                model_state,
                point_mass,
                inverse_mass,
                vert_diff,
                fall_rate,
                cloud_frac,
                tables,
            )
        ),
        spec=pl.BlockSpec(memory_space=pltpu.HBM),
    )
    known, y_near, y_far = call(
        functools.partial(turn_kernel, size_x),
        "turn",
        [whole, edge, edge],
        [scratch(2 * size_x, padded), scratch(2 * size_x, padded)],
        total,
        masses,
        operator,
        *exchanged(x_near, x_far, "gx"),
    )
    total, x_near, x_far = call(
        functools.partial(second_kernel, size_x),
        "second",
        [whole, line, line],
        [scratch(columns, width), scratch(2 * size_x, padded), scratch(2 * size_x, padded)],
        known,
        masses,
        operator,
        *exchanged(y_near, y_far, "gy"),
    )
    coefs, _ = lax.optimization_barrier((coefs, y_near))
    peers = lax.axis_size("gx")
    if peers == 4:
        across = swapped(coefs, "gx", lambda i: i ^ 2)
        pieces = [coefs, across]
        pieces += [swapped(piece, "gx", lambda i: i ^ 1) for piece in pieces]
        owners = [lambda bits=bits: lax.axis_index("gx") ^ bits for bits in (0, 2, 1, 3)]
    else:
        pieces = list(lax.all_gather(coefs, "gx"))
        owners = [lambda peer=peer: peer for peer in range(peers)]
    (factors,) = call(
        functools.partial(factor_kernel, levels, owners),
        "factors",
        [array(6 * levels, columns)],
        [],
        span_slot,
        *pieces,
    )

    (result,) = call(
        functools.partial(third_kernel, levels),
        "third",
        [array(size_x, size_y, width)],
        [scratch(columns, width), scratch(width, columns), scratch(levels, 16, columns)],
        here,
        hyper,
        total,
        masses,
        factors,
        *exchanged(x_near, x_far, "gx"),
    )
    return result


def solution(mesh):
    placed = (
        P("gx", "gy", None),
        P(),
        P("gx", "gy"),
        P("gx", "gy"),
        P("gx", "gy"),
        P("gy", None, "gx"),
        P("gy", None, "gx"),
        P("gy", None, "gx"),
    )
    return jax.shard_map(
        local, mesh=mesh, in_specs=placed, out_specs=P("gx", "gy", None), check_vma=False
    )
```

```python
import functools

import jax
import jax.numpy as jnp
import numpy as np
from jax import lax
from jax.experimental import pallas as pl
from jax.experimental.pallas import tpu as pltpu
from jax.sharding import PartitionSpec as P

VMEM = pl.BlockSpec(memory_space=pltpu.VMEM)
PARAMS = pltpu.CompilerParams(vmem_limit_bytes=16 * 1024 * 1024)


def second_table():
    nodes = np.array([-1.0, -1.0 / np.sqrt(5.0), 1.0 / np.sqrt(5.0), 1.0])
    deriv = np.zeros((4, 4))
    for i in range(4):
        for j in range(4):
            if i == j:
                deriv[i, j] = sum(1.0 / (nodes[i] - nodes[k]) for k in range(4) if k != i)
            else:
                upper = np.prod([nodes[i] - nodes[k] for k in range(4) if k != i])
                lower = np.prod([nodes[j] - nodes[k] for k in range(4) if k != j])
                deriv[i, j] = upper / (lower * (nodes[i] - nodes[j]))
    return deriv @ deriv


def laplacian_tables(size_x, size_y):
    second = second_table()
    lap = np.kron(np.kron(np.eye(size_x // 4), second), np.eye(size_y))
    lap = lap + np.kron(np.eye(size_x), np.kron(np.eye(size_y // 4), second))
    partner = np.zeros_like(lap)
    for x in range(size_x):
        for y in range(size_y):
            other = y - 1 if y % 4 == 0 else y + 1 if y % 4 == 3 else -1
            if 0 <= other < size_y:
                partner[x * size_y + y] = lap[x * size_y + other]
    return np.stack([lap, partner]).astype(np.float32)


def split(value):
    high = value.astype(jnp.bfloat16)
    return high, (value - high.astype(jnp.float32)).astype(jnp.bfloat16)


def product(left, right):
    left_high, left_low = left
    right_high, right_low = right
    dot = functools.partial(jnp.dot, preferred_element_type=jnp.float32)
    return dot(left_high, right_high) + (dot(left_high, right_low) + dot(left_low, right_high))


def to_column(plane, partner=False):
    size_x, size_y = plane.shape
    row = lax.broadcasted_iota(jnp.int32, (size_y, size_y), 0)
    lane = lax.broadcasted_iota(jnp.int32, (size_y, size_y), 1)
    if partner:
        row = jnp.where(row % 4 == 0, row - 1, jnp.where(row % 4 == 3, row + 1, -1))
    pick = row == lane
    parts = [
        jnp.sum(jnp.where(pick, plane[x : x + 1, :], 0.0), axis=1, keepdims=True)
        for x in range(size_x)
    ]
    return jnp.concatenate(parts, axis=0)


def even(axis):
    return lax.rem(lax.axis_index(axis), 2) == 0


def x_rows(count, size_y):
    near = jnp.where(even("gx"), count - size_y, 0)
    far = count - size_y - near
    return tuple(pl.ds(pl.multiple_of(start, size_y), size_y) for start in (near, far))


COEF_ROWS = 32


def write_coefs(message, start, coefs):
    rows, lanes = coefs.shape
    for i, first in enumerate(range(0, rows, COEF_ROWS)):
        part = coefs[first : min(first + COEF_ROWS, rows)]
        message[start : start + part.shape[0], i * lanes : (i + 1) * lanes] = part


def read_coefs(message, start, rows, lanes):
    parts = []
    for i, first in enumerate(range(0, rows, COEF_ROWS)):
        count = min(COEF_ROWS, rows - first)
        parts.append(message[start : start + count, i * lanes : (i + 1) * lanes])
    return jnp.concatenate(parts, axis=0)


def start_kernel(
    state,
    mass,
    inverse,
    diff,
    fall,
    cloud,
    tables,
    here,
    total,
    x_near,
    x_far,
    y_near,
    y_far,
    operator,
    columns,
    coefs,
    mass_here,
    inverse_here,
    tables_here,
    low,
    high,
    sems,
):
    size_x, size_y, width = state.shape
    levels = diff.shape[1]
    pairs = [(mass, mass_here), (tables, tables_here), (inverse, inverse_here), (state, here)]
    for i, source in enumerate((diff, fall, cloud)):
        pairs.append((source.at[0], coefs.at[i * levels : (i + 1) * levels]))
    copies = [
        pltpu.make_async_copy(source, target, sems.at[i])
        for i, (source, target) in enumerate(pairs)
    ]
    for copy in copies:
        copy.start()
    for copy in copies[:3]:
        copy.wait()
    own = to_column(mass_here[...])
    lane = lax.broadcasted_iota(jnp.int32, columns.shape, 1)
    columns[...] = jnp.where(lane == 0, own, to_column(inverse_here[...]))
    matrix = own * tables_here[0] + to_column(mass_here[...], True) * tables_here[1]
    operator[...] = matrix
    copies[3].wait()
    total[...] = product(split(matrix), split(here[...].reshape(size_x * size_y, width)))
    for first, message in ((0, low), (size_y - 4, high)):
        for x in range(size_x):
            for i in range(4):
                row = x * size_y + first + i
                place = i * size_x + x
                message[place : place + 1, :width] = total[row : row + 1, :]
                message[place : place + 1, width : width + 2] = columns[row : row + 1, :2]
    y_near[...] = jnp.where(even("gy"), high[...], low[...])
    y_far[...] = jnp.where(even("gy"), low[...], high[...])
    near, far = x_rows(size_x * size_y, size_y)
    x_near[...] = total[near]
    x_far[:size_y, :width] = total[far]
    for copy in copies[4:]:
        copy.wait()
    if x_far.shape[0] > size_y:
        write_coefs(x_far, size_y, coefs)


def forward_kernel(size_x, width, from_far, from_near, x_near, x_far):
    low = jnp.where(even("gy"), from_far[...], from_near[...])
    high = jnp.where(even("gy"), from_near[...], from_far[...])

    def edge(x):
        rows = [
            side[i * size_x + x : i * size_x + x + 1, :width]
            for side in (low, high)
            for i in range(4)
        ]
        return jnp.concatenate(rows, axis=0)

    first, last = edge(0), edge(size_x - 1)
    x_near[...] = jnp.where(even("gx"), last, first)
    x_far[...] = jnp.where(even("gx"), first, last)


def second_kernel(
    size_x,
    total,
    columns,
    operator,
    coefs,
    from_far,
    from_near,
    y_from_far,
    y_from_near,
    corner_far,
    corner_near,
    out,
    x_near,
    x_far,
    work,
    low,
    high,
):
    size_y, width = from_near.shape
    second = second_table()
    near, far = x_rows(size_x * size_y, size_y)
    work[...] = total[...]
    work[near] += from_near[...]
    work[far] += from_far[:size_y, :width]
    low[...] = jnp.where(even("gy"), y_from_far[...], y_from_near[...])
    high[...] = jnp.where(even("gy"), y_from_near[...], y_from_far[...])
    corners = (
        (0, jnp.where(even("gx"), corner_far[...], corner_near[...])),
        (size_x - 1, jnp.where(even("gx"), corner_near[...], corner_far[...])),
    )
    beyond = []
    for side, (message, y, line) in enumerate(((low, 0, 3), (high, size_y - 1, 0))):
        for x, rows in corners:
            for i in range(4):
                place = i * size_x + x
                message[place : place + 1, :width] += rows[side * 4 + i : side * 4 + i + 1]
        for x in range(size_x):
            place, row = line * size_x + x, x * size_y + y
            joined = message[place : place + 1, :width] + work[row : row + 1, :]
            message[place : place + 1, :width] = joined
            work[row : row + 1, :] = joined
        once = message[:, width + 1 : width + 2] * message[:, :width]
        lines = [once[i * size_x : (i + 1) * size_x] for i in range(4)]
        value = sum(float(second[line, i]) * lines[i] for i in range(4))
        place = lax.broadcasted_iota(jnp.int32, (size_x, 1), 0)
        for i in range(size_x):
            factor = jnp.zeros((size_x, 1), jnp.float32)
            for x in range(size_x):
                factor = jnp.where(place == x, float(second[x, i]), factor)
            value = value + factor * lines[line][i : i + 1]
        mass = message[line * size_x : (line + 1) * size_x, width : width + 1]
        beyond.append(mass * value)
    out[...] = product(split(operator[...]), split(columns[:, 1:2] * work[...]))
    for y, rows in zip((0, size_y - 1), beyond):
        for x in range(size_x):
            out[x * size_y + y : x * size_y + y + 1, :] += rows[x : x + 1]
    x_far[...] = out[far]
    x_near[:size_y, :width] = out[near]
    if x_near.shape[0] > size_y:
        write_coefs(x_near, size_y, coefs)
        x_near[size_y + COEF_ROWS :, :] = from_far[size_y:, :]


def third_kernel(
    levels, state, hyper, total, masses, factors, from_far, from_near, out, work, turned, values
):
    columns, width = total.shape
    size_x, size_y, _ = state.shape
    variables = width // levels
    near, far = x_rows(columns, size_y)
    work[...] = total[...]
    work[near] += from_near[:size_y, :width]
    work[far] += from_far[...]
    twice = masses[:, 1:2] * work[...]
    turned[...] = (state[...].reshape(columns, width) - hyper[...] * twice).T
    scale, down, up, keep, flow, cloud = (
        factors.at[i * levels : (i + 1) * levels] for i in range(6)
    )
    value = jnp.zeros((variables, columns), jnp.float32)
    for k in range(levels):
        rows = turned[pl.ds(k, variables, stride=levels), :]
        value = rows * scale[k : k + 1, :] + down[k : k + 1, :] * value
        values[k, :variables, :] = value
    solved = jnp.zeros((variables, columns), jnp.float32)
    for k in reversed(range(levels)):
        solved = values[k, :variables, :] + up[k : k + 1, :] * solved
        turned[pl.ds(k, variables, stride=levels), :] = solved
    heat, vapour, liquid = (turned.at[i * levels : (i + 1) * levels] for i in range(3))
    condensed = cloud[...] * 0.5 * jnp.maximum(vapour[...] - 0.3 * heat[...], 0.0)
    vapour[...] = vapour[...] - condensed
    heat[...] = heat[...] + 2.0 * condensed
    liquid[...] = (liquid[...] + condensed) * keep[...]
    settled = jnp.zeros((1, columns), jnp.float32)
    for k in range(levels):
        settled = liquid[k : k + 1, :] + flow[k : k + 1, :] * settled
        liquid[k : k + 1, :] = settled
    out[...] = turned[...].T.reshape(out.shape)


def factor_kernel(levels, span, slots, *refs):
    rows = 3 * levels
    size_x, size_y = slots.shape
    columns = size_x * size_y
    factors = refs[-1]
    if len(refs) == 4:
        own, from_far, from_near = refs[:3]
        here = lax.axis_index("gx")
        pieces = [
            (here, own[...]),
            (here ^ 3, read_coefs(from_far, size_y, rows, span)),
            (here ^ 1, read_coefs(from_near, size_y, rows, span)),
            (here ^ 2, read_coefs(from_near, size_y + COEF_ROWS, rows, span)),
        ]
    else:
        pieces = [(peer, refs[0][peer]) for peer in range(refs[0].shape[0])]
    picked = jnp.zeros((rows, columns), jnp.float32)
    wanted = jnp.concatenate([slots[x : x + 1, :] for x in range(size_x)], axis=1)
    for owner, rest in pieces:
        entry = lax.broadcasted_iota(jnp.int32, (span, columns), 0) + owner * span
        choice = (entry == wanted).astype(jnp.float32).astype(jnp.bfloat16)
        for _ in range(3):
            part = rest.astype(jnp.bfloat16)
            rest = rest - part.astype(jnp.float32)
            picked = picked + jnp.dot(part, choice, preferred_element_type=jnp.float32)
    mixing, falling, covered = (picked[i * levels : (i + 1) * levels] for i in range(3))
    scale, down, up, keep, flow, cover = (
        factors.at[i * levels : (i + 1) * levels] for i in range(6)
    )
    gain = jnp.zeros((1, columns), jnp.float32)
    for k in range(levels):
        above = mixing[k : k + 1] if k else jnp.zeros_like(gain)
        below = mixing[k + 1 : k + 2] if k + 1 < levels else jnp.zeros_like(gain)
        centre = 1.0 + above + (below if k + 1 < levels else mixing[:1])
        inverse = 1.0 / (centre - above * gain)
        gain = below * inverse
        scale[k : k + 1, :] = inverse
        down[k : k + 1, :] = above * inverse
        up[k : k + 1, :] = gain
    kept = 1.0 / (1.0 + falling)
    keep[...] = kept
    flow[:1, :] = jnp.zeros((1, columns), jnp.float32)
    flow[1:, :] = falling[:-1] * kept[1:]
    cover[...] = covered


def swapped(value, axis, partner):
    return lax.ppermute(value, axis, [(i, partner(i)) for i in range(lax.axis_size(axis))])


def exchanged(near, far, axis):
    size = lax.axis_size(axis)
    from_far = swapped(far, axis, lambda i: (i + (1 if i % 2 else -1)) % size)
    from_near = swapped(near, axis, lambda i: i ^ 1)
    return from_far, from_near


def local(
    model_state, hyper_coef, point_mass, inverse_mass, span_slot, vert_diff, fall_rate, cloud_frac
):
    size_x, size_y, width = model_state.shape
    levels, span = vert_diff.shape[1:]
    columns = size_x * size_y
    hyper = hyper_coef.reshape(1, width)
    padded = -(-(width + 2) // 128) * 128
    tables = jnp.asarray(laplacian_tables(size_x, size_y))

    def array(*shape):
        return jax.ShapeDtypeStruct(shape, jnp.float32)

    def scratch(*shape):
        return pltpu.VMEM(shape, jnp.float32)

    def call(kernel, name, outs, scratches, *operands, spec=VMEM):
        return pl.pallas_call(
            kernel,
            out_shape=outs,
            in_specs=[spec] * len(operands),
            out_specs=[VMEM] * len(outs),
            scratch_shapes=scratches,
            compiler_params=PARAMS,
            name=name,
        )(*operands)

    riding = lax.axis_size("gx") == 4
    extra = COEF_ROWS if riding else 0
    whole, line = array(columns, width), array(size_y, width)
    edge, corner = array(4 * size_x, padded), array(8, width)
    here, total, x_near, x_far, y_near, y_far, operator, masses, coefs = call(
        start_kernel,
        "start",
        [
            array(size_x, size_y, width),
            whole,
            line,
            array(size_y + extra, padded),
            edge,
            edge,
            array(columns, columns),
            array(columns, 128),
            array(3 * levels, span),
        ],
        [
            scratch(size_x, size_y),
            scratch(size_x, size_y),
            scratch(*tables.shape),
            scratch(*edge.shape),
            scratch(*edge.shape),
            pltpu.SemaphoreType.DMA((7,)),
        ],
        *(
            pltpu.with_memory_space_constraint(value, pltpu.HBM)
            for value in (
                model_state,
                point_mass,
                inverse_mass,
                vert_diff,
                fall_rate,
                cloud_frac,
                tables,
            )
        ),
        spec=pl.BlockSpec(memory_space=pltpu.HBM),
    )
    from_y = exchanged(y_near, y_far, "gy")
    from_x = exchanged(x_near, x_far, "gx")
    corner_near, corner_far = call(
        functools.partial(forward_kernel, size_x, width),
        "forward",
        [corner, corner],
        [],
        *from_y,
    )
    from_corner = exchanged(corner_near, corner_far, "gx")
    total, x_near, x_far = call(
        functools.partial(second_kernel, size_x),
        "second",
        [whole, array(size_y + 2 * extra, padded), line],
        [scratch(columns, width), scratch(*edge.shape), scratch(*edge.shape)],
        total,
        masses,
        operator,
        coefs,
        *from_x,
        *from_y,
        *from_corner,
    )
    last_x = exchanged(x_near, x_far, "gx")
    if riding:
        pieces = [coefs, from_x[0], last_x[1]]
    else:
        pieces = [lax.all_gather(coefs, "gx")]
    (factors,) = call(
        functools.partial(factor_kernel, levels, span),
        "factors",
        [array(6 * levels, columns)],
        [],
        span_slot,
        *pieces,
    )
    (result,) = call(
        functools.partial(third_kernel, levels),
        "third",
        [array(size_x, size_y, width)],
        [scratch(columns, width), scratch(width, columns), scratch(levels, 16, columns)],
        here,
        hyper,
        total,
        masses,
        factors,
        *last_x,
    )
    return result


def solution(mesh):
    placed = (
        P("gx", "gy", None),
        P(),
        P("gx", "gy"),
        P("gx", "gy"),
        P("gx", "gy"),
        P("gy", None, "gx"),
        P("gy", None, "gx"),
        P("gy", None, "gx"),
    )
    return jax.shard_map(
        local, mesh=mesh, in_specs=placed, out_specs=P("gx", "gy", None), check_vma=False
    )
```

```python
import functools

import jax
import jax.numpy as jnp
import numpy as np
from jax import lax
from jax.experimental import pallas as pl
from jax.experimental.pallas import tpu as pltpu
from jax.sharding import PartitionSpec as P

VMEM = pl.BlockSpec(memory_space=pltpu.VMEM)
PARAMS = pltpu.CompilerParams(vmem_limit_bytes=16 * 1024 * 1024)


def second_table():
    nodes = np.array([-1.0, -1.0 / np.sqrt(5.0), 1.0 / np.sqrt(5.0), 1.0])
    deriv = np.zeros((4, 4))
    for i in range(4):
        for j in range(4):
            if i == j:
                deriv[i, j] = sum(1.0 / (nodes[i] - nodes[k]) for k in range(4) if k != i)
            else:
                upper = np.prod([nodes[i] - nodes[k] for k in range(4) if k != i])
                lower = np.prod([nodes[j] - nodes[k] for k in range(4) if k != j])
                deriv[i, j] = upper / (lower * (nodes[i] - nodes[j]))
    return deriv @ deriv


def laplacian_tables(size_x, size_y):
    second = second_table()
    lap = np.kron(np.kron(np.eye(size_x // 4), second), np.eye(size_y))
    lap = lap + np.kron(np.eye(size_x), np.kron(np.eye(size_y // 4), second))
    partner = np.zeros_like(lap)
    for x in range(size_x):
        for y in range(size_y):
            other = y - 1 if y % 4 == 0 else y + 1 if y % 4 == 3 else -1
            if 0 <= other < size_y:
                partner[x * size_y + y] = lap[x * size_y + other]
    return np.stack([lap, partner]).astype(np.float32)


def split(value):
    high = value.astype(jnp.bfloat16)
    return high, (value - high.astype(jnp.float32)).astype(jnp.bfloat16)


def product(left, right):
    left_high, left_low = left
    right_high, right_low = right
    dot = functools.partial(jnp.dot, preferred_element_type=jnp.float32)
    return dot(left_high, right_high) + (dot(left_high, right_low) + dot(left_low, right_high))


def to_column(plane, partner=False):
    size_x, size_y = plane.shape
    row = lax.broadcasted_iota(jnp.int32, (size_y, size_y), 0)
    lane = lax.broadcasted_iota(jnp.int32, (size_y, size_y), 1)
    if partner:
        row = jnp.where(row % 4 == 0, row - 1, jnp.where(row % 4 == 3, row + 1, -1))
    pick = row == lane
    parts = [
        jnp.sum(jnp.where(pick, plane[x : x + 1, :], 0.0), axis=1, keepdims=True)
        for x in range(size_x)
    ]
    return jnp.concatenate(parts, axis=0)


def even(axis):
    return lax.rem(lax.axis_index(axis), 2) == 0


def x_rows(count, size_y):
    near = jnp.where(even("gx"), count - size_y, 0)
    far = count - size_y - near
    return tuple(pl.ds(pl.multiple_of(start, size_y), size_y) for start in (near, far))


COEF_ROWS = 32


def write_coefs(message, start, coefs):
    rows, lanes = coefs.shape
    for i, first in enumerate(range(0, rows, COEF_ROWS)):
        part = coefs[first : min(first + COEF_ROWS, rows)]
        message[start : start + part.shape[0], i * lanes : (i + 1) * lanes] = part


def read_coefs(message, start, rows, lanes):
    parts = []
    for i, first in enumerate(range(0, rows, COEF_ROWS)):
        count = min(COEF_ROWS, rows - first)
        parts.append(message[start : start + count, i * lanes : (i + 1) * lanes])
    return jnp.concatenate(parts, axis=0)


def start_kernel(
    state,
    mass,
    inverse,
    diff,
    fall,
    cloud,
    tables,
    here,
    total,
    x_near,
    x_far,
    y_near,
    y_far,
    operator,
    columns,
    coefs,
    mass_here,
    inverse_here,
    tables_here,
    low,
    high,
    sems,
):
    size_x, size_y, width = state.shape
    levels = diff.shape[1]
    pairs = [(mass, mass_here), (tables, tables_here), (inverse, inverse_here), (state, here)]
    for i, source in enumerate((diff, fall, cloud)):
        pairs.append((source.at[0], coefs.at[i * levels : (i + 1) * levels]))
    copies = [
        pltpu.make_async_copy(source, target, sems.at[i])
        for i, (source, target) in enumerate(pairs)
    ]
    for copy in copies:
        copy.start()
    for copy in copies[:3]:
        copy.wait()
    own = to_column(mass_here[...])
    lane = lax.broadcasted_iota(jnp.int32, columns.shape, 1)
    partner = to_column(mass_here[...], True)
    inverses = to_column(inverse_here[...])
    columns[...] = jnp.where(lane == 0, own, jnp.where(lane == 1, inverses, partner))
    matrix = own * tables_here[0] + partner * tables_here[1]
    operator[...] = matrix
    copies[3].wait()
    total[...] = product(split(matrix), split(here[...].reshape(size_x * size_y, width)))
    for first, message in ((0, low), (size_y - 4, high)):
        for x in range(size_x):
            for i in range(4):
                row = x * size_y + first + i
                place = i * size_x + x
                message[place : place + 1, :width] = total[row : row + 1, :]
                message[place : place + 1, width : width + 2] = columns[row : row + 1, :2]
    y_near[...] = jnp.where(even("gy"), high[...], low[...])
    y_far[...] = jnp.where(even("gy"), low[...], high[...])
    near, far = x_rows(size_x * size_y, size_y)
    x_near[...] = total[near]
    x_far[:size_y, :width] = total[far]
    for copy in copies[4:]:
        copy.wait()
    if x_far.shape[0] > size_y:
        write_coefs(x_far, size_y, coefs)


def edge_rows(ref, y, size_x, size_y):
    return jnp.concatenate(
        [ref[x * size_y + y : x * size_y + y + 1, :] for x in range(size_x)], axis=0
    )


def node_column(values, start, count):
    row = lax.broadcasted_iota(jnp.int32, (count, 1), 0)
    result = jnp.zeros((count, 1), jnp.float32)
    for i, value in enumerate(values):
        result = jnp.where(row == start + i, float(value), result)
    return result


def edge_weights(columns, message, size_x, size_y, width, edge, line):
    second = second_table()
    other = size_x - 1 - edge
    low = line == 3
    y, first = (0, 0) if low else (size_y - 1, size_y - 8)
    rows = slice(edge * size_y + first, edge * size_y + first + 8)
    here, there = (slice(x * size_y + y, x * size_y + y + 1) for x in (edge, other))
    mass, inverse = columns[here, 0:1], columns[here, 1:2]
    beyond = slice(line * size_x + edge, line * size_x + edge + 1)
    beyond_mass = message[beyond, width : width + 1]

    def beyond_inverse(i, x):
        return message[i * size_x + x : i * size_x + x + 1, width + 1 : width + 2]

    if low:
        own, partner = node_column(second[:, 0], 0, 8), node_column(second[3:, 0], 4, 8)
    else:
        own, partner = node_column(second[:, 3], 4, 8), node_column(second[:1, 3], 3, 8)
    along = inverse * (own * columns[rows, 0:1] + partner * columns[rows, 2:3])
    lane = lax.broadcasted_iota(jnp.int32, (8, 128), 1) - width % 128
    place = lax.broadcasted_iota(jnp.int32, (8, 128), 0)
    tile = jnp.where(lane == line, along, 0.0)
    for i in range(4):
        value = float(second[line, i]) * beyond_mass * beyond_inverse(i, edge)
        if i == line:
            across = beyond_mass * beyond_inverse(line, edge) + mass * inverse
            value = value + float(second[edge, edge]) * across
        tile = tile + jnp.where((place == y - first) & (lane == i), value, 0.0)
    across = beyond_mass * beyond_inverse(line, other) + mass * columns[there, 1:2]
    value = float(second[edge, other]) * across
    return tile + jnp.where((place == y - first) & (lane == 4), value, 0.0)


def second_kernel(
    size_x,
    total,
    columns,
    operator,
    coefs,
    from_far,
    from_near,
    y_from_first,
    y_from_near,
    y_from_second,
    out,
    x_near,
    x_far,
    line_ends,
    inner,
    work,
    low,
    high,
):
    size_y, width = from_near.shape
    second = second_table()
    near, far = x_rows(size_x * size_y, size_y)
    work[...] = total[...]
    work[near] += from_near[...]
    work[far] += from_far[:size_y, :width]
    low[...] = jnp.where(even("gy"), y_from_first[...], y_from_near[...])
    high[...] = jnp.where(even("gy"), y_from_near[...], y_from_second[...])
    sides = ((low, 0, 3, 0), (high, size_y - 1, 0, size_y - 8))
    beyond = []
    for message, y, line, _ in sides:
        lines = [message[i * size_x : (i + 1) * size_x, :width] for i in range(4)]
        lines[line] = lines[line] + edge_rows(work, y, size_x, size_y)
        for x in range(size_x):
            work[x * size_y + y : x * size_y + y + 1, :] = lines[line][x : x + 1]
        for i in range(4):
            inverse = message[i * size_x : (i + 1) * size_x, width + 1 : width + 2]
            lines[i] = inverse * lines[i]
        value = sum(float(second[line, i]) * lines[i] for i in range(4))
        for x in range(size_x):
            value = value + node_column(second[:, x], 0, size_x) * lines[line][x : x + 1]
        mass = message[line * size_x : (line + 1) * size_x, width : width + 1]
        beyond.append(mass * value)
    out[...] = product(split(operator[...]), split(columns[:, 1:2] * work[...]))
    for (_, y, _, _), rows in zip(sides, beyond):
        for x in range(size_x):
            out[x * size_y + y : x * size_y + y + 1, :] += rows[x : x + 1]

    first, last = 0, size_x - 1
    x_near[:size_y, :width] = out[near]
    x_far[:size_y, :width] = out[far]
    for side, (message, y, line, start) in enumerate(sides):
        tiles = {
            edge: edge_weights(columns, message, size_x, size_y, width, edge, line)
            for edge in (first, last)
        }
        behind = slice(width % 128, 128)
        rows = slice(start, start + 8)
        x_near[rows, width:] = jnp.where(even("gx"), tiles[last], tiles[first])[:, behind]
        x_far[rows, width:] = jnp.where(even("gx"), tiles[first], tiles[last])[:, behind]
        for i in range(4):
            rows = [message[i * size_x + x : i * size_x + x + 1, :width] for x in (first, last)]
            at_near = jnp.where(even("gx"), rows[1], rows[0])
            at_far = jnp.where(even("gx"), rows[0], rows[1])
            place = size_y + 4 * side + i
            x_near[place : place + 1, :width] = at_near
            x_far[place : place + 1, :width] = at_far
            if i == line:
                line_ends[2 * side : 2 * side + 1, :] = at_far
                line_ends[2 * side + 1 : 2 * side + 2, :] = at_near
        mass = message[line * size_x : (line + 1) * size_x, width : width + 1]
        own = edge_rows(columns, y, size_x, size_y)
        weights = []
        for edge in (first, last):
            inverse = message[line * size_x + edge : line * size_x + edge + 1, width + 1 : width + 2]
            across = mass * inverse + own[:, 0:1] * own[edge : edge + 1, 1:2]
            weights.append(node_column(second[:, edge], 0, size_x) * across)
        lane = lax.broadcasted_iota(jnp.int32, (size_x, 128), 1)
        from_last = jnp.where(even("gx"), 0, 1)
        inner[side * size_x : (side + 1) * size_x, :] = jnp.where(
            lane == from_last, weights[1], weights[0]
        )
    if x_near.shape[0] > size_y + 8:
        write_coefs(x_near, size_y + 8, coefs)
        x_near[size_y + 8 + COEF_ROWS :, :] = from_far[size_y:, :]


def third_kernel(
    levels,
    state,
    hyper,
    total,
    masses,
    inner,
    factors,
    to_near,
    to_far,
    from_far,
    from_near,
    ends_near,
    ends_far,
    out,
    work,
    turned,
    values,
):
    columns, width = total.shape
    size_x, size_y, _ = state.shape
    variables = width // levels
    near = jnp.where(even("gx"), columns - size_y, 0)
    sides = ((0, 0, 3, 0), (1, size_y - 1, 0, size_y - 8))
    partners = (
        (near, to_near, from_near, from_far, ends_near, 0),
        (columns - size_y - near, to_far, from_far, from_near, ends_far, 1),
    )
    work[...] = total[...]
    for start, _, theirs, _, _, _ in partners:
        work[pl.ds(pl.multiple_of(start, size_y), size_y), :] += theirs[:size_y, :width]
    for side, y, line, first in sides:
        place = size_y + 4 * side
        tile = slice(first, first + 8)
        for start, mine, theirs, others, ends, which in partners:
            terms = [
                (weights, i, rows, place + i)
                for i in range(4)
                for weights, rows in ((mine, theirs), (theirs, mine))
            ]
            terms += [(mine, 4, others, place + line), (theirs, 4, ends, 2 * side + which)]
            added = sum(
                weights[tile, width + i : width + i + 1] * rows[row : row + 1, :width]
                for weights, i, rows, row in terms
            )
            work[pl.ds(pl.multiple_of(start + first, 8), 8), :] += added
        for x in range(1, size_x - 1):
            row, weight = x * size_y + y, side * size_x + x
            work[row : row + 1, :] += (
                inner[weight : weight + 1, 0:1] * from_near[place + line : place + line + 1, :width]
                + inner[weight : weight + 1, 1:2] * from_far[place + line : place + line + 1, :width]
            )
    twice = masses[:, 1:2] * work[...]
    turned[...] = (state[...].reshape(columns, width) - hyper[...] * twice).T
    scale, down, up, keep, flow, cloud = (
        factors.at[i * levels : (i + 1) * levels] for i in range(6)
    )
    value = jnp.zeros((variables, columns), jnp.float32)
    for k in range(levels):
        rows = turned[pl.ds(k, variables, stride=levels), :]
        value = rows * scale[k : k + 1, :] + down[k : k + 1, :] * value
        values[k, :variables, :] = value
    solved = jnp.zeros((variables, columns), jnp.float32)
    for k in reversed(range(levels)):
        solved = values[k, :variables, :] + up[k : k + 1, :] * solved
        turned[pl.ds(k, variables, stride=levels), :] = solved
    heat, vapour, liquid = (turned.at[i * levels : (i + 1) * levels] for i in range(3))
    condensed = cloud[...] * 0.5 * jnp.maximum(vapour[...] - 0.3 * heat[...], 0.0)
    vapour[...] = vapour[...] - condensed
    heat[...] = heat[...] + 2.0 * condensed
    liquid[...] = (liquid[...] + condensed) * keep[...]
    settled = jnp.zeros((1, columns), jnp.float32)
    for k in range(levels):
        settled = liquid[k : k + 1, :] + flow[k : k + 1, :] * settled
        liquid[k : k + 1, :] = settled
    out[...] = turned[...].T.reshape(out.shape)


def factor_kernel(levels, span, slots, *refs):
    rows = 3 * levels
    size_x, size_y = slots.shape
    columns = size_x * size_y
    factors = refs[-1]
    if len(refs) == 4:
        own, from_far, from_near = refs[:3]
        here = lax.axis_index("gx")
        pieces = [
            (here, own[...]),
            (here ^ 3, read_coefs(from_far, size_y, rows, span)),
            (here ^ 1, read_coefs(from_near, size_y + 8, rows, span)),
            (here ^ 2, read_coefs(from_near, size_y + 8 + COEF_ROWS, rows, span)),
        ]
    else:
        pieces = [(peer, refs[0][peer]) for peer in range(refs[0].shape[0])]
    picked = jnp.zeros((rows, columns), jnp.float32)
    wanted = jnp.concatenate([slots[x : x + 1, :] for x in range(size_x)], axis=1)
    for owner, rest in pieces:
        entry = lax.broadcasted_iota(jnp.int32, (span, columns), 0) + owner * span
        choice = (entry == wanted).astype(jnp.float32).astype(jnp.bfloat16)
        for _ in range(3):
            part = rest.astype(jnp.bfloat16)
            rest = rest - part.astype(jnp.float32)
            picked = picked + jnp.dot(part, choice, preferred_element_type=jnp.float32)
    mixing, falling, covered = (picked[i * levels : (i + 1) * levels] for i in range(3))
    scale, down, up, keep, flow, cover = (
        factors.at[i * levels : (i + 1) * levels] for i in range(6)
    )
    gain = jnp.zeros((1, columns), jnp.float32)
    for k in range(levels):
        above = mixing[k : k + 1] if k else jnp.zeros_like(gain)
        below = mixing[k + 1 : k + 2] if k + 1 < levels else jnp.zeros_like(gain)
        centre = 1.0 + above + (below if k + 1 < levels else mixing[:1])
        inverse = 1.0 / (centre - above * gain)
        gain = below * inverse
        scale[k : k + 1, :] = inverse
        down[k : k + 1, :] = above * inverse
        up[k : k + 1, :] = gain
    kept = 1.0 / (1.0 + falling)
    keep[...] = kept
    flow[:1, :] = jnp.zeros((1, columns), jnp.float32)
    flow[1:, :] = falling[:-1] * kept[1:]
    cover[...] = covered


def swapped(value, axis, partner):
    return lax.ppermute(value, axis, [(i, partner(i)) for i in range(lax.axis_size(axis))])


def exchanged(near, far, axis):
    size = lax.axis_size(axis)
    from_far = swapped(far, axis, lambda i: (i + (1 if i % 2 else -1)) % size)
    from_near = swapped(near, axis, lambda i: i ^ 1)
    return from_far, from_near


def one_way(value, axis, odd):
    size = lax.axis_size(axis)
    step = 1 if odd else -1
    return lax.ppermute(value, axis, [(i, (i + step) % size) for i in range(odd, size, 2)])


def local(
    model_state, hyper_coef, point_mass, inverse_mass, span_slot, vert_diff, fall_rate, cloud_frac
):
    size_x, size_y, width = model_state.shape
    levels, span = vert_diff.shape[1:]
    columns = size_x * size_y
    hyper = hyper_coef.reshape(1, width)
    padded = -(-(width + 5) // 128) * 128
    tables = jnp.asarray(laplacian_tables(size_x, size_y))

    def array(*shape):
        return jax.ShapeDtypeStruct(shape, jnp.float32)

    def scratch(*shape):
        return pltpu.VMEM(shape, jnp.float32)

    def call(kernel, name, outs, scratches, *operands, spec=VMEM):
        return pl.pallas_call(
            kernel,
            out_shape=outs,
            in_specs=[spec] * len(operands),
            out_specs=[VMEM] * len(outs),
            scratch_shapes=scratches,
            compiler_params=PARAMS,
            name=name,
        )(*operands)

    riding = lax.axis_size("gx") == 4
    extra = COEF_ROWS if riding else 0
    whole, line = array(columns, width), array(size_y, width)
    edge = array(4 * size_x, padded)
    here, total, x_near, x_far, y_near, y_far, operator, masses, coefs = call(
        start_kernel,
        "start",
        [
            array(size_x, size_y, width),
            whole,
            line,
            array(size_y + extra, padded),
            edge,
            edge,
            array(columns, columns),
            array(columns, 128),
            array(3 * levels, span),
        ],
        [
            scratch(size_x, size_y),
            scratch(size_x, size_y),
            scratch(*tables.shape),
            scratch(*edge.shape),
            scratch(*edge.shape),
            pltpu.SemaphoreType.DMA((7,)),
        ],
        *(
            pltpu.with_memory_space_constraint(value, pltpu.HBM)
            for value in (
                model_state,
                point_mass,
                inverse_mass,
                vert_diff,
                fall_rate,
                cloud_frac,
                tables,
            )
        ),
        spec=pl.BlockSpec(memory_space=pltpu.HBM),
    )
    from_x = exchanged(x_near, x_far, "gx")
    y_last, _ = lax.optimization_barrier((y_far, from_x[1]))
    total, x_near, x_far, line_ends, inner = call(
        functools.partial(second_kernel, size_x),
        "second",
        [
            whole,
            array(size_y + 8 + 2 * extra, padded),
            array(size_y + 8, padded),
            array(4, width),
            array(2 * size_x, 128),
        ],
        [scratch(columns, width), scratch(*edge.shape), scratch(*edge.shape)],
        total,
        masses,
        operator,
        coefs,
        *from_x,
        one_way(y_far, "gy", 1),
        swapped(y_near, "gy", lambda i: i ^ 1),
        one_way(y_last, "gy", 0),
    )
    last_x = exchanged(x_near, x_far, "gx")
    peers = lax.axis_size("gx")
    ends_near = swapped(line_ends, "gx", lambda i: (i + (2 if i % 2 else -2)) % peers)
    ends_far = ends_near
    if peers != 4:
        ends_far = swapped(line_ends, "gx", lambda i: (i - (2 if i % 2 else -2)) % peers)
    if riding:
        pieces = [coefs, from_x[0], last_x[1]]
    else:
        pieces = [lax.all_gather(coefs, "gx")]
    (factors,) = call(
        functools.partial(factor_kernel, levels, span),
        "factors",
        [array(6 * levels, columns)],
        [],
        span_slot,
        *pieces,
    )
    (result,) = call(
        functools.partial(third_kernel, levels),
        "third",
        [array(size_x, size_y, width)],
        [scratch(columns, width), scratch(width, columns), scratch(levels, 16, columns)],
        here,
        hyper,
        total,
        masses,
        inner,
        factors,
        x_near,
        x_far,
        *last_x,
        ends_near,
        ends_far,
    )
    return result


def solution(mesh):
    placed = (
        P("gx", "gy", None),
        P(),
        P("gx", "gy"),
        P("gx", "gy"),
        P("gx", "gy"),
        P("gy", None, "gx"),
        P("gy", None, "gx"),
        P("gy", None, "gx"),
    )
    return jax.shard_map(
        local, mesh=mesh, in_specs=placed, out_specs=P("gx", "gy", None), check_vma=False
    )
```

```python
import functools

import jax
import jax.numpy as jnp
import numpy as np
from jax import lax
from jax.experimental import pallas as pl
from jax.experimental.pallas import tpu as pltpu
from jax.sharding import PartitionSpec as P

VMEM = pl.BlockSpec(memory_space=pltpu.VMEM)
PARAMS = pltpu.CompilerParams(vmem_limit_bytes=16 * 1024 * 1024)


def second_table():
    nodes = np.array([-1.0, -1.0 / np.sqrt(5.0), 1.0 / np.sqrt(5.0), 1.0])
    deriv = np.zeros((4, 4))
    for i in range(4):
        for j in range(4):
            if i == j:
                deriv[i, j] = sum(1.0 / (nodes[i] - nodes[k]) for k in range(4) if k != i)
            else:
                upper = np.prod([nodes[i] - nodes[k] for k in range(4) if k != i])
                lower = np.prod([nodes[j] - nodes[k] for k in range(4) if k != j])
                deriv[i, j] = upper / (lower * (nodes[i] - nodes[j]))
    return deriv @ deriv


def laplacian_tables(size_x, size_y):
    second = second_table()
    lap = np.kron(np.kron(np.eye(size_x // 4), second), np.eye(size_y))
    lap = lap + np.kron(np.eye(size_x), np.kron(np.eye(size_y // 4), second))
    partner = np.zeros_like(lap)
    for x in range(size_x):
        for y in range(size_y):
            other = y - 1 if y % 4 == 0 else y + 1 if y % 4 == 3 else -1
            if 0 <= other < size_y:
                partner[x * size_y + y] = lap[x * size_y + other]
    return np.stack([lap, partner]).astype(np.float32)


def split(value):
    high = value.astype(jnp.bfloat16)
    return high, (value - high.astype(jnp.float32)).astype(jnp.bfloat16)


def product(left, right):
    left_high, left_low = left
    right_high, right_low = right
    dot = functools.partial(jnp.dot, preferred_element_type=jnp.float32)
    return dot(left_high, right_high) + (dot(left_high, right_low) + dot(left_low, right_high))


def to_column(plane, partner=False):
    size_x, size_y = plane.shape
    row = lax.broadcasted_iota(jnp.int32, (size_y, size_y), 0)
    lane = lax.broadcasted_iota(jnp.int32, (size_y, size_y), 1)
    if partner:
        row = jnp.where(row % 4 == 0, row - 1, jnp.where(row % 4 == 3, row + 1, -1))
    pick = row == lane
    parts = [
        jnp.sum(jnp.where(pick, plane[x : x + 1, :], 0.0), axis=1, keepdims=True)
        for x in range(size_x)
    ]
    return jnp.concatenate(parts, axis=0)


def even(axis):
    return lax.rem(lax.axis_index(axis), 2) == 0


def x_rows(count, size_y):
    near = jnp.where(even("gx"), count - size_y, 0)
    far = count - size_y - near
    return tuple(pl.ds(pl.multiple_of(start, size_y), size_y) for start in (near, far))


COEF_ROWS = 32


def write_coefs(message, start, coefs):
    rows, lanes = coefs.shape
    for i, first in enumerate(range(0, rows, COEF_ROWS)):
        part = coefs[first : min(first + COEF_ROWS, rows)]
        message[start : start + part.shape[0], i * lanes : (i + 1) * lanes] = part


def read_coefs(message, start, rows, lanes):
    parts = []
    for i, first in enumerate(range(0, rows, COEF_ROWS)):
        count = min(COEF_ROWS, rows - first)
        parts.append(message[start : start + count, i * lanes : (i + 1) * lanes])
    return jnp.concatenate(parts, axis=0)


def start_kernel(
    state,
    mass,
    inverse,
    diff,
    fall,
    cloud,
    tables,
    here,
    total,
    x_near,
    x_far,
    low,
    high,
    operator,
    columns,
    coefs,
    mass_here,
    inverse_here,
    tables_here,
    sems,
):
    size_x, size_y, width = state.shape
    levels = diff.shape[1]
    pairs = [(mass, mass_here), (tables, tables_here), (inverse, inverse_here), (state, here)]
    for i, source in enumerate((diff, fall, cloud)):
        pairs.append((source.at[0], coefs.at[i * levels : (i + 1) * levels]))
    copies = [
        pltpu.make_async_copy(source, target, sems.at[i])
        for i, (source, target) in enumerate(pairs)
    ]
    for copy in copies:
        copy.start()
    for copy in copies[:3]:
        copy.wait()
    own = to_column(mass_here[...])
    lane = lax.broadcasted_iota(jnp.int32, columns.shape, 1)
    partner = to_column(mass_here[...], True)
    inverses = to_column(inverse_here[...])
    columns[...] = jnp.where(lane == 0, own, jnp.where(lane == 1, inverses, partner))
    matrix = own * tables_here[0] + partner * tables_here[1]
    operator[...] = matrix
    copies[3].wait()
    total[...] = product(split(matrix), split(here[...].reshape(size_x * size_y, width)))
    for first, message in ((0, low), (size_y - 4, high)):
        for x in range(size_x):
            for i in range(4):
                row = x * size_y + first + i
                place = i * size_x + x
                message[place : place + 1, :width] = total[row : row + 1, :]
                message[place : place + 1, width : width + 2] = columns[row : row + 1, :2]
    near, far = x_rows(size_x * size_y, size_y)
    x_near[...] = total[near]
    x_far[:size_y, :width] = total[far]
    for copy in copies[4:]:
        copy.wait()
    if x_far.shape[0] > size_y:
        write_coefs(x_far, size_y, coefs)


def edge_rows(ref, y, size_x, size_y):
    return jnp.concatenate(
        [ref[x * size_y + y : x * size_y + y + 1, :] for x in range(size_x)], axis=0
    )


def node_column(values, start, count):
    row = lax.broadcasted_iota(jnp.int32, (count, 1), 0)
    result = jnp.zeros((count, 1), jnp.float32)
    for i, value in enumerate(values):
        result = jnp.where(row == start + i, float(value), result)
    return result


def edge_weights(columns, message, size_x, size_y, width, edge, line):
    second = second_table()
    other = size_x - 1 - edge
    low = line == 3
    y, first = (0, 0) if low else (size_y - 1, size_y - 8)
    rows = slice(edge * size_y + first, edge * size_y + first + 8)
    here, there = (slice(x * size_y + y, x * size_y + y + 1) for x in (edge, other))
    mass, inverse = columns[here, 0:1], columns[here, 1:2]
    beyond = slice(line * size_x + edge, line * size_x + edge + 1)
    beyond_mass = message[beyond, width : width + 1]

    def beyond_inverse(i, x):
        return message[i * size_x + x : i * size_x + x + 1, width + 1 : width + 2]

    if low:
        own, partner = node_column(second[:, 0], 0, 8), node_column(second[3:, 0], 4, 8)
    else:
        own, partner = node_column(second[:, 3], 4, 8), node_column(second[:1, 3], 3, 8)
    along = inverse * (own * columns[rows, 0:1] + partner * columns[rows, 2:3])
    lane = lax.broadcasted_iota(jnp.int32, (8, 128), 1) - width % 128
    place = lax.broadcasted_iota(jnp.int32, (8, 128), 0)
    tile = jnp.where(lane == line, along, 0.0)
    for i in range(4):
        value = float(second[line, i]) * beyond_mass * beyond_inverse(i, edge)
        if i == line:
            across = beyond_mass * beyond_inverse(line, edge) + mass * inverse
            value = value + float(second[edge, edge]) * across
        tile = tile + jnp.where((place == y - first) & (lane == i), value, 0.0)
    across = beyond_mass * beyond_inverse(line, other) + mass * columns[there, 1:2]
    value = float(second[edge, other]) * across
    return tile + jnp.where((place == y - first) & (lane == 4), value, 0.0)


def second_kernel(
    size_x,
    total,
    columns,
    operator,
    coefs,
    from_far,
    from_near,
    low,
    high,
    out,
    x_near,
    x_far,
    line_ends,
    inner,
    work,
):
    size_y, width = from_near.shape
    second = second_table()
    near, far = x_rows(size_x * size_y, size_y)
    work[...] = total[...]
    work[near] += from_near[...]
    work[far] += from_far[:size_y, :width]
    sides = ((low, 0, 3, 0), (high, size_y - 1, 0, size_y - 8))
    beyond = []
    for message, y, line, _ in sides:
        lines = [message[i * size_x : (i + 1) * size_x, :width] for i in range(4)]
        lines[line] = lines[line] + edge_rows(work, y, size_x, size_y)
        for x in range(size_x):
            work[x * size_y + y : x * size_y + y + 1, :] = lines[line][x : x + 1]
        for i in range(4):
            inverse = message[i * size_x : (i + 1) * size_x, width + 1 : width + 2]
            lines[i] = inverse * lines[i]
        value = sum(float(second[line, i]) * lines[i] for i in range(4))
        for x in range(size_x):
            value = value + node_column(second[:, x], 0, size_x) * lines[line][x : x + 1]
        mass = message[line * size_x : (line + 1) * size_x, width : width + 1]
        beyond.append(mass * value)
    out[...] = product(split(operator[...]), split(columns[:, 1:2] * work[...]))
    for (_, y, _, _), rows in zip(sides, beyond):
        for x in range(size_x):
            out[x * size_y + y : x * size_y + y + 1, :] += rows[x : x + 1]

    first, last = 0, size_x - 1
    x_near[:size_y, :width] = out[near]
    x_far[:size_y, :width] = out[far]
    for side, (message, y, line, start) in enumerate(sides):
        tiles = {
            edge: edge_weights(columns, message, size_x, size_y, width, edge, line)
            for edge in (first, last)
        }
        behind = slice(width % 128, 128)
        rows = slice(start, start + 8)
        x_near[rows, width:] = jnp.where(even("gx"), tiles[last], tiles[first])[:, behind]
        x_far[rows, width:] = jnp.where(even("gx"), tiles[first], tiles[last])[:, behind]
        for i in range(4):
            rows = [message[i * size_x + x : i * size_x + x + 1, :width] for x in (first, last)]
            at_near = jnp.where(even("gx"), rows[1], rows[0])
            at_far = jnp.where(even("gx"), rows[0], rows[1])
            place = size_y + 4 * side + i
            x_near[place : place + 1, :width] = at_near
            x_far[place : place + 1, :width] = at_far
            if i == line:
                line_ends[2 * side : 2 * side + 1, :] = at_far
                line_ends[2 * side + 1 : 2 * side + 2, :] = at_near
        mass = message[line * size_x : (line + 1) * size_x, width : width + 1]
        own = edge_rows(columns, y, size_x, size_y)
        weights = []
        for edge in (first, last):
            inverse = message[line * size_x + edge : line * size_x + edge + 1, width + 1 : width + 2]
            across = mass * inverse + own[:, 0:1] * own[edge : edge + 1, 1:2]
            weights.append(node_column(second[:, edge], 0, size_x) * across)
        lane = lax.broadcasted_iota(jnp.int32, (size_x, 128), 1)
        from_last = jnp.where(even("gx"), 0, 1)
        inner[side * size_x : (side + 1) * size_x, :] = jnp.where(
            lane == from_last, weights[1], weights[0]
        )
    if x_near.shape[0] > size_y + 8:
        write_coefs(x_near, size_y + 8, coefs)
        x_near[size_y + 8 + COEF_ROWS :, :] = from_far[size_y:, :]


def third_kernel(
    levels,
    state,
    hyper,
    total,
    masses,
    inner,
    factors,
    to_near,
    to_far,
    from_far,
    from_near,
    ends_near,
    ends_far,
    out,
    work,
    turned,
    values,
):
    columns, width = total.shape
    size_x, size_y, _ = state.shape
    variables = width // levels
    near = jnp.where(even("gx"), columns - size_y, 0)
    sides = ((0, 0, 3, 0), (1, size_y - 1, 0, size_y - 8))
    partners = (
        (near, to_near, from_near, from_far, ends_near, 0),
        (columns - size_y - near, to_far, from_far, from_near, ends_far, 1),
    )
    work[...] = total[...]
    for start, _, theirs, _, _, _ in partners:
        work[pl.ds(pl.multiple_of(start, size_y), size_y), :] += theirs[:size_y, :width]
    for side, y, line, first in sides:
        place = size_y + 4 * side
        tile = slice(first, first + 8)
        for start, mine, theirs, others, ends, which in partners:
            terms = [
                (weights, i, rows, place + i)
                for i in range(4)
                for weights, rows in ((mine, theirs), (theirs, mine))
            ]
            terms += [(mine, 4, others, place + line), (theirs, 4, ends, 2 * side + which)]
            added = sum(
                weights[tile, width + i : width + i + 1] * rows[row : row + 1, :width]
                for weights, i, rows, row in terms
            )
            work[pl.ds(pl.multiple_of(start + first, 8), 8), :] += added
        for x in range(1, size_x - 1):
            row, weight = x * size_y + y, side * size_x + x
            work[row : row + 1, :] += (
                inner[weight : weight + 1, 0:1] * from_near[place + line : place + line + 1, :width]
                + inner[weight : weight + 1, 1:2] * from_far[place + line : place + line + 1, :width]
            )
    twice = masses[:, 1:2] * work[...]
    turned[...] = (state[...].reshape(columns, width) - hyper[...] * twice).T
    scale, down, up, keep, flow, cloud = (
        factors.at[i * levels : (i + 1) * levels] for i in range(6)
    )
    value = jnp.zeros((variables, columns), jnp.float32)
    for k in range(levels):
        rows = turned[pl.ds(k, variables, stride=levels), :]
        value = rows * scale[k : k + 1, :] + down[k : k + 1, :] * value
        values[k, :variables, :] = value
    solved = jnp.zeros((variables, columns), jnp.float32)
    for k in reversed(range(levels)):
        solved = values[k, :variables, :] + up[k : k + 1, :] * solved
        turned[pl.ds(k, variables, stride=levels), :] = solved
    heat, vapour, liquid = (turned.at[i * levels : (i + 1) * levels] for i in range(3))
    condensed = cloud[...] * 0.5 * jnp.maximum(vapour[...] - 0.3 * heat[...], 0.0)
    vapour[...] = vapour[...] - condensed
    heat[...] = heat[...] + 2.0 * condensed
    liquid[...] = (liquid[...] + condensed) * keep[...]
    settled = jnp.zeros((1, columns), jnp.float32)
    for k in range(levels):
        settled = liquid[k : k + 1, :] + flow[k : k + 1, :] * settled
        liquid[k : k + 1, :] = settled
    out[...] = turned[...].T.reshape(out.shape)


def factor_kernel(levels, span, slots, *refs):
    rows = 3 * levels
    size_x, size_y = slots.shape
    columns = size_x * size_y
    factors = refs[-1]
    if len(refs) == 4:
        own, from_far, from_near = refs[:3]
        here = lax.axis_index("gx")
        pieces = [
            (here, own[...]),
            (here ^ 3, read_coefs(from_far, size_y, rows, span)),
            (here ^ 1, read_coefs(from_near, size_y + 8, rows, span)),
            (here ^ 2, read_coefs(from_near, size_y + 8 + COEF_ROWS, rows, span)),
        ]
    else:
        pieces = [(peer, refs[0][peer]) for peer in range(refs[0].shape[0])]
    picked = jnp.zeros((rows, columns), jnp.float32)
    wanted = jnp.concatenate([slots[x : x + 1, :] for x in range(size_x)], axis=1)
    for owner, rest in pieces:
        entry = lax.broadcasted_iota(jnp.int32, (span, columns), 0) + owner * span
        choice = (entry == wanted).astype(jnp.float32).astype(jnp.bfloat16)
        for _ in range(3):
            part = rest.astype(jnp.bfloat16)
            rest = rest - part.astype(jnp.float32)
            picked = picked + jnp.dot(part, choice, preferred_element_type=jnp.float32)
    mixing, falling, covered = (picked[i * levels : (i + 1) * levels] for i in range(3))
    scale, down, up, keep, flow, cover = (
        factors.at[i * levels : (i + 1) * levels] for i in range(6)
    )
    gain = jnp.zeros((1, columns), jnp.float32)
    for k in range(levels):
        above = mixing[k : k + 1] if k else jnp.zeros_like(gain)
        below = mixing[k + 1 : k + 2] if k + 1 < levels else jnp.zeros_like(gain)
        centre = 1.0 + above + (below if k + 1 < levels else mixing[:1])
        inverse = 1.0 / (centre - above * gain)
        gain = below * inverse
        scale[k : k + 1, :] = inverse
        down[k : k + 1, :] = above * inverse
        up[k : k + 1, :] = gain
    kept = 1.0 / (1.0 + falling)
    keep[...] = kept
    flow[:1, :] = jnp.zeros((1, columns), jnp.float32)
    flow[1:, :] = falling[:-1] * kept[1:]
    cover[...] = covered


def swapped(value, axis, partner):
    return lax.ppermute(value, axis, [(i, partner(i)) for i in range(lax.axis_size(axis))])


def exchanged(near, far, axis):
    size = lax.axis_size(axis)
    from_far = swapped(far, axis, lambda i: (i + (1 if i % 2 else -1)) % size)
    from_near = swapped(near, axis, lambda i: i ^ 1)
    return from_far, from_near


def shifted(value, axis, step):
    size = lax.axis_size(axis)
    return lax.ppermute(value, axis, [(i, (i + step) % size) for i in range(size)])


def local(
    model_state, hyper_coef, point_mass, inverse_mass, span_slot, vert_diff, fall_rate, cloud_frac
):
    size_x, size_y, width = model_state.shape
    levels, span = vert_diff.shape[1:]
    columns = size_x * size_y
    hyper = hyper_coef.reshape(1, width)
    padded = -(-(width + 5) // 128) * 128
    tables = jnp.asarray(laplacian_tables(size_x, size_y))

    def array(*shape):
        return jax.ShapeDtypeStruct(shape, jnp.float32)

    def scratch(*shape):
        return pltpu.VMEM(shape, jnp.float32)

    def call(kernel, name, outs, scratches, *operands, spec=VMEM):
        return pl.pallas_call(
            kernel,
            out_shape=outs,
            in_specs=[spec] * len(operands),
            out_specs=[VMEM] * len(outs),
            scratch_shapes=scratches,
            compiler_params=PARAMS,
            name=name,
        )(*operands)

    riding = lax.axis_size("gx") == 4
    extra = COEF_ROWS if riding else 0
    whole, line = array(columns, width), array(size_y, width)
    edge = array(4 * size_x, padded)
    here, total, x_near, x_far, y_low, y_high, operator, masses, coefs = call(
        start_kernel,
        "start",
        [
            array(size_x, size_y, width),
            whole,
            line,
            array(size_y + extra, padded),
            edge,
            edge,
            array(columns, columns),
            array(columns, 128),
            array(3 * levels, span),
        ],
        [
            scratch(size_x, size_y),
            scratch(size_x, size_y),
            scratch(*tables.shape),
            pltpu.SemaphoreType.DMA((7,)),
        ],
        *(
            pltpu.with_memory_space_constraint(value, pltpu.HBM)
            for value in (
                model_state,
                point_mass,
                inverse_mass,
                vert_diff,
                fall_rate,
                cloud_frac,
                tables,
            )
        ),
        spec=pl.BlockSpec(memory_space=pltpu.HBM),
    )
    from_x = exchanged(x_near, x_far, "gx")
    total, x_near, x_far, line_ends, inner = call(
        functools.partial(second_kernel, size_x),
        "second",
        [
            whole,
            array(size_y + 8 + 2 * extra, padded),
            array(size_y + 8, padded),
            array(4, width),
            array(2 * size_x, 128),
        ],
        [scratch(columns, width)],
        total,
        masses,
        operator,
        coefs,
        *from_x,
        shifted(y_high, "gy", 1),
        shifted(y_low, "gy", -1),
    )
    last_x = exchanged(x_near, x_far, "gx")
    peers = lax.axis_size("gx")
    ends_near = swapped(line_ends, "gx", lambda i: (i + (2 if i % 2 else -2)) % peers)
    ends_far = ends_near
    if peers != 4:
        ends_far = swapped(line_ends, "gx", lambda i: (i - (2 if i % 2 else -2)) % peers)
    if riding:
        pieces = [coefs, from_x[0], last_x[1]]
    else:
        pieces = [lax.all_gather(coefs, "gx")]
    (factors,) = call(
        functools.partial(factor_kernel, levels, span),
        "factors",
        [array(6 * levels, columns)],
        [],
        span_slot,
        *pieces,
    )
    (result,) = call(
        functools.partial(third_kernel, levels),
        "third",
        [array(size_x, size_y, width)],
        [scratch(columns, width), scratch(width, columns), scratch(levels, 16, columns)],
        here,
        hyper,
        total,
        masses,
        inner,
        factors,
        x_near,
        x_far,
        *last_x,
        ends_near,
        ends_far,
    )
    return result


def solution(mesh):
    placed = (
        P("gx", "gy", None),
        P(),
        P("gx", "gy"),
        P("gx", "gy"),
        P("gx", "gy"),
        P("gy", None, "gx"),
        P("gy", None, "gx"),
        P("gy", None, "gx"),
    )
    return jax.shard_map(
        local, mesh=mesh, in_specs=placed, out_specs=P("gx", "gy", None), check_vma=False
    )
```

```python
import functools

import jax
import jax.numpy as jnp
import numpy as np
from jax import lax
from jax.experimental import pallas as pl
from jax.experimental.pallas import tpu as pltpu
from jax.sharding import PartitionSpec as P

VMEM = pl.BlockSpec(memory_space=pltpu.VMEM)
LONG = pl.CostEstimate(flops=100_000_000_000, bytes_accessed=30_000_000, transcendentals=0)
PARAMS = pltpu.CompilerParams(vmem_limit_bytes=16 * 1024 * 1024)


def second_table():
    nodes = np.array([-1.0, -1.0 / np.sqrt(5.0), 1.0 / np.sqrt(5.0), 1.0])
    deriv = np.zeros((4, 4))
    for i in range(4):
        for j in range(4):
            if i == j:
                deriv[i, j] = sum(1.0 / (nodes[i] - nodes[k]) for k in range(4) if k != i)
            else:
                upper = np.prod([nodes[i] - nodes[k] for k in range(4) if k != i])
                lower = np.prod([nodes[j] - nodes[k] for k in range(4) if k != j])
                deriv[i, j] = upper / (lower * (nodes[i] - nodes[j]))
    return deriv @ deriv


def laplacian_tables(size_x, size_y):
    second = second_table()
    lap = np.kron(np.kron(np.eye(size_x // 4), second), np.eye(size_y))
    lap = lap + np.kron(np.eye(size_x), np.kron(np.eye(size_y // 4), second))
    partner = np.zeros_like(lap)
    for x in range(size_x):
        for y in range(size_y):
            other = y - 1 if y % 4 == 0 else y + 1 if y % 4 == 3 else -1
            if 0 <= other < size_y:
                partner[x * size_y + y] = lap[x * size_y + other]
    return np.stack([lap, partner]).astype(np.float32)


def split(value):
    high = value.astype(jnp.bfloat16)
    return high, (value - high.astype(jnp.float32)).astype(jnp.bfloat16)


def product(left, right):
    left_high, left_low = left
    right_high, right_low = right
    dot = functools.partial(jnp.dot, preferred_element_type=jnp.float32)
    return dot(left_high, right_high) + (dot(left_high, right_low) + dot(left_low, right_high))


def to_column(plane, partner=False):
    size_x, size_y = plane.shape
    row = lax.broadcasted_iota(jnp.int32, (size_y, size_y), 0)
    lane = lax.broadcasted_iota(jnp.int32, (size_y, size_y), 1)
    if partner:
        row = jnp.where(row % 4 == 0, row - 1, jnp.where(row % 4 == 3, row + 1, -1))
    pick = row == lane
    parts = [
        jnp.sum(jnp.where(pick, plane[x : x + 1, :], 0.0), axis=1, keepdims=True)
        for x in range(size_x)
    ]
    return jnp.concatenate(parts, axis=0)


def even(axis):
    return lax.rem(lax.axis_index(axis), 2) == 0


def x_rows(count, size_y):
    near = jnp.where(even("gx"), count - size_y, 0)
    far = count - size_y - near
    return tuple(pl.ds(pl.multiple_of(start, size_y), size_y) for start in (near, far))


COEF_ROWS = 32


def write_coefs(message, start, coefs):
    rows, lanes = coefs.shape
    for i, first in enumerate(range(0, rows, COEF_ROWS)):
        part = coefs[first : min(first + COEF_ROWS, rows)]
        message[start : start + part.shape[0], i * lanes : (i + 1) * lanes] = part


def read_coefs(message, start, rows, lanes):
    parts = []
    for i, first in enumerate(range(0, rows, COEF_ROWS)):
        count = min(COEF_ROWS, rows - first)
        parts.append(message[start : start + count, i * lanes : (i + 1) * lanes])
    return jnp.concatenate(parts, axis=0)


def edge_rows(ref, y, size_x, size_y):
    return jnp.concatenate(
        [ref[x * size_y + y : x * size_y + y + 1, :] for x in range(size_x)], axis=0
    )


def start_kernel(
    state,
    mass,
    inverse,
    diff,
    fall,
    cloud,
    tables,
    here,
    total,
    x_near,
    x_far,
    low,
    high,
    operator,
    columns,
    coefs,
    mass_here,
    inverse_here,
    tables_here,
    sems,
):
    size_x, size_y, width = state.shape
    levels = diff.shape[1]
    pairs = [(mass, mass_here), (tables, tables_here), (inverse, inverse_here), (state, here)]
    for i, source in enumerate((diff, fall, cloud)):
        pairs.append((source.at[0], coefs.at[i * levels : (i + 1) * levels]))
    copies = [
        pltpu.make_async_copy(source, target, sems.at[i])
        for i, (source, target) in enumerate(pairs)
    ]
    for copy in copies:
        copy.start()
    for copy in copies[:3]:
        copy.wait()
    own = to_column(mass_here[...])
    lane = lax.broadcasted_iota(jnp.int32, columns.shape, 1)
    partner = to_column(mass_here[...], True)
    inverses = to_column(inverse_here[...])
    columns[...] = jnp.where(lane == 0, own, jnp.where(lane == 1, inverses, partner))
    matrix = own * tables_here[0] + partner * tables_here[1]
    operator[...] = matrix
    matrix = split(matrix)
    copies[3].wait()
    total[...] = product(matrix, split(here[...].reshape(size_x * size_y, width)))
    near, far = x_rows(size_x * size_y, size_y)
    x_near[:size_y, :width] = total[near]
    x_far[:, :width] = total[far]
    for first, message in ((0, low), (size_y - 4, high)):
        for i in range(4):
            rows = slice(i * size_x, (i + 1) * size_x)
            message[rows, :width] = edge_rows(total, first + i, size_x, size_y)
            message[rows, width : width + 2] = edge_rows(columns, first + i, size_x, size_y)[:, :2]
    for copy in copies[4:]:
        copy.wait()
    if x_near.shape[0] > size_y:
        write_coefs(x_near, size_y, coefs)


def node_column(values, start, count):
    row = lax.broadcasted_iota(jnp.int32, (count, 1), 0)
    result = jnp.zeros((count, 1), jnp.float32)
    for i, value in enumerate(values):
        result = jnp.where(row == start + i, float(value), result)
    return result


def edge_weights(columns, message, size_x, size_y, width, edge, line):
    second = second_table()
    other = size_x - 1 - edge
    low = line == 3
    y, first = (0, 0) if low else (size_y - 1, size_y - 8)
    rows = slice(edge * size_y + first, edge * size_y + first + 8)
    here, there = (slice(x * size_y + y, x * size_y + y + 1) for x in (edge, other))
    mass, inverse = columns[here, 0:1], columns[here, 1:2]
    beyond = slice(line * size_x + edge, line * size_x + edge + 1)
    beyond_mass = message[beyond, width : width + 1]

    def beyond_inverse(i, x):
        return message[i * size_x + x : i * size_x + x + 1, width + 1 : width + 2]

    if low:
        own, partner = node_column(second[:, 0], 0, 8), node_column(second[3:, 0], 4, 8)
    else:
        own, partner = node_column(second[:, 3], 4, 8), node_column(second[:1, 3], 3, 8)
    along = inverse * (own * columns[rows, 0:1] + partner * columns[rows, 2:3])
    lane = lax.broadcasted_iota(jnp.int32, (8, 128), 1) - width % 128
    place = lax.broadcasted_iota(jnp.int32, (8, 128), 0)
    tile = jnp.where(lane == line, along, 0.0)
    for i in range(4):
        value = float(second[line, i]) * beyond_mass * beyond_inverse(i, edge)
        if i == line:
            across = beyond_mass * beyond_inverse(line, edge) + mass * inverse
            value = value + float(second[edge, edge]) * across
        tile = tile + jnp.where((place == y - first) & (lane == i), value, 0.0)
    across = beyond_mass * beyond_inverse(line, other) + mass * columns[there, 1:2]
    value = float(second[edge, other]) * across
    return tile + jnp.where((place == y - first) & (lane == 4), value, 0.0)


def side_weights(columns, message, size_x, size_y, width, line):
    second = second_table()
    first, last = 0, size_x - 1
    tiles = [
        edge_weights(columns, message, size_x, size_y, width, edge, line) for edge in (first, last)
    ]
    mass = message[line * size_x : (line + 1) * size_x, width : width + 1]
    own = edge_rows(columns, 0 if line == 3 else size_y - 1, size_x, size_y)
    inner = []
    for edge in (first, last):
        inverse = message[line * size_x + edge : line * size_x + edge + 1, width + 1 : width + 2]
        across = mass * inverse + own[:, 0:1] * own[edge : edge + 1, 1:2]
        inner.append(node_column(second[:, edge], 0, size_x) * across)
    lane = lax.broadcasted_iota(jnp.int32, (size_x, 128), 1)
    from_last = jnp.where(even("gx"), 0, 1)
    return (
        jnp.where(even("gx"), tiles[1], tiles[0]),
        jnp.where(even("gx"), tiles[0], tiles[1]),
        jnp.where(lane == from_last, inner[1], inner[0]),
    )


def weights_kernel(size_x, size_y, width, columns, message, out):
    near, far, inner = side_weights(columns, message, size_x, size_y, width, 3)
    out[0:8, :] = near
    out[8:16, :] = far
    out[16 : 16 + size_x, :] = inner


def second_kernel(
    size_x,
    total,
    columns,
    operator,
    low_weights,
    low,
    from_far,
    from_near,
    high,
    out,
    x_near,
    x_far,
    line_ends,
    inner,
    work,
):
    size_y, width = from_far.shape[0], total.shape[1]
    second = second_table()
    near, far = x_rows(size_x * size_y, size_y)
    work[...] = total[...]
    work[near] += from_near[:size_y, :width]
    work[far] += from_far[:, :width]
    sides = ((low, 0, 3, 0), (high, size_y - 1, 0, size_y - 8))
    beyond = []
    for message, y, line, _ in sides:
        lines = [message[i * size_x : (i + 1) * size_x, :width] for i in range(4)]
        lines[line] = lines[line] + edge_rows(work, y, size_x, size_y)
        for x in range(size_x):
            work[x * size_y + y : x * size_y + y + 1, :] = lines[line][x : x + 1]
        for i in range(4):
            inverse = message[i * size_x : (i + 1) * size_x, width + 1 : width + 2]
            lines[i] = inverse * lines[i]
        value = sum(float(second[line, i]) * lines[i] for i in range(4))
        for x in range(size_x):
            value = value + node_column(second[:, x], 0, size_x) * lines[line][x : x + 1]
        mass = message[line * size_x : (line + 1) * size_x, width : width + 1]
        beyond.append(mass * value)
    out[...] = product(split(operator[...]), split(columns[:, 1:2] * work[...]))
    for (_, y, _, _), rows in zip(sides, beyond):
        for x in range(size_x):
            out[x * size_y + y : x * size_y + y + 1, :] += rows[x : x + 1]

    x_near[:size_y, :width] = out[near]
    x_far[:size_y, :width] = out[far]
    high_weights = side_weights(columns, high, size_x, size_y, width, 0)
    for side, (message, y, line, start) in enumerate(sides):
        weights = high_weights if side else [low_weights[i : i + 8] for i in (0, 8, 16)]
        behind = slice(width % 128, 128)
        x_near[start : start + 8, width:] = weights[0][:, behind]
        x_far[start : start + 8, width:] = weights[1][:, behind]
        inner[side * size_x : (side + 1) * size_x, :] = weights[2][:size_x]
        for i in range(4):
            rows = [
                message[i * size_x + x : i * size_x + x + 1, :width] for x in (0, size_x - 1)
            ]
            at_near = jnp.where(even("gx"), rows[1], rows[0])
            at_far = jnp.where(even("gx"), rows[0], rows[1])
            place = size_y + 4 * side + i
            x_near[place : place + 1, :width] = at_near
            x_far[place : place + 1, :width] = at_far
            if i == line:
                line_ends[2 * side : 2 * side + 1, :] = at_far
                line_ends[2 * side + 1 : 2 * side + 2, :] = at_near


def third_kernel(
    levels,
    state,
    hyper,
    total,
    masses,
    inner,
    factors,
    to_near,
    to_far,
    from_far,
    from_near,
    ends_near,
    ends_far,
    out,
    work,
    turned,
    values,
):
    columns, width = total.shape
    size_x, size_y, _ = state.shape
    variables = width // levels
    near = jnp.where(even("gx"), columns - size_y, 0)
    sides = ((0, 0, 3, 0), (1, size_y - 1, 0, size_y - 8))
    partners = (
        (near, to_near, from_near, from_far, ends_near, 0),
        (columns - size_y - near, to_far, from_far, from_near, ends_far, 1),
    )
    work[...] = total[...]
    for start, _, theirs, _, _, _ in partners:
        work[pl.ds(pl.multiple_of(start, size_y), size_y), :] += theirs[:size_y, :width]
    for side, y, line, first in sides:
        place = size_y + 4 * side
        tile = slice(first, first + 8)
        for start, mine, theirs, others, ends, which in partners:
            terms = [
                (weights, i, rows, place + i)
                for i in range(4)
                for weights, rows in ((mine, theirs), (theirs, mine))
            ]
            terms += [(mine, 4, others, place + line), (theirs, 4, ends, 2 * side + which)]
            added = sum(
                weights[tile, width + i : width + i + 1] * rows[row : row + 1, :width]
                for weights, i, rows, row in terms
            )
            work[pl.ds(pl.multiple_of(start + first, 8), 8), :] += added
        for x in range(1, size_x - 1):
            row, weight = x * size_y + y, side * size_x + x
            work[row : row + 1, :] += (
                inner[weight : weight + 1, 0:1] * from_near[place + line : place + line + 1, :width]
                + inner[weight : weight + 1, 1:2] * from_far[place + line : place + line + 1, :width]
            )
    twice = masses[:, 1:2] * work[...]
    turned[...] = (state[...].reshape(columns, width) - hyper[...] * twice).T
    scale, down, up, keep, flow, cloud = (
        factors.at[i * levels : (i + 1) * levels] for i in range(6)
    )
    value = jnp.zeros((variables, columns), jnp.float32)
    for k in range(levels):
        rows = turned[pl.ds(k, variables, stride=levels), :]
        value = rows * scale[k : k + 1, :] + down[k : k + 1, :] * value
        values[k, :variables, :] = value
    solved = jnp.zeros((variables, columns), jnp.float32)
    for k in reversed(range(levels)):
        solved = values[k, :variables, :] + up[k : k + 1, :] * solved
        turned[pl.ds(k, variables, stride=levels), :] = solved
    heat, vapour, liquid = (turned.at[i * levels : (i + 1) * levels] for i in range(3))
    condensed = cloud[...] * 0.5 * jnp.maximum(vapour[...] - 0.3 * heat[...], 0.0)
    vapour[...] = vapour[...] - condensed
    heat[...] = heat[...] + 2.0 * condensed
    liquid[...] = (liquid[...] + condensed) * keep[...]
    settled = jnp.zeros((1, columns), jnp.float32)
    for k in range(levels):
        settled = liquid[k : k + 1, :] + flow[k : k + 1, :] * settled
        liquid[k : k + 1, :] = settled
    out[...] = turned[...].T.reshape(out.shape)


def pick(slots, pieces):
    size_x, size_y = slots.shape
    columns = size_x * size_y
    wanted = jnp.concatenate([slots[x : x + 1, :] for x in range(size_x)], axis=1)
    picked = 0.0
    for owner, rest in pieces:
        span = rest.shape[1]
        entry = lax.broadcasted_iota(jnp.int32, (span, columns), 0) + owner * span
        choice = (entry == wanted).astype(jnp.float32).astype(jnp.bfloat16)
        for _ in range(3):
            part = rest.astype(jnp.bfloat16)
            rest = rest - part.astype(jnp.float32)
            picked = picked + jnp.dot(part, choice, preferred_element_type=jnp.float32)
    return picked


def pick_kernel(slots, own, from_near, from_far, picked, passed):
    here = lax.axis_index("gx")
    size_y = slots.shape[1]
    near = read_coefs(from_near, size_y, *own.shape)
    pieces = [(here, own[...]), (here ^ 1, near), (here ^ 3, from_far[...])]
    passed[...] = from_far[...]
    picked[...] = pick(slots, pieces)


def factor_kernel(levels, slots, *refs):
    factors = refs[-1]
    columns = factors.shape[1]
    if len(refs) == 3:
        here = lax.axis_index("gx")
        picked = refs[0][...] + pick(slots, [(here ^ 2, refs[1][...])])
    else:
        picked = pick(slots, [(peer, refs[0][peer]) for peer in range(refs[0].shape[0])])
    mixing, falling, covered = (picked[i * levels : (i + 1) * levels] for i in range(3))
    scale, down, up, keep, flow, cover = (
        factors.at[i * levels : (i + 1) * levels] for i in range(6)
    )
    gain = jnp.zeros((1, columns), jnp.float32)
    for k in range(levels):
        above = mixing[k : k + 1] if k else jnp.zeros_like(gain)
        below = mixing[k + 1 : k + 2] if k + 1 < levels else jnp.zeros_like(gain)
        centre = 1.0 + above + (below if k + 1 < levels else mixing[:1])
        inverse = 1.0 / (centre - above * gain)
        gain = below * inverse
        scale[k : k + 1, :] = inverse
        down[k : k + 1, :] = above * inverse
        up[k : k + 1, :] = gain
    kept = 1.0 / (1.0 + falling)
    keep[...] = kept
    flow[:1, :] = jnp.zeros((1, columns), jnp.float32)
    flow[1:, :] = falling[:-1] * kept[1:]
    cover[...] = covered


def swapped(value, axis, partner):
    return lax.ppermute(value, axis, [(i, partner(i)) for i in range(lax.axis_size(axis))])


def exchanged(near, far, axis):
    size = lax.axis_size(axis)
    from_far = swapped(far, axis, lambda i: (i + (1 if i % 2 else -1)) % size)
    from_near = swapped(near, axis, lambda i: i ^ 1)
    return from_far, from_near


def shifted(value, axis, step):
    size = lax.axis_size(axis)
    return lax.ppermute(value, axis, [(i, (i + step) % size) for i in range(size)])


def local(
    model_state, hyper_coef, point_mass, inverse_mass, span_slot, vert_diff, fall_rate, cloud_frac
):
    size_x, size_y, width = model_state.shape
    levels, span = vert_diff.shape[1:]
    columns = size_x * size_y
    hyper = hyper_coef.reshape(1, width)
    padded = -(-(width + 5) // 128) * 128
    tables = jnp.asarray(laplacian_tables(size_x, size_y))

    def array(*shape):
        return jax.ShapeDtypeStruct(shape, jnp.float32)

    def scratch(*shape):
        return pltpu.VMEM(shape, jnp.float32)

    def call(kernel, name, outs, scratches, *operands, spec=VMEM, cost=None):
        return pl.pallas_call(
            kernel,
            out_shape=outs,
            in_specs=[spec] * len(operands),
            out_specs=[VMEM] * len(outs),
            scratch_shapes=scratches,
            compiler_params=PARAMS,
            cost_estimate=cost,
            name=name,
        )(*operands)

    riding = lax.axis_size("gx") == 4
    whole = array(columns, width)
    edge, message = array(4 * size_x, padded), array(size_y + 8, padded)
    here, total, x_near, x_far, y_low, y_high, operator, masses, coefs = call(
        start_kernel,
        "start",
        [
            array(size_x, size_y, width),
            whole,
            array(size_y + (COEF_ROWS if riding else 0), padded),
            array(size_y, padded),
            edge,
            edge,
            array(columns, columns),
            array(columns, 128),
            array(3 * levels, span),
        ],
        [
            scratch(size_x, size_y),
            scratch(size_x, size_y),
            scratch(*tables.shape),
            pltpu.SemaphoreType.DMA((7,)),
        ],
        *(
            pltpu.with_memory_space_constraint(value, pltpu.HBM)
            for value in (
                model_state,
                point_mass,
                inverse_mass,
                vert_diff,
                fall_rate,
                cloud_frac,
                tables,
            )
        ),
        spec=pl.BlockSpec(memory_space=pltpu.HBM),
    )
    low = shifted(y_high, "gy", 1)
    from_far, from_near = exchanged(x_near, x_far, "gx")
    sent, y_low, _ = lax.optimization_barrier((coefs, y_low, from_near))
    coefs_far = swapped(sent, "gx", lambda i: i ^ 3) if riding else None
    high = shifted(y_low, "gy", -1)
    (low_weights,) = call(
        functools.partial(weights_kernel, size_x, size_y, width),
        "weights",
        [array(24, 128)],
        [],
        masses,
        low,
        cost=LONG,
    )
    total, x_near, x_far, line_ends, inner = call(
        functools.partial(second_kernel, size_x),
        "second",
        [whole, message, message, array(4, width), array(2 * size_x, 128)],
        [scratch(columns, width)],
        total,
        masses,
        operator,
        low_weights,
        low,
        from_far,
        from_near,
        high,
    )
    last_x = exchanged(x_near, x_far, "gx")
    peers = lax.axis_size("gx")
    ends_near = swapped(line_ends, "gx", lambda i: (i + (2 if i % 2 else -2)) % peers)
    ends_far = ends_near
    if peers != 4:
        ends_far = swapped(line_ends, "gx", lambda i: (i - (2 if i % 2 else -2)) % peers)
    if riding:
        picked, passed = call(
            pick_kernel,
            "pick",
            [array(3 * levels, columns), array(3 * levels, span)],
            [],
            span_slot,
            coefs,
            from_near,
            coefs_far,
        )
        pieces = [picked, swapped(passed, "gx", lambda i: i ^ 1)]
    else:
        pieces = [lax.all_gather(coefs, "gx")]
    (factors,) = call(
        functools.partial(factor_kernel, levels),
        "factors",
        [array(6 * levels, columns)],
        [],
        span_slot,
        *pieces,
    )
    (result,) = call(
        functools.partial(third_kernel, levels),
        "third",
        [array(size_x, size_y, width)],
        [scratch(columns, width), scratch(width, columns), scratch(levels, 16, columns)],
        here,
        hyper,
        total,
        masses,
        inner,
        factors,
        x_near,
        x_far,
        *last_x,
        ends_near,
        ends_far,
    )
    return result


def solution(mesh):
    placed = (
        P("gx", "gy", None),
        P(),
        P("gx", "gy"),
        P("gx", "gy"),
        P("gx", "gy"),
        P("gy", None, "gx"),
        P("gy", None, "gx"),
        P("gy", None, "gx"),
    )
    return jax.shard_map(
        local, mesh=mesh, in_specs=placed, out_specs=P("gx", "gy", None), check_vma=False
    )
```

```python
import functools

import jax
import jax.numpy as jnp
import numpy as np
from jax import lax
from jax.experimental import pallas as pl
from jax.experimental.pallas import tpu as pltpu
from jax.sharding import PartitionSpec as P

VMEM = pl.BlockSpec(memory_space=pltpu.VMEM)
LONG = pl.CostEstimate(flops=100_000_000_000, bytes_accessed=30_000_000, transcendentals=0)
PARAMS = pltpu.CompilerParams(vmem_limit_bytes=16 * 1024 * 1024)


def second_table():
    nodes = np.array([-1.0, -1.0 / np.sqrt(5.0), 1.0 / np.sqrt(5.0), 1.0])
    deriv = np.zeros((4, 4))
    for i in range(4):
        for j in range(4):
            if i == j:
                deriv[i, j] = sum(1.0 / (nodes[i] - nodes[k]) for k in range(4) if k != i)
            else:
                upper = np.prod([nodes[i] - nodes[k] for k in range(4) if k != i])
                lower = np.prod([nodes[j] - nodes[k] for k in range(4) if k != j])
                deriv[i, j] = upper / (lower * (nodes[i] - nodes[j]))
    return deriv @ deriv


def laplacian_tables(size_x, size_y):
    second = second_table()
    lap = np.kron(np.kron(np.eye(size_x // 4), second), np.eye(size_y))
    lap = lap + np.kron(np.eye(size_x), np.kron(np.eye(size_y // 4), second))
    partner = np.zeros_like(lap)
    for x in range(size_x):
        for y in range(size_y):
            other = y - 1 if y % 4 == 0 else y + 1 if y % 4 == 3 else -1
            if 0 <= other < size_y:
                partner[x * size_y + y] = lap[x * size_y + other]
    return np.stack([lap, partner]).astype(np.float32)


def split(value):
    high = value.astype(jnp.bfloat16)
    return high, (value - high.astype(jnp.float32)).astype(jnp.bfloat16)


def product(left, right):
    left_high, left_low = left
    right_high, right_low = right
    dot = functools.partial(jnp.dot, preferred_element_type=jnp.float32)
    return dot(left_high, right_high) + (dot(left_high, right_low) + dot(left_low, right_high))


def to_column(plane, partner=False):
    size_x, size_y = plane.shape
    row = lax.broadcasted_iota(jnp.int32, (size_y, size_y), 0)
    lane = lax.broadcasted_iota(jnp.int32, (size_y, size_y), 1)
    if partner:
        row = jnp.where(row % 4 == 0, row - 1, jnp.where(row % 4 == 3, row + 1, -1))
    pick = row == lane
    parts = [
        jnp.sum(jnp.where(pick, plane[x : x + 1, :], 0.0), axis=1, keepdims=True)
        for x in range(size_x)
    ]
    return jnp.concatenate(parts, axis=0)


def even(axis):
    return lax.rem(lax.axis_index(axis), 2) == 0


def x_rows(count, size_y):
    near = jnp.where(even("gx"), count - size_y, 0)
    far = count - size_y - near
    return tuple(pl.ds(pl.multiple_of(start, size_y), size_y) for start in (near, far))


COEF_ROWS = 32


def write_coefs(message, start, coefs):
    rows, lanes = coefs.shape
    for i, first in enumerate(range(0, rows, COEF_ROWS)):
        part = coefs[first : min(first + COEF_ROWS, rows)]
        message[start : start + part.shape[0], i * lanes : (i + 1) * lanes] = part


def read_coefs(message, start, rows, lanes):
    parts = []
    for i, first in enumerate(range(0, rows, COEF_ROWS)):
        count = min(COEF_ROWS, rows - first)
        parts.append(message[start : start + count, i * lanes : (i + 1) * lanes])
    return jnp.concatenate(parts, axis=0)


def edge_rows(ref, y, size_x, size_y):
    return jnp.concatenate(
        [ref[x * size_y + y : x * size_y + y + 1, :] for x in range(size_x)], axis=0
    )


def start_kernel(
    state,
    mass,
    inverse,
    diff,
    fall,
    cloud,
    tables,
    here,
    total,
    x_near,
    x_far,
    low,
    high,
    operator,
    columns,
    coefs,
    mass_here,
    inverse_here,
    tables_here,
    sems,
):
    size_x, size_y, width = state.shape
    levels = diff.shape[1]
    pairs = [(mass, mass_here), (tables, tables_here), (inverse, inverse_here), (state, here)]
    for i, source in enumerate((diff, fall, cloud)):
        pairs.append((source.at[0], coefs.at[i * levels : (i + 1) * levels]))
    copies = [
        pltpu.make_async_copy(source, target, sems.at[i])
        for i, (source, target) in enumerate(pairs)
    ]
    for copy in copies:
        copy.start()
    for copy in copies[:3]:
        copy.wait()
    own = to_column(mass_here[...])
    lane = lax.broadcasted_iota(jnp.int32, columns.shape, 1)
    partner = to_column(mass_here[...], True)
    inverses = to_column(inverse_here[...])
    columns[...] = jnp.where(lane == 0, own, jnp.where(lane == 1, inverses, partner))
    matrix = own * tables_here[0] + partner * tables_here[1]
    operator[...] = matrix
    matrix = split(matrix)
    copies[3].wait()
    total[...] = product(matrix, split(here[...].reshape(size_x * size_y, width)))
    near, far = x_rows(size_x * size_y, size_y)
    x_near[:, :width] = total[near]
    x_far[:, :width] = total[far]
    for first, message in ((0, low), (size_y - 4, high)):
        for i in range(4):
            rows = slice(i * size_x, (i + 1) * size_x)
            message[rows, :width] = edge_rows(total, first + i, size_x, size_y)
            message[rows, width : width + 2] = edge_rows(columns, first + i, size_x, size_y)[:, :2]
    for copy in copies[4:]:
        copy.wait()


def node_column(values, start, count):
    row = lax.broadcasted_iota(jnp.int32, (count, 1), 0)
    result = jnp.zeros((count, 1), jnp.float32)
    for i, value in enumerate(values):
        result = jnp.where(row == start + i, float(value), result)
    return result


def edge_weights(columns, message, size_x, size_y, width, edge, line):
    second = second_table()
    other = size_x - 1 - edge
    low = line == 3
    y, first = (0, 0) if low else (size_y - 1, size_y - 8)
    rows = slice(edge * size_y + first, edge * size_y + first + 8)
    here, there = (slice(x * size_y + y, x * size_y + y + 1) for x in (edge, other))
    mass, inverse = columns[here, 0:1], columns[here, 1:2]
    beyond = slice(line * size_x + edge, line * size_x + edge + 1)
    beyond_mass = message[beyond, width : width + 1]

    def beyond_inverse(i, x):
        return message[i * size_x + x : i * size_x + x + 1, width + 1 : width + 2]

    if low:
        own, partner = node_column(second[:, 0], 0, 8), node_column(second[3:, 0], 4, 8)
    else:
        own, partner = node_column(second[:, 3], 4, 8), node_column(second[:1, 3], 3, 8)
    along = inverse * (own * columns[rows, 0:1] + partner * columns[rows, 2:3])
    lane = lax.broadcasted_iota(jnp.int32, (8, 128), 1) - width % 128
    place = lax.broadcasted_iota(jnp.int32, (8, 128), 0)
    tile = jnp.where(lane == line, along, 0.0)
    for i in range(4):
        value = float(second[line, i]) * beyond_mass * beyond_inverse(i, edge)
        if i == line:
            across = beyond_mass * beyond_inverse(line, edge) + mass * inverse
            value = value + float(second[edge, edge]) * across
        tile = tile + jnp.where((place == y - first) & (lane == i), value, 0.0)
    across = beyond_mass * beyond_inverse(line, other) + mass * columns[there, 1:2]
    value = float(second[edge, other]) * across
    return tile + jnp.where((place == y - first) & (lane == 4), value, 0.0)


def side_weights(columns, message, size_x, size_y, width, line):
    second = second_table()
    first, last = 0, size_x - 1
    tiles = [
        edge_weights(columns, message, size_x, size_y, width, edge, line) for edge in (first, last)
    ]
    mass = message[line * size_x : (line + 1) * size_x, width : width + 1]
    own = edge_rows(columns, 0 if line == 3 else size_y - 1, size_x, size_y)
    inner = []
    for edge in (first, last):
        inverse = message[line * size_x + edge : line * size_x + edge + 1, width + 1 : width + 2]
        across = mass * inverse + own[:, 0:1] * own[edge : edge + 1, 1:2]
        inner.append(node_column(second[:, edge], 0, size_x) * across)
    lane = lax.broadcasted_iota(jnp.int32, (size_x, 128), 1)
    from_last = jnp.where(even("gx"), 0, 1)
    return (
        jnp.where(even("gx"), tiles[1], tiles[0]),
        jnp.where(even("gx"), tiles[0], tiles[1]),
        jnp.where(lane == from_last, inner[1], inner[0]),
    )


def weights_kernel(size_x, size_y, width, columns, message, out):
    near, far, inner = side_weights(columns, message, size_x, size_y, width, 3)
    out[0:8, :] = near
    out[8:16, :] = far
    out[16 : 16 + size_x, :] = inner


def second_kernel(
    size_x,
    total,
    columns,
    operator,
    coefs,
    low_weights,
    low,
    from_far,
    from_near,
    high,
    out,
    x_near,
    x_far,
    line_ends,
    inner,
    work,
):
    size_y, width = from_far.shape[0], total.shape[1]
    second = second_table()
    near, far = x_rows(size_x * size_y, size_y)
    work[...] = total[...]
    work[near] += from_near[:, :width]
    work[far] += from_far[:, :width]
    sides = ((low, 0, 3, 0), (high, size_y - 1, 0, size_y - 8))
    beyond = []
    for message, y, line, _ in sides:
        lines = [message[i * size_x : (i + 1) * size_x, :width] for i in range(4)]
        lines[line] = lines[line] + edge_rows(work, y, size_x, size_y)
        for x in range(size_x):
            work[x * size_y + y : x * size_y + y + 1, :] = lines[line][x : x + 1]
        for i in range(4):
            inverse = message[i * size_x : (i + 1) * size_x, width + 1 : width + 2]
            lines[i] = inverse * lines[i]
        value = sum(float(second[line, i]) * lines[i] for i in range(4))
        for x in range(size_x):
            value = value + node_column(second[:, x], 0, size_x) * lines[line][x : x + 1]
        mass = message[line * size_x : (line + 1) * size_x, width : width + 1]
        beyond.append(mass * value)
    out[...] = product(split(operator[...]), split(columns[:, 1:2] * work[...]))
    for (_, y, _, _), rows in zip(sides, beyond):
        for x in range(size_x):
            out[x * size_y + y : x * size_y + y + 1, :] += rows[x : x + 1]

    x_near[:size_y, :width] = out[near]
    x_far[:size_y, :width] = out[far]
    high_weights = side_weights(columns, high, size_x, size_y, width, 0)
    for side, (message, y, line, start) in enumerate(sides):
        weights = high_weights if side else [low_weights[i : i + 8] for i in (0, 8, 16)]
        behind = slice(width % 128, 128)
        x_near[start : start + 8, width:] = weights[0][:, behind]
        x_far[start : start + 8, width:] = weights[1][:, behind]
        inner[side * size_x : (side + 1) * size_x, :] = weights[2][:size_x]
        for i in range(4):
            rows = [
                message[i * size_x + x : i * size_x + x + 1, :width] for x in (0, size_x - 1)
            ]
            at_near = jnp.where(even("gx"), rows[1], rows[0])
            at_far = jnp.where(even("gx"), rows[0], rows[1])
            place = size_y + 4 * side + i
            x_near[place : place + 1, :width] = at_near
            x_far[place : place + 1, :width] = at_far
            if i == line:
                line_ends[2 * side : 2 * side + 1, :] = at_far
                line_ends[2 * side + 1 : 2 * side + 2, :] = at_near
    if x_near.shape[0] > size_y + 8:
        write_coefs(x_near, size_y + 8, coefs)


def third_kernel(
    levels,
    state,
    hyper,
    total,
    masses,
    inner,
    factors,
    to_near,
    to_far,
    from_far,
    from_near,
    ends_near,
    ends_far,
    out,
    work,
    turned,
    values,
):
    columns, width = total.shape
    size_x, size_y, _ = state.shape
    variables = width // levels
    near = jnp.where(even("gx"), columns - size_y, 0)
    sides = ((0, 0, 3, 0), (1, size_y - 1, 0, size_y - 8))
    partners = (
        (near, to_near, from_near, from_far, ends_near, 0),
        (columns - size_y - near, to_far, from_far, from_near, ends_far, 1),
    )
    work[...] = total[...]
    for start, _, theirs, _, _, _ in partners:
        work[pl.ds(pl.multiple_of(start, size_y), size_y), :] += theirs[:size_y, :width]
    for side, y, line, first in sides:
        place = size_y + 4 * side
        tile = slice(first, first + 8)
        for start, mine, theirs, others, ends, which in partners:
            terms = [
                (weights, i, rows, place + i)
                for i in range(4)
                for weights, rows in ((mine, theirs), (theirs, mine))
            ]
            terms += [(mine, 4, others, place + line), (theirs, 4, ends, 2 * side + which)]
            added = sum(
                weights[tile, width + i : width + i + 1] * rows[row : row + 1, :width]
                for weights, i, rows, row in terms
            )
            work[pl.ds(pl.multiple_of(start + first, 8), 8), :] += added
        for x in range(1, size_x - 1):
            row, weight = x * size_y + y, side * size_x + x
            work[row : row + 1, :] += (
                inner[weight : weight + 1, 0:1] * from_near[place + line : place + line + 1, :width]
                + inner[weight : weight + 1, 1:2] * from_far[place + line : place + line + 1, :width]
            )
    twice = masses[:, 1:2] * work[...]
    turned[...] = (state[...].reshape(columns, width) - hyper[...] * twice).T
    scale, down, up, keep, flow, cloud = (
        factors.at[i * levels : (i + 1) * levels] for i in range(6)
    )
    value = jnp.zeros((variables, columns), jnp.float32)
    for k in range(levels):
        rows = turned[pl.ds(k, variables, stride=levels), :]
        value = rows * scale[k : k + 1, :] + down[k : k + 1, :] * value
        values[k, :variables, :] = value
    solved = jnp.zeros((variables, columns), jnp.float32)
    for k in reversed(range(levels)):
        solved = values[k, :variables, :] + up[k : k + 1, :] * solved
        turned[pl.ds(k, variables, stride=levels), :] = solved
    heat, vapour, liquid = (turned.at[i * levels : (i + 1) * levels] for i in range(3))
    condensed = cloud[...] * 0.5 * jnp.maximum(vapour[...] - 0.3 * heat[...], 0.0)
    vapour[...] = vapour[...] - condensed
    heat[...] = heat[...] + 2.0 * condensed
    liquid[...] = (liquid[...] + condensed) * keep[...]
    settled = jnp.zeros((1, columns), jnp.float32)
    for k in range(levels):
        settled = liquid[k : k + 1, :] + flow[k : k + 1, :] * settled
        liquid[k : k + 1, :] = settled
    out[...] = turned[...].T.reshape(out.shape)


def pick(slots, pieces):
    size_x, size_y = slots.shape
    columns = size_x * size_y
    wanted = jnp.concatenate([slots[x : x + 1, :] for x in range(size_x)], axis=1)
    picked = 0.0
    for owner, rest in pieces:
        span = rest.shape[1]
        entry = lax.broadcasted_iota(jnp.int32, (span, columns), 0) + owner * span
        choice = (entry == wanted).astype(jnp.float32).astype(jnp.bfloat16)
        for _ in range(3):
            part = rest.astype(jnp.bfloat16)
            rest = rest - part.astype(jnp.float32)
            picked = picked + jnp.dot(part, choice, preferred_element_type=jnp.float32)
    return picked


def pass_kernel(arrived, passed):
    passed[...] = arrived[...]


def factor_kernel(levels, slots, *refs):
    factors = refs[-1]
    if len(refs) == 5:
        own, from_far, relayed, from_near = refs[:4]
        here = lax.axis_index("gx")
        near = read_coefs(from_near, slots.shape[1] + 8, *own.shape)
        pieces = [
            (here, own[...]),
            (here ^ 3, from_far[...]),
            (here ^ 2, relayed[...]),
            (here ^ 1, near),
        ]
    else:
        pieces = [(peer, refs[0][peer]) for peer in range(refs[0].shape[0])]
    columns = factors.shape[1]
    picked = pick(slots, pieces)
    mixing, falling, covered = (picked[i * levels : (i + 1) * levels] for i in range(3))
    scale, down, up, keep, flow, cover = (
        factors.at[i * levels : (i + 1) * levels] for i in range(6)
    )
    gain = jnp.zeros((1, columns), jnp.float32)
    for k in range(levels):
        above = mixing[k : k + 1] if k else jnp.zeros_like(gain)
        below = mixing[k + 1 : k + 2] if k + 1 < levels else jnp.zeros_like(gain)
        centre = 1.0 + above + (below if k + 1 < levels else mixing[:1])
        inverse = 1.0 / (centre - above * gain)
        gain = below * inverse
        scale[k : k + 1, :] = inverse
        down[k : k + 1, :] = above * inverse
        up[k : k + 1, :] = gain
    kept = 1.0 / (1.0 + falling)
    keep[...] = kept
    flow[:1, :] = jnp.zeros((1, columns), jnp.float32)
    flow[1:, :] = falling[:-1] * kept[1:]
    cover[...] = covered


def swapped(value, axis, partner):
    return lax.ppermute(value, axis, [(i, partner(i)) for i in range(lax.axis_size(axis))])


def exchanged(near, far, axis):
    size = lax.axis_size(axis)
    from_far = swapped(far, axis, lambda i: (i + (1 if i % 2 else -1)) % size)
    from_near = swapped(near, axis, lambda i: i ^ 1)
    return from_far, from_near


def shifted(value, axis, step):
    size = lax.axis_size(axis)
    return lax.ppermute(value, axis, [(i, (i + step) % size) for i in range(size)])


def local(
    model_state, hyper_coef, point_mass, inverse_mass, span_slot, vert_diff, fall_rate, cloud_frac
):
    size_x, size_y, width = model_state.shape
    levels, span = vert_diff.shape[1:]
    columns = size_x * size_y
    hyper = hyper_coef.reshape(1, width)
    padded = -(-(width + 5) // 128) * 128
    tables = jnp.asarray(laplacian_tables(size_x, size_y))

    def array(*shape):
        return jax.ShapeDtypeStruct(shape, jnp.float32)

    def scratch(*shape):
        return pltpu.VMEM(shape, jnp.float32)

    def call(kernel, name, outs, scratches, *operands, spec=VMEM, cost=None):
        return pl.pallas_call(
            kernel,
            out_shape=outs,
            in_specs=[spec] * len(operands),
            out_specs=[VMEM] * len(outs),
            scratch_shapes=scratches,
            compiler_params=PARAMS,
            cost_estimate=cost,
            name=name,
        )(*operands)

    riding = lax.axis_size("gx") == 4
    whole = array(columns, width)
    edge = array(4 * size_x, padded)
    here, total, x_near, x_far, y_low, y_high, operator, masses, coefs = call(
        start_kernel,
        "start",
        [
            array(size_x, size_y, width),
            whole,
            array(size_y, padded),
            array(size_y, padded),
            edge,
            edge,
            array(columns, columns),
            array(columns, 128),
            array(3 * levels, span),
        ],
        [
            scratch(size_x, size_y),
            scratch(size_x, size_y),
            scratch(*tables.shape),
            pltpu.SemaphoreType.DMA((7,)),
        ],
        *(
            pltpu.with_memory_space_constraint(value, pltpu.HBM)
            for value in (
                model_state,
                point_mass,
                inverse_mass,
                vert_diff,
                fall_rate,
                cloud_frac,
                tables,
            )
        ),
        spec=pl.BlockSpec(memory_space=pltpu.HBM),
    )
    low = shifted(y_high, "gy", 1)
    from_far, from_near = exchanged(x_near, x_far, "gx")
    y_low, _ = lax.optimization_barrier((y_low, from_near))
    sent, _ = lax.optimization_barrier((coefs, from_near))
    coefs_far = swapped(sent, "gx", lambda i: i ^ 3) if riding else None
    high = shifted(y_low, "gy", -1)
    (low_weights,) = call(
        functools.partial(weights_kernel, size_x, size_y, width),
        "weights",
        [array(24, 128)],
        [],
        masses,
        low,
        cost=LONG,
    )
    total, x_near, x_far, line_ends, inner = call(
        functools.partial(second_kernel, size_x),
        "second",
        [
            whole,
            array(size_y + 8 + (COEF_ROWS if riding else 0), padded),
            array(size_y + 8, padded),
            array(4, width),
            array(2 * size_x, 128),
        ],
        [scratch(columns, width)],
        total,
        masses,
        operator,
        coefs,
        low_weights,
        low,
        from_far,
        from_near,
        high,
    )
    last_x = exchanged(x_near, x_far, "gx")
    peers = lax.axis_size("gx")
    ends_near = swapped(line_ends, "gx", lambda i: (i + (2 if i % 2 else -2)) % peers)
    ends_far = ends_near
    if peers != 4:
        ends_far = swapped(line_ends, "gx", lambda i: (i - (2 if i % 2 else -2)) % peers)
    if riding:
        (passed,) = call(
            pass_kernel,
            "pass",
            [array(3 * levels, span)],
            [],
            coefs_far,
            cost=LONG,
        )
        relayed = swapped(passed, "gx", lambda i: i ^ 1)
        pieces = [coefs, coefs_far, relayed, last_x[1]]
    else:
        pieces = [lax.all_gather(coefs, "gx")]
    (factors,) = call(
        functools.partial(factor_kernel, levels),
        "factors",
        [array(6 * levels, columns)],
        [],
        span_slot,
        *pieces,
    )
    (result,) = call(
        functools.partial(third_kernel, levels),
        "third",
        [array(size_x, size_y, width)],
        [scratch(columns, width), scratch(width, columns), scratch(levels, 16, columns)],
        here,
        hyper,
        total,
        masses,
        inner,
        factors,
        x_near,
        x_far,
        *last_x,
        ends_near,
        ends_far,
    )
    return result


def solution(mesh):
    placed = (
        P("gx", "gy", None),
        P(),
        P("gx", "gy"),
        P("gx", "gy"),
        P("gx", "gy"),
        P("gy", None, "gx"),
        P("gy", None, "gx"),
        P("gy", None, "gx"),
    )
    return jax.shard_map(
        local, mesh=mesh, in_specs=placed, out_specs=P("gx", "gy", None), check_vma=False
    )
```

```python
import functools

import jax
import jax.numpy as jnp
import numpy as np
from jax import lax
from jax.experimental import pallas as pl
from jax.experimental.pallas import tpu as pltpu
from jax.sharding import PartitionSpec as P

VMEM = pl.BlockSpec(memory_space=pltpu.VMEM)
LONG = pl.CostEstimate(flops=100_000_000_000, bytes_accessed=30_000_000, transcendentals=0)
PARAMS = pltpu.CompilerParams(vmem_limit_bytes=16 * 1024 * 1024)


def second_table():
    nodes = np.array([-1.0, -1.0 / np.sqrt(5.0), 1.0 / np.sqrt(5.0), 1.0])
    deriv = np.zeros((4, 4))
    for i in range(4):
        for j in range(4):
            if i == j:
                deriv[i, j] = sum(1.0 / (nodes[i] - nodes[k]) for k in range(4) if k != i)
            else:
                upper = np.prod([nodes[i] - nodes[k] for k in range(4) if k != i])
                lower = np.prod([nodes[j] - nodes[k] for k in range(4) if k != j])
                deriv[i, j] = upper / (lower * (nodes[i] - nodes[j]))
    return deriv @ deriv


def laplacian_tables(size_x, size_y):
    second = second_table()
    lap = np.kron(np.kron(np.eye(size_x // 4), second), np.eye(size_y))
    lap = lap + np.kron(np.eye(size_x), np.kron(np.eye(size_y // 4), second))
    partner = np.zeros_like(lap)
    for x in range(size_x):
        for y in range(size_y):
            other = y - 1 if y % 4 == 0 else y + 1 if y % 4 == 3 else -1
            if 0 <= other < size_y:
                partner[x * size_y + y] = lap[x * size_y + other]
    return np.stack([lap, partner]).astype(np.float32)


def split(value):
    high = value.astype(jnp.bfloat16)
    return high, (value - high.astype(jnp.float32)).astype(jnp.bfloat16)


def product(left, right):
    left_high, left_low = left
    right_high, right_low = right
    dot = functools.partial(jnp.dot, preferred_element_type=jnp.float32)
    return dot(left_high, right_high) + (dot(left_high, right_low) + dot(left_low, right_high))


def to_column(plane, partner=False):
    size_x, size_y = plane.shape
    row = lax.broadcasted_iota(jnp.int32, (size_y, size_y), 0)
    lane = lax.broadcasted_iota(jnp.int32, (size_y, size_y), 1)
    if partner:
        row = jnp.where(row % 4 == 0, row - 1, jnp.where(row % 4 == 3, row + 1, -1))
    pick = row == lane
    parts = [
        jnp.sum(jnp.where(pick, plane[x : x + 1, :], 0.0), axis=1, keepdims=True)
        for x in range(size_x)
    ]
    return jnp.concatenate(parts, axis=0)


def even(axis):
    return lax.rem(lax.axis_index(axis), 2) == 0


def x_starts(count, size_y):
    near = jnp.where(even("gx"), count - size_y, 0)
    return near, count - size_y - near


def x_rows(count, size_y):
    starts = x_starts(count, size_y)
    return tuple(pl.ds(pl.multiple_of(start, size_y), size_y) for start in starts)


def add_packed(work, start, message, rows):
    def write(first, count, lanes, value):
        work[pl.ds(pl.multiple_of(start + first, 8), count), lanes] += value

    unpack(message, rows, work.shape[1], write)


def packed_rows(rows, width):
    return rows * (width // 128) + 8


def pack(value, message):
    rows, width = value.shape
    full, left = width // 128, width % 128
    for i in range(full):
        message[i * rows : (i + 1) * rows, :] = value[:, i * 128 : (i + 1) * 128]
    for i in range(rows // 8):
        lanes = slice(i * left, (i + 1) * left)
        message[full * rows : full * rows + 8, lanes] = value[i * 8 : (i + 1) * 8, full * 128 :]


def unpack(message, rows, width, write):
    full, left = width // 128, width % 128
    for i in range(full):
        write(0, rows, slice(i * 128, (i + 1) * 128), message[i * rows : (i + 1) * rows, :])
    for i in range(rows // 8):
        value = message[full * rows : full * rows + 8, i * left : (i + 1) * left]
        write(i * 8, 8, slice(full * 128, width), value)


def edge_rows(ref, y, size_x, size_y):
    return jnp.concatenate(
        [ref[x * size_y + y : x * size_y + y + 1, :] for x in range(size_x)], axis=0
    )


def start_kernel(
    state,
    mass,
    inverse,
    diff,
    fall,
    cloud,
    tables,
    here,
    total,
    x_near,
    x_far,
    low,
    high,
    operator,
    columns,
    coefs,
    mass_here,
    inverse_here,
    tables_here,
    sems,
):
    size_x, size_y, width = state.shape
    levels = diff.shape[1]
    pairs = [(mass, mass_here), (tables, tables_here), (inverse, inverse_here), (state, here)]
    for i, source in enumerate((diff, fall, cloud)):
        pairs.append((source.at[0], coefs.at[i * levels : (i + 1) * levels]))
    copies = [
        pltpu.make_async_copy(source, target, sems.at[i])
        for i, (source, target) in enumerate(pairs)
    ]
    for copy in copies:
        copy.start()
    for copy in copies[:3]:
        copy.wait()
    own = to_column(mass_here[...])
    lane = lax.broadcasted_iota(jnp.int32, columns.shape, 1)
    partner = to_column(mass_here[...], True)
    inverses = to_column(inverse_here[...])
    columns[...] = jnp.where(lane == 0, own, jnp.where(lane == 1, inverses, partner))
    matrix = own * tables_here[0] + partner * tables_here[1]
    operator[...] = matrix
    matrix = split(matrix)
    copies[3].wait()
    total[...] = product(matrix, split(here[...].reshape(size_x * size_y, width)))
    near, far = x_rows(size_x * size_y, size_y)
    pack(total[near], x_near)
    pack(total[far], x_far)
    for first, message in ((0, low), (size_y - 4, high)):
        for i in range(4):
            rows = slice(i * size_x, (i + 1) * size_x)
            message[rows, :width] = edge_rows(total, first + i, size_x, size_y)
            message[rows, width : width + 2] = edge_rows(columns, first + i, size_x, size_y)[:, :2]
    for copy in copies[4:]:
        copy.wait()
    if x_far.shape[0] > x_near.shape[0]:
        x_far[x_near.shape[0] :, :] = coefs[...]


def node_column(values, start, count):
    row = lax.broadcasted_iota(jnp.int32, (count, 1), 0)
    result = jnp.zeros((count, 1), jnp.float32)
    for i, value in enumerate(values):
        result = jnp.where(row == start + i, float(value), result)
    return result


def edge_weights(columns, message, size_x, size_y, width, edge, line):
    second = second_table()
    other = size_x - 1 - edge
    low = line == 3
    y, first = (0, 0) if low else (size_y - 1, size_y - 8)
    rows = slice(edge * size_y + first, edge * size_y + first + 8)
    here, there = (slice(x * size_y + y, x * size_y + y + 1) for x in (edge, other))
    mass, inverse = columns[here, 0:1], columns[here, 1:2]
    beyond = slice(line * size_x + edge, line * size_x + edge + 1)
    beyond_mass = message[beyond, width : width + 1]

    def beyond_inverse(i, x):
        return message[i * size_x + x : i * size_x + x + 1, width + 1 : width + 2]

    if low:
        own, partner = node_column(second[:, 0], 0, 8), node_column(second[3:, 0], 4, 8)
    else:
        own, partner = node_column(second[:, 3], 4, 8), node_column(second[:1, 3], 3, 8)
    along = inverse * (own * columns[rows, 0:1] + partner * columns[rows, 2:3])
    lane = lax.broadcasted_iota(jnp.int32, (8, 128), 1)
    place = lax.broadcasted_iota(jnp.int32, (8, 128), 0)
    tile = jnp.where(lane == line, along, 0.0)
    for i in range(4):
        value = float(second[line, i]) * beyond_mass * beyond_inverse(i, edge)
        if i == line:
            across = beyond_mass * beyond_inverse(line, edge) + mass * inverse
            value = value + float(second[edge, edge]) * across
        tile = tile + jnp.where((place == y - first) & (lane == i), value, 0.0)
    across = beyond_mass * beyond_inverse(line, other) + mass * columns[there, 1:2]
    value = float(second[edge, other]) * across
    return tile + jnp.where((place == y - first) & (lane == 4), value, 0.0)


def side_weights(columns, message, size_x, size_y, width, line):
    second = second_table()
    first, last = 0, size_x - 1
    tiles = [
        edge_weights(columns, message, size_x, size_y, width, edge, line) for edge in (first, last)
    ]
    mass = message[line * size_x : (line + 1) * size_x, width : width + 1]
    own = edge_rows(columns, 0 if line == 3 else size_y - 1, size_x, size_y)
    inner = []
    for edge in (first, last):
        inverse = message[line * size_x + edge : line * size_x + edge + 1, width + 1 : width + 2]
        across = mass * inverse + own[:, 0:1] * own[edge : edge + 1, 1:2]
        inner.append(node_column(second[:, edge], 0, size_x) * across)
    lane = lax.broadcasted_iota(jnp.int32, (size_x, 128), 1)
    from_last = jnp.where(even("gx"), 0, 1)
    return (
        jnp.where(even("gx"), tiles[1], tiles[0]),
        jnp.where(even("gx"), tiles[0], tiles[1]),
        jnp.where(lane == from_last, inner[1], inner[0]),
    )


def weights_kernel(size_x, size_y, width, columns, message, out):
    near, far, inner = side_weights(columns, message, size_x, size_y, width, 3)
    out[0:8, :] = near
    out[8:16, :] = far
    out[16 : 16 + size_x, :] = inner


def second_kernel(
    size_x,
    total,
    columns,
    operator,
    coefs,
    low_weights,
    low,
    from_far,
    from_near,
    high,
    out,
    x_near,
    x_far,
    line_ends,
    inner,
    work,
    at_near,
    at_far,
):
    size_y, width = total.shape[0] // size_x, total.shape[1]
    depth = size_y + 8
    second = second_table()
    near, far = x_starts(size_x * size_y, size_y)
    work[...] = total[...]
    add_packed(work, near, from_near, size_y)
    add_packed(work, far, from_far, size_y)
    sides = ((low, 0, 3, 0), (high, size_y - 1, 0, size_y - 8))
    beyond = []
    for message, y, line, _ in sides:
        lines = [message[i * size_x : (i + 1) * size_x, :width] for i in range(4)]
        lines[line] = lines[line] + edge_rows(work, y, size_x, size_y)
        for x in range(size_x):
            work[x * size_y + y : x * size_y + y + 1, :] = lines[line][x : x + 1]
        for i in range(4):
            inverse = message[i * size_x : (i + 1) * size_x, width + 1 : width + 2]
            lines[i] = inverse * lines[i]
        value = sum(float(second[line, i]) * lines[i] for i in range(4))
        for x in range(size_x):
            value = value + node_column(second[:, x], 0, size_x) * lines[line][x : x + 1]
        mass = message[line * size_x : (line + 1) * size_x, width : width + 1]
        beyond.append(mass * value)
    out[...] = product(split(operator[...]), split(columns[:, 1:2] * work[...]))
    for (_, y, _, _), rows in zip(sides, beyond):
        for x in range(size_x):
            out[x * size_y + y : x * size_y + y + 1, :] += rows[x : x + 1]

    near, far = x_rows(size_x * size_y, size_y)
    at_near[:size_y, :] = out[near]
    at_far[:size_y, :] = out[far]
    last = depth * (width // 128)
    lanes = depth // 8 * (width % 128)
    high_weights = side_weights(columns, high, size_x, size_y, width, 0)
    for side, (message, _, line, _) in enumerate(sides):
        weights = high_weights if side else [low_weights[i : i + 8] for i in (0, 8, 16)]
        inner[side * size_x : (side + 1) * size_x, :] = weights[2][:size_x]
        place = slice(lanes + 8 * side, lanes + 8 * side + 5)
        x_near[last : last + 8, place] = weights[0][:, :5]
        x_far[last : last + 8, place] = weights[1][:, :5]
        for i in range(4):
            first, final = (
                message[i * size_x + x : i * size_x + x + 1, :width] for x in (0, size_x - 1)
            )
            row_near = jnp.where(even("gx"), final, first)
            row_far = jnp.where(even("gx"), first, final)
            place = size_y + 4 * side + i
            at_near[place : place + 1, :] = row_near
            at_far[place : place + 1, :] = row_far
            if i == line:
                line_ends[2 * side : 2 * side + 1, :] = row_far
                line_ends[2 * side + 1 : 2 * side + 2, :] = row_near
    pack(at_near[...], x_near)
    pack(at_far[...], x_far)
    if x_near.shape[0] > x_far.shape[0]:
        count = coefs.shape[0]
        start = last + 8
        x_near[start : start + count, :] = coefs[...]
        x_near[start + count :, :] = from_far[packed_rows(size_y, width) :, :]


def third_kernel(
    levels,
    state,
    hyper,
    total,
    masses,
    inner,
    factors,
    to_near,
    to_far,
    from_far,
    from_near,
    ends_near,
    ends_far,
    out,
    work,
    turned,
    values,
    *unpacked,
):
    columns, width = total.shape
    size_x, size_y, _ = state.shape
    variables = width // levels
    rows = size_y + 8
    last, lanes = rows * (width // 128), rows // 8 * (width % 128)
    messages = (to_near, to_far, from_near, from_far)
    for message, target in zip(messages, unpacked):

        def write(first, count, lanes, value, target=target):
            target[first : first + count, lanes] = value

        unpack(message, rows, width, write)
    to_near, to_far, from_near, from_far = unpacked
    near, far = x_starts(columns, size_y)
    sides = ((0, 0, 3, 0), (1, size_y - 1, 0, size_y - 8))
    partners = (
        (near, to_near, from_near, from_far, ends_near, 0),
        (far, to_far, from_far, from_near, ends_far, 1),
    )
    work[...] = total[...]
    for start, _, theirs, _, _, _ in partners:
        work[pl.ds(pl.multiple_of(start, size_y), size_y), :] += theirs[:size_y, :width]
    for side, y, line, first in sides:
        place = size_y + 4 * side
        weights = [
            message[last : last + 8, lanes + 8 * side : lanes + 8 * side + 5] for message in messages
        ]
        for which, (start, mine, theirs, others, ends, _) in enumerate(partners):
            own, beyond = weights[which], weights[2 + which]
            terms = [
                (weight[:, i : i + 1], values, place + i)
                for i in range(4)
                for weight, values in ((own, theirs), (beyond, mine))
            ]
            terms += [(own[:, 4:5], others, place + line), (beyond[:, 4:5], ends, 2 * side + which)]
            added = sum(weight * values[row : row + 1, :width] for weight, values, row in terms)
            work[pl.ds(pl.multiple_of(start + first, 8), 8), :] += added
        for x in range(1, size_x - 1):
            row, weight = x * size_y + y, side * size_x + x
            work[row : row + 1, :] += (
                inner[weight : weight + 1, 0:1] * from_near[place + line : place + line + 1, :width]
                + inner[weight : weight + 1, 1:2] * from_far[place + line : place + line + 1, :width]
            )
    twice = masses[:, 1:2] * work[...]
    turned[...] = (state[...].reshape(columns, width) - hyper[...] * twice).T
    scale, down, up, keep, flow, cloud = (
        factors.at[i * levels : (i + 1) * levels] for i in range(6)
    )
    value = jnp.zeros((variables, columns), jnp.float32)
    for k in range(levels):
        rows = turned[pl.ds(k, variables, stride=levels), :]
        value = rows * scale[k : k + 1, :] + down[k : k + 1, :] * value
        values[k, :variables, :] = value
    solved = jnp.zeros((variables, columns), jnp.float32)
    for k in reversed(range(levels)):
        solved = values[k, :variables, :] + up[k : k + 1, :] * solved
        turned[pl.ds(k, variables, stride=levels), :] = solved
    heat, vapour, liquid = (turned.at[i * levels : (i + 1) * levels] for i in range(3))
    condensed = cloud[...] * 0.5 * jnp.maximum(vapour[...] - 0.3 * heat[...], 0.0)
    vapour[...] = vapour[...] - condensed
    heat[...] = heat[...] + 2.0 * condensed
    liquid[...] = (liquid[...] + condensed) * keep[...]
    settled = jnp.zeros((1, columns), jnp.float32)
    for k in range(levels):
        settled = liquid[k : k + 1, :] + flow[k : k + 1, :] * settled
        liquid[k : k + 1, :] = settled
    out[...] = turned[...].T.reshape(out.shape)


def pick(slots, pieces):
    size_x, size_y = slots.shape
    columns = size_x * size_y
    wanted = jnp.concatenate([slots[x : x + 1, :] for x in range(size_x)], axis=1)
    picked = 0.0
    for owner, rest in pieces:
        span = rest.shape[1]
        entry = lax.broadcasted_iota(jnp.int32, (span, columns), 0) + owner * span
        choice = (entry == wanted).astype(jnp.float32).astype(jnp.bfloat16)
        for _ in range(3):
            part = rest.astype(jnp.bfloat16)
            rest = rest - part.astype(jnp.float32)
            picked = picked + jnp.dot(part, choice, preferred_element_type=jnp.float32)
    return picked


def factor_kernel(levels, slots, *refs):
    factors = refs[-1]
    if len(refs) == 4:
        own, from_far, from_near = refs[:3]
        here = lax.axis_index("gx")
        count = own.shape[0]
        far, near = from_far.shape[0] - count, from_near.shape[0] - 2 * count
        pieces = [
            (here, own[...]),
            (here ^ 3, from_far[far:, :]),
            (here ^ 1, from_near[near : near + count, :]),
            (here ^ 2, from_near[near + count :, :]),
        ]
    else:
        pieces = [(peer, refs[0][peer]) for peer in range(refs[0].shape[0])]
    columns = factors.shape[1]
    picked = pick(slots, pieces)
    mixing, falling, covered = (picked[i * levels : (i + 1) * levels] for i in range(3))
    scale, down, up, keep, flow, cover = (
        factors.at[i * levels : (i + 1) * levels] for i in range(6)
    )
    gain = jnp.zeros((1, columns), jnp.float32)
    for k in range(levels):
        above = mixing[k : k + 1] if k else jnp.zeros_like(gain)
        below = mixing[k + 1 : k + 2] if k + 1 < levels else jnp.zeros_like(gain)
        centre = 1.0 + above + (below if k + 1 < levels else mixing[:1])
        inverse = 1.0 / (centre - above * gain)
        gain = below * inverse
        scale[k : k + 1, :] = inverse
        down[k : k + 1, :] = above * inverse
        up[k : k + 1, :] = gain
    kept = 1.0 / (1.0 + falling)
    keep[...] = kept
    flow[:1, :] = jnp.zeros((1, columns), jnp.float32)
    flow[1:, :] = falling[:-1] * kept[1:]
    cover[...] = covered


def swapped(value, axis, partner):
    return lax.ppermute(value, axis, [(i, partner(i)) for i in range(lax.axis_size(axis))])


def exchanged(near, far, axis):
    size = lax.axis_size(axis)
    from_far = swapped(far, axis, lambda i: (i + (1 if i % 2 else -1)) % size)
    from_near = swapped(near, axis, lambda i: i ^ 1)
    return from_far, from_near


def shifted(value, axis, step):
    size = lax.axis_size(axis)
    return lax.ppermute(value, axis, [(i, (i + step) % size) for i in range(size)])


def local(
    model_state, hyper_coef, point_mass, inverse_mass, span_slot, vert_diff, fall_rate, cloud_frac
):
    size_x, size_y, width = model_state.shape
    levels, span = vert_diff.shape[1:]
    columns = size_x * size_y
    hyper = hyper_coef.reshape(1, width)
    padded = -(-(width + 5) // 128) * 128
    tables = jnp.asarray(laplacian_tables(size_x, size_y))

    def array(*shape):
        return jax.ShapeDtypeStruct(shape, jnp.float32)

    def scratch(*shape):
        return pltpu.VMEM(shape, jnp.float32)

    def call(kernel, name, outs, scratches, *operands, spec=VMEM, cost=None):
        return pl.pallas_call(
            kernel,
            out_shape=outs,
            in_specs=[spec] * len(operands),
            out_specs=[VMEM] * len(outs),
            scratch_shapes=scratches,
            compiler_params=PARAMS,
            cost_estimate=cost,
            name=name,
        )(*operands)

    riding = lax.axis_size("gx") == 4
    whole = array(columns, width)
    edge = array(4 * size_x, padded)
    extra = 3 * levels if riding else 0
    first_rows, last_rows = packed_rows(size_y, width), packed_rows(size_y + 8, width)
    here, total, x_near, x_far, y_low, y_high, operator, masses, coefs = call(
        start_kernel,
        "start",
        [
            array(size_x, size_y, width),
            whole,
            array(first_rows, 128),
            array(first_rows + extra, 128),
            edge,
            edge,
            array(columns, columns),
            array(columns, 128),
            array(3 * levels, span),
        ],
        [
            scratch(size_x, size_y),
            scratch(size_x, size_y),
            scratch(*tables.shape),
            pltpu.SemaphoreType.DMA((7,)),
        ],
        *(
            pltpu.with_memory_space_constraint(value, pltpu.HBM)
            for value in (
                model_state,
                point_mass,
                inverse_mass,
                vert_diff,
                fall_rate,
                cloud_frac,
                tables,
            )
        ),
        spec=pl.BlockSpec(memory_space=pltpu.HBM),
    )
    low = shifted(y_high, "gy", 1)
    from_far, from_near = exchanged(x_near, x_far, "gx")
    y_low, _ = lax.optimization_barrier((y_low, from_near))
    high = shifted(y_low, "gy", -1)
    (low_weights,) = call(
        functools.partial(weights_kernel, size_x, size_y, width),
        "weights",
        [array(24, 128)],
        [],
        masses,
        low,
        cost=LONG,
    )
    total, x_near, x_far, line_ends, inner = call(
        functools.partial(second_kernel, size_x),
        "second",
        [
            whole,
            array(last_rows + 2 * extra, 128),
            array(last_rows, 128),
            array(4, width),
            array(2 * size_x, 128),
        ],
        [scratch(columns, width), scratch(size_y + 8, width), scratch(size_y + 8, width)],
        total,
        masses,
        operator,
        coefs,
        low_weights,
        low,
        from_far,
        from_near,
        high,
    )
    last_x = exchanged(x_near, x_far, "gx")
    peers = lax.axis_size("gx")
    ends_near = swapped(line_ends, "gx", lambda i: (i + (2 if i % 2 else -2)) % peers)
    ends_far = ends_near
    if peers != 4:
        ends_far = swapped(line_ends, "gx", lambda i: (i - (2 if i % 2 else -2)) % peers)
    if riding:
        pieces = [coefs, from_far, last_x[1]]
    else:
        pieces = [lax.all_gather(coefs, "gx")]
    (factors,) = call(
        functools.partial(factor_kernel, levels),
        "factors",
        [array(6 * levels, columns)],
        [],
        span_slot,
        *pieces,
    )
    (result,) = call(
        functools.partial(third_kernel, levels),
        "third",
        [array(size_x, size_y, width)],
        [scratch(columns, width), scratch(width, columns), scratch(levels, 16, columns)]
        + [scratch(size_y + 8, width)] * 4,
        here,
        hyper,
        total,
        masses,
        inner,
        factors,
        x_near,
        x_far,
        *last_x,
        ends_near,
        ends_far,
    )
    return result


def solution(mesh):
    placed = (
        P("gx", "gy", None),
        P(),
        P("gx", "gy"),
        P("gx", "gy"),
        P("gx", "gy"),
        P("gy", None, "gx"),
        P("gy", None, "gx"),
        P("gy", None, "gx"),
    )
    return jax.shard_map(
        local, mesh=mesh, in_specs=placed, out_specs=P("gx", "gy", None), check_vma=False
    )
```

```python
import functools

import jax
import jax.numpy as jnp
import numpy as np
from jax import lax
from jax.experimental import pallas as pl
from jax.experimental.pallas import tpu as pltpu
from jax.sharding import PartitionSpec as P

VMEM = pl.BlockSpec(memory_space=pltpu.VMEM)
LONG = pl.CostEstimate(flops=100_000_000_000, bytes_accessed=30_000_000, transcendentals=0)
PARAMS = pltpu.CompilerParams(vmem_limit_bytes=16 * 1024 * 1024)


def second_table():
    nodes = np.array([-1.0, -1.0 / np.sqrt(5.0), 1.0 / np.sqrt(5.0), 1.0])
    deriv = np.zeros((4, 4))
    for i in range(4):
        for j in range(4):
            if i == j:
                deriv[i, j] = sum(1.0 / (nodes[i] - nodes[k]) for k in range(4) if k != i)
            else:
                upper = np.prod([nodes[i] - nodes[k] for k in range(4) if k != i])
                lower = np.prod([nodes[j] - nodes[k] for k in range(4) if k != j])
                deriv[i, j] = upper / (lower * (nodes[i] - nodes[j]))
    return deriv @ deriv


def split(value):
    high = value.astype(jnp.bfloat16)
    return high, (value - high.astype(jnp.float32)).astype(jnp.bfloat16)


def product(left, right):
    left = jnp.concatenate([left[0], left[1], left[0]], axis=1)
    right = jnp.concatenate([right[0], right[0], right[1]], axis=0)
    return jnp.dot(left, right, preferred_element_type=jnp.float32)


def lookup(row, lane):
    second = second_table()
    row, lane = lax.rem(row, 4), lax.rem(lane, 4)
    result = jnp.zeros(row.shape, jnp.float32)
    for j in range(4):
        column = jnp.full(row.shape, float(second[3, j]), jnp.float32)
        for i in range(3):
            column = jnp.where(row == i, float(second[i, j]), column)
        result = jnp.where(lane == j, column, result)
    return result


def laplacian(size_x, size_y):
    count = size_x * size_y
    row, lane = (lax.broadcasted_iota(jnp.int32, (count, count), i) for i in range(2))
    row_x, lane_x = lax.div(row, size_y), lax.div(lane, size_y)
    row_y, lane_y = lax.rem(row, size_y), lax.rem(lane, size_y)
    same_x = (row_y == lane_y) & (lax.div(row_x, 4) == lax.div(lane_x, 4))
    same_y = (row_x == lane_x) & (lax.div(row_y, 4) == lax.div(lane_y, 4))
    along_x = jnp.where(same_x, lookup(row_x, lane_x), 0.0)
    return along_x + jnp.where(same_y, lookup(row_y, lane_y), 0.0)


def of_partner(values, size_y):
    count = values.shape[0]
    row_y = lax.rem(lax.broadcasted_iota(jnp.int32, values.shape, 0), size_y)
    phase = lax.rem(row_y, 4)
    before = jnp.where((phase == 0) & (row_y > 0), pltpu.roll(values, 1, 0), 0.0)
    after = (phase == 3) & (row_y < size_y - 1)
    return jnp.where(after, pltpu.roll(values, count - 1, 0), before)


def to_column(plane):
    size_x, size_y = plane.shape
    row = lax.broadcasted_iota(jnp.int32, (size_y, size_y), 0)
    lane = lax.broadcasted_iota(jnp.int32, (size_y, size_y), 1)
    parts = [
        jnp.sum(jnp.where(row == lane, plane[x : x + 1, :], 0.0), axis=1, keepdims=True)
        for x in range(size_x)
    ]
    return jnp.concatenate(parts, axis=0)


def even(axis):
    return lax.rem(lax.axis_index(axis), 2) == 0


def x_starts(count, size_y):
    near = jnp.where(even("gx"), count - size_y, 0)
    return near, count - size_y - near


def x_rows(count, size_y):
    starts = x_starts(count, size_y)
    return tuple(pl.ds(pl.multiple_of(start, size_y), size_y) for start in starts)


def add_packed(work, start, message, rows):
    def write(first, count, lanes, value):
        work[pl.ds(pl.multiple_of(start + first, 8), count), lanes] += value

    unpack(message, rows, work.shape[1], write)


def packed_rows(rows, width):
    return rows * (width // 128) + 8


def pack(value, message):
    rows, width = value.shape
    full, left = width // 128, width % 128
    for i in range(full):
        message[i * rows : (i + 1) * rows, :] = value[:, i * 128 : (i + 1) * 128]
    for i in range(rows // 8):
        lanes = slice(i * left, (i + 1) * left)
        message[full * rows : full * rows + 8, lanes] = value[i * 8 : (i + 1) * 8, full * 128 :]


def unpack(message, rows, width, write):
    full, left = width // 128, width % 128
    for i in range(full):
        write(0, rows, slice(i * 128, (i + 1) * 128), message[i * rows : (i + 1) * rows, :])
    for i in range(rows // 8):
        value = message[full * rows : full * rows + 8, i * left : (i + 1) * left]
        write(i * 8, 8, slice(full * 128, width), value)


def edge_rows(ref, y, size_x, size_y):
    return jnp.concatenate(
        [ref[x * size_y + y : x * size_y + y + 1, :] for x in range(size_x)], axis=0
    )


def start_kernel(
    state,
    mass,
    inverse,
    diff,
    fall,
    cloud,
    here,
    total,
    x_near,
    x_far,
    low,
    high,
    operator,
    columns,
    coefs,
    mass_here,
    inverse_here,
    sems,
):
    size_x, size_y, width = state.shape
    levels = diff.shape[1]
    pairs = [(mass, mass_here), (inverse, inverse_here)]
    pairs += [(state.at[x], here.at[x]) for x in range(size_x)]
    for i, source in enumerate((diff, fall, cloud)):
        pairs.append((source.at[0], coefs.at[i * levels : (i + 1) * levels]))
    copies = [
        pltpu.make_async_copy(source, target, sems.at[i])
        for i, (source, target) in enumerate(pairs)
    ]
    for copy in copies:
        copy.start()
    count = size_x * size_y
    matrix = laplacian(size_x, size_y)
    for copy in copies[:2]:
        copy.wait()
    own = jnp.broadcast_to(to_column(mass_here[...]), (count, count))
    matrix = own * matrix
    matrix = matrix + of_partner(matrix, size_y)
    operator[...] = matrix
    partner = of_partner(own, size_y)
    inverses = to_column(inverse_here[...])
    lane = lax.broadcasted_iota(jnp.int32, columns.shape, 1)
    columns[...] = jnp.where(lane == 0, own, jnp.where(lane == 1, inverses, partner))
    for copy in copies[2 : 2 + size_x]:
        copy.wait()
    total[...] = product(split(matrix), split(here[...].reshape(count, width)))
    near, far = x_rows(count, size_y)
    pack(total[near], x_near)
    pack(total[far], x_far)
    for first, message in ((0, low), (size_y - 4, high)):
        for i in range(4):
            rows = slice(i * size_x, (i + 1) * size_x)
            message[rows, :width] = edge_rows(total, first + i, size_x, size_y)
            message[rows, width : width + 2] = edge_rows(columns, first + i, size_x, size_y)[:, :2]
    for copy in copies[2 + size_x :]:
        copy.wait()
    if x_far.shape[0] > x_near.shape[0]:
        x_far[x_near.shape[0] :, :] = coefs[...]


def node_column(values, start, count):
    row = lax.broadcasted_iota(jnp.int32, (count, 1), 0)
    result = jnp.zeros((count, 1), jnp.float32)
    for i, value in enumerate(values):
        result = jnp.where(row == start + i, float(value), result)
    return result


def edge_weights(columns, message, size_x, size_y, width, edge, line):
    second = second_table()
    other = size_x - 1 - edge
    low = line == 3
    y, first = (0, 0) if low else (size_y - 1, size_y - 8)
    rows = slice(edge * size_y + first, edge * size_y + first + 8)
    here, there = (slice(x * size_y + y, x * size_y + y + 1) for x in (edge, other))
    mass, inverse = columns[here, 0:1], columns[here, 1:2]
    beyond = slice(line * size_x + edge, line * size_x + edge + 1)
    beyond_mass = message[beyond, width : width + 1]

    def beyond_inverse(i, x):
        return message[i * size_x + x : i * size_x + x + 1, width + 1 : width + 2]

    if low:
        own, partner = node_column(second[:, 0], 0, 8), node_column(second[3:, 0], 4, 8)
    else:
        own, partner = node_column(second[:, 3], 4, 8), node_column(second[:1, 3], 3, 8)
    along = inverse * (own * columns[rows, 0:1] + partner * columns[rows, 2:3])
    lane = lax.broadcasted_iota(jnp.int32, (8, 128), 1)
    place = lax.broadcasted_iota(jnp.int32, (8, 128), 0)
    tile = jnp.where(lane == line, along, 0.0)
    for i in range(4):
        value = float(second[line, i]) * beyond_mass * beyond_inverse(i, edge)
        if i == line:
            across = beyond_mass * beyond_inverse(line, edge) + mass * inverse
            value = value + float(second[edge, edge]) * across
        tile = tile + jnp.where((place == y - first) & (lane == i), value, 0.0)
    across = beyond_mass * beyond_inverse(line, other) + mass * columns[there, 1:2]
    value = float(second[edge, other]) * across
    return tile + jnp.where((place == y - first) & (lane == 4), value, 0.0)


def side_weights(columns, message, size_x, size_y, width, line):
    second = second_table()
    first, last = 0, size_x - 1
    tiles = [
        edge_weights(columns, message, size_x, size_y, width, edge, line) for edge in (first, last)
    ]
    mass = message[line * size_x : (line + 1) * size_x, width : width + 1]
    own = edge_rows(columns, 0 if line == 3 else size_y - 1, size_x, size_y)
    inner = []
    for edge in (first, last):
        inverse = message[line * size_x + edge : line * size_x + edge + 1, width + 1 : width + 2]
        across = mass * inverse + own[:, 0:1] * own[edge : edge + 1, 1:2]
        inner.append(node_column(second[:, edge], 0, size_x) * across)
    lane = lax.broadcasted_iota(jnp.int32, (size_x, 128), 1)
    from_last = jnp.where(even("gx"), 0, 1)
    return (
        jnp.where(even("gx"), tiles[1], tiles[0]),
        jnp.where(even("gx"), tiles[0], tiles[1]),
        jnp.where(lane == from_last, inner[1], inner[0]),
    )


def weights_kernel(size_x, size_y, width, columns, message, out):
    near, far, inner = side_weights(columns, message, size_x, size_y, width, 3)
    out[0:8, :] = near
    out[8:16, :] = far
    out[16 : 16 + size_x, :] = inner


def second_kernel(
    size_x,
    total,
    columns,
    operator,
    coefs,
    low_weights,
    low,
    from_far,
    from_near,
    high,
    out,
    x_near,
    x_far,
    line_ends,
    inner,
    work,
    at_near,
    at_far,
):
    size_y, width = total.shape[0] // size_x, total.shape[1]
    depth = size_y + 8
    second = second_table()
    near, far = x_starts(size_x * size_y, size_y)
    work[...] = total[...]
    add_packed(work, near, from_near, size_y)
    add_packed(work, far, from_far, size_y)
    sides = ((low, 0, 3, 0), (high, size_y - 1, 0, size_y - 8))
    beyond = []
    for message, y, line, _ in sides:
        lines = [message[i * size_x : (i + 1) * size_x, :width] for i in range(4)]
        lines[line] = lines[line] + edge_rows(work, y, size_x, size_y)
        for x in range(size_x):
            work[x * size_y + y : x * size_y + y + 1, :] = lines[line][x : x + 1]
        for i in range(4):
            inverse = message[i * size_x : (i + 1) * size_x, width + 1 : width + 2]
            lines[i] = inverse * lines[i]
        value = sum(float(second[line, i]) * lines[i] for i in range(4))
        for x in range(size_x):
            value = value + node_column(second[:, x], 0, size_x) * lines[line][x : x + 1]
        mass = message[line * size_x : (line + 1) * size_x, width : width + 1]
        beyond.append(mass * value)
    out[...] = product(split(operator[...]), split(columns[:, 1:2] * work[...]))
    for (_, y, _, _), rows in zip(sides, beyond):
        for x in range(size_x):
            out[x * size_y + y : x * size_y + y + 1, :] += rows[x : x + 1]

    near, far = x_rows(size_x * size_y, size_y)
    at_near[:size_y, :] = out[near]
    at_far[:size_y, :] = out[far]
    last = depth * (width // 128)
    lanes = depth // 8 * (width % 128)
    high_weights = side_weights(columns, high, size_x, size_y, width, 0)
    for side, (message, _, line, _) in enumerate(sides):
        weights = high_weights if side else [low_weights[i : i + 8] for i in (0, 8, 16)]
        inner[side * size_x : (side + 1) * size_x, :] = weights[2][:size_x]
        place = slice(lanes + 8 * side, lanes + 8 * side + 5)
        x_near[last : last + 8, place] = weights[0][:, :5]
        x_far[last : last + 8, place] = weights[1][:, :5]
        for i in range(4):
            first, final = (
                message[i * size_x + x : i * size_x + x + 1, :width] for x in (0, size_x - 1)
            )
            row_near = jnp.where(even("gx"), final, first)
            row_far = jnp.where(even("gx"), first, final)
            place = size_y + 4 * side + i
            at_near[place : place + 1, :] = row_near
            at_far[place : place + 1, :] = row_far
            if i == line:
                line_ends[2 * side : 2 * side + 1, :] = row_far
                line_ends[2 * side + 1 : 2 * side + 2, :] = row_near
    pack(at_near[...], x_near)
    pack(at_far[...], x_far)
    if x_near.shape[0] > x_far.shape[0]:
        count = coefs.shape[0]
        start = last + 8
        x_near[start : start + count, :] = coefs[...]
        x_near[start + count :, :] = from_far[packed_rows(size_y, width) :, :]


def third_kernel(
    levels,
    state,
    hyper,
    total,
    masses,
    inner,
    factors,
    to_near,
    to_far,
    from_far,
    from_near,
    ends_near,
    ends_far,
    out,
    work,
    turned,
    values,
    staged,
    sems,
    *unpacked,
):
    columns, width = total.shape
    size_x, size_y, _ = state.shape
    variables = width // levels
    rows = size_y + 8
    last, lanes = rows * (width // 128), rows // 8 * (width % 128)
    messages = (to_near, to_far, from_near, from_far)
    for message, target in zip(messages, unpacked):

        def write(first, count, lanes, value, target=target):
            target[first : first + count, lanes] = value

        unpack(message, rows, width, write)
    to_near, to_far, from_near, from_far = unpacked
    near, far = x_starts(columns, size_y)
    sides = ((0, 0, 3, 0), (1, size_y - 1, 0, size_y - 8))
    partners = (
        (near, to_near, from_near, from_far, ends_near, 0),
        (far, to_far, from_far, from_near, ends_far, 1),
    )
    work[...] = total[...]
    for start, _, theirs, _, _, _ in partners:
        work[pl.ds(pl.multiple_of(start, size_y), size_y), :] += theirs[:size_y, :width]
    for side, y, line, first in sides:
        place = size_y + 4 * side
        weights = [
            message[last : last + 8, lanes + 8 * side : lanes + 8 * side + 5] for message in messages
        ]
        for which, (start, mine, theirs, others, ends, _) in enumerate(partners):
            own, beyond = weights[which], weights[2 + which]
            terms = [
                (weight[:, i : i + 1], values, place + i)
                for i in range(4)
                for weight, values in ((own, theirs), (beyond, mine))
            ]
            terms += [(own[:, 4:5], others, place + line), (beyond[:, 4:5], ends, 2 * side + which)]
            added = sum(weight * values[row : row + 1, :width] for weight, values, row in terms)
            work[pl.ds(pl.multiple_of(start + first, 8), 8), :] += added
        for x in range(1, size_x - 1):
            row, weight = x * size_y + y, side * size_x + x
            work[row : row + 1, :] += (
                inner[weight : weight + 1, 0:1] * from_near[place + line : place + line + 1, :width]
                + inner[weight : weight + 1, 1:2] * from_far[place + line : place + line + 1, :width]
            )
    twice = masses[:, 1:2] * work[...]
    turned[...] = (state[...].reshape(columns, width) - hyper[...] * twice).T
    scale, carry, gain, keep, flow, cloud = (
        factors.at[i * levels : (i + 1) * levels] for i in range(6)
    )

    def level(k):
        return pl.ds(k, variables, stride=levels)

    half = levels // 2
    known = [jnp.zeros((variables, columns), jnp.float32)] * 2
    for i in range(half):
        for side, k in enumerate((i, levels - 1 - i)):
            scaled = turned[level(k), :] * scale[k : k + 1, :]
            known[side] = scaled + carry[k : k + 1, :] * known[side]
            values[k, :variables, :] = known[side]
    meet = factors[6 * levels + half : 6 * levels + half + 1, :]
    first = (known[0] + gain[half - 1 : half, :] * known[1]) * meet
    solved = [first, known[1] + gain[half : half + 1, :] * first]
    for i in reversed(range(half)):
        for side, k in enumerate((i, levels - 1 - i)):
            if i < half - 1:
                solved[side] = values[k, :variables, :] + gain[k : k + 1, :] * solved[side]
            turned[level(k), :] = solved[side]

    def leave(i):
        lanes = slice(i * 128, min((i + 1) * 128, width))
        staged[:, :, lanes] = turned[lanes, :].T.reshape(size_x, size_y, -1)
        copy = pltpu.make_async_copy(staged.at[:, :, lanes], out.at[:, :, lanes], sems.at[i])
        copy.start()
        return copy

    tiles = -(-width // 128)
    settled_tiles = -(-3 * levels // 128)
    copies = [leave(i) for i in range(settled_tiles, tiles)]
    heat, vapour, liquid = (turned.at[i * levels : (i + 1) * levels] for i in range(3))
    condensed = cloud[...] * 0.5 * jnp.maximum(vapour[...] - 0.3 * heat[...], 0.0)
    vapour[...] = vapour[...] - condensed
    heat[...] = heat[...] + 2.0 * condensed
    liquid[...] = (liquid[...] + condensed) * keep[...]
    settled = [jnp.zeros((1, columns), jnp.float32)] * 2
    for i in range(half):
        for side, k in enumerate((i, half + i)):
            settled[side] = liquid[k : k + 1, :] + flow[k : k + 1, :] * settled[side]
            liquid[k : k + 1, :] = settled[side]
    through = factors[6 * levels : 6 * levels + half, :]
    liquid[half:, :] = liquid[half:, :] + through * settled[0]
    copies += [leave(i) for i in range(settled_tiles)]
    for copy in copies:
        copy.wait()


def pick(slots, pieces):
    size_x, size_y = slots.shape
    columns = size_x * size_y
    wanted = jnp.concatenate([slots[x : x + 1, :] for x in range(size_x)], axis=1)
    picked = 0.0
    for owner, rest in pieces:
        span = rest.shape[1]
        entry = lax.broadcasted_iota(jnp.int32, (span, columns), 0) + owner * span
        choice = (entry == wanted).astype(jnp.float32).astype(jnp.bfloat16)
        for _ in range(3):
            part = rest.astype(jnp.bfloat16)
            rest = rest - part.astype(jnp.float32)
            picked = picked + jnp.dot(part, choice, preferred_element_type=jnp.float32)
    return picked


def factor_kernel(levels, slots, *refs):
    factors = refs[-1]
    if len(refs) == 4:
        own, from_far, from_near = refs[:3]
        here = lax.axis_index("gx")
        count = own.shape[0]
        far, near = from_far.shape[0] - count, from_near.shape[0] - 2 * count
        pieces = [
            (here, own[...]),
            (here ^ 3, from_far[far:, :]),
            (here ^ 1, from_near[near : near + count, :]),
            (here ^ 2, from_near[near + count :, :]),
        ]
    else:
        pieces = [(peer, refs[0][peer]) for peer in range(refs[0].shape[0])]
    columns = factors.shape[1]
    picked = pick(slots, pieces)
    mixing, falling, covered = (picked[i * levels : (i + 1) * levels] for i in range(3))
    scale, carry, gain, keep, flow, cover = (
        factors.at[i * levels : (i + 1) * levels] for i in range(6)
    )
    zero = jnp.zeros((1, columns), jnp.float32)
    kept = 1.0 / (1.0 + falling)
    keep[...] = kept
    flow[:1, :] = zero
    flow[1:, :] = falling[:-1] * kept[1:]
    cover[...] = covered
    half = levels // 2
    gains = [zero, zero]
    through = jnp.ones((1, columns), jnp.float32)
    for i in range(half):
        for side, k in enumerate((i, levels - 1 - i)):
            above = mixing[k : k + 1] if k else zero
            below = mixing[k + 1 : k + 2] if k + 1 < levels else zero
            centre = 1.0 + above + (below if k + 1 < levels else mixing[:1])
            behind, ahead = (above, below) if side == 0 else (below, above)
            inverse = 1.0 / (centre - behind * gains[side])
            gains[side] = ahead * inverse
            scale[k : k + 1, :] = inverse
            carry[k : k + 1, :] = behind * inverse
            gain[k : k + 1, :] = gains[side]
        k = half + i
        through = through * falling[k - 1 : k] * kept[k : k + 1]
        factors[6 * levels + i : 6 * levels + i + 1, :] = through
    last = 6 * levels + half
    factors[last : last + 1, :] = 1.0 / (1.0 - gains[0] * gains[1])


def swapped(value, axis, partner):
    return lax.ppermute(value, axis, [(i, partner(i)) for i in range(lax.axis_size(axis))])


def exchanged(near, far, axis):
    size = lax.axis_size(axis)
    from_far = swapped(far, axis, lambda i: (i + (1 if i % 2 else -1)) % size)
    from_near = swapped(near, axis, lambda i: i ^ 1)
    return from_far, from_near


def shifted(value, axis, step):
    size = lax.axis_size(axis)
    return lax.ppermute(value, axis, [(i, (i + step) % size) for i in range(size)])


def local(
    model_state, hyper_coef, point_mass, inverse_mass, span_slot, vert_diff, fall_rate, cloud_frac
):
    size_x, size_y, width = model_state.shape
    levels, span = vert_diff.shape[1:]
    columns = size_x * size_y
    hyper = hyper_coef.reshape(1, width)
    padded = -(-(width + 5) // 128) * 128

    def array(*shape):
        return jax.ShapeDtypeStruct(shape, jnp.float32)

    def scratch(*shape):
        return pltpu.VMEM(shape, jnp.float32)

    def call(kernel, name, outs, scratches, *operands, spec=VMEM, out=VMEM, cost=None):
        return pl.pallas_call(
            kernel,
            out_shape=outs,
            in_specs=[spec] * len(operands),
            out_specs=[out] * len(outs),
            scratch_shapes=scratches,
            compiler_params=PARAMS,
            cost_estimate=cost,
            name=name,
        )(*operands)

    riding = lax.axis_size("gx") == 4
    whole = array(columns, width)
    edge = array(4 * size_x, padded)
    extra = 3 * levels if riding else 0
    first_rows, last_rows = packed_rows(size_y, width), packed_rows(size_y + 8, width)
    here, total, x_near, x_far, y_low, y_high, operator, masses, coefs = call(
        start_kernel,
        "start",
        [
            array(size_x, size_y, width),
            whole,
            array(first_rows, 128),
            array(first_rows + extra, 128),
            edge,
            edge,
            array(columns, columns),
            array(columns, 128),
            array(3 * levels, span),
        ],
        [
            scratch(size_x, size_y),
            scratch(size_x, size_y),
            pltpu.SemaphoreType.DMA((size_x + 5,)),
        ],
        *(
            pltpu.with_memory_space_constraint(value, pltpu.HBM)
            for value in (
                model_state,
                point_mass,
                inverse_mass,
                vert_diff,
                fall_rate,
                cloud_frac,
            )
        ),
        spec=pl.BlockSpec(memory_space=pltpu.HBM),
    )
    low = shifted(y_high, "gy", 1)
    from_far, from_near = exchanged(x_near, x_far, "gx")
    y_low, _ = lax.optimization_barrier((y_low, from_near))
    high = shifted(y_low, "gy", -1)
    (low_weights,) = call(
        functools.partial(weights_kernel, size_x, size_y, width),
        "weights",
        [array(24, 128)],
        [],
        masses,
        low,
        cost=LONG,
    )
    total, x_near, x_far, line_ends, inner = call(
        functools.partial(second_kernel, size_x),
        "second",
        [
            whole,
            array(last_rows + 2 * extra, 128),
            array(last_rows, 128),
            array(4, width),
            array(2 * size_x, 128),
        ],
        [scratch(columns, width), scratch(size_y + 8, width), scratch(size_y + 8, width)],
        total,
        masses,
        operator,
        coefs,
        low_weights,
        low,
        from_far,
        from_near,
        high,
    )
    last_x = exchanged(x_near, x_far, "gx")
    peers = lax.axis_size("gx")
    ends_near = swapped(line_ends, "gx", lambda i: (i + (2 if i % 2 else -2)) % peers)
    ends_far = ends_near
    if peers != 4:
        ends_far = swapped(line_ends, "gx", lambda i: (i - (2 if i % 2 else -2)) % peers)
    if riding:
        pieces = [coefs, from_far, last_x[1]]
    else:
        pieces = [lax.all_gather(coefs, "gx")]
    (factors,) = call(
        functools.partial(factor_kernel, levels),
        "factors",
        [array(6 * levels + levels // 2 + 8, columns)],
        [],
        span_slot,
        *pieces,
    )
    (result,) = call(
        functools.partial(third_kernel, levels),
        "third",
        [array(size_x, size_y, width)],
        [
            scratch(columns, width),
            scratch(width, columns),
            scratch(levels, 16, columns),
            scratch(size_x, size_y, width),
            pltpu.SemaphoreType.DMA((-(-width // 128),)),
        ]
        + [scratch(size_y + 8, width)] * 4,
        here,
        hyper,
        total,
        masses,
        inner,
        factors,
        x_near,
        x_far,
        *last_x,
        ends_near,
        ends_far,
        out=pl.BlockSpec(memory_space=pltpu.HBM),
    )
    return result


def solution(mesh):
    placed = (
        P("gx", "gy", None),
        P(),
        P("gx", "gy"),
        P("gx", "gy"),
        P("gx", "gy"),
        P("gy", None, "gx"),
        P("gy", None, "gx"),
        P("gy", None, "gx"),
    )
    return jax.shard_map(
        local, mesh=mesh, in_specs=placed, out_specs=P("gx", "gy", None), check_vma=False
    )
```

```python
import functools

import jax
import jax.numpy as jnp
import numpy as np
from jax import lax
from jax.experimental import pallas as pl
from jax.experimental.pallas import tpu as pltpu
from jax.sharding import PartitionSpec as P

VMEM = pl.BlockSpec(memory_space=pltpu.VMEM)
LONG = pl.CostEstimate(flops=100_000_000_000, bytes_accessed=30_000_000, transcendentals=0)
PARAMS = pltpu.CompilerParams(vmem_limit_bytes=16 * 1024 * 1024)


def second_table():
    nodes = np.array([-1.0, -1.0 / np.sqrt(5.0), 1.0 / np.sqrt(5.0), 1.0])
    deriv = np.zeros((4, 4))
    for i in range(4):
        for j in range(4):
            if i == j:
                deriv[i, j] = sum(1.0 / (nodes[i] - nodes[k]) for k in range(4) if k != i)
            else:
                upper = np.prod([nodes[i] - nodes[k] for k in range(4) if k != i])
                lower = np.prod([nodes[j] - nodes[k] for k in range(4) if k != j])
                deriv[i, j] = upper / (lower * (nodes[i] - nodes[j]))
    return deriv @ deriv


def split(value):
    high = value.astype(jnp.bfloat16)
    return high, (value - high.astype(jnp.float32)).astype(jnp.bfloat16)


def product(left, right):
    left = jnp.concatenate([left[0], left[1], left[0]], axis=1)
    right = jnp.concatenate([right[0], right[0], right[1]], axis=0)
    return jnp.dot(left, right, preferred_element_type=jnp.float32)


def lookup(row, lane):
    second = second_table()
    row, lane = lax.rem(row, 4), lax.rem(lane, 4)
    result = jnp.zeros(row.shape, jnp.float32)
    for j in range(4):
        column = jnp.full(row.shape, float(second[3, j]), jnp.float32)
        for i in range(3):
            column = jnp.where(row == i, float(second[i, j]), column)
        result = jnp.where(lane == j, column, result)
    return result


def laplacian(size_x, size_y):
    count = size_x * size_y
    row, lane = (lax.broadcasted_iota(jnp.int32, (count, count), i) for i in range(2))
    row_x, lane_x = lax.div(row, size_y), lax.div(lane, size_y)
    row_y, lane_y = lax.rem(row, size_y), lax.rem(lane, size_y)
    same_x = (row_y == lane_y) & (lax.div(row_x, 4) == lax.div(lane_x, 4))
    same_y = (row_x == lane_x) & (lax.div(row_y, 4) == lax.div(lane_y, 4))
    along_x = jnp.where(same_x, lookup(row_x, lane_x), 0.0)
    return along_x + jnp.where(same_y, lookup(row_y, lane_y), 0.0)


def of_partner(values, size_y):
    count = values.shape[0]
    row_y = lax.rem(lax.broadcasted_iota(jnp.int32, values.shape, 0), size_y)
    phase = lax.rem(row_y, 4)
    before = jnp.where((phase == 0) & (row_y > 0), pltpu.roll(values, 1, 0), 0.0)
    after = (phase == 3) & (row_y < size_y - 1)
    return jnp.where(after, pltpu.roll(values, count - 1, 0), before)


def to_column(plane):
    size_x, size_y = plane.shape
    row = lax.broadcasted_iota(jnp.int32, (size_y, size_y), 0)
    lane = lax.broadcasted_iota(jnp.int32, (size_y, size_y), 1)
    parts = [
        jnp.sum(jnp.where(row == lane, plane[x : x + 1, :], 0.0), axis=1, keepdims=True)
        for x in range(size_x)
    ]
    return jnp.concatenate(parts, axis=0)


def even(axis):
    return lax.rem(lax.axis_index(axis), 2) == 0


def x_starts(count, size_y):
    near = jnp.where(even("gx"), count - size_y, 0)
    return near, count - size_y - near


def x_rows(count, size_y):
    starts = x_starts(count, size_y)
    return tuple(pl.ds(pl.multiple_of(start, size_y), size_y) for start in starts)


def add_packed(work, start, message, rows, left_message=None):
    def write(first, count, lanes, value):
        work[pl.ds(pl.multiple_of(start + first, 8), count), lanes] += value

    unpack(message, rows, work.shape[1], write, left_message)


def packed_rows(rows, width):
    return rows * (width // 128) + 8


def pack(value, message, left_message=None):
    rows, width = value.shape
    full, left = width // 128, width % 128
    for i in range(full):
        message[i * rows : (i + 1) * rows, :] = value[:, i * 128 : (i + 1) * 128]
    if left_message is None:
        left_message = message.at[full * rows : full * rows + 8]
    for i in range(rows // 8):
        lanes = slice(i * left, (i + 1) * left)
        left_message[:, lanes] = value[i * 8 : (i + 1) * 8, full * 128 :]


def unpack(message, rows, width, write, left_message=None):
    full, left = width // 128, width % 128
    for i in range(full):
        write(0, rows, slice(i * 128, (i + 1) * 128), message[i * rows : (i + 1) * rows, :])
    if left_message is None:
        left_message = message.at[full * rows : full * rows + 8]
    for i in range(rows // 8):
        value = left_message[:, i * left : (i + 1) * left]
        write(i * 8, 8, slice(full * 128, width), value)


def edge_rows(ref, y, size_x, size_y):
    return jnp.concatenate(
        [ref[x * size_y + y : x * size_y + y + 1, :] for x in range(size_x)], axis=0
    )


def start_kernel(
    state,
    mass,
    inverse,
    diff,
    fall,
    cloud,
    here,
    total,
    x_near,
    x_left,
    x_far,
    low,
    high,
    operator,
    columns,
    coefs,
    mass_here,
    inverse_here,
    sems,
):
    size_x, size_y, width = state.shape
    levels = diff.shape[1]
    pairs = [(mass, mass_here), (inverse, inverse_here)]
    pairs += [(state.at[x], here.at[x]) for x in range(size_x)]
    for i, source in enumerate((diff, fall, cloud)):
        pairs.append((source.at[0], coefs.at[i * levels : (i + 1) * levels]))
    copies = [
        pltpu.make_async_copy(source, target, sems.at[i])
        for i, (source, target) in enumerate(pairs)
    ]
    for copy in copies:
        copy.start()
    count = size_x * size_y
    matrix = laplacian(size_x, size_y)
    for copy in copies[:2]:
        copy.wait()
    own = jnp.broadcast_to(to_column(mass_here[...]), (count, count))
    matrix = own * matrix
    matrix = matrix + of_partner(matrix, size_y)
    operator[...] = matrix
    partner = of_partner(own, size_y)
    inverses = to_column(inverse_here[...])
    lane = lax.broadcasted_iota(jnp.int32, columns.shape, 1)
    columns[...] = jnp.where(lane == 0, own, jnp.where(lane == 1, inverses, partner))
    for copy in copies[2 : 2 + size_x]:
        copy.wait()
    total[...] = product(split(matrix), split(here[...].reshape(count, width)))
    near, far = x_rows(count, size_y)
    pack(total[near], x_near, x_left)
    pack(total[far], x_far)
    for first, message in ((0, low), (size_y - 4, high)):
        for i in range(4):
            rows = slice(i * size_x, (i + 1) * size_x)
            message[rows, :width] = edge_rows(total, first + i, size_x, size_y)
            message[rows, width : width + 2] = edge_rows(columns, first + i, size_x, size_y)[:, :2]
    for copy in copies[2 + size_x :]:
        copy.wait()
    used = x_near.shape[0] + 8
    if x_far.shape[0] > used:
        x_far[used:, :] = coefs[...]


def node_column(values, start, count):
    row = lax.broadcasted_iota(jnp.int32, (count, 1), 0)
    result = jnp.zeros((count, 1), jnp.float32)
    for i, value in enumerate(values):
        result = jnp.where(row == start + i, float(value), result)
    return result


def edge_weights(columns, message, size_x, size_y, width, edge, line):
    second = second_table()
    other = size_x - 1 - edge
    low = line == 3
    y, first = (0, 0) if low else (size_y - 1, size_y - 8)
    rows = slice(edge * size_y + first, edge * size_y + first + 8)
    here, there = (slice(x * size_y + y, x * size_y + y + 1) for x in (edge, other))
    mass, inverse = columns[here, 0:1], columns[here, 1:2]
    beyond = slice(line * size_x + edge, line * size_x + edge + 1)
    beyond_mass = message[beyond, width : width + 1]

    def beyond_inverse(i, x):
        return message[i * size_x + x : i * size_x + x + 1, width + 1 : width + 2]

    if low:
        own, partner = node_column(second[:, 0], 0, 8), node_column(second[3:, 0], 4, 8)
    else:
        own, partner = node_column(second[:, 3], 4, 8), node_column(second[:1, 3], 3, 8)
    along = inverse * (own * columns[rows, 0:1] + partner * columns[rows, 2:3])
    lane = lax.broadcasted_iota(jnp.int32, (8, 128), 1)
    place = lax.broadcasted_iota(jnp.int32, (8, 128), 0)
    tile = jnp.where(lane == line, along, 0.0)
    for i in range(4):
        value = float(second[line, i]) * beyond_mass * beyond_inverse(i, edge)
        if i == line:
            across = beyond_mass * beyond_inverse(line, edge) + mass * inverse
            value = value + float(second[edge, edge]) * across
        tile = tile + jnp.where((place == y - first) & (lane == i), value, 0.0)
    across = beyond_mass * beyond_inverse(line, other) + mass * columns[there, 1:2]
    value = float(second[edge, other]) * across
    return tile + jnp.where((place == y - first) & (lane == 4), value, 0.0)


def side_weights(columns, message, size_x, size_y, width, line):
    second = second_table()
    first, last = 0, size_x - 1
    tiles = [
        edge_weights(columns, message, size_x, size_y, width, edge, line) for edge in (first, last)
    ]
    mass = message[line * size_x : (line + 1) * size_x, width : width + 1]
    own = edge_rows(columns, 0 if line == 3 else size_y - 1, size_x, size_y)
    inner = []
    for edge in (first, last):
        inverse = message[line * size_x + edge : line * size_x + edge + 1, width + 1 : width + 2]
        across = mass * inverse + own[:, 0:1] * own[edge : edge + 1, 1:2]
        inner.append(node_column(second[:, edge], 0, size_x) * across)
    lane = lax.broadcasted_iota(jnp.int32, (size_x, 128), 1)
    from_last = jnp.where(even("gx"), 0, 1)
    return (
        jnp.where(even("gx"), tiles[1], tiles[0]),
        jnp.where(even("gx"), tiles[0], tiles[1]),
        jnp.where(lane == from_last, inner[1], inner[0]),
    )


def weights_kernel(size_x, size_y, width, columns, message, out):
    near, far, inner = side_weights(columns, message, size_x, size_y, width, 3)
    out[0:8, :] = near
    out[8:16, :] = far
    out[16 : 16 + size_x, :] = inner


def second_kernel(
    size_x,
    total,
    columns,
    operator,
    coefs,
    low_weights,
    low,
    from_far,
    from_near,
    left_near,
    high,
    out,
    x_near,
    x_far,
    line_ends,
    inner,
    work,
    at_near,
    at_far,
):
    size_y, width = total.shape[0] // size_x, total.shape[1]
    depth = size_y + 8
    second = second_table()
    near, far = x_starts(size_x * size_y, size_y)
    work[...] = total[...]
    add_packed(work, near, from_near, size_y, left_near)
    add_packed(work, far, from_far, size_y)
    sides = ((low, 0, 3, 0), (high, size_y - 1, 0, size_y - 8))
    beyond = []
    for message, y, line, _ in sides:
        lines = [message[i * size_x : (i + 1) * size_x, :width] for i in range(4)]
        lines[line] = lines[line] + edge_rows(work, y, size_x, size_y)
        for x in range(size_x):
            work[x * size_y + y : x * size_y + y + 1, :] = lines[line][x : x + 1]
        for i in range(4):
            inverse = message[i * size_x : (i + 1) * size_x, width + 1 : width + 2]
            lines[i] = inverse * lines[i]
        value = sum(float(second[line, i]) * lines[i] for i in range(4))
        for x in range(size_x):
            value = value + node_column(second[:, x], 0, size_x) * lines[line][x : x + 1]
        mass = message[line * size_x : (line + 1) * size_x, width : width + 1]
        beyond.append(mass * value)
    out[...] = product(split(operator[...]), split(columns[:, 1:2] * work[...]))
    for (_, y, _, _), rows in zip(sides, beyond):
        for x in range(size_x):
            out[x * size_y + y : x * size_y + y + 1, :] += rows[x : x + 1]

    near, far = x_rows(size_x * size_y, size_y)
    at_near[:size_y, :] = out[near]
    at_far[:size_y, :] = out[far]
    last = depth * (width // 128)
    lanes = depth // 8 * (width % 128)
    high_weights = side_weights(columns, high, size_x, size_y, width, 0)
    for side, (message, _, line, _) in enumerate(sides):
        weights = high_weights if side else [low_weights[i : i + 8] for i in (0, 8, 16)]
        inner[side * size_x : (side + 1) * size_x, :] = weights[2][:size_x]
        place = slice(lanes + 8 * side, lanes + 8 * side + 5)
        x_near[last : last + 8, place] = weights[0][:, :5]
        x_far[last : last + 8, place] = weights[1][:, :5]
        for i in range(4):
            first, final = (
                message[i * size_x + x : i * size_x + x + 1, :width] for x in (0, size_x - 1)
            )
            row_near = jnp.where(even("gx"), final, first)
            row_far = jnp.where(even("gx"), first, final)
            place = size_y + 4 * side + i
            at_near[place : place + 1, :] = row_near
            at_far[place : place + 1, :] = row_far
            if i == line:
                line_ends[2 * side : 2 * side + 1, :] = row_far
                line_ends[2 * side + 1 : 2 * side + 2, :] = row_near
    pack(at_near[...], x_near)
    pack(at_far[...], x_far)
    if x_near.shape[0] > x_far.shape[0]:
        count = coefs.shape[0]
        start = last + 8
        x_near[start : start + count, :] = coefs[...]
        x_near[start + count :, :] = from_far[packed_rows(size_y, width) :, :]


def third_kernel(
    levels,
    state,
    hyper,
    total,
    masses,
    inner,
    factors,
    to_near,
    to_far,
    from_far,
    from_near,
    ends_near,
    ends_far,
    out,
    work,
    turned,
    values,
    staged,
    sems,
    *beyond_rows,
):
    columns, width = total.shape
    size_x, size_y, _ = state.shape
    variables = width // levels
    rows = size_y + 8
    last, lanes = rows * (width // 128), rows // 8 * (width % 128)
    messages = (to_near, to_far, from_near, from_far)
    for message, target in zip(messages, beyond_rows):
        for i in range(width // 128):
            target[:, i * 128 : (i + 1) * 128] = message[i * rows + size_y : (i + 1) * rows, :]
        left = width % 128
        lanes_before = size_y // 8 * left
        target[:, width - left :] = message[last : last + 8, lanes_before : lanes_before + left]
    at_near, at_far, over_near, over_far = beyond_rows
    near, far = x_starts(columns, size_y)
    sides = ((0, 0, 3, 0), (1, size_y - 1, 0, size_y - 8))
    partners = (
        (near, at_near, over_near, over_far, ends_near),
        (far, at_far, over_far, over_near, ends_far),
    )
    work[...] = total[...]
    for start, message in ((near, from_near), (far, from_far)):
        for i in range(width // 128):
            place = pl.ds(pl.multiple_of(start, size_y), size_y)
            work[place, i * 128 : (i + 1) * 128] += message[i * rows : i * rows + size_y, :]
        for i in range(size_y // 8):
            place = pl.ds(pl.multiple_of(start + i * 8, 8), 8)
            left = width % 128
            work[place, width - left :] += message[last : last + 8, i * left : (i + 1) * left]
    for side, y, line, first in sides:
        place = 4 * side
        weights = [
            message[last : last + 8, lanes + 8 * side : lanes + 8 * side + 5] for message in messages
        ]
        for which, (start, mine, theirs, others, ends) in enumerate(partners):
            own, beyond = weights[which], weights[2 + which]
            terms = [
                (weight[:, i : i + 1], values, place + i)
                for i in range(4)
                for weight, values in ((own, theirs), (beyond, mine))
            ]
            terms += [(own[:, 4:5], others, place + line), (beyond[:, 4:5], ends, 2 * side + which)]
            added = sum(weight * values[row : row + 1, :width] for weight, values, row in terms)
            work[pl.ds(pl.multiple_of(start + first, 8), 8), :] += added
        for x in range(1, size_x - 1):
            row, weight = x * size_y + y, side * size_x + x
            work[row : row + 1, :] += (
                inner[weight : weight + 1, 0:1] * over_near[place + line : place + line + 1, :]
                + inner[weight : weight + 1, 1:2] * over_far[place + line : place + line + 1, :]
            )
    twice = masses[:, 1:2] * work[...]
    turned[...] = (state[...].reshape(columns, width) - hyper[...] * twice).T
    scale, carry, gain, keep, flow, cloud = (
        factors.at[i * levels : (i + 1) * levels] for i in range(6)
    )

    def level(k):
        return pl.ds(k, variables, stride=levels)

    half = levels // 2
    known = [jnp.zeros((variables, columns), jnp.float32)] * 2
    for i in range(half):
        for side, k in enumerate((i, levels - 1 - i)):
            scaled = turned[level(k), :] * scale[k : k + 1, :]
            known[side] = scaled + carry[k : k + 1, :] * known[side]
            values[k, :variables, :] = known[side]
    meet = factors[6 * levels + half : 6 * levels + half + 1, :]
    first = (known[0] + gain[half - 1 : half, :] * known[1]) * meet
    solved = [first, known[1] + gain[half : half + 1, :] * first]
    for i in reversed(range(half)):
        for side, k in enumerate((i, levels - 1 - i)):
            if i < half - 1:
                solved[side] = values[k, :variables, :] + gain[k : k + 1, :] * solved[side]
            turned[level(k), :] = solved[side]

    def leave(i):
        lanes = slice(i * 128, min((i + 1) * 128, width))
        staged[:, :, lanes] = turned[lanes, :].T.reshape(size_x, size_y, -1)
        copy = pltpu.make_async_copy(staged.at[:, :, lanes], out.at[:, :, lanes], sems.at[i])
        copy.start()
        return copy

    tiles = -(-width // 128)
    settled_tiles = -(-3 * levels // 128)
    copies = [leave(i) for i in range(settled_tiles, tiles)]
    heat, vapour, liquid = (turned.at[i * levels : (i + 1) * levels] for i in range(3))
    condensed = cloud[...] * 0.5 * jnp.maximum(vapour[...] - 0.3 * heat[...], 0.0)
    vapour[...] = vapour[...] - condensed
    heat[...] = heat[...] + 2.0 * condensed
    liquid[...] = (liquid[...] + condensed) * keep[...]
    settled = [jnp.zeros((1, columns), jnp.float32)] * 2
    for i in range(half):
        for side, k in enumerate((i, half + i)):
            settled[side] = liquid[k : k + 1, :] + flow[k : k + 1, :] * settled[side]
            liquid[k : k + 1, :] = settled[side]
    through = factors[6 * levels : 6 * levels + half, :]
    liquid[half:, :] = liquid[half:, :] + through * settled[0]
    copies += [leave(i) for i in range(settled_tiles)]
    for copy in copies:
        copy.wait()


def pick(slots, pieces):
    size_x, size_y = slots.shape
    columns = size_x * size_y
    wanted = jnp.concatenate([slots[x : x + 1, :] for x in range(size_x)], axis=1)
    picked = 0.0
    for owner, rest in pieces:
        span = rest.shape[1]
        entry = lax.broadcasted_iota(jnp.int32, (span, columns), 0) + owner * span
        choice = (entry == wanted).astype(jnp.float32).astype(jnp.bfloat16)
        for _ in range(3):
            part = rest.astype(jnp.bfloat16)
            rest = rest - part.astype(jnp.float32)
            picked = picked + jnp.dot(part, choice, preferred_element_type=jnp.float32)
    return picked


def factor_kernel(levels, slots, *refs):
    factors = refs[-1]
    if len(refs) == 4:
        own, from_far, from_near = refs[:3]
        here = lax.axis_index("gx")
        count = own.shape[0]
        far, near = from_far.shape[0] - count, from_near.shape[0] - 2 * count
        pieces = [
            (here, own[...]),
            (here ^ 3, from_far[far:, :]),
            (here ^ 1, from_near[near : near + count, :]),
            (here ^ 2, from_near[near + count :, :]),
        ]
    else:
        pieces = [(peer, refs[0][peer]) for peer in range(refs[0].shape[0])]
    columns = factors.shape[1]
    picked = pick(slots, pieces)
    mixing, falling, covered = (picked[i * levels : (i + 1) * levels] for i in range(3))
    scale, carry, gain, keep, flow, cover = (
        factors.at[i * levels : (i + 1) * levels] for i in range(6)
    )
    zero = jnp.zeros((1, columns), jnp.float32)
    kept = 1.0 / (1.0 + falling)
    keep[...] = kept
    flow[:1, :] = zero
    flow[1:, :] = falling[:-1] * kept[1:]
    cover[...] = covered
    half = levels // 2
    gains = [zero, zero]
    through = jnp.ones((1, columns), jnp.float32)
    for i in range(half):
        for side, k in enumerate((i, levels - 1 - i)):
            above = mixing[k : k + 1] if k else zero
            below = mixing[k + 1 : k + 2] if k + 1 < levels else zero
            centre = 1.0 + above + (below if k + 1 < levels else mixing[:1])
            behind, ahead = (above, below) if side == 0 else (below, above)
            inverse = 1.0 / (centre - behind * gains[side])
            gains[side] = ahead * inverse
            scale[k : k + 1, :] = inverse
            carry[k : k + 1, :] = behind * inverse
            gain[k : k + 1, :] = gains[side]
        k = half + i
        through = through * falling[k - 1 : k] * kept[k : k + 1]
        factors[6 * levels + i : 6 * levels + i + 1, :] = through
    last = 6 * levels + half
    factors[last : last + 1, :] = 1.0 / (1.0 - gains[0] * gains[1])


def swapped(value, axis, partner):
    return lax.ppermute(value, axis, [(i, partner(i)) for i in range(lax.axis_size(axis))])


def exchanged(near, far, axis):
    size = lax.axis_size(axis)
    from_far = swapped(far, axis, lambda i: (i + (1 if i % 2 else -1)) % size)
    from_near = swapped(near, axis, lambda i: i ^ 1)
    return from_far, from_near


def shifted(value, axis, step):
    size = lax.axis_size(axis)
    return lax.ppermute(value, axis, [(i, (i + step) % size) for i in range(size)])


def local(
    model_state, hyper_coef, point_mass, inverse_mass, span_slot, vert_diff, fall_rate, cloud_frac
):
    size_x, size_y, width = model_state.shape
    levels, span = vert_diff.shape[1:]
    columns = size_x * size_y
    hyper = hyper_coef.reshape(1, width)
    padded = -(-(width + 5) // 128) * 128

    def array(*shape):
        return jax.ShapeDtypeStruct(shape, jnp.float32)

    def scratch(*shape):
        return pltpu.VMEM(shape, jnp.float32)

    def call(kernel, name, outs, scratches, *operands, spec=VMEM, out=VMEM, cost=None):
        return pl.pallas_call(
            kernel,
            out_shape=outs,
            in_specs=[spec] * len(operands),
            out_specs=[out] * len(outs),
            scratch_shapes=scratches,
            compiler_params=PARAMS,
            cost_estimate=cost,
            name=name,
        )(*operands)

    riding = lax.axis_size("gx") == 4
    whole = array(columns, width)
    edge = array(4 * size_x, padded)
    extra = 3 * levels if riding else 0
    first_rows, last_rows = packed_rows(size_y, width), packed_rows(size_y + 8, width)
    here, total, x_near, x_left, x_far, y_low, y_high, operator, masses, coefs = call(
        start_kernel,
        "start",
        [
            array(size_x, size_y, width),
            whole,
            array(first_rows - 8, 128),
            array(8, 128),
            array(first_rows + extra, 128),
            edge,
            edge,
            array(columns, columns),
            array(columns, 128),
            array(3 * levels, span),
        ],
        [
            scratch(size_x, size_y),
            scratch(size_x, size_y),
            pltpu.SemaphoreType.DMA((size_x + 5,)),
        ],
        *(
            pltpu.with_memory_space_constraint(value, pltpu.HBM)
            for value in (
                model_state,
                point_mass,
                inverse_mass,
                vert_diff,
                fall_rate,
                cloud_frac,
            )
        ),
        spec=pl.BlockSpec(memory_space=pltpu.HBM),
    )
    low = shifted(y_high, "gy", 1)
    left_near = swapped(x_left, "gx", lambda i: i ^ 1)
    from_far, from_near = exchanged(x_near, x_far, "gx")
    y_low, _ = lax.optimization_barrier((y_low, left_near))
    high = shifted(y_low, "gy", -1)
    (low_weights,) = call(
        functools.partial(weights_kernel, size_x, size_y, width),
        "weights",
        [array(24, 128)],
        [],
        masses,
        low,
        cost=LONG,
    )
    total, x_near, x_far, line_ends, inner = call(
        functools.partial(second_kernel, size_x),
        "second",
        [
            whole,
            array(last_rows + 2 * extra, 128),
            array(last_rows, 128),
            array(4, width),
            array(2 * size_x, 128),
        ],
        [scratch(columns, width), scratch(size_y + 8, width), scratch(size_y + 8, width)],
        total,
        masses,
        operator,
        coefs,
        low_weights,
        low,
        from_far,
        from_near,
        left_near,
        high,
    )
    last_x = exchanged(x_near, x_far, "gx")
    peers = lax.axis_size("gx")
    ends_near = swapped(line_ends, "gx", lambda i: (i + (2 if i % 2 else -2)) % peers)
    ends_far = ends_near
    if peers != 4:
        ends_far = swapped(line_ends, "gx", lambda i: (i - (2 if i % 2 else -2)) % peers)
    if riding:
        pieces = [coefs, from_far, last_x[1]]
    else:
        pieces = [lax.all_gather(coefs, "gx")]
    (factors,) = call(
        functools.partial(factor_kernel, levels),
        "factors",
        [array(6 * levels + levels // 2 + 8, columns)],
        [],
        span_slot,
        *pieces,
    )
    (result,) = call(
        functools.partial(third_kernel, levels),
        "third",
        [array(size_x, size_y, width)],
        [
            scratch(columns, width),
            scratch(width, columns),
            scratch(levels, 16, columns),
            scratch(size_x, size_y, width),
            pltpu.SemaphoreType.DMA((-(-width // 128),)),
        ]
        + [scratch(8, width)] * 4,
        here,
        hyper,
        total,
        masses,
        inner,
        factors,
        x_near,
        x_far,
        *last_x,
        ends_near,
        ends_far,
        out=pl.BlockSpec(memory_space=pltpu.HBM),
    )
    return result


def solution(mesh):
    placed = (
        P("gx", "gy", None),
        P(),
        P("gx", "gy"),
        P("gx", "gy"),
        P("gx", "gy"),
        P("gy", None, "gx"),
        P("gy", None, "gx"),
        P("gy", None, "gx"),
    )
    return jax.shard_map(
        local, mesh=mesh, in_specs=placed, out_specs=P("gx", "gy", None), check_vma=False
    )
```

```python
import functools

import jax
import jax.numpy as jnp
import numpy as np
from jax import lax
from jax.experimental import pallas as pl
from jax.experimental.pallas import tpu as pltpu
from jax.sharding import PartitionSpec as P

VMEM = pl.BlockSpec(memory_space=pltpu.VMEM)
LONG = pl.CostEstimate(flops=100_000_000_000, bytes_accessed=30_000_000, transcendentals=0)
PARAMS = pltpu.CompilerParams(vmem_limit_bytes=16 * 1024 * 1024)


def second_table():
    nodes = np.array([-1.0, -1.0 / np.sqrt(5.0), 1.0 / np.sqrt(5.0), 1.0])
    deriv = np.zeros((4, 4))
    for i in range(4):
        for j in range(4):
            if i == j:
                deriv[i, j] = sum(1.0 / (nodes[i] - nodes[k]) for k in range(4) if k != i)
            else:
                upper = np.prod([nodes[i] - nodes[k] for k in range(4) if k != i])
                lower = np.prod([nodes[j] - nodes[k] for k in range(4) if k != j])
                deriv[i, j] = upper / (lower * (nodes[i] - nodes[j]))
    return deriv @ deriv


def split(value):
    high = value.astype(jnp.bfloat16)
    return high, (value - high.astype(jnp.float32)).astype(jnp.bfloat16)


def product(left, right):
    left = jnp.concatenate([left[0], left[1], left[0]], axis=1)
    right = jnp.concatenate([right[0], right[0], right[1]], axis=0)
    return jnp.dot(left, right, preferred_element_type=jnp.float32)


def lookup(row, lane):
    second = second_table()
    row, lane = lax.rem(row, 4), lax.rem(lane, 4)
    result = jnp.zeros(row.shape, jnp.float32)
    for j in range(4):
        column = jnp.full(row.shape, float(second[3, j]), jnp.float32)
        for i in range(3):
            column = jnp.where(row == i, float(second[i, j]), column)
        result = jnp.where(lane == j, column, result)
    return result


def laplacian(size_x, size_y):
    count = size_x * size_y
    row, lane = (lax.broadcasted_iota(jnp.int32, (count, count), i) for i in range(2))
    row_x, lane_x = lax.div(row, size_y), lax.div(lane, size_y)
    row_y, lane_y = lax.rem(row, size_y), lax.rem(lane, size_y)
    same_x = (row_y == lane_y) & (lax.div(row_x, 4) == lax.div(lane_x, 4))
    same_y = (row_x == lane_x) & (lax.div(row_y, 4) == lax.div(lane_y, 4))
    along_x = jnp.where(same_x, lookup(row_x, lane_x), 0.0)
    return along_x + jnp.where(same_y, lookup(row_y, lane_y), 0.0)


def of_partner(values, size_y):
    count = values.shape[0]
    row_y = lax.rem(lax.broadcasted_iota(jnp.int32, values.shape, 0), size_y)
    phase = lax.rem(row_y, 4)
    before = jnp.where((phase == 0) & (row_y > 0), pltpu.roll(values, 1, 0), 0.0)
    after = (phase == 3) & (row_y < size_y - 1)
    return jnp.where(after, pltpu.roll(values, count - 1, 0), before)


def to_column(plane):
    size_x, size_y = plane.shape
    row = lax.broadcasted_iota(jnp.int32, (size_y, size_y), 0)
    lane = lax.broadcasted_iota(jnp.int32, (size_y, size_y), 1)
    parts = [
        jnp.sum(jnp.where(row == lane, plane[x : x + 1, :], 0.0), axis=1, keepdims=True)
        for x in range(size_x)
    ]
    return jnp.concatenate(parts, axis=0)


def even(axis):
    return lax.rem(lax.axis_index(axis), 2) == 0


def x_starts(count, size_y):
    near = jnp.where(even("gx"), count - size_y, 0)
    return near, count - size_y - near


def x_rows(count, size_y):
    starts = x_starts(count, size_y)
    return tuple(pl.ds(pl.multiple_of(start, size_y), size_y) for start in starts)


def add_packed(work, start, message, rows, left_message=None):
    def write(first, count, lanes, value):
        work[pl.ds(pl.multiple_of(start + first, 8), count), lanes] += value

    unpack(message, rows, work.shape[1], write, left_message)


def packed_rows(rows, width):
    return rows * (width // 128) + 8


def pack(value, message, left_message=None):
    rows, width = value.shape
    full, left = width // 128, width % 128
    for i in range(full):
        message[i * rows : (i + 1) * rows, :] = value[:, i * 128 : (i + 1) * 128]
    if left_message is None:
        left_message = message.at[full * rows : full * rows + 8]
    for i in range(rows // 8):
        lanes = slice(i * left, (i + 1) * left)
        left_message[:, lanes] = value[i * 8 : (i + 1) * 8, full * 128 :]


def unpack(message, rows, width, write, left_message=None):
    full, left = width // 128, width % 128
    for i in range(full):
        write(0, rows, slice(i * 128, (i + 1) * 128), message[i * rows : (i + 1) * rows, :])
    if left_message is None:
        left_message = message.at[full * rows : full * rows + 8]
    for i in range(rows // 8):
        value = left_message[:, i * left : (i + 1) * left]
        write(i * 8, 8, slice(full * 128, width), value)


def edge_rows(ref, y, size_x, size_y):
    return jnp.concatenate(
        [ref[x * size_y + y : x * size_y + y + 1, :] for x in range(size_x)], axis=0
    )


def start_kernel(
    state,
    mass,
    inverse,
    diff,
    fall,
    cloud,
    here,
    total,
    x_near,
    x_left,
    x_far,
    low,
    high,
    operator,
    columns,
    coefs,
    mass_here,
    inverse_here,
    sems,
):
    size_x, size_y, width = state.shape
    levels = diff.shape[1]
    pairs = [(mass, mass_here), (inverse, inverse_here)]
    pairs += [(state.at[x], here.at[x]) for x in range(size_x)]
    for i, source in enumerate((diff, fall, cloud)):
        pairs.append((source.at[0], coefs.at[i * levels : (i + 1) * levels]))
    copies = [
        pltpu.make_async_copy(source, target, sems.at[i])
        for i, (source, target) in enumerate(pairs)
    ]
    for copy in copies:
        copy.start()
    count = size_x * size_y
    matrix = laplacian(size_x, size_y)
    for copy in copies[:2]:
        copy.wait()
    own = jnp.broadcast_to(to_column(mass_here[...]), (count, count))
    matrix = own * matrix
    matrix = matrix + of_partner(matrix, size_y)
    operator[...] = matrix
    partner = of_partner(own, size_y)
    inverses = to_column(inverse_here[...])
    lane = lax.broadcasted_iota(jnp.int32, columns.shape, 1)
    columns[...] = jnp.where(lane == 0, own, jnp.where(lane == 1, inverses, partner))
    for copy in copies[2 : 2 + size_x]:
        copy.wait()
    total[...] = product(split(matrix), split(here[...].reshape(count, width)))
    near, far = x_rows(count, size_y)
    pack(total[near], x_near, x_left)
    pack(total[far], x_far)
    for first, message in ((0, low), (size_y - 4, high)):
        for i in range(4):
            rows = slice(i * size_x, (i + 1) * size_x)
            message[rows, :width] = edge_rows(total, first + i, size_x, size_y)
            message[rows, width : width + 2] = edge_rows(columns, first + i, size_x, size_y)[:, :2]
    for copy in copies[2 + size_x :]:
        copy.wait()
    used = x_near.shape[0] + 8
    if x_far.shape[0] > used:
        x_far[used:, :] = coefs[...]


def node_column(values, start, count):
    row = lax.broadcasted_iota(jnp.int32, (count, 1), 0)
    result = jnp.zeros((count, 1), jnp.float32)
    for i, value in enumerate(values):
        result = jnp.where(row == start + i, float(value), result)
    return result


def edge_weights(columns, message, size_x, size_y, width, edge, line):
    second = second_table()
    other = size_x - 1 - edge
    low = line == 3
    y, first = (0, 0) if low else (size_y - 1, size_y - 8)
    rows = slice(edge * size_y + first, edge * size_y + first + 8)
    here, there = (slice(x * size_y + y, x * size_y + y + 1) for x in (edge, other))
    mass, inverse = columns[here, 0:1], columns[here, 1:2]
    beyond = slice(line * size_x + edge, line * size_x + edge + 1)
    beyond_mass = message[beyond, width : width + 1]

    def beyond_inverse(i, x):
        return message[i * size_x + x : i * size_x + x + 1, width + 1 : width + 2]

    if low:
        own, partner = node_column(second[:, 0], 0, 8), node_column(second[3:, 0], 4, 8)
    else:
        own, partner = node_column(second[:, 3], 4, 8), node_column(second[:1, 3], 3, 8)
    along = inverse * (own * columns[rows, 0:1] + partner * columns[rows, 2:3])
    lane = lax.broadcasted_iota(jnp.int32, (8, 128), 1)
    place = lax.broadcasted_iota(jnp.int32, (8, 128), 0)
    tile = jnp.where(lane == line, along, 0.0)
    for i in range(4):
        value = float(second[line, i]) * beyond_mass * beyond_inverse(i, edge)
        if i == line:
            across = beyond_mass * beyond_inverse(line, edge) + mass * inverse
            value = value + float(second[edge, edge]) * across
        tile = tile + jnp.where((place == y - first) & (lane == i), value, 0.0)
    across = beyond_mass * beyond_inverse(line, other) + mass * columns[there, 1:2]
    value = float(second[edge, other]) * across
    return tile + jnp.where((place == y - first) & (lane == 4), value, 0.0)


def side_weights(columns, message, size_x, size_y, width, line):
    second = second_table()
    first, last = 0, size_x - 1
    tiles = [
        edge_weights(columns, message, size_x, size_y, width, edge, line) for edge in (first, last)
    ]
    mass = message[line * size_x : (line + 1) * size_x, width : width + 1]
    own = edge_rows(columns, 0 if line == 3 else size_y - 1, size_x, size_y)
    inner = []
    for edge in (first, last):
        inverse = message[line * size_x + edge : line * size_x + edge + 1, width + 1 : width + 2]
        across = mass * inverse + own[:, 0:1] * own[edge : edge + 1, 1:2]
        inner.append(node_column(second[:, edge], 0, size_x) * across)
    lane = lax.broadcasted_iota(jnp.int32, (size_x, 128), 1)
    from_last = jnp.where(even("gx"), 0, 1)
    return (
        jnp.where(even("gx"), tiles[1], tiles[0]),
        jnp.where(even("gx"), tiles[0], tiles[1]),
        jnp.where(lane == from_last, inner[1], inner[0]),
    )


def weights_kernel(size_x, size_y, width, columns, message, out):
    near, far, inner = side_weights(columns, message, size_x, size_y, width, 3)
    out[0:8, :] = near
    out[8:16, :] = far
    out[16 : 16 + size_x, :] = inner


def second_kernel(
    size_x,
    total,
    columns,
    operator,
    coefs,
    low_weights,
    low,
    from_far,
    from_near,
    left_near,
    high,
    out,
    x_near,
    x_far,
    line_ends,
    inner,
    work,
    at_near,
    at_far,
):
    size_y, width = total.shape[0] // size_x, total.shape[1]
    depth = size_y + 8
    second = second_table()
    near, far = x_starts(size_x * size_y, size_y)
    work[...] = total[...]
    add_packed(work, near, from_near, size_y, left_near)
    add_packed(work, far, from_far, size_y)
    sides = ((low, 0, 3, 0), (high, size_y - 1, 0, size_y - 8))
    beyond = []
    for message, y, line, _ in sides:
        lines = [message[i * size_x : (i + 1) * size_x, :width] for i in range(4)]
        lines[line] = lines[line] + edge_rows(work, y, size_x, size_y)
        for x in range(size_x):
            work[x * size_y + y : x * size_y + y + 1, :] = lines[line][x : x + 1]
        for i in range(4):
            inverse = message[i * size_x : (i + 1) * size_x, width + 1 : width + 2]
            lines[i] = inverse * lines[i]
        value = sum(float(second[line, i]) * lines[i] for i in range(4))
        for x in range(size_x):
            value = value + node_column(second[:, x], 0, size_x) * lines[line][x : x + 1]
        mass = message[line * size_x : (line + 1) * size_x, width : width + 1]
        beyond.append(mass * value)
    out[...] = product(split(operator[...]), split(columns[:, 1:2] * work[...]))
    for (_, y, _, _), rows in zip(sides, beyond):
        for x in range(size_x):
            out[x * size_y + y : x * size_y + y + 1, :] += rows[x : x + 1]

    near, far = x_rows(size_x * size_y, size_y)
    at_near[:size_y, :] = out[near]
    at_far[:size_y, :] = out[far]
    last = depth * (width // 128)
    lanes = depth // 8 * (width % 128)
    high_weights = side_weights(columns, high, size_x, size_y, width, 0)
    for side, (message, _, line, _) in enumerate(sides):
        weights = high_weights if side else [low_weights[i : i + 8] for i in (0, 8, 16)]
        inner[side * size_x : (side + 1) * size_x, :] = weights[2][:size_x]
        place = slice(lanes + 8 * side, lanes + 8 * side + 5)
        x_near[last : last + 8, place] = weights[0][:, :5]
        x_far[last : last + 8, place] = weights[1][:, :5]
        for i in range(4):
            first, final = (
                message[i * size_x + x : i * size_x + x + 1, :width] for x in (0, size_x - 1)
            )
            row_near = jnp.where(even("gx"), final, first)
            row_far = jnp.where(even("gx"), first, final)
            place = size_y + 4 * side + i
            at_near[place : place + 1, :] = row_near
            at_far[place : place + 1, :] = row_far
            if i == line:
                line_ends[2 * side : 2 * side + 1, :] = row_far
                line_ends[2 * side + 1 : 2 * side + 2, :] = row_near
    pack(at_near[...], x_near)
    pack(at_far[...], x_far)
    if x_near.shape[0] > x_far.shape[0]:
        count = coefs.shape[0]
        start = last + 8
        x_near[start : start + count, :] = coefs[...]
        x_near[start + count :, :] = from_far[packed_rows(size_y, width) :, :]


def third_kernel(
    levels,
    state,
    hyper,
    total,
    masses,
    inner,
    factors,
    to_near,
    to_far,
    from_far,
    from_near,
    ends_near,
    ends_far,
    out,
    work,
    turned,
    values,
    staged,
    sems,
    *beyond_rows,
):
    columns, width = total.shape
    size_x, size_y, _ = state.shape
    variables = width // levels
    rows = size_y + 8
    last, lanes = rows * (width // 128), rows // 8 * (width % 128)
    messages = (to_near, to_far, from_near, from_far)
    for message, target in zip(messages, beyond_rows):
        for i in range(width // 128):
            target[:, i * 128 : (i + 1) * 128] = message[i * rows + size_y : (i + 1) * rows, :]
        left = width % 128
        lanes_before = size_y // 8 * left
        target[:, width - left :] = message[last : last + 8, lanes_before : lanes_before + left]
    at_near, at_far, over_near, over_far = beyond_rows
    near, far = x_starts(columns, size_y)
    sides = ((0, 0, 3, 0), (1, size_y - 1, 0, size_y - 8))
    partners = (
        (near, at_near, over_near, over_far, ends_near),
        (far, at_far, over_far, over_near, ends_far),
    )
    work[...] = total[...]
    for start, message in ((near, from_near), (far, from_far)):
        for i in range(width // 128):
            place = pl.ds(pl.multiple_of(start, size_y), size_y)
            work[place, i * 128 : (i + 1) * 128] += message[i * rows : i * rows + size_y, :]
        for i in range(size_y // 8):
            place = pl.ds(pl.multiple_of(start + i * 8, 8), 8)
            left = width % 128
            work[place, width - left :] += message[last : last + 8, i * left : (i + 1) * left]
    for side, y, line, first in sides:
        place = 4 * side
        weights = [
            message[last : last + 8, lanes + 8 * side : lanes + 8 * side + 5] for message in messages
        ]
        for which, (start, mine, theirs, others, ends) in enumerate(partners):
            own, beyond = weights[which], weights[2 + which]
            terms = [
                (weight[:, i : i + 1], values, place + i)
                for i in range(4)
                for weight, values in ((own, theirs), (beyond, mine))
            ]
            terms += [(own[:, 4:5], others, place + line), (beyond[:, 4:5], ends, 2 * side + which)]
            added = sum(weight * values[row : row + 1, :width] for weight, values, row in terms)
            work[pl.ds(pl.multiple_of(start + first, 8), 8), :] += added
        for x in range(1, size_x - 1):
            row, weight = x * size_y + y, side * size_x + x
            work[row : row + 1, :] += (
                inner[weight : weight + 1, 0:1] * over_near[place + line : place + line + 1, :]
                + inner[weight : weight + 1, 1:2] * over_far[place + line : place + line + 1, :]
            )
    twice = masses[:, 1:2] * work[...]
    dynamic = (state[...].reshape(columns, width) - hyper[...] * twice).T
    pitch = levels + 1
    for i in range(variables):
        turned[i * pitch : i * pitch + levels, :] = dynamic[i * levels : (i + 1) * levels]
    scale, carry, gain, keep, flow, cloud = (
        factors.at[i * levels : (i + 1) * levels] for i in range(6)
    )

    def level(k):
        return pl.ds(k, variables, stride=pitch)

    half = levels // 2
    known = [jnp.zeros((variables, columns), jnp.float32)] * 2
    for i in range(half):
        for side, k in enumerate((i, levels - 1 - i)):
            scaled = turned[level(k), :] * scale[k : k + 1, :]
            known[side] = scaled + carry[k : k + 1, :] * known[side]
            values[k, :variables, :] = known[side]
    meet = factors[6 * levels + half : 6 * levels + half + 1, :]
    first = (known[0] + gain[half - 1 : half, :] * known[1]) * meet
    solved = [first, known[1] + gain[half : half + 1, :] * first]
    for i in reversed(range(half)):
        for side, k in enumerate((i, levels - 1 - i)):
            if i < half - 1:
                solved[side] = values[k, :variables, :] + gain[k : k + 1, :] * solved[side]
            turned[level(k), :] = solved[side]

    def leave(i):
        lanes = slice(i * 128, min((i + 1) * 128, width))
        parts = []
        for j in range(variables):
            first, last = max(lanes.start, j * levels), min(lanes.stop, (j + 1) * levels)
            if first < last:
                parts.append(turned[first + j : last + j, :])
        rows = jnp.concatenate(parts, axis=0)
        staged[:, :, lanes] = rows.T.reshape(size_x, size_y, -1)
        copy = pltpu.make_async_copy(staged.at[:, :, lanes], out.at[:, :, lanes], sems.at[i])
        copy.start()
        return copy

    tiles = -(-width // 128)
    settled_tiles = -(-3 * levels // 128)
    copies = [leave(i) for i in range(settled_tiles, tiles)]
    heat, vapour, liquid = (turned.at[i * pitch : i * pitch + levels] for i in range(3))
    condensed = cloud[...] * 0.5 * jnp.maximum(vapour[...] - 0.3 * heat[...], 0.0)
    vapour[...] = vapour[...] - condensed
    heat[...] = heat[...] + 2.0 * condensed
    liquid[...] = (liquid[...] + condensed) * keep[...]
    settled = [jnp.zeros((1, columns), jnp.float32)] * 2
    for i in range(half):
        for side, k in enumerate((i, half + i)):
            settled[side] = liquid[k : k + 1, :] + flow[k : k + 1, :] * settled[side]
            liquid[k : k + 1, :] = settled[side]
    through = factors[6 * levels : 6 * levels + half, :]
    liquid[half:, :] = liquid[half:, :] + through * settled[0]
    copies += [leave(i) for i in range(settled_tiles)]
    for copy in copies:
        copy.wait()


def pick(slots, pieces):
    size_x, size_y = slots.shape
    columns = size_x * size_y
    wanted = jnp.concatenate([slots[x : x + 1, :] for x in range(size_x)], axis=1)
    picked = 0.0
    for owner, rest in pieces:
        span = rest.shape[1]
        entry = lax.broadcasted_iota(jnp.int32, (span, columns), 0) + owner * span
        choice = (entry == wanted).astype(jnp.float32).astype(jnp.bfloat16)
        for _ in range(3):
            part = rest.astype(jnp.bfloat16)
            rest = rest - part.astype(jnp.float32)
            picked = picked + jnp.dot(part, choice, preferred_element_type=jnp.float32)
    return picked


def factor_kernel(levels, slots, *refs):
    factors = refs[-1]
    if len(refs) == 4:
        own, from_far, from_near = refs[:3]
        here = lax.axis_index("gx")
        count = own.shape[0]
        far, near = from_far.shape[0] - count, from_near.shape[0] - 2 * count
        pieces = [
            (here, own[...]),
            (here ^ 3, from_far[far:, :]),
            (here ^ 1, from_near[near : near + count, :]),
            (here ^ 2, from_near[near + count :, :]),
        ]
    else:
        pieces = [(peer, refs[0][peer]) for peer in range(refs[0].shape[0])]
    columns = factors.shape[1]
    picked = pick(slots, pieces)
    mixing, falling, covered = (picked[i * levels : (i + 1) * levels] for i in range(3))
    scale, carry, gain, keep, flow, cover = (
        factors.at[i * levels : (i + 1) * levels] for i in range(6)
    )
    zero = jnp.zeros((1, columns), jnp.float32)
    kept = 1.0 / (1.0 + falling)
    keep[...] = kept
    flow[:1, :] = zero
    flow[1:, :] = falling[:-1] * kept[1:]
    cover[...] = covered
    half = levels // 2
    gains = [zero, zero]
    through = jnp.ones((1, columns), jnp.float32)
    for i in range(half):
        for side, k in enumerate((i, levels - 1 - i)):
            above = mixing[k : k + 1] if k else zero
            below = mixing[k + 1 : k + 2] if k + 1 < levels else zero
            centre = 1.0 + above + (below if k + 1 < levels else mixing[:1])
            behind, ahead = (above, below) if side == 0 else (below, above)
            inverse = 1.0 / (centre - behind * gains[side])
            gains[side] = ahead * inverse
            scale[k : k + 1, :] = inverse
            carry[k : k + 1, :] = behind * inverse
            gain[k : k + 1, :] = gains[side]
        k = half + i
        through = through * falling[k - 1 : k] * kept[k : k + 1]
        factors[6 * levels + i : 6 * levels + i + 1, :] = through
    last = 6 * levels + half
    factors[last : last + 1, :] = 1.0 / (1.0 - gains[0] * gains[1])


def swapped(value, axis, partner):
    return lax.ppermute(value, axis, [(i, partner(i)) for i in range(lax.axis_size(axis))])


def exchanged(near, far, axis):
    size = lax.axis_size(axis)
    from_far = swapped(far, axis, lambda i: (i + (1 if i % 2 else -1)) % size)
    from_near = swapped(near, axis, lambda i: i ^ 1)
    return from_far, from_near


def shifted(value, axis, step):
    size = lax.axis_size(axis)
    return lax.ppermute(value, axis, [(i, (i + step) % size) for i in range(size)])


def local(
    model_state, hyper_coef, point_mass, inverse_mass, span_slot, vert_diff, fall_rate, cloud_frac
):
    size_x, size_y, width = model_state.shape
    levels, span = vert_diff.shape[1:]
    columns = size_x * size_y
    hyper = hyper_coef.reshape(1, width)
    padded = -(-(width + 5) // 128) * 128

    def array(*shape):
        return jax.ShapeDtypeStruct(shape, jnp.float32)

    def scratch(*shape):
        return pltpu.VMEM(shape, jnp.float32)

    def call(kernel, name, outs, scratches, *operands, spec=VMEM, out=VMEM, cost=None):
        return pl.pallas_call(
            kernel,
            out_shape=outs,
            in_specs=[spec] * len(operands),
            out_specs=[out] * len(outs),
            scratch_shapes=scratches,
            compiler_params=PARAMS,
            cost_estimate=cost,
            name=name,
        )(*operands)

    riding = lax.axis_size("gx") == 4
    whole = array(columns, width)
    edge = array(4 * size_x, padded)
    extra = 3 * levels if riding else 0
    first_rows, last_rows = packed_rows(size_y, width), packed_rows(size_y + 8, width)
    here, total, x_near, x_left, x_far, y_low, y_high, operator, masses, coefs = call(
        start_kernel,
        "start",
        [
            array(size_x, size_y, width),
            whole,
            array(first_rows - 8, 128),
            array(8, 128),
            array(first_rows + extra, 128),
            edge,
            edge,
            array(columns, columns),
            array(columns, 128),
            array(3 * levels, span),
        ],
        [
            scratch(size_x, size_y),
            scratch(size_x, size_y),
            pltpu.SemaphoreType.DMA((size_x + 5,)),
        ],
        *(
            pltpu.with_memory_space_constraint(value, pltpu.HBM)
            for value in (
                model_state,
                point_mass,
                inverse_mass,
                vert_diff,
                fall_rate,
                cloud_frac,
            )
        ),
        spec=pl.BlockSpec(memory_space=pltpu.HBM),
    )
    low = shifted(y_high, "gy", 1)
    left_near = swapped(x_left, "gx", lambda i: i ^ 1)
    from_far, from_near = exchanged(x_near, x_far, "gx")
    y_low, _ = lax.optimization_barrier((y_low, left_near))
    high = shifted(y_low, "gy", -1)
    (low_weights,) = call(
        functools.partial(weights_kernel, size_x, size_y, width),
        "weights",
        [array(24, 128)],
        [],
        masses,
        low,
        cost=LONG,
    )
    total, x_near, x_far, line_ends, inner = call(
        functools.partial(second_kernel, size_x),
        "second",
        [
            whole,
            array(last_rows + 2 * extra, 128),
            array(last_rows, 128),
            array(4, width),
            array(2 * size_x, 128),
        ],
        [scratch(columns, width), scratch(size_y + 8, width), scratch(size_y + 8, width)],
        total,
        masses,
        operator,
        coefs,
        low_weights,
        low,
        from_far,
        from_near,
        left_near,
        high,
    )
    last_x = exchanged(x_near, x_far, "gx")
    peers = lax.axis_size("gx")
    ends_near = swapped(line_ends, "gx", lambda i: (i + (2 if i % 2 else -2)) % peers)
    ends_far = ends_near
    if peers != 4:
        ends_far = swapped(line_ends, "gx", lambda i: (i - (2 if i % 2 else -2)) % peers)
    if riding:
        pieces = [coefs, from_far, last_x[1]]
    else:
        pieces = [lax.all_gather(coefs, "gx")]
    (factors,) = call(
        functools.partial(factor_kernel, levels),
        "factors",
        [array(6 * levels + levels // 2 + 8, columns)],
        [],
        span_slot,
        *pieces,
    )
    (result,) = call(
        functools.partial(third_kernel, levels),
        "third",
        [array(size_x, size_y, width)],
        [
            scratch(columns, width),
            scratch(width // levels * (levels + 1), columns),
            scratch(levels, 16, columns),
            scratch(size_x, size_y, width),
            pltpu.SemaphoreType.DMA((-(-width // 128),)),
        ]
        + [scratch(8, width)] * 4,
        here,
        hyper,
        total,
        masses,
        inner,
        factors,
        x_near,
        x_far,
        *last_x,
        ends_near,
        ends_far,
        out=pl.BlockSpec(memory_space=pltpu.HBM),
    )
    return result


def solution(mesh):
    placed = (
        P("gx", "gy", None),
        P(),
        P("gx", "gy"),
        P("gx", "gy"),
        P("gx", "gy"),
        P("gy", None, "gx"),
        P("gy", None, "gx"),
        P("gy", None, "gx"),
    )
    return jax.shard_map(
        local, mesh=mesh, in_specs=placed, out_specs=P("gx", "gy", None), check_vma=False
    )
```

```python
import functools

import jax
import jax.numpy as jnp
import numpy as np
from jax import lax
from jax.experimental import pallas as pl
from jax.experimental.pallas import tpu as pltpu
from jax.sharding import PartitionSpec as P

VMEM = pl.BlockSpec(memory_space=pltpu.VMEM)
LONG = pl.CostEstimate(flops=100_000_000_000, bytes_accessed=30_000_000, transcendentals=0)
PARAMS = pltpu.CompilerParams(vmem_limit_bytes=16 * 1024 * 1024)


def second_table():
    nodes = np.array([-1.0, -1.0 / np.sqrt(5.0), 1.0 / np.sqrt(5.0), 1.0])
    deriv = np.zeros((4, 4))
    for i in range(4):
        for j in range(4):
            if i == j:
                deriv[i, j] = sum(1.0 / (nodes[i] - nodes[k]) for k in range(4) if k != i)
            else:
                upper = np.prod([nodes[i] - nodes[k] for k in range(4) if k != i])
                lower = np.prod([nodes[j] - nodes[k] for k in range(4) if k != j])
                deriv[i, j] = upper / (lower * (nodes[i] - nodes[j]))
    return deriv @ deriv


def split(value):
    high = value.astype(jnp.bfloat16)
    return high, (value - high.astype(jnp.float32)).astype(jnp.bfloat16)


def product(left, right):
    left = jnp.concatenate([left[0], left[1], left[0]], axis=1)
    right = jnp.concatenate([right[0], right[0], right[1]], axis=0)
    return jnp.dot(left, right, preferred_element_type=jnp.float32)


def lookup(row, lane):
    second = second_table()
    row, lane = lax.rem(row, 4), lax.rem(lane, 4)
    result = jnp.zeros(row.shape, jnp.float32)
    for j in range(4):
        column = jnp.full(row.shape, float(second[3, j]), jnp.float32)
        for i in range(3):
            column = jnp.where(row == i, float(second[i, j]), column)
        result = jnp.where(lane == j, column, result)
    return result


def laplacian(size_x, size_y):
    count = size_x * size_y
    row, lane = (lax.broadcasted_iota(jnp.int32, (count, count), i) for i in range(2))
    row_x, lane_x = lax.div(row, size_y), lax.div(lane, size_y)
    row_y, lane_y = lax.rem(row, size_y), lax.rem(lane, size_y)
    same_x = (row_y == lane_y) & (lax.div(row_x, 4) == lax.div(lane_x, 4))
    same_y = (row_x == lane_x) & (lax.div(row_y, 4) == lax.div(lane_y, 4))
    along_x = jnp.where(same_x, lookup(row_x, lane_x), 0.0)
    return along_x + jnp.where(same_y, lookup(row_y, lane_y), 0.0)


def of_partner(values, size_y):
    count = values.shape[0]
    row_y = lax.rem(lax.broadcasted_iota(jnp.int32, values.shape, 0), size_y)
    phase = lax.rem(row_y, 4)
    before = jnp.where((phase == 0) & (row_y > 0), pltpu.roll(values, 1, 0), 0.0)
    after = (phase == 3) & (row_y < size_y - 1)
    return jnp.where(after, pltpu.roll(values, count - 1, 0), before)


def to_column(plane):
    size_x, size_y = plane.shape
    row = lax.broadcasted_iota(jnp.int32, (size_y, size_y), 0)
    lane = lax.broadcasted_iota(jnp.int32, (size_y, size_y), 1)
    parts = [
        jnp.sum(jnp.where(row == lane, plane[x : x + 1, :], 0.0), axis=1, keepdims=True)
        for x in range(size_x)
    ]
    return jnp.concatenate(parts, axis=0)


def even(axis):
    return lax.rem(lax.axis_index(axis), 2) == 0


def x_starts(count, size_y):
    near = jnp.where(even("gx"), count - size_y, 0)
    return near, count - size_y - near


def x_rows(count, size_y):
    starts = x_starts(count, size_y)
    return tuple(pl.ds(pl.multiple_of(start, size_y), size_y) for start in starts)


def add_packed(work, start, message, rows, left_message=None):
    def write(first, count, lanes, value):
        work[pl.ds(pl.multiple_of(start + first, 8), count), lanes] += value

    unpack(message, rows, work.shape[1], write, left_message)


def packed_rows(rows, width):
    return rows * (width // 128) + 8


def pack(value, message, left_message=None):
    rows, width = value.shape
    full, left = width // 128, width % 128
    for i in range(full):
        message[i * rows : (i + 1) * rows, :] = value[:, i * 128 : (i + 1) * 128]
    if left_message is None:
        left_message = message.at[full * rows : full * rows + 8]
    for i in range(rows // 8):
        lanes = slice(i * left, (i + 1) * left)
        left_message[:, lanes] = value[i * 8 : (i + 1) * 8, full * 128 :]


def unpack(message, rows, width, write, left_message=None):
    full, left = width // 128, width % 128
    for i in range(full):
        write(0, rows, slice(i * 128, (i + 1) * 128), message[i * rows : (i + 1) * rows, :])
    if left_message is None:
        left_message = message.at[full * rows : full * rows + 8]
    for i in range(rows // 8):
        value = left_message[:, i * left : (i + 1) * left]
        write(i * 8, 8, slice(full * 128, width), value)


def edge_rows(ref, y, size_x, size_y):
    return jnp.concatenate(
        [ref[x * size_y + y : x * size_y + y + 1, :] for x in range(size_x)], axis=0
    )


def start_kernel(
    state,
    mass,
    inverse,
    diff,
    fall,
    cloud,
    here,
    total,
    x_near,
    x_left,
    x_far,
    low,
    high,
    operator,
    columns,
    coefs,
    mass_here,
    inverse_here,
    sems,
):
    size_x, size_y, width = state.shape
    levels = diff.shape[1]
    pairs = [(mass, mass_here), (inverse, inverse_here)]
    pairs += [(state.at[x], here.at[x]) for x in range(size_x)]
    for i, source in enumerate((diff, fall, cloud)):
        pairs.append((source.at[0], coefs.at[i * levels : (i + 1) * levels]))
    copies = [
        pltpu.make_async_copy(source, target, sems.at[i])
        for i, (source, target) in enumerate(pairs)
    ]
    for copy in copies:
        copy.start()
    count = size_x * size_y
    matrix = laplacian(size_x, size_y)
    for copy in copies[:2]:
        copy.wait()
    own = jnp.broadcast_to(to_column(mass_here[...]), (count, count))
    matrix = own * matrix
    matrix = matrix + of_partner(matrix, size_y)
    operator[...] = matrix
    partner = of_partner(own, size_y)
    inverses = to_column(inverse_here[...])
    lane = lax.broadcasted_iota(jnp.int32, columns.shape, 1)
    columns[...] = jnp.where(lane == 0, own, jnp.where(lane == 1, inverses, partner))
    for copy in copies[2 : 2 + size_x]:
        copy.wait()
    total[...] = product(split(matrix), split(here[...].reshape(count, width)))
    near, far = x_rows(count, size_y)
    pack(total[near], x_near, x_left)
    pack(total[far], x_far)
    for first, message in ((0, low), (size_y - 4, high)):
        for i in range(4):
            rows = slice(i * size_x, (i + 1) * size_x)
            message[rows, :width] = edge_rows(total, first + i, size_x, size_y)
            message[rows, width : width + 2] = edge_rows(columns, first + i, size_x, size_y)[:, :2]
    for copy in copies[2 + size_x :]:
        copy.wait()
    used = x_near.shape[0] + 8
    if x_far.shape[0] > used:
        x_far[used:, :] = coefs[...]


def node_column(values, start, count):
    row = lax.broadcasted_iota(jnp.int32, (count, 1), 0)
    result = jnp.zeros((count, 1), jnp.float32)
    for i, value in enumerate(values):
        result = jnp.where(row == start + i, float(value), result)
    return result


def edge_weights(columns, message, size_x, size_y, width, edge, line):
    second = second_table()
    other = size_x - 1 - edge
    low = line == 3
    y, first = (0, 0) if low else (size_y - 1, size_y - 8)
    rows = slice(edge * size_y + first, edge * size_y + first + 8)
    here, there = (slice(x * size_y + y, x * size_y + y + 1) for x in (edge, other))
    mass, inverse = columns[here, 0:1], columns[here, 1:2]
    beyond = slice(line * size_x + edge, line * size_x + edge + 1)
    beyond_mass = message[beyond, width : width + 1]

    def beyond_inverse(i, x):
        return message[i * size_x + x : i * size_x + x + 1, width + 1 : width + 2]

    if low:
        own, partner = node_column(second[:, 0], 0, 8), node_column(second[3:, 0], 4, 8)
    else:
        own, partner = node_column(second[:, 3], 4, 8), node_column(second[:1, 3], 3, 8)
    along = inverse * (own * columns[rows, 0:1] + partner * columns[rows, 2:3])
    lane = lax.broadcasted_iota(jnp.int32, (8, 128), 1)
    place = lax.broadcasted_iota(jnp.int32, (8, 128), 0)
    tile = jnp.where(lane == line, along, 0.0)
    for i in range(4):
        value = float(second[line, i]) * beyond_mass * beyond_inverse(i, edge)
        if i == line:
            across = beyond_mass * beyond_inverse(line, edge) + mass * inverse
            value = value + float(second[edge, edge]) * across
        tile = tile + jnp.where((place == y - first) & (lane == i), value, 0.0)
    across = beyond_mass * beyond_inverse(line, other) + mass * columns[there, 1:2]
    value = float(second[edge, other]) * across
    return tile + jnp.where((place == y - first) & (lane == 4), value, 0.0)


def side_weights(columns, message, size_x, size_y, width, line):
    second = second_table()
    first, last = 0, size_x - 1
    tiles = [
        edge_weights(columns, message, size_x, size_y, width, edge, line) for edge in (first, last)
    ]
    mass = message[line * size_x : (line + 1) * size_x, width : width + 1]
    own = edge_rows(columns, 0 if line == 3 else size_y - 1, size_x, size_y)
    inner = []
    for edge in (first, last):
        inverse = message[line * size_x + edge : line * size_x + edge + 1, width + 1 : width + 2]
        across = mass * inverse + own[:, 0:1] * own[edge : edge + 1, 1:2]
        inner.append(node_column(second[:, edge], 0, size_x) * across)
    lane = lax.broadcasted_iota(jnp.int32, (size_x, 128), 1)
    from_last = jnp.where(even("gx"), 0, 1)
    return (
        jnp.where(even("gx"), tiles[1], tiles[0]),
        jnp.where(even("gx"), tiles[0], tiles[1]),
        jnp.where(lane == from_last, inner[1], inner[0]),
    )


def weights_kernel(size_x, size_y, width, columns, message, out):
    near, far, inner = side_weights(columns, message, size_x, size_y, width, 3)
    out[0:8, :] = near
    out[8:16, :] = far
    out[16 : 16 + size_x, :] = inner


def second_kernel(
    size_x,
    total,
    columns,
    operator,
    coefs,
    low_weights,
    low,
    from_far,
    from_near,
    left_near,
    high,
    out,
    x_near,
    x_far,
    line_ends,
    inner,
    work,
    at_near,
    at_far,
):
    size_y, width = total.shape[0] // size_x, total.shape[1]
    depth = size_y + 8
    second = second_table()
    near, far = x_starts(size_x * size_y, size_y)
    work[...] = total[...]
    add_packed(work, near, from_near, size_y, left_near)
    add_packed(work, far, from_far, size_y)
    sides = ((low, 0, 3, 0), (high, size_y - 1, 0, size_y - 8))
    beyond = []
    for message, y, line, _ in sides:
        lines = [message[i * size_x : (i + 1) * size_x, :width] for i in range(4)]
        lines[line] = lines[line] + edge_rows(work, y, size_x, size_y)
        for x in range(size_x):
            work[x * size_y + y : x * size_y + y + 1, :] = lines[line][x : x + 1]
        for i in range(4):
            inverse = message[i * size_x : (i + 1) * size_x, width + 1 : width + 2]
            lines[i] = inverse * lines[i]
        value = sum(float(second[line, i]) * lines[i] for i in range(4))
        for x in range(size_x):
            value = value + node_column(second[:, x], 0, size_x) * lines[line][x : x + 1]
        mass = message[line * size_x : (line + 1) * size_x, width : width + 1]
        beyond.append(mass * value)
    out[...] = product(split(operator[...]), split(columns[:, 1:2] * work[...]))
    for (_, y, _, _), rows in zip(sides, beyond):
        for x in range(size_x):
            out[x * size_y + y : x * size_y + y + 1, :] += rows[x : x + 1]

    near, far = x_rows(size_x * size_y, size_y)
    at_near[:size_y, :] = out[near]
    at_far[:size_y, :] = out[far]
    last = depth * (width // 128)
    lanes = depth // 8 * (width % 128)
    high_weights = side_weights(columns, high, size_x, size_y, width, 0)
    for side, (message, _, line, _) in enumerate(sides):
        weights = high_weights if side else [low_weights[i : i + 8] for i in (0, 8, 16)]
        inner[side * size_x : (side + 1) * size_x, :] = weights[2][:size_x]
        place = slice(lanes + 8 * side, lanes + 8 * side + 5)
        x_near[last : last + 8, place] = weights[0][:, :5]
        x_far[last : last + 8, place] = weights[1][:, :5]
        for i in range(4):
            first, final = (
                message[i * size_x + x : i * size_x + x + 1, :width] for x in (0, size_x - 1)
            )
            row_near = jnp.where(even("gx"), final, first)
            row_far = jnp.where(even("gx"), first, final)
            place = size_y + 4 * side + i
            at_near[place : place + 1, :] = row_near
            at_far[place : place + 1, :] = row_far
            if i == line:
                line_ends[2 * side : 2 * side + 1, :] = row_far
                line_ends[2 * side + 1 : 2 * side + 2, :] = row_near
    pack(at_near[...], x_near)
    pack(at_far[...], x_far)
    if x_near.shape[0] > x_far.shape[0]:
        count = coefs.shape[0]
        start = last + 8
        x_near[start : start + count, :] = coefs[...]
        x_near[start + count :, :] = from_far[packed_rows(size_y, width) :, :]


def third_kernel(
    levels,
    hyper,
    base,
    masses,
    inner,
    factors,
    to_near,
    to_far,
    from_far,
    from_near,
    ends_near,
    ends_far,
    out,
    work,
    turned,
    turned_rest,
    values,
    values_rest,
    staged,
    sems,
    *beyond_rows,
):
    columns, width = base.shape
    size_x, size_y, _ = out.shape
    variables = width // levels
    rows = size_y + 8
    last, lanes = rows * (width // 128), rows // 8 * (width % 128)
    messages = (to_near, to_far, from_near, from_far)
    for message, target in zip(messages, beyond_rows):
        for i in range(width // 128):
            target[:, i * 128 : (i + 1) * 128] = message[i * rows + size_y : (i + 1) * rows, :]
        left = width % 128
        lanes_before = size_y // 8 * left
        target[:, width - left :] = message[last : last + 8, lanes_before : lanes_before + left]
    at_near, at_far, over_near, over_far = beyond_rows
    near, far = x_starts(columns, size_y)
    sides = ((0, 0, 3, 0), (1, size_y - 1, 0, size_y - 8))
    partners = (
        (near, at_near, over_near, over_far, ends_near),
        (far, at_far, over_far, over_near, ends_far),
    )
    for x in range(1, size_x - 1):
        for first in (0, size_y - 8):
            work[x * size_y + first : x * size_y + first + 8, :] = jnp.zeros((8, width), jnp.float32)
    for start, message in ((near, from_near), (far, from_far)):
        for i in range(width // 128):
            place = pl.ds(pl.multiple_of(start, size_y), size_y)
            work[place, i * 128 : (i + 1) * 128] = message[i * rows : i * rows + size_y, :]
        for i in range(size_y // 8):
            place = pl.ds(pl.multiple_of(start + i * 8, 8), 8)
            left = width % 128
            work[place, width - left :] = message[last : last + 8, i * left : (i + 1) * left]
    for side, y, line, first in sides:
        place = 4 * side
        weights = [
            message[last : last + 8, lanes + 8 * side : lanes + 8 * side + 5] for message in messages
        ]
        for which, (start, mine, theirs, others, ends) in enumerate(partners):
            own, beyond = weights[which], weights[2 + which]
            terms = [
                (weight[:, i : i + 1], values, place + i)
                for i in range(4)
                for weight, values in ((own, theirs), (beyond, mine))
            ]
            terms += [(own[:, 4:5], others, place + line), (beyond[:, 4:5], ends, 2 * side + which)]
            added = sum(weight * values[row : row + 1, :width] for weight, values, row in terms)
            work[pl.ds(pl.multiple_of(start + first, 8), 8), :] += added
        for x in range(1, size_x - 1):
            row, weight = x * size_y + y, side * size_x + x
            work[row : row + 1, :] += (
                inner[weight : weight + 1, 0:1] * over_near[place + line : place + line + 1, :]
                + inner[weight : weight + 1, 1:2] * over_far[place + line : place + line + 1, :]
            )
    for start in (near, far):
        place = pl.ds(pl.multiple_of(start, size_y), size_y)
        work[place, :] = base[place, :] - hyper[...] * (masses[place, 1:2] * work[place, :])
    for x in range(1, size_x - 1):
        for first in (0, size_y - 8):
            rows = slice(x * size_y + first, x * size_y + first + 8)
            work[rows, :] = base[rows, :] - hyper[...] * (masses[rows, 1:2] * work[rows, :])
        rows = slice(x * size_y + 8, (x + 1) * size_y - 8)
        work[rows, :] = base[rows, :]
    pitch, half = levels + 1, levels // 2
    scale, carry, gain, keep, flow, cloud = (
        factors.at[i * levels : (i + 1) * levels] for i in range(6)
    )
    groups = [(first, min(8, variables - first)) for first in range(0, variables, 8)]
    buffers = list(zip(groups, (turned, turned_rest), (values, values_rest)))

    def turn(group, turned):
        first, count = group
        start, stop = first * levels, (first + count) * levels
        tile = start // 128 * 128
        rows = work[:, tile:stop].T
        for i in range(count):
            row = start - tile + i * levels
            turned[i * pitch : i * pitch + levels, :] = rows[row : row + levels]

    def forward(group, turned, values):
        count = group[1]
        known = [jnp.zeros((count, columns), jnp.float32)] * 2
        for i in range(half):
            for side, k in enumerate((i, levels - 1 - i)):
                scaled = turned[pl.ds(k, count, stride=pitch), :] * scale[k : k + 1, :]
                known[side] = scaled + carry[k : k + 1, :] * known[side]
                values[k, :count, :] = known[side]
        return known

    def back(group, turned, values, known):
        count = group[1]
        meet = factors[6 * levels + half : 6 * levels + half + 1, :]
        first = (known[0] + gain[half - 1 : half, :] * known[1]) * meet
        solved = [first, known[1] + gain[half : half + 1, :] * first]
        for i in reversed(range(half)):
            for side, k in enumerate((i, levels - 1 - i)):
                if i < half - 1:
                    solved[side] = values[k, :count, :] + gain[k : k + 1, :] * solved[side]
                turned[pl.ds(k, count, stride=pitch), :] = solved[side]

    def leave(i):
        lanes = slice(i * 128, min((i + 1) * 128, width))
        parts = []
        for (start, count), source, _ in buffers:
            for j in range(start, start + count):
                first, last = max(lanes.start, j * levels), min(lanes.stop, (j + 1) * levels)
                if first < last:
                    offset = (j - start) * pitch - j * levels
                    parts.append(source[first + offset : last + offset, :])
        rows = jnp.concatenate(parts, axis=0)
        staged[:, :, lanes] = rows.T.reshape(size_x, size_y, -1)
        copy = pltpu.make_async_copy(staged.at[:, :, lanes], out.at[:, :, lanes], sems.at[i])
        copy.start()
        return copy

    (main, main_turned, main_values), (rest, rest_turned, rest_values) = buffers
    turn(main, main_turned)
    main_known = forward(main, main_turned, main_values)
    turn(rest, rest_turned)
    rest_known = forward(rest, rest_turned, rest_values)
    back(main, main_turned, main_values, main_known)
    tiles = -(-width // 128)
    settled_tiles, main_tiles = -(-3 * levels // 128), main[1] * levels // 128
    copies = [leave(i) for i in range(settled_tiles, main_tiles)]
    heat, vapour, liquid = (turned.at[i * pitch : i * pitch + levels] for i in range(3))
    condensed = cloud[...] * 0.5 * jnp.maximum(vapour[...] - 0.3 * heat[...], 0.0)
    vapour[...] = vapour[...] - condensed
    heat[...] = heat[...] + 2.0 * condensed
    liquid[...] = (liquid[...] + condensed) * keep[...]
    settled = [jnp.zeros((1, columns), jnp.float32)] * 2
    for i in range(half):
        for side, k in enumerate((i, half + i)):
            settled[side] = liquid[k : k + 1, :] + flow[k : k + 1, :] * settled[side]
            liquid[k : k + 1, :] = settled[side]
    through = factors[6 * levels : 6 * levels + half, :]
    liquid[half:, :] = liquid[half:, :] + through * settled[0]
    back(rest, rest_turned, rest_values, rest_known)
    copies += [leave(i) for i in range(settled_tiles)]
    copies += [leave(i) for i in range(main_tiles, tiles)]
    for copy in copies:
        copy.wait()


def base_kernel(state, hyper, total, masses, base):
    columns, width = total.shape
    twice = masses[:, 1:2] * total[...]
    base[...] = state[...].reshape(columns, width) - hyper[...] * twice


def pick(slots, pieces):
    size_x, size_y = slots.shape
    columns = size_x * size_y
    wanted = jnp.concatenate([slots[x : x + 1, :] for x in range(size_x)], axis=1)
    picked = 0.0
    for owner, rest in pieces:
        span = rest.shape[1]
        entry = lax.broadcasted_iota(jnp.int32, (span, columns), 0) + owner * span
        choice = (entry == wanted).astype(jnp.float32).astype(jnp.bfloat16)
        for _ in range(3):
            part = rest.astype(jnp.bfloat16)
            rest = rest - part.astype(jnp.float32)
            picked = picked + jnp.dot(part, choice, preferred_element_type=jnp.float32)
    return picked


def factor_kernel(levels, slots, *refs):
    factors = refs[-1]
    if len(refs) == 4:
        own, from_far, from_near = refs[:3]
        here = lax.axis_index("gx")
        count = own.shape[0]
        far, near = from_far.shape[0] - count, from_near.shape[0] - 2 * count
        pieces = [
            (here, own[...]),
            (here ^ 3, from_far[far:, :]),
            (here ^ 1, from_near[near : near + count, :]),
            (here ^ 2, from_near[near + count :, :]),
        ]
    else:
        pieces = [(peer, refs[0][peer]) for peer in range(refs[0].shape[0])]
    columns = factors.shape[1]
    picked = pick(slots, pieces)
    mixing, falling, covered = (picked[i * levels : (i + 1) * levels] for i in range(3))
    scale, carry, gain, keep, flow, cover = (
        factors.at[i * levels : (i + 1) * levels] for i in range(6)
    )
    zero = jnp.zeros((1, columns), jnp.float32)
    kept = 1.0 / (1.0 + falling)
    keep[...] = kept
    flow[:1, :] = zero
    flow[1:, :] = falling[:-1] * kept[1:]
    cover[...] = covered
    half = levels // 2
    gains = [zero, zero]
    through = jnp.ones((1, columns), jnp.float32)
    for i in range(half):
        for side, k in enumerate((i, levels - 1 - i)):
            above = mixing[k : k + 1] if k else zero
            below = mixing[k + 1 : k + 2] if k + 1 < levels else zero
            centre = 1.0 + above + (below if k + 1 < levels else mixing[:1])
            behind, ahead = (above, below) if side == 0 else (below, above)
            inverse = 1.0 / (centre - behind * gains[side])
            gains[side] = ahead * inverse
            scale[k : k + 1, :] = inverse
            carry[k : k + 1, :] = behind * inverse
            gain[k : k + 1, :] = gains[side]
        k = half + i
        through = through * falling[k - 1 : k] * kept[k : k + 1]
        factors[6 * levels + i : 6 * levels + i + 1, :] = through
    last = 6 * levels + half
    factors[last : last + 1, :] = 1.0 / (1.0 - gains[0] * gains[1])


def swapped(value, axis, partner):
    return lax.ppermute(value, axis, [(i, partner(i)) for i in range(lax.axis_size(axis))])


def exchanged(near, far, axis):
    size = lax.axis_size(axis)
    from_far = swapped(far, axis, lambda i: (i + (1 if i % 2 else -1)) % size)
    from_near = swapped(near, axis, lambda i: i ^ 1)
    return from_far, from_near


def shifted(value, axis, step):
    size = lax.axis_size(axis)
    return lax.ppermute(value, axis, [(i, (i + step) % size) for i in range(size)])


def local(
    model_state, hyper_coef, point_mass, inverse_mass, span_slot, vert_diff, fall_rate, cloud_frac
):
    size_x, size_y, width = model_state.shape
    levels, span = vert_diff.shape[1:]
    columns = size_x * size_y
    hyper = hyper_coef.reshape(1, width)
    padded = -(-(width + 5) // 128) * 128

    def array(*shape):
        return jax.ShapeDtypeStruct(shape, jnp.float32)

    def scratch(*shape):
        return pltpu.VMEM(shape, jnp.float32)

    def call(kernel, name, outs, scratches, *operands, spec=VMEM, out=VMEM, cost=None):
        return pl.pallas_call(
            kernel,
            out_shape=outs,
            in_specs=[spec] * len(operands),
            out_specs=[out] * len(outs),
            scratch_shapes=scratches,
            compiler_params=PARAMS,
            cost_estimate=cost,
            name=name,
        )(*operands)

    riding = lax.axis_size("gx") == 4
    whole = array(columns, width)
    edge = array(4 * size_x, padded)
    extra = 3 * levels if riding else 0
    first_rows, last_rows = packed_rows(size_y, width), packed_rows(size_y + 8, width)
    here, total, x_near, x_left, x_far, y_low, y_high, operator, masses, coefs = call(
        start_kernel,
        "start",
        [
            array(size_x, size_y, width),
            whole,
            array(first_rows - 8, 128),
            array(8, 128),
            array(first_rows + extra, 128),
            edge,
            edge,
            array(columns, columns),
            array(columns, 128),
            array(3 * levels, span),
        ],
        [
            scratch(size_x, size_y),
            scratch(size_x, size_y),
            pltpu.SemaphoreType.DMA((size_x + 5,)),
        ],
        *(
            pltpu.with_memory_space_constraint(value, pltpu.HBM)
            for value in (
                model_state,
                point_mass,
                inverse_mass,
                vert_diff,
                fall_rate,
                cloud_frac,
            )
        ),
        spec=pl.BlockSpec(memory_space=pltpu.HBM),
    )
    low = shifted(y_high, "gy", 1)
    left_near = swapped(x_left, "gx", lambda i: i ^ 1)
    from_far, from_near = exchanged(x_near, x_far, "gx")
    y_low, _ = lax.optimization_barrier((y_low, left_near))
    high = shifted(y_low, "gy", -1)
    (low_weights,) = call(
        functools.partial(weights_kernel, size_x, size_y, width),
        "weights",
        [array(24, 128)],
        [],
        masses,
        low,
        cost=LONG,
    )
    total, x_near, x_far, line_ends, inner = call(
        functools.partial(second_kernel, size_x),
        "second",
        [
            whole,
            array(last_rows + 2 * extra, 128),
            array(last_rows, 128),
            array(4, width),
            array(2 * size_x, 128),
        ],
        [scratch(columns, width), scratch(size_y + 8, width), scratch(size_y + 8, width)],
        total,
        masses,
        operator,
        coefs,
        low_weights,
        low,
        from_far,
        from_near,
        left_near,
        high,
    )
    last_x = exchanged(x_near, x_far, "gx")
    peers = lax.axis_size("gx")
    ends_near = swapped(line_ends, "gx", lambda i: (i + (2 if i % 2 else -2)) % peers)
    ends_far = ends_near
    if peers != 4:
        ends_far = swapped(line_ends, "gx", lambda i: (i - (2 if i % 2 else -2)) % peers)
    if riding:
        pieces = [coefs, from_far, last_x[1]]
    else:
        pieces = [lax.all_gather(coefs, "gx")]
    (factors,) = call(
        functools.partial(factor_kernel, levels),
        "factors",
        [array(6 * levels + levels // 2 + 8, columns)],
        [],
        span_slot,
        *pieces,
    )
    (base,) = call(base_kernel, "base", [whole], [], here, hyper, total, masses)
    (result,) = call(
        functools.partial(third_kernel, levels),
        "third",
        [array(size_x, size_y, width)],
        [
            scratch(columns, width),
            scratch(8 * (levels + 1), columns),
            scratch((width // levels - 8) * (levels + 1), columns),
            scratch(levels, 8, columns),
            scratch(levels, 8, columns),
            scratch(size_x, size_y, width),
            pltpu.SemaphoreType.DMA((-(-width // 128),)),
        ]
        + [scratch(8, width)] * 4,
        hyper,
        base,
        masses,
        inner,
        factors,
        x_near,
        x_far,
        *last_x,
        ends_near,
        ends_far,
        out=pl.BlockSpec(memory_space=pltpu.HBM),
    )
    return result


def solution(mesh):
    placed = (
        P("gx", "gy", None),
        P(),
        P("gx", "gy"),
        P("gx", "gy"),
        P("gx", "gy"),
        P("gy", None, "gx"),
        P("gy", None, "gx"),
        P("gy", None, "gx"),
    )
    return jax.shard_map(
        local, mesh=mesh, in_specs=placed, out_specs=P("gx", "gy", None), check_vma=False
    )
```

```python
import functools

import jax
import jax.numpy as jnp
import numpy as np
from jax import lax
from jax.experimental import pallas as pl
from jax.experimental.pallas import tpu as pltpu
from jax.sharding import PartitionSpec as P

VMEM = pl.BlockSpec(memory_space=pltpu.VMEM)
LONG = pl.CostEstimate(flops=100_000_000_000, bytes_accessed=30_000_000, transcendentals=0)
PARAMS = pltpu.CompilerParams(vmem_limit_bytes=16 * 1024 * 1024)


def second_table():
    nodes = np.array([-1.0, -1.0 / np.sqrt(5.0), 1.0 / np.sqrt(5.0), 1.0])
    deriv = np.zeros((4, 4))
    for i in range(4):
        for j in range(4):
            if i == j:
                deriv[i, j] = sum(1.0 / (nodes[i] - nodes[k]) for k in range(4) if k != i)
            else:
                upper = np.prod([nodes[i] - nodes[k] for k in range(4) if k != i])
                lower = np.prod([nodes[j] - nodes[k] for k in range(4) if k != j])
                deriv[i, j] = upper / (lower * (nodes[i] - nodes[j]))
    return deriv @ deriv


def split(value):
    high = value.astype(jnp.bfloat16)
    return high, (value - high.astype(jnp.float32)).astype(jnp.bfloat16)


def product(left, right):
    left = jnp.concatenate([left[0], left[1], left[0]], axis=1)
    right = jnp.concatenate([right[0], right[0], right[1]], axis=0)
    return jnp.dot(left, right, preferred_element_type=jnp.float32)


def lookup(row, lane):
    second = second_table()
    row, lane = lax.rem(row, 4), lax.rem(lane, 4)
    result = jnp.zeros(row.shape, jnp.float32)
    for j in range(4):
        column = jnp.full(row.shape, float(second[3, j]), jnp.float32)
        for i in range(3):
            column = jnp.where(row == i, float(second[i, j]), column)
        result = jnp.where(lane == j, column, result)
    return result


def laplacian(size_x, size_y):
    count = size_x * size_y
    row, lane = (lax.broadcasted_iota(jnp.int32, (count, count), i) for i in range(2))
    row_x, lane_x = lax.div(row, size_y), lax.div(lane, size_y)
    row_y, lane_y = lax.rem(row, size_y), lax.rem(lane, size_y)
    same_x = (row_y == lane_y) & (lax.div(row_x, 4) == lax.div(lane_x, 4))
    same_y = (row_x == lane_x) & (lax.div(row_y, 4) == lax.div(lane_y, 4))
    along_x = jnp.where(same_x, lookup(row_x, lane_x), 0.0)
    return along_x + jnp.where(same_y, lookup(row_y, lane_y), 0.0)


def of_partner(values, size_y):
    count = values.shape[0]
    row_y = lax.rem(lax.broadcasted_iota(jnp.int32, values.shape, 0), size_y)
    phase = lax.rem(row_y, 4)
    before = jnp.where((phase == 0) & (row_y > 0), pltpu.roll(values, 1, 0), 0.0)
    after = (phase == 3) & (row_y < size_y - 1)
    return jnp.where(after, pltpu.roll(values, count - 1, 0), before)


def to_column(plane):
    size_x, size_y = plane.shape
    row = lax.broadcasted_iota(jnp.int32, (size_y, size_y), 0)
    lane = lax.broadcasted_iota(jnp.int32, (size_y, size_y), 1)
    parts = [
        jnp.sum(jnp.where(row == lane, plane[x : x + 1, :], 0.0), axis=1, keepdims=True)
        for x in range(size_x)
    ]
    return jnp.concatenate(parts, axis=0)


def even(axis):
    return lax.rem(lax.axis_index(axis), 2) == 0


def x_starts(count, size_y):
    near = jnp.where(even("gx"), count - size_y, 0)
    return near, count - size_y - near


def x_rows(count, size_y):
    starts = x_starts(count, size_y)
    return tuple(pl.ds(pl.multiple_of(start, size_y), size_y) for start in starts)


def add_packed(work, start, message, rows):
    def write(first, count, lanes, value):
        work[pl.ds(pl.multiple_of(start + first, 8), count), lanes] += value

    unpack(message, rows, work.shape[1], write)


def packed_rows(rows, width):
    return rows * (width // 128) + 8


def pack(value, message):
    rows, width = value.shape
    full, left = width // 128, width % 128
    for i in range(full):
        message[i * rows : (i + 1) * rows, :] = value[:, i * 128 : (i + 1) * 128]
    for i in range(rows // 8):
        lanes = slice(i * left, (i + 1) * left)
        message[full * rows : full * rows + 8, lanes] = value[i * 8 : (i + 1) * 8, full * 128 :]


def unpack(message, rows, width, write):
    full, left = width // 128, width % 128
    for i in range(full):
        write(0, rows, slice(i * 128, (i + 1) * 128), message[i * rows : (i + 1) * rows, :])
    for i in range(rows // 8):
        value = message[full * rows : full * rows + 8, i * left : (i + 1) * left]
        write(i * 8, 8, slice(full * 128, width), value)


def edge_rows(ref, y, size_x, size_y):
    return jnp.concatenate(
        [ref[x * size_y + y : x * size_y + y + 1, :] for x in range(size_x)], axis=0
    )


def start_kernel(
    state,
    mass,
    inverse,
    diff,
    fall,
    cloud,
    here,
    total,
    x_near,
    x_far,
    low,
    high,
    operator,
    columns,
    coefs,
    mass_here,
    inverse_here,
    sems,
):
    size_x, size_y, width = state.shape
    levels = diff.shape[1]
    pairs = [(mass, mass_here), (inverse, inverse_here)]
    pairs += [(state.at[x], here.at[x]) for x in range(size_x)]
    for i, source in enumerate((diff, fall, cloud)):
        pairs.append((source.at[0], coefs.at[i * levels : (i + 1) * levels]))
    copies = [
        pltpu.make_async_copy(source, target, sems.at[i])
        for i, (source, target) in enumerate(pairs)
    ]
    for copy in copies:
        copy.start()
    count = size_x * size_y
    matrix = laplacian(size_x, size_y)
    for copy in copies[:2]:
        copy.wait()
    own = jnp.broadcast_to(to_column(mass_here[...]), (count, count))
    matrix = own * matrix
    matrix = matrix + of_partner(matrix, size_y)
    operator[...] = matrix
    partner = of_partner(own, size_y)
    inverses = to_column(inverse_here[...])
    lane = lax.broadcasted_iota(jnp.int32, columns.shape, 1)
    columns[...] = jnp.where(lane == 0, own, jnp.where(lane == 1, inverses, partner))
    for copy in copies[2 : 2 + size_x]:
        copy.wait()
    total[...] = product(split(matrix), split(here[...].reshape(count, width)))
    near, far = x_rows(count, size_y)
    pack(total[near], x_near)
    pack(total[far], x_far)
    for first, message in ((0, low), (size_y - 4, high)):
        for i in range(4):
            rows = slice(i * size_x, (i + 1) * size_x)
            message[rows, :width] = edge_rows(total, first + i, size_x, size_y)
            message[rows, width : width + 2] = edge_rows(columns, first + i, size_x, size_y)[:, :2]
    for copy in copies[2 + size_x :]:
        copy.wait()
    if x_far.shape[0] > x_near.shape[0]:
        x_far[x_near.shape[0] :, :] = coefs[...]


def node_column(values, start, count):
    row = lax.broadcasted_iota(jnp.int32, (count, 1), 0)
    result = jnp.zeros((count, 1), jnp.float32)
    for i, value in enumerate(values):
        result = jnp.where(row == start + i, float(value), result)
    return result


def edge_weights(columns, message, size_x, size_y, width, edge, line):
    second = second_table()
    other = size_x - 1 - edge
    low = line == 3
    y, first = (0, 0) if low else (size_y - 1, size_y - 8)
    rows = slice(edge * size_y + first, edge * size_y + first + 8)
    here, there = (slice(x * size_y + y, x * size_y + y + 1) for x in (edge, other))
    mass, inverse = columns[here, 0:1], columns[here, 1:2]
    beyond = slice(line * size_x + edge, line * size_x + edge + 1)
    beyond_mass = message[beyond, width : width + 1]

    def beyond_inverse(i, x):
        return message[i * size_x + x : i * size_x + x + 1, width + 1 : width + 2]

    if low:
        own, partner = node_column(second[:, 0], 0, 8), node_column(second[3:, 0], 4, 8)
    else:
        own, partner = node_column(second[:, 3], 4, 8), node_column(second[:1, 3], 3, 8)
    along = inverse * (own * columns[rows, 0:1] + partner * columns[rows, 2:3])
    lane = lax.broadcasted_iota(jnp.int32, (8, 128), 1)
    place = lax.broadcasted_iota(jnp.int32, (8, 128), 0)
    tile = jnp.where(lane == line, along, 0.0)
    for i in range(4):
        value = float(second[line, i]) * beyond_mass * beyond_inverse(i, edge)
        if i == line:
            across = beyond_mass * beyond_inverse(line, edge) + mass * inverse
            value = value + float(second[edge, edge]) * across
        tile = tile + jnp.where((place == y - first) & (lane == i), value, 0.0)
    across = beyond_mass * beyond_inverse(line, other) + mass * columns[there, 1:2]
    value = float(second[edge, other]) * across
    return tile + jnp.where((place == y - first) & (lane == 4), value, 0.0)


def side_weights(columns, message, size_x, size_y, width, line):
    second = second_table()
    first, last = 0, size_x - 1
    tiles = [
        edge_weights(columns, message, size_x, size_y, width, edge, line) for edge in (first, last)
    ]
    mass = message[line * size_x : (line + 1) * size_x, width : width + 1]
    own = edge_rows(columns, 0 if line == 3 else size_y - 1, size_x, size_y)
    inner = []
    for edge in (first, last):
        inverse = message[line * size_x + edge : line * size_x + edge + 1, width + 1 : width + 2]
        across = mass * inverse + own[:, 0:1] * own[edge : edge + 1, 1:2]
        inner.append(node_column(second[:, edge], 0, size_x) * across)
    lane = lax.broadcasted_iota(jnp.int32, (size_x, 128), 1)
    from_last = jnp.where(even("gx"), 0, 1)
    return (
        jnp.where(even("gx"), tiles[1], tiles[0]),
        jnp.where(even("gx"), tiles[0], tiles[1]),
        jnp.where(lane == from_last, inner[1], inner[0]),
    )


def weights_kernel(size_x, size_y, width, columns, message, out):
    near, far, inner = side_weights(columns, message, size_x, size_y, width, 3)
    out[0:8, :] = near
    out[8:16, :] = far
    out[16 : 16 + size_x, :] = inner


def second_kernel(
    size_x,
    total,
    columns,
    operator,
    coefs,
    low_weights,
    low,
    from_far,
    from_near,
    high,
    out,
    x_near,
    x_far,
    line_ends,
    inner,
    work,
    at_near,
    at_far,
):
    size_y, width = total.shape[0] // size_x, total.shape[1]
    depth = size_y + 8
    second = second_table()
    near, far = x_starts(size_x * size_y, size_y)
    work[...] = total[...]
    add_packed(work, near, from_near, size_y)
    add_packed(work, far, from_far, size_y)
    sides = ((low, 0, 3, 0), (high, size_y - 1, 0, size_y - 8))
    beyond = []
    for message, y, line, _ in sides:
        lines = [message[i * size_x : (i + 1) * size_x, :width] for i in range(4)]
        lines[line] = lines[line] + edge_rows(work, y, size_x, size_y)
        for x in range(size_x):
            work[x * size_y + y : x * size_y + y + 1, :] = lines[line][x : x + 1]
        for i in range(4):
            inverse = message[i * size_x : (i + 1) * size_x, width + 1 : width + 2]
            lines[i] = inverse * lines[i]
        value = sum(float(second[line, i]) * lines[i] for i in range(4))
        for x in range(size_x):
            value = value + node_column(second[:, x], 0, size_x) * lines[line][x : x + 1]
        mass = message[line * size_x : (line + 1) * size_x, width : width + 1]
        beyond.append(mass * value)
    out[...] = product(split(operator[...]), split(columns[:, 1:2] * work[...]))
    for (_, y, _, _), rows in zip(sides, beyond):
        for x in range(size_x):
            out[x * size_y + y : x * size_y + y + 1, :] += rows[x : x + 1]

    near, far = x_rows(size_x * size_y, size_y)
    at_near[:size_y, :] = out[near]
    at_far[:size_y, :] = out[far]
    last = depth * (width // 128)
    lanes = depth // 8 * (width % 128)
    high_weights = side_weights(columns, high, size_x, size_y, width, 0)
    for side, (message, _, line, _) in enumerate(sides):
        weights = high_weights if side else [low_weights[i : i + 8] for i in (0, 8, 16)]
        inner[side * size_x : (side + 1) * size_x, :] = weights[2][:size_x]
        place = slice(lanes + 8 * side, lanes + 8 * side + 5)
        x_near[last : last + 8, place] = weights[0][:, :5]
        x_far[last : last + 8, place] = weights[1][:, :5]
        for i in range(4):
            first, final = (
                message[i * size_x + x : i * size_x + x + 1, :width] for x in (0, size_x - 1)
            )
            row_near = jnp.where(even("gx"), final, first)
            row_far = jnp.where(even("gx"), first, final)
            place = size_y + 4 * side + i
            at_near[place : place + 1, :] = row_near
            at_far[place : place + 1, :] = row_far
            if i == line:
                line_ends[2 * side : 2 * side + 1, :] = row_far
                line_ends[2 * side + 1 : 2 * side + 2, :] = row_near
    pack(at_near[...], x_near)
    pack(at_far[...], x_far)
    if x_near.shape[0] > x_far.shape[0]:
        count = coefs.shape[0]
        start = last + 8
        x_near[start : start + count, :] = coefs[...]
        x_near[start + count :, :] = from_far[packed_rows(size_y, width) :, :]


def third_kernel(
    levels,
    hyper,
    base,
    masses,
    inner,
    factors,
    to_near,
    to_far,
    from_far,
    from_near,
    ends_near,
    ends_far,
    out,
    work,
    turned,
    turned_rest,
    values,
    values_rest,
    staged,
    sems,
    *beyond_rows,
):
    columns, width = base.shape
    size_x, size_y, _ = out.shape
    variables = width // levels
    rows = size_y + 8
    last, lanes = rows * (width // 128), rows // 8 * (width % 128)
    messages = (to_near, to_far, from_near, from_far)
    for message, target in zip(messages, beyond_rows):
        for i in range(width // 128):
            target[:, i * 128 : (i + 1) * 128] = message[i * rows + size_y : (i + 1) * rows, :]
        left = width % 128
        lanes_before = size_y // 8 * left
        target[:, width - left :] = message[last : last + 8, lanes_before : lanes_before + left]
    at_near, at_far, over_near, over_far = beyond_rows
    near, far = x_starts(columns, size_y)
    sides = ((0, 0, 3, 0), (1, size_y - 1, 0, size_y - 8))
    partners = (
        (near, at_near, over_near, over_far, ends_near),
        (far, at_far, over_far, over_near, ends_far),
    )
    for x in range(1, size_x - 1):
        for first in (0, size_y - 8):
            work[x * size_y + first : x * size_y + first + 8, :] = jnp.zeros((8, width), jnp.float32)
    for start, message in ((near, from_near), (far, from_far)):
        for i in range(width // 128):
            place = pl.ds(pl.multiple_of(start, size_y), size_y)
            work[place, i * 128 : (i + 1) * 128] = message[i * rows : i * rows + size_y, :]
        for i in range(size_y // 8):
            place = pl.ds(pl.multiple_of(start + i * 8, 8), 8)
            left = width % 128
            work[place, width - left :] = message[last : last + 8, i * left : (i + 1) * left]
    for side, y, line, first in sides:
        place = 4 * side
        weights = [
            message[last : last + 8, lanes + 8 * side : lanes + 8 * side + 5] for message in messages
        ]
        for which, (start, mine, theirs, others, ends) in enumerate(partners):
            own, beyond = weights[which], weights[2 + which]
            terms = [
                (weight[:, i : i + 1], values, place + i)
                for i in range(4)
                for weight, values in ((own, theirs), (beyond, mine))
            ]
            terms += [(own[:, 4:5], others, place + line), (beyond[:, 4:5], ends, 2 * side + which)]
            added = sum(weight * values[row : row + 1, :width] for weight, values, row in terms)
            work[pl.ds(pl.multiple_of(start + first, 8), 8), :] += added
        for x in range(1, size_x - 1):
            row, weight = x * size_y + y, side * size_x + x
            work[row : row + 1, :] += (
                inner[weight : weight + 1, 0:1] * over_near[place + line : place + line + 1, :]
                + inner[weight : weight + 1, 1:2] * over_far[place + line : place + line + 1, :]
            )
    for start in (near, far):
        place = pl.ds(pl.multiple_of(start, size_y), size_y)
        work[place, :] = base[place, :] - hyper[...] * (masses[place, 1:2] * work[place, :])
    for x in range(1, size_x - 1):
        for first in (0, size_y - 8):
            rows = slice(x * size_y + first, x * size_y + first + 8)
            work[rows, :] = base[rows, :] - hyper[...] * (masses[rows, 1:2] * work[rows, :])
        rows = slice(x * size_y + 8, (x + 1) * size_y - 8)
        work[rows, :] = base[rows, :]
    pitch, half = levels + 1, levels // 2
    scale, carry, gain, keep, flow, cloud = (
        factors.at[i * levels : (i + 1) * levels] for i in range(6)
    )
    groups = [(first, min(8, variables - first)) for first in range(0, variables, 8)]
    buffers = list(zip(groups, (turned, turned_rest), (values, values_rest)))

    def turn(group, turned):
        first, count = group
        start, stop = first * levels, (first + count) * levels
        tile = start // 128 * 128
        rows = work[:, tile:stop].T
        for i in range(count):
            row = start - tile + i * levels
            turned[i * pitch : i * pitch + levels, :] = rows[row : row + levels]

    def forward(group, turned, values):
        count = group[1]
        known = [jnp.zeros((count, columns), jnp.float32)] * 2
        for i in range(half):
            for side, k in enumerate((i, levels - 1 - i)):
                scaled = turned[pl.ds(k, count, stride=pitch), :] * scale[k : k + 1, :]
                known[side] = scaled + carry[k : k + 1, :] * known[side]
                values[k, :count, :] = known[side]
        return known

    def back(group, turned, values, known):
        count = group[1]
        meet = factors[6 * levels + half : 6 * levels + half + 1, :]
        first = (known[0] + gain[half - 1 : half, :] * known[1]) * meet
        solved = [first, known[1] + gain[half : half + 1, :] * first]
        for i in reversed(range(half)):
            for side, k in enumerate((i, levels - 1 - i)):
                if i < half - 1:
                    solved[side] = values[k, :count, :] + gain[k : k + 1, :] * solved[side]
                turned[pl.ds(k, count, stride=pitch), :] = solved[side]

    def leave(i):
        lanes = slice(i * 128, min((i + 1) * 128, width))
        parts = []
        for (start, count), source, _ in buffers:
            for j in range(start, start + count):
                first, last = max(lanes.start, j * levels), min(lanes.stop, (j + 1) * levels)
                if first < last:
                    offset = (j - start) * pitch - j * levels
                    parts.append(source[first + offset : last + offset, :])
        rows = jnp.concatenate(parts, axis=0)
        staged[:, :, lanes] = rows.T.reshape(size_x, size_y, -1)
        copy = pltpu.make_async_copy(staged.at[:, :, lanes], out.at[:, :, lanes], sems.at[i])
        copy.start()
        return copy

    (main, main_turned, main_values), (rest, rest_turned, rest_values) = buffers
    turn(main, main_turned)
    main_known = forward(main, main_turned, main_values)
    turn(rest, rest_turned)
    rest_known = forward(rest, rest_turned, rest_values)
    back(main, main_turned, main_values, main_known)
    tiles = -(-width // 128)
    settled_tiles, main_tiles = -(-3 * levels // 128), main[1] * levels // 128
    copies = [leave(i) for i in range(settled_tiles, main_tiles)]
    heat, vapour, liquid = (turned.at[i * pitch : i * pitch + levels] for i in range(3))
    condensed = cloud[...] * 0.5 * jnp.maximum(vapour[...] - 0.3 * heat[...], 0.0)
    vapour[...] = vapour[...] - condensed
    heat[...] = heat[...] + 2.0 * condensed
    liquid[...] = (liquid[...] + condensed) * keep[...]
    settled = [jnp.zeros((1, columns), jnp.float32)] * 2
    for i in range(half):
        for side, k in enumerate((i, half + i)):
            settled[side] = liquid[k : k + 1, :] + flow[k : k + 1, :] * settled[side]
            liquid[k : k + 1, :] = settled[side]
    through = factors[6 * levels : 6 * levels + half, :]
    liquid[half:, :] = liquid[half:, :] + through * settled[0]
    back(rest, rest_turned, rest_values, rest_known)
    copies += [leave(i) for i in range(settled_tiles)]
    copies += [leave(i) for i in range(main_tiles, tiles)]
    for copy in copies:
        copy.wait()


def base_kernel(state, hyper, total, masses, base):
    columns, width = total.shape
    twice = masses[:, 1:2] * total[...]
    base[...] = state[...].reshape(columns, width) - hyper[...] * twice


def pick(slots, pieces):
    size_x, size_y = slots.shape
    columns = size_x * size_y
    wanted = jnp.concatenate([slots[x : x + 1, :] for x in range(size_x)], axis=1)
    picked = 0.0
    for owner, rest in pieces:
        span = rest.shape[1]
        entry = lax.broadcasted_iota(jnp.int32, (span, columns), 0) + owner * span
        choice = (entry == wanted).astype(jnp.float32).astype(jnp.bfloat16)
        for _ in range(3):
            part = rest.astype(jnp.bfloat16)
            rest = rest - part.astype(jnp.float32)
            picked = picked + jnp.dot(part, choice, preferred_element_type=jnp.float32)
    return picked


def factor_kernel(levels, slots, *refs):
    factors = refs[-1]
    if len(refs) == 3:
        here = lax.axis_index("gx")
        pieces = []
        for message, owner in zip(refs, (here, here ^ 1)):
            start = message.shape[0] - 6 * levels
            pieces.append((owner, message[start : start + 3 * levels, :]))
            pieces.append((owner ^ 3, message[start + 3 * levels :, :]))
    else:
        pieces = [(peer, refs[0][peer]) for peer in range(refs[0].shape[0])]
    columns = factors.shape[1]
    picked = pick(slots, pieces)
    mixing, falling, covered = (picked[i * levels : (i + 1) * levels] for i in range(3))
    scale, carry, gain, keep, flow, cover = (
        factors.at[i * levels : (i + 1) * levels] for i in range(6)
    )
    zero = jnp.zeros((1, columns), jnp.float32)
    kept = 1.0 / (1.0 + falling)
    keep[...] = kept
    flow[:1, :] = zero
    flow[1:, :] = falling[:-1] * kept[1:]
    cover[...] = covered
    half = levels // 2
    gains = [zero, zero]
    through = jnp.ones((1, columns), jnp.float32)
    for i in range(half):
        for side, k in enumerate((i, levels - 1 - i)):
            above = mixing[k : k + 1] if k else zero
            below = mixing[k + 1 : k + 2] if k + 1 < levels else zero
            centre = 1.0 + above + (below if k + 1 < levels else mixing[:1])
            behind, ahead = (above, below) if side == 0 else (below, above)
            inverse = 1.0 / (centre - behind * gains[side])
            gains[side] = ahead * inverse
            scale[k : k + 1, :] = inverse
            carry[k : k + 1, :] = behind * inverse
            gain[k : k + 1, :] = gains[side]
        k = half + i
        through = through * falling[k - 1 : k] * kept[k : k + 1]
        factors[6 * levels + i : 6 * levels + i + 1, :] = through
    last = 6 * levels + half
    factors[last : last + 1, :] = 1.0 / (1.0 - gains[0] * gains[1])


def swapped(value, axis, partner):
    return lax.ppermute(value, axis, [(i, partner(i)) for i in range(lax.axis_size(axis))])


def exchanged(near, far, axis):
    size = lax.axis_size(axis)
    from_far = swapped(far, axis, lambda i: (i + (1 if i % 2 else -1)) % size)
    from_near = swapped(near, axis, lambda i: i ^ 1)
    return from_far, from_near


def shifted(value, axis, step):
    size = lax.axis_size(axis)
    return lax.ppermute(value, axis, [(i, (i + step) % size) for i in range(size)])


def local(
    model_state, hyper_coef, point_mass, inverse_mass, span_slot, vert_diff, fall_rate, cloud_frac
):
    size_x, size_y, width = model_state.shape
    levels, span = vert_diff.shape[1:]
    columns = size_x * size_y
    hyper = hyper_coef.reshape(1, width)
    padded = -(-(width + 5) // 128) * 128

    def array(*shape):
        return jax.ShapeDtypeStruct(shape, jnp.float32)

    def scratch(*shape):
        return pltpu.VMEM(shape, jnp.float32)

    def call(kernel, name, outs, scratches, *operands, spec=VMEM, out=VMEM, cost=None):
        return pl.pallas_call(
            kernel,
            out_shape=outs,
            in_specs=[spec] * len(operands),
            out_specs=[out] * len(outs),
            scratch_shapes=scratches,
            compiler_params=PARAMS,
            cost_estimate=cost,
            name=name,
        )(*operands)

    riding = lax.axis_size("gx") == 4
    whole = array(columns, width)
    edge = array(4 * size_x, padded)
    extra = 3 * levels if riding else 0
    first_rows, last_rows = packed_rows(size_y, width), packed_rows(size_y + 8, width)
    here, total, x_near, x_far, y_low, y_high, operator, masses, coefs = call(
        start_kernel,
        "start",
        [
            array(size_x, size_y, width),
            whole,
            array(first_rows, 128),
            array(first_rows + extra, 128),
            edge,
            edge,
            array(columns, columns),
            array(columns, 128),
            array(3 * levels, span),
        ],
        [
            scratch(size_x, size_y),
            scratch(size_x, size_y),
            pltpu.SemaphoreType.DMA((size_x + 5,)),
        ],
        *(
            pltpu.with_memory_space_constraint(value, pltpu.HBM)
            for value in (
                model_state,
                point_mass,
                inverse_mass,
                vert_diff,
                fall_rate,
                cloud_frac,
            )
        ),
        spec=pl.BlockSpec(memory_space=pltpu.HBM),
    )
    low = shifted(y_high, "gy", 1)
    from_far, from_near = exchanged(x_near, x_far, "gx")
    high = shifted(y_low, "gy", -1)
    (low_weights,) = call(
        functools.partial(weights_kernel, size_x, size_y, width),
        "weights",
        [array(24, 128)],
        [],
        masses,
        low,
        cost=LONG,
    )
    total, x_near, x_far, line_ends, inner = call(
        functools.partial(second_kernel, size_x),
        "second",
        [
            whole,
            array(last_rows + 2 * extra, 128),
            array(last_rows, 128),
            array(4, width),
            array(2 * size_x, 128),
        ],
        [scratch(columns, width), scratch(size_y + 8, width), scratch(size_y + 8, width)],
        total,
        masses,
        operator,
        coefs,
        low_weights,
        low,
        from_far,
        from_near,
        high,
    )
    last_x = exchanged(x_near, x_far, "gx")
    peers = lax.axis_size("gx")
    ends_near = swapped(line_ends, "gx", lambda i: (i + (2 if i % 2 else -2)) % peers)
    ends_far = ends_near
    if peers != 4:
        ends_far = swapped(line_ends, "gx", lambda i: (i - (2 if i % 2 else -2)) % peers)
    if riding:
        pieces = [x_near, last_x[1]]
    else:
        pieces = [lax.all_gather(coefs, "gx")]
    (factors,) = call(
        functools.partial(factor_kernel, levels),
        "factors",
        [array(6 * levels + levels // 2 + 8, columns)],
        [],
        span_slot,
        *pieces,
    )
    (base,) = call(base_kernel, "base", [whole], [], here, hyper, total, masses)
    (result,) = call(
        functools.partial(third_kernel, levels),
        "third",
        [array(size_x, size_y, width)],
        [
            scratch(columns, width),
            scratch(8 * (levels + 1), columns),
            scratch((width // levels - 8) * (levels + 1), columns),
            scratch(levels, 8, columns),
            scratch(levels, 8, columns),
            scratch(size_x, size_y, width),
            pltpu.SemaphoreType.DMA((-(-width // 128),)),
        ]
        + [scratch(8, width)] * 4,
        hyper,
        base,
        masses,
        inner,
        factors,
        x_near,
        x_far,
        *last_x,
        ends_near,
        ends_far,
        out=pl.BlockSpec(memory_space=pltpu.HBM),
    )
    return result


def solution(mesh):
    placed = (
        P("gx", "gy", None),
        P(),
        P("gx", "gy"),
        P("gx", "gy"),
        P("gx", "gy"),
        P("gy", None, "gx"),
        P("gy", None, "gx"),
        P("gy", None, "gx"),
    )
    return jax.shard_map(
        local, mesh=mesh, in_specs=placed, out_specs=P("gx", "gy", None), check_vma=False
    )
```

```python
import functools

import jax
import jax.numpy as jnp
import numpy as np
from jax import lax
from jax.experimental import pallas as pl
from jax.experimental.pallas import tpu as pltpu
from jax.sharding import PartitionSpec as P

VMEM = pl.BlockSpec(memory_space=pltpu.VMEM)
LONG = pl.CostEstimate(flops=100_000_000_000, bytes_accessed=30_000_000, transcendentals=0)
PARAMS = pltpu.CompilerParams(vmem_limit_bytes=16 * 1024 * 1024)


def second_table():
    nodes = np.array([-1.0, -1.0 / np.sqrt(5.0), 1.0 / np.sqrt(5.0), 1.0])
    deriv = np.zeros((4, 4))
    for i in range(4):
        for j in range(4):
            if i == j:
                deriv[i, j] = sum(1.0 / (nodes[i] - nodes[k]) for k in range(4) if k != i)
            else:
                upper = np.prod([nodes[i] - nodes[k] for k in range(4) if k != i])
                lower = np.prod([nodes[j] - nodes[k] for k in range(4) if k != j])
                deriv[i, j] = upper / (lower * (nodes[i] - nodes[j]))
    return deriv @ deriv


def split(value):
    high = value.astype(jnp.bfloat16)
    return high, (value - high.astype(jnp.float32)).astype(jnp.bfloat16)


def product(left, right):
    left = jnp.concatenate([left[0], left[1], left[0]], axis=1)
    right = jnp.concatenate([right[0], right[0], right[1]], axis=0)
    return jnp.dot(left, right, preferred_element_type=jnp.float32)


def lookup(row, lane):
    second = second_table()
    row, lane = lax.rem(row, 4), lax.rem(lane, 4)
    result = jnp.zeros(row.shape, jnp.float32)
    for j in range(4):
        column = jnp.full(row.shape, float(second[3, j]), jnp.float32)
        for i in range(3):
            column = jnp.where(row == i, float(second[i, j]), column)
        result = jnp.where(lane == j, column, result)
    return result


def laplacian(size_x, size_y):
    count = size_x * size_y
    row, lane = (lax.broadcasted_iota(jnp.int32, (count, count), i) for i in range(2))
    row_x, lane_x = lax.div(row, size_y), lax.div(lane, size_y)
    row_y, lane_y = lax.rem(row, size_y), lax.rem(lane, size_y)
    same_x = (row_y == lane_y) & (lax.div(row_x, 4) == lax.div(lane_x, 4))
    same_y = (row_x == lane_x) & (lax.div(row_y, 4) == lax.div(lane_y, 4))
    along_x = jnp.where(same_x, lookup(row_x, lane_x), 0.0)
    return along_x + jnp.where(same_y, lookup(row_y, lane_y), 0.0)


def of_partner(values, size_y):
    count = values.shape[0]
    row_y = lax.rem(lax.broadcasted_iota(jnp.int32, values.shape, 0), size_y)
    phase = lax.rem(row_y, 4)
    before = jnp.where((phase == 0) & (row_y > 0), pltpu.roll(values, 1, 0), 0.0)
    after = (phase == 3) & (row_y < size_y - 1)
    return jnp.where(after, pltpu.roll(values, count - 1, 0), before)


def to_column(plane):
    size_x, size_y = plane.shape
    row = lax.broadcasted_iota(jnp.int32, (size_y, size_y), 0)
    lane = lax.broadcasted_iota(jnp.int32, (size_y, size_y), 1)
    parts = [
        jnp.sum(jnp.where(row == lane, plane[x : x + 1, :], 0.0), axis=1, keepdims=True)
        for x in range(size_x)
    ]
    return jnp.concatenate(parts, axis=0)


def even(axis):
    return lax.rem(lax.axis_index(axis), 2) == 0


def x_starts(count, size_y):
    near = jnp.where(even("gx"), count - size_y, 0)
    return near, count - size_y - near


def x_rows(count, size_y):
    starts = x_starts(count, size_y)
    return tuple(pl.ds(pl.multiple_of(start, size_y), size_y) for start in starts)


def add_packed(work, start, message, rows):
    def write(first, count, lanes, value):
        work[pl.ds(pl.multiple_of(start + first, 8), count), lanes] += value

    unpack(message, rows, work.shape[1], write)


def packed_rows(rows, width):
    return rows * (width // 128) + 8


def pack(value, message):
    rows, width = value.shape
    full, left = width // 128, width % 128
    for i in range(full):
        message[i * rows : (i + 1) * rows, :] = value[:, i * 128 : (i + 1) * 128]
    for i in range(rows // 8):
        lanes = slice(i * left, (i + 1) * left)
        message[full * rows : full * rows + 8, lanes] = value[i * 8 : (i + 1) * 8, full * 128 :]


def unpack(message, rows, width, write):
    full, left = width // 128, width % 128
    for i in range(full):
        write(0, rows, slice(i * 128, (i + 1) * 128), message[i * rows : (i + 1) * rows, :])
    for i in range(rows // 8):
        value = message[full * rows : full * rows + 8, i * left : (i + 1) * left]
        write(i * 8, 8, slice(full * 128, width), value)


def edge_rows(ref, y, size_x, size_y):
    return jnp.concatenate(
        [ref[x * size_y + y : x * size_y + y + 1, :] for x in range(size_x)], axis=0
    )


def start_kernel(
    state,
    mass,
    inverse,
    diff,
    fall,
    cloud,
    here,
    total,
    x_near,
    x_near_rest,
    x_far,
    low,
    high,
    operator,
    columns,
    coefs,
    mass_here,
    inverse_here,
    near_rows,
    sems,
):
    size_x, size_y, width = state.shape
    levels = diff.shape[1]
    pairs = [(mass, mass_here), (inverse, inverse_here)]
    pairs += [(state.at[x], here.at[x]) for x in range(size_x)]
    for i, source in enumerate((diff, fall, cloud)):
        pairs.append((source.at[0], coefs.at[i * levels : (i + 1) * levels]))
    copies = [
        pltpu.make_async_copy(source, target, sems.at[i])
        for i, (source, target) in enumerate(pairs)
    ]
    for copy in copies:
        copy.start()
    count = size_x * size_y
    matrix = laplacian(size_x, size_y)
    for copy in copies[:2]:
        copy.wait()
    own = jnp.broadcast_to(to_column(mass_here[...]), (count, count))
    matrix = own * matrix
    matrix = matrix + of_partner(matrix, size_y)
    operator[...] = matrix
    partner = of_partner(own, size_y)
    inverses = to_column(inverse_here[...])
    lane = lax.broadcasted_iota(jnp.int32, columns.shape, 1)
    columns[...] = jnp.where(lane == 0, own, jnp.where(lane == 1, inverses, partner))
    for copy in copies[2 : 2 + size_x]:
        copy.wait()
    total[...] = product(split(matrix), split(here[...].reshape(count, width)))
    near, far = x_rows(count, size_y)
    pack(total[near], near_rows)
    rest = x_near_rest.shape[0]
    x_near_rest[...] = near_rows[:rest, :]
    x_near[...] = near_rows[rest:, :]
    pack(total[far], x_far)
    for first, message in ((0, low), (size_y - 4, high)):
        for i in range(4):
            rows = slice(i * size_x, (i + 1) * size_x)
            message[rows, :width] = edge_rows(total, first + i, size_x, size_y)
            message[rows, width : width + 2] = edge_rows(columns, first + i, size_x, size_y)[:, :2]
    for copy in copies[2 + size_x :]:
        copy.wait()
    if x_far.shape[0] > near_rows.shape[0]:
        x_far[near_rows.shape[0] :, :] = coefs[...]


def node_column(values, start, count):
    row = lax.broadcasted_iota(jnp.int32, (count, 1), 0)
    result = jnp.zeros((count, 1), jnp.float32)
    for i, value in enumerate(values):
        result = jnp.where(row == start + i, float(value), result)
    return result


def edge_weights(columns, message, size_x, size_y, width, edge, line):
    second = second_table()
    other = size_x - 1 - edge
    low = line == 3
    y, first = (0, 0) if low else (size_y - 1, size_y - 8)
    rows = slice(edge * size_y + first, edge * size_y + first + 8)
    here, there = (slice(x * size_y + y, x * size_y + y + 1) for x in (edge, other))
    mass, inverse = columns[here, 0:1], columns[here, 1:2]
    beyond = slice(line * size_x + edge, line * size_x + edge + 1)
    beyond_mass = message[beyond, width : width + 1]

    def beyond_inverse(i, x):
        return message[i * size_x + x : i * size_x + x + 1, width + 1 : width + 2]

    if low:
        own, partner = node_column(second[:, 0], 0, 8), node_column(second[3:, 0], 4, 8)
    else:
        own, partner = node_column(second[:, 3], 4, 8), node_column(second[:1, 3], 3, 8)
    along = inverse * (own * columns[rows, 0:1] + partner * columns[rows, 2:3])
    lane = lax.broadcasted_iota(jnp.int32, (8, 128), 1)
    place = lax.broadcasted_iota(jnp.int32, (8, 128), 0)
    tile = jnp.where(lane == line, along, 0.0)
    for i in range(4):
        value = float(second[line, i]) * beyond_mass * beyond_inverse(i, edge)
        if i == line:
            across = beyond_mass * beyond_inverse(line, edge) + mass * inverse
            value = value + float(second[edge, edge]) * across
        tile = tile + jnp.where((place == y - first) & (lane == i), value, 0.0)
    across = beyond_mass * beyond_inverse(line, other) + mass * columns[there, 1:2]
    value = float(second[edge, other]) * across
    return tile + jnp.where((place == y - first) & (lane == 4), value, 0.0)


def side_weights(columns, message, size_x, size_y, width, line):
    second = second_table()
    first, last = 0, size_x - 1
    tiles = [
        edge_weights(columns, message, size_x, size_y, width, edge, line) for edge in (first, last)
    ]
    mass = message[line * size_x : (line + 1) * size_x, width : width + 1]
    own = edge_rows(columns, 0 if line == 3 else size_y - 1, size_x, size_y)
    inner = []
    for edge in (first, last):
        inverse = message[line * size_x + edge : line * size_x + edge + 1, width + 1 : width + 2]
        across = mass * inverse + own[:, 0:1] * own[edge : edge + 1, 1:2]
        inner.append(node_column(second[:, edge], 0, size_x) * across)
    lane = lax.broadcasted_iota(jnp.int32, (size_x, 128), 1)
    from_last = jnp.where(even("gx"), 0, 1)
    return (
        jnp.where(even("gx"), tiles[1], tiles[0]),
        jnp.where(even("gx"), tiles[0], tiles[1]),
        jnp.where(lane == from_last, inner[1], inner[0]),
    )


def weights_kernel(size_x, size_y, width, columns, message, out):
    near, far, inner = side_weights(columns, message, size_x, size_y, width, 3)
    out[0:8, :] = near
    out[8:16, :] = far
    out[16 : 16 + size_x, :] = inner


def second_kernel(
    size_x,
    total,
    columns,
    operator,
    coefs,
    low_weights,
    low,
    from_far,
    from_near,
    from_near_rest,
    high,
    out,
    x_near,
    x_far,
    line_ends,
    inner,
    work,
    at_near,
    at_far,
    near_rows,
):
    size_y, width = total.shape[0] // size_x, total.shape[1]
    depth = size_y + 8
    second = second_table()
    near, far = x_starts(size_x * size_y, size_y)
    work[...] = total[...]
    rest = from_near_rest.shape[0]
    near_rows[:rest, :] = from_near_rest[...]
    near_rows[rest:, :] = from_near[...]
    add_packed(work, near, near_rows, size_y)
    add_packed(work, far, from_far, size_y)
    sides = ((low, 0, 3, 0), (high, size_y - 1, 0, size_y - 8))
    beyond = []
    for message, y, line, _ in sides:
        lines = [message[i * size_x : (i + 1) * size_x, :width] for i in range(4)]
        lines[line] = lines[line] + edge_rows(work, y, size_x, size_y)
        for x in range(size_x):
            work[x * size_y + y : x * size_y + y + 1, :] = lines[line][x : x + 1]
        for i in range(4):
            inverse = message[i * size_x : (i + 1) * size_x, width + 1 : width + 2]
            lines[i] = inverse * lines[i]
        value = sum(float(second[line, i]) * lines[i] for i in range(4))
        for x in range(size_x):
            value = value + node_column(second[:, x], 0, size_x) * lines[line][x : x + 1]
        mass = message[line * size_x : (line + 1) * size_x, width : width + 1]
        beyond.append(mass * value)
    out[...] = product(split(operator[...]), split(columns[:, 1:2] * work[...]))
    for (_, y, _, _), rows in zip(sides, beyond):
        for x in range(size_x):
            out[x * size_y + y : x * size_y + y + 1, :] += rows[x : x + 1]

    near, far = x_rows(size_x * size_y, size_y)
    at_near[:size_y, :] = out[near]
    at_far[:size_y, :] = out[far]
    last = depth * (width // 128)
    lanes = depth // 8 * (width % 128)
    high_weights = side_weights(columns, high, size_x, size_y, width, 0)
    for side, (message, _, line, _) in enumerate(sides):
        weights = high_weights if side else [low_weights[i : i + 8] for i in (0, 8, 16)]
        inner[side * size_x : (side + 1) * size_x, :] = weights[2][:size_x]
        place = slice(lanes + 8 * side, lanes + 8 * side + 5)
        x_near[last : last + 8, place] = weights[0][:, :5]
        x_far[last : last + 8, place] = weights[1][:, :5]
        for i in range(4):
            first, final = (
                message[i * size_x + x : i * size_x + x + 1, :width] for x in (0, size_x - 1)
            )
            row_near = jnp.where(even("gx"), final, first)
            row_far = jnp.where(even("gx"), first, final)
            place = size_y + 4 * side + i
            at_near[place : place + 1, :] = row_near
            at_far[place : place + 1, :] = row_far
            if i == line:
                line_ends[2 * side : 2 * side + 1, :] = row_far
                line_ends[2 * side + 1 : 2 * side + 2, :] = row_near
    pack(at_near[...], x_near)
    pack(at_far[...], x_far)
    if x_near.shape[0] > x_far.shape[0]:
        count = coefs.shape[0]
        start = last + 8
        x_near[start : start + count, :] = coefs[...]
        x_near[start + count :, :] = from_far[packed_rows(size_y, width) :, :]


def third_kernel(
    levels,
    hyper,
    base,
    masses,
    inner,
    factors,
    to_near,
    to_far,
    from_far,
    from_near,
    ends_near,
    ends_far,
    out,
    work,
    turned,
    turned_rest,
    values,
    values_rest,
    staged,
    sems,
    *beyond_rows,
):
    columns, width = base.shape
    size_x, size_y, _ = out.shape
    variables = width // levels
    rows = size_y + 8
    last, lanes = rows * (width // 128), rows // 8 * (width % 128)
    messages = (to_near, to_far, from_near, from_far)
    for message, target in zip(messages, beyond_rows):
        for i in range(width // 128):
            target[:, i * 128 : (i + 1) * 128] = message[i * rows + size_y : (i + 1) * rows, :]
        left = width % 128
        lanes_before = size_y // 8 * left
        target[:, width - left :] = message[last : last + 8, lanes_before : lanes_before + left]
    at_near, at_far, over_near, over_far = beyond_rows
    near, far = x_starts(columns, size_y)
    sides = ((0, 0, 3, 0), (1, size_y - 1, 0, size_y - 8))
    partners = (
        (near, at_near, over_near, over_far, ends_near),
        (far, at_far, over_far, over_near, ends_far),
    )
    for x in range(1, size_x - 1):
        for first in (0, size_y - 8):
            work[x * size_y + first : x * size_y + first + 8, :] = jnp.zeros((8, width), jnp.float32)
    for start, message in ((near, from_near), (far, from_far)):
        for i in range(width // 128):
            place = pl.ds(pl.multiple_of(start, size_y), size_y)
            work[place, i * 128 : (i + 1) * 128] = message[i * rows : i * rows + size_y, :]
        for i in range(size_y // 8):
            place = pl.ds(pl.multiple_of(start + i * 8, 8), 8)
            left = width % 128
            work[place, width - left :] = message[last : last + 8, i * left : (i + 1) * left]
    for side, y, line, first in sides:
        place = 4 * side
        weights = [
            message[last : last + 8, lanes + 8 * side : lanes + 8 * side + 5] for message in messages
        ]
        for which, (start, mine, theirs, others, ends) in enumerate(partners):
            own, beyond = weights[which], weights[2 + which]
            terms = [
                (weight[:, i : i + 1], values, place + i)
                for i in range(4)
                for weight, values in ((own, theirs), (beyond, mine))
            ]
            terms += [(own[:, 4:5], others, place + line), (beyond[:, 4:5], ends, 2 * side + which)]
            added = sum(weight * values[row : row + 1, :width] for weight, values, row in terms)
            work[pl.ds(pl.multiple_of(start + first, 8), 8), :] += added
        for x in range(1, size_x - 1):
            row, weight = x * size_y + y, side * size_x + x
            work[row : row + 1, :] += (
                inner[weight : weight + 1, 0:1] * over_near[place + line : place + line + 1, :]
                + inner[weight : weight + 1, 1:2] * over_far[place + line : place + line + 1, :]
            )
    for start in (near, far):
        place = pl.ds(pl.multiple_of(start, size_y), size_y)
        work[place, :] = base[place, :] - hyper[...] * (masses[place, 1:2] * work[place, :])
    for x in range(1, size_x - 1):
        for first in (0, size_y - 8):
            rows = slice(x * size_y + first, x * size_y + first + 8)
            work[rows, :] = base[rows, :] - hyper[...] * (masses[rows, 1:2] * work[rows, :])
        rows = slice(x * size_y + 8, (x + 1) * size_y - 8)
        work[rows, :] = base[rows, :]
    pitch, half = levels + 1, levels // 2
    scale, carry, gain, keep, flow, cloud = (
        factors.at[i * levels : (i + 1) * levels] for i in range(6)
    )
    groups = [(first, min(8, variables - first)) for first in range(0, variables, 8)]
    buffers = list(zip(groups, (turned, turned_rest), (values, values_rest)))

    def turn(group, turned):
        first, count = group
        start, stop = first * levels, (first + count) * levels
        tile = start // 128 * 128
        rows = work[:, tile:stop].T
        for i in range(count):
            row = start - tile + i * levels
            turned[i * pitch : i * pitch + levels, :] = rows[row : row + levels]

    def forward(group, turned, values):
        count = group[1]
        known = [jnp.zeros((count, columns), jnp.float32)] * 2
        for i in range(half):
            for side, k in enumerate((i, levels - 1 - i)):
                scaled = turned[pl.ds(k, count, stride=pitch), :] * scale[k : k + 1, :]
                known[side] = scaled + carry[k : k + 1, :] * known[side]
                values[k, :count, :] = known[side]
        return known

    def back(group, turned, values, known):
        count = group[1]
        meet = factors[6 * levels + half : 6 * levels + half + 1, :]
        first = (known[0] + gain[half - 1 : half, :] * known[1]) * meet
        solved = [first, known[1] + gain[half : half + 1, :] * first]
        for i in reversed(range(half)):
            for side, k in enumerate((i, levels - 1 - i)):
                if i < half - 1:
                    solved[side] = values[k, :count, :] + gain[k : k + 1, :] * solved[side]
                turned[pl.ds(k, count, stride=pitch), :] = solved[side]

    def leave(i):
        lanes = slice(i * 128, min((i + 1) * 128, width))
        parts = []
        for (start, count), source, _ in buffers:
            for j in range(start, start + count):
                first, last = max(lanes.start, j * levels), min(lanes.stop, (j + 1) * levels)
                if first < last:
                    offset = (j - start) * pitch - j * levels
                    parts.append(source[first + offset : last + offset, :])
        rows = jnp.concatenate(parts, axis=0)
        staged[:, :, lanes] = rows.T.reshape(size_x, size_y, -1)
        copy = pltpu.make_async_copy(staged.at[:, :, lanes], out.at[:, :, lanes], sems.at[i])
        copy.start()
        return copy

    (main, main_turned, main_values), (rest, rest_turned, rest_values) = buffers
    turn(main, main_turned)
    main_known = forward(main, main_turned, main_values)
    turn(rest, rest_turned)
    rest_known = forward(rest, rest_turned, rest_values)
    back(main, main_turned, main_values, main_known)
    tiles = -(-width // 128)
    settled_tiles, main_tiles = -(-3 * levels // 128), main[1] * levels // 128
    copies = [leave(i) for i in range(settled_tiles, main_tiles)]
    heat, vapour, liquid = (turned.at[i * pitch : i * pitch + levels] for i in range(3))
    condensed = cloud[...] * 0.5 * jnp.maximum(vapour[...] - 0.3 * heat[...], 0.0)
    vapour[...] = vapour[...] - condensed
    heat[...] = heat[...] + 2.0 * condensed
    liquid[...] = (liquid[...] + condensed) * keep[...]
    settled = [jnp.zeros((1, columns), jnp.float32)] * 2
    for i in range(half):
        for side, k in enumerate((i, half + i)):
            settled[side] = liquid[k : k + 1, :] + flow[k : k + 1, :] * settled[side]
            liquid[k : k + 1, :] = settled[side]
    through = factors[6 * levels : 6 * levels + half, :]
    liquid[half:, :] = liquid[half:, :] + through * settled[0]
    back(rest, rest_turned, rest_values, rest_known)
    copies += [leave(i) for i in range(settled_tiles)]
    copies += [leave(i) for i in range(main_tiles, tiles)]
    for copy in copies:
        copy.wait()


def base_kernel(state, hyper, total, masses, base):
    columns, width = total.shape
    twice = masses[:, 1:2] * total[...]
    base[...] = state[...].reshape(columns, width) - hyper[...] * twice


def pick(slots, pieces):
    size_x, size_y = slots.shape
    columns = size_x * size_y
    wanted = jnp.concatenate([slots[x : x + 1, :] for x in range(size_x)], axis=1)
    picked = 0.0
    for owner, rest in pieces:
        span = rest.shape[1]
        entry = lax.broadcasted_iota(jnp.int32, (span, columns), 0) + owner * span
        choice = (entry == wanted).astype(jnp.float32).astype(jnp.bfloat16)
        for _ in range(3):
            part = rest.astype(jnp.bfloat16)
            rest = rest - part.astype(jnp.float32)
            picked = picked + jnp.dot(part, choice, preferred_element_type=jnp.float32)
    return picked


def factor_kernel(levels, slots, *refs):
    factors = refs[-1]
    if len(refs) == 3:
        here = lax.axis_index("gx")
        pieces = []
        for message, owner in zip(refs, (here, here ^ 1)):
            start = message.shape[0] - 6 * levels
            pieces.append((owner, message[start : start + 3 * levels, :]))
            pieces.append((owner ^ 3, message[start + 3 * levels :, :]))
    else:
        pieces = [(peer, refs[0][peer]) for peer in range(refs[0].shape[0])]
    columns = factors.shape[1]
    picked = pick(slots, pieces)
    mixing, falling, covered = (picked[i * levels : (i + 1) * levels] for i in range(3))
    scale, carry, gain, keep, flow, cover = (
        factors.at[i * levels : (i + 1) * levels] for i in range(6)
    )
    zero = jnp.zeros((1, columns), jnp.float32)
    kept = 1.0 / (1.0 + falling)
    keep[...] = kept
    flow[:1, :] = zero
    flow[1:, :] = falling[:-1] * kept[1:]
    cover[...] = covered
    half = levels // 2
    gains = [zero, zero]
    through = jnp.ones((1, columns), jnp.float32)
    for i in range(half):
        for side, k in enumerate((i, levels - 1 - i)):
            above = mixing[k : k + 1] if k else zero
            below = mixing[k + 1 : k + 2] if k + 1 < levels else zero
            centre = 1.0 + above + (below if k + 1 < levels else mixing[:1])
            behind, ahead = (above, below) if side == 0 else (below, above)
            inverse = 1.0 / (centre - behind * gains[side])
            gains[side] = ahead * inverse
            scale[k : k + 1, :] = inverse
            carry[k : k + 1, :] = behind * inverse
            gain[k : k + 1, :] = gains[side]
        k = half + i
        through = through * falling[k - 1 : k] * kept[k : k + 1]
        factors[6 * levels + i : 6 * levels + i + 1, :] = through
    last = 6 * levels + half
    factors[last : last + 1, :] = 1.0 / (1.0 - gains[0] * gains[1])


def swapped(value, axis, partner):
    return lax.ppermute(value, axis, [(i, partner(i)) for i in range(lax.axis_size(axis))])


def exchanged(near, far, axis):
    size = lax.axis_size(axis)
    from_far = swapped(far, axis, lambda i: (i + (1 if i % 2 else -1)) % size)
    from_near = swapped(near, axis, lambda i: i ^ 1)
    return from_far, from_near


def shifted(value, axis, step):
    size = lax.axis_size(axis)
    return lax.ppermute(value, axis, [(i, (i + step) % size) for i in range(size)])


def local(
    model_state, hyper_coef, point_mass, inverse_mass, span_slot, vert_diff, fall_rate, cloud_frac
):
    size_x, size_y, width = model_state.shape
    levels, span = vert_diff.shape[1:]
    columns = size_x * size_y
    hyper = hyper_coef.reshape(1, width)
    padded = -(-(width + 5) // 128) * 128

    def array(*shape):
        return jax.ShapeDtypeStruct(shape, jnp.float32)

    def scratch(*shape):
        return pltpu.VMEM(shape, jnp.float32)

    def call(kernel, name, outs, scratches, *operands, spec=VMEM, out=VMEM, cost=None):
        return pl.pallas_call(
            kernel,
            out_shape=outs,
            in_specs=[spec] * len(operands),
            out_specs=[out] * len(outs),
            scratch_shapes=scratches,
            compiler_params=PARAMS,
            cost_estimate=cost,
            name=name,
        )(*operands)

    riding = lax.axis_size("gx") == 4
    whole = array(columns, width)
    edge = array(4 * size_x, padded)
    extra = 3 * levels if riding else 0
    rest = width // 256 * size_y
    first_rows, last_rows = packed_rows(size_y, width), packed_rows(size_y + 8, width)
    here, total, x_near, x_near_rest, x_far, y_low, y_high, operator, masses, coefs = call(
        start_kernel,
        "start",
        [
            array(size_x, size_y, width),
            whole,
            array(first_rows - rest, 128),
            array(rest, 128),
            array(first_rows + extra, 128),
            edge,
            edge,
            array(columns, columns),
            array(columns, 128),
            array(3 * levels, span),
        ],
        [
            scratch(size_x, size_y),
            scratch(size_x, size_y),
            scratch(first_rows, 128),
            pltpu.SemaphoreType.DMA((size_x + 5,)),
        ],
        *(
            pltpu.with_memory_space_constraint(value, pltpu.HBM)
            for value in (
                model_state,
                point_mass,
                inverse_mass,
                vert_diff,
                fall_rate,
                cloud_frac,
            )
        ),
        spec=pl.BlockSpec(memory_space=pltpu.HBM),
    )
    low = shifted(y_high, "gy", 1)
    from_far, from_near = exchanged(x_near, x_far, "gx")
    from_near_rest = swapped(x_near_rest, "gx", lambda i: i ^ 1)
    high = shifted(y_low, "gy", -1)
    (low_weights,) = call(
        functools.partial(weights_kernel, size_x, size_y, width),
        "weights",
        [array(24, 128)],
        [],
        masses,
        low,
        cost=LONG,
    )
    total, x_near, x_far, line_ends, inner = call(
        functools.partial(second_kernel, size_x),
        "second",
        [
            whole,
            array(last_rows + 2 * extra, 128),
            array(last_rows, 128),
            array(4, width),
            array(2 * size_x, 128),
        ],
        [
            scratch(columns, width),
            scratch(size_y + 8, width),
            scratch(size_y + 8, width),
            scratch(first_rows, 128),
        ],
        total,
        masses,
        operator,
        coefs,
        low_weights,
        low,
        from_far,
        from_near,
        from_near_rest,
        high,
    )
    last_x = exchanged(x_near, x_far, "gx")
    peers = lax.axis_size("gx")
    ends_near = swapped(line_ends, "gx", lambda i: (i + (2 if i % 2 else -2)) % peers)
    ends_far = ends_near
    if peers != 4:
        ends_far = swapped(line_ends, "gx", lambda i: (i - (2 if i % 2 else -2)) % peers)
    if riding:
        pieces = [x_near, last_x[1]]
    else:
        pieces = [lax.all_gather(coefs, "gx")]
    (factors,) = call(
        functools.partial(factor_kernel, levels),
        "factors",
        [array(6 * levels + levels // 2 + 8, columns)],
        [],
        span_slot,
        *pieces,
    )
    (base,) = call(base_kernel, "base", [whole], [], here, hyper, total, masses)
    (result,) = call(
        functools.partial(third_kernel, levels),
        "third",
        [array(size_x, size_y, width)],
        [
            scratch(columns, width),
            scratch(8 * (levels + 1), columns),
            scratch((width // levels - 8) * (levels + 1), columns),
            scratch(levels, 8, columns),
            scratch(levels, 8, columns),
            scratch(size_x, size_y, width),
            pltpu.SemaphoreType.DMA((-(-width // 128),)),
        ]
        + [scratch(8, width)] * 4,
        hyper,
        base,
        masses,
        inner,
        factors,
        x_near,
        x_far,
        *last_x,
        ends_near,
        ends_far,
        out=pl.BlockSpec(memory_space=pltpu.HBM),
    )
    return result


def solution(mesh):
    placed = (
        P("gx", "gy", None),
        P(),
        P("gx", "gy"),
        P("gx", "gy"),
        P("gx", "gy"),
        P("gy", None, "gx"),
        P("gy", None, "gx"),
        P("gy", None, "gx"),
    )
    return jax.shard_map(
        local, mesh=mesh, in_specs=placed, out_specs=P("gx", "gy", None), check_vma=False
    )
```

```python
import functools

import jax
import jax.numpy as jnp
import numpy as np
from jax import lax
from jax.experimental import pallas as pl
from jax.experimental.pallas import tpu as pltpu
from jax.sharding import PartitionSpec as P

VMEM = pl.BlockSpec(memory_space=pltpu.VMEM)
LONG = pl.CostEstimate(flops=100_000_000_000, bytes_accessed=30_000_000, transcendentals=0)
PARAMS = pltpu.CompilerParams(vmem_limit_bytes=16 * 1024 * 1024)


def second_table():
    nodes = np.array([-1.0, -1.0 / np.sqrt(5.0), 1.0 / np.sqrt(5.0), 1.0])
    deriv = np.zeros((4, 4))
    for i in range(4):
        for j in range(4):
            if i == j:
                deriv[i, j] = sum(1.0 / (nodes[i] - nodes[k]) for k in range(4) if k != i)
            else:
                upper = np.prod([nodes[i] - nodes[k] for k in range(4) if k != i])
                lower = np.prod([nodes[j] - nodes[k] for k in range(4) if k != j])
                deriv[i, j] = upper / (lower * (nodes[i] - nodes[j]))
    return deriv @ deriv


def split(value):
    high = value.astype(jnp.bfloat16)
    return high, (value - high.astype(jnp.float32)).astype(jnp.bfloat16)


def product(left, right):
    left = jnp.concatenate([left[0], left[1], left[0]], axis=1)
    right = jnp.concatenate([right[0], right[0], right[1]], axis=0)
    return jnp.dot(left, right, preferred_element_type=jnp.float32)


def lookup(row, lane):
    second = second_table()
    row, lane = lax.rem(row, 4), lax.rem(lane, 4)
    result = jnp.zeros(row.shape, jnp.float32)
    for j in range(4):
        column = jnp.full(row.shape, float(second[3, j]), jnp.float32)
        for i in range(3):
            column = jnp.where(row == i, float(second[i, j]), column)
        result = jnp.where(lane == j, column, result)
    return result


def laplacian(size_x, size_y):
    count = size_x * size_y
    row, lane = (lax.broadcasted_iota(jnp.int32, (count, count), i) for i in range(2))
    row_x, lane_x = lax.div(row, size_y), lax.div(lane, size_y)
    row_y, lane_y = lax.rem(row, size_y), lax.rem(lane, size_y)
    same_x = (row_y == lane_y) & (lax.div(row_x, 4) == lax.div(lane_x, 4))
    same_y = (row_x == lane_x) & (lax.div(row_y, 4) == lax.div(lane_y, 4))
    along_x = jnp.where(same_x, lookup(row_x, lane_x), 0.0)
    return along_x + jnp.where(same_y, lookup(row_y, lane_y), 0.0)


def of_partner(values, size_y):
    count = values.shape[0]
    row_y = lax.rem(lax.broadcasted_iota(jnp.int32, values.shape, 0), size_y)
    phase = lax.rem(row_y, 4)
    before = jnp.where((phase == 0) & (row_y > 0), pltpu.roll(values, 1, 0), 0.0)
    after = (phase == 3) & (row_y < size_y - 1)
    return jnp.where(after, pltpu.roll(values, count - 1, 0), before)


def to_column(plane):
    size_x, size_y = plane.shape
    row = lax.broadcasted_iota(jnp.int32, (size_y, size_y), 0)
    lane = lax.broadcasted_iota(jnp.int32, (size_y, size_y), 1)
    parts = [
        jnp.sum(jnp.where(row == lane, plane[x : x + 1, :], 0.0), axis=1, keepdims=True)
        for x in range(size_x)
    ]
    return jnp.concatenate(parts, axis=0)


def even(axis):
    return lax.rem(lax.axis_index(axis), 2) == 0


def x_starts(count, size_y):
    near = jnp.where(even("gx"), count - size_y, 0)
    return near, count - size_y - near


def x_rows(count, size_y):
    starts = x_starts(count, size_y)
    return tuple(pl.ds(pl.multiple_of(start, size_y), size_y) for start in starts)


def add_packed(work, start, message, rows):
    def write(first, count, lanes, value):
        work[pl.ds(pl.multiple_of(start + first, 8), count), lanes] += value

    unpack(message, rows, work.shape[1], write)


def packed_rows(rows, width):
    return rows * (width // 128) + 8


def pack(value, message):
    rows, width = value.shape
    full, left = width // 128, width % 128
    for i in range(full):
        message[i * rows : (i + 1) * rows, :] = value[:, i * 128 : (i + 1) * 128]
    for i in range(rows // 8):
        lanes = slice(i * left, (i + 1) * left)
        message[full * rows : full * rows + 8, lanes] = value[i * 8 : (i + 1) * 8, full * 128 :]


def unpack(message, rows, width, write):
    full, left = width // 128, width % 128
    for i in range(full):
        write(0, rows, slice(i * 128, (i + 1) * 128), message[i * rows : (i + 1) * rows, :])
    for i in range(rows // 8):
        value = message[full * rows : full * rows + 8, i * left : (i + 1) * left]
        write(i * 8, 8, slice(full * 128, width), value)


def edge_rows(ref, y, size_x, size_y):
    return jnp.concatenate(
        [ref[x * size_y + y : x * size_y + y + 1, :] for x in range(size_x)], axis=0
    )


def start_kernel(
    state,
    mass,
    inverse,
    diff,
    fall,
    cloud,
    here,
    total,
    x_near,
    x_near_rest,
    x_far,
    low,
    high,
    operator,
    columns,
    coefs,
    mass_here,
    inverse_here,
    near_rows,
    sems,
):
    size_x, size_y, width = state.shape
    levels = diff.shape[1]
    pairs = [(mass, mass_here), (inverse, inverse_here)]
    pairs += [(state.at[x], here.at[x]) for x in range(size_x)]
    for i, source in enumerate((diff, fall, cloud)):
        pairs.append((source.at[0], coefs.at[i * levels : (i + 1) * levels]))
    copies = [
        pltpu.make_async_copy(source, target, sems.at[i])
        for i, (source, target) in enumerate(pairs)
    ]
    for copy in copies:
        copy.start()
    count = size_x * size_y
    matrix = laplacian(size_x, size_y)
    for copy in copies[:2]:
        copy.wait()
    own = jnp.broadcast_to(to_column(mass_here[...]), (count, count))
    matrix = own * matrix
    matrix = matrix + of_partner(matrix, size_y)
    operator[...] = matrix
    partner = of_partner(own, size_y)
    inverses = to_column(inverse_here[...])
    lane = lax.broadcasted_iota(jnp.int32, columns.shape, 1)
    columns[...] = jnp.where(lane == 0, own, jnp.where(lane == 1, inverses, partner))
    for copy in copies[2 : 2 + size_x]:
        copy.wait()
    total[...] = product(split(matrix), split(here[...].reshape(count, width)))
    near, far = x_rows(count, size_y)
    pack(total[near], near_rows)
    rest = x_near_rest.shape[0]
    x_near_rest[...] = near_rows[:rest, :]
    x_near[...] = near_rows[rest:, :]
    pack(total[far], x_far)
    for first, message in ((0, low), (size_y - 4, high)):
        for i in range(4):
            rows = slice(i * size_x, (i + 1) * size_x)
            message[rows, :width] = edge_rows(total, first + i, size_x, size_y)
            message[rows, width : width + 2] = edge_rows(columns, first + i, size_x, size_y)[:, :2]
    for copy in copies[2 + size_x :]:
        copy.wait()
    if x_far.shape[0] > near_rows.shape[0]:
        x_far[near_rows.shape[0] :, :] = coefs[...]


def node_column(values, start, count):
    row = lax.broadcasted_iota(jnp.int32, (count, 1), 0)
    result = jnp.zeros((count, 1), jnp.float32)
    for i, value in enumerate(values):
        result = jnp.where(row == start + i, float(value), result)
    return result


def edge_weights(columns, message, size_x, size_y, width, edge, line):
    second = second_table()
    other = size_x - 1 - edge
    low = line == 3
    y, first = (0, 0) if low else (size_y - 1, size_y - 8)
    rows = slice(edge * size_y + first, edge * size_y + first + 8)
    here, there = (slice(x * size_y + y, x * size_y + y + 1) for x in (edge, other))
    mass, inverse = columns[here, 0:1], columns[here, 1:2]
    beyond = slice(line * size_x + edge, line * size_x + edge + 1)
    beyond_mass = message[beyond, width : width + 1]

    def beyond_inverse(i, x):
        return message[i * size_x + x : i * size_x + x + 1, width + 1 : width + 2]

    if low:
        own, partner = node_column(second[:, 0], 0, 8), node_column(second[3:, 0], 4, 8)
    else:
        own, partner = node_column(second[:, 3], 4, 8), node_column(second[:1, 3], 3, 8)
    along = inverse * (own * columns[rows, 0:1] + partner * columns[rows, 2:3])
    lane = lax.broadcasted_iota(jnp.int32, (8, 128), 1)
    place = lax.broadcasted_iota(jnp.int32, (8, 128), 0)
    tile = jnp.where(lane == line, along, 0.0)
    for i in range(4):
        value = float(second[line, i]) * beyond_mass * beyond_inverse(i, edge)
        if i == line:
            across = beyond_mass * beyond_inverse(line, edge) + mass * inverse
            value = value + float(second[edge, edge]) * across
        tile = tile + jnp.where((place == y - first) & (lane == i), value, 0.0)
    across = beyond_mass * beyond_inverse(line, other) + mass * columns[there, 1:2]
    value = float(second[edge, other]) * across
    return tile + jnp.where((place == y - first) & (lane == 4), value, 0.0)


def side_weights(columns, message, size_x, size_y, width, line):
    second = second_table()
    first, last = 0, size_x - 1
    tiles = [
        edge_weights(columns, message, size_x, size_y, width, edge, line) for edge in (first, last)
    ]
    mass = message[line * size_x : (line + 1) * size_x, width : width + 1]
    own = edge_rows(columns, 0 if line == 3 else size_y - 1, size_x, size_y)
    inner = []
    for edge in (first, last):
        inverse = message[line * size_x + edge : line * size_x + edge + 1, width + 1 : width + 2]
        across = mass * inverse + own[:, 0:1] * own[edge : edge + 1, 1:2]
        inner.append(node_column(second[:, edge], 0, size_x) * across)
    lane = lax.broadcasted_iota(jnp.int32, (size_x, 128), 1)
    from_last = jnp.where(even("gx"), 0, 1)
    return (
        jnp.where(even("gx"), tiles[1], tiles[0]),
        jnp.where(even("gx"), tiles[0], tiles[1]),
        jnp.where(lane == from_last, inner[1], inner[0]),
    )


def weights_kernel(size_x, size_y, width, columns, message, out):
    near, far, inner = side_weights(columns, message, size_x, size_y, width, 3)
    out[0:8, :] = near
    out[8:16, :] = far
    out[16 : 16 + size_x, :] = inner


def second_kernel(
    size_x,
    total,
    columns,
    operator,
    coefs,
    low_weights,
    low,
    from_far,
    from_near,
    from_near_rest,
    high,
    out,
    x_near,
    x_far,
    line_ends,
    inner,
    own_coefs,
    far_coefs,
    work,
    at_near,
    at_far,
    near_rows,
):
    size_y, width = total.shape[0] // size_x, total.shape[1]
    depth = size_y + 8
    second = second_table()
    near, far = x_starts(size_x * size_y, size_y)
    work[...] = total[...]
    rest = from_near_rest.shape[0]
    near_rows[:rest, :] = from_near_rest[...]
    near_rows[rest:, :] = from_near[...]
    add_packed(work, near, near_rows, size_y)
    add_packed(work, far, from_far, size_y)
    sides = ((low, 0, 3, 0), (high, size_y - 1, 0, size_y - 8))
    beyond = []
    for message, y, line, _ in sides:
        lines = [message[i * size_x : (i + 1) * size_x, :width] for i in range(4)]
        lines[line] = lines[line] + edge_rows(work, y, size_x, size_y)
        for x in range(size_x):
            work[x * size_y + y : x * size_y + y + 1, :] = lines[line][x : x + 1]
        for i in range(4):
            inverse = message[i * size_x : (i + 1) * size_x, width + 1 : width + 2]
            lines[i] = inverse * lines[i]
        value = sum(float(second[line, i]) * lines[i] for i in range(4))
        for x in range(size_x):
            value = value + node_column(second[:, x], 0, size_x) * lines[line][x : x + 1]
        mass = message[line * size_x : (line + 1) * size_x, width : width + 1]
        beyond.append(mass * value)
    out[...] = product(split(operator[...]), split(columns[:, 1:2] * work[...]))
    for (_, y, _, _), rows in zip(sides, beyond):
        for x in range(size_x):
            out[x * size_y + y : x * size_y + y + 1, :] += rows[x : x + 1]

    near, far = x_rows(size_x * size_y, size_y)
    at_near[:size_y, :] = out[near]
    at_far[:size_y, :] = out[far]
    last = depth * (width // 128)
    lanes = depth // 8 * (width % 128)
    high_weights = side_weights(columns, high, size_x, size_y, width, 0)
    for side, (message, _, line, _) in enumerate(sides):
        weights = high_weights if side else [low_weights[i : i + 8] for i in (0, 8, 16)]
        inner[side * size_x : (side + 1) * size_x, :] = weights[2][:size_x]
        place = slice(lanes + 8 * side, lanes + 8 * side + 5)
        x_near[last : last + 8, place] = weights[0][:, :5]
        x_far[last : last + 8, place] = weights[1][:, :5]
        for i in range(4):
            first, final = (
                message[i * size_x + x : i * size_x + x + 1, :width] for x in (0, size_x - 1)
            )
            row_near = jnp.where(even("gx"), final, first)
            row_far = jnp.where(even("gx"), first, final)
            place = size_y + 4 * side + i
            at_near[place : place + 1, :] = row_near
            at_far[place : place + 1, :] = row_far
            if i == line:
                line_ends[2 * side : 2 * side + 1, :] = row_far
                line_ends[2 * side + 1 : 2 * side + 2, :] = row_near
    pack(at_near[...], x_near)
    pack(at_far[...], x_far)
    own_coefs[...] = coefs[...]
    start = packed_rows(size_y, width)
    if from_far.shape[0] > start:
        far_coefs[...] = from_far[start:, :]


def third_kernel(
    levels,
    hyper,
    base,
    masses,
    inner,
    factors,
    to_near,
    to_far,
    from_far,
    from_near,
    ends_near,
    ends_far,
    out,
    work,
    turned,
    turned_rest,
    values,
    values_rest,
    staged,
    sems,
    *beyond_rows,
):
    columns, width = base.shape
    size_x, size_y, _ = out.shape
    variables = width // levels
    rows = size_y + 8
    last, lanes = rows * (width // 128), rows // 8 * (width % 128)
    messages = (to_near, to_far, from_near, from_far)
    for message, target in zip(messages, beyond_rows):
        for i in range(width // 128):
            target[:, i * 128 : (i + 1) * 128] = message[i * rows + size_y : (i + 1) * rows, :]
        left = width % 128
        lanes_before = size_y // 8 * left
        target[:, width - left :] = message[last : last + 8, lanes_before : lanes_before + left]
    at_near, at_far, over_near, over_far = beyond_rows
    near, far = x_starts(columns, size_y)
    sides = ((0, 0, 3, 0), (1, size_y - 1, 0, size_y - 8))
    partners = (
        (near, at_near, over_near, over_far, ends_near),
        (far, at_far, over_far, over_near, ends_far),
    )
    for x in range(1, size_x - 1):
        for first in (0, size_y - 8):
            work[x * size_y + first : x * size_y + first + 8, :] = jnp.zeros((8, width), jnp.float32)
    for start, message in ((near, from_near), (far, from_far)):
        for i in range(width // 128):
            place = pl.ds(pl.multiple_of(start, size_y), size_y)
            work[place, i * 128 : (i + 1) * 128] = message[i * rows : i * rows + size_y, :]
        for i in range(size_y // 8):
            place = pl.ds(pl.multiple_of(start + i * 8, 8), 8)
            left = width % 128
            work[place, width - left :] = message[last : last + 8, i * left : (i + 1) * left]
    for side, y, line, first in sides:
        place = 4 * side
        weights = [
            message[last : last + 8, lanes + 8 * side : lanes + 8 * side + 5] for message in messages
        ]
        for which, (start, mine, theirs, others, ends) in enumerate(partners):
            own, beyond = weights[which], weights[2 + which]
            terms = [
                (weight[:, i : i + 1], values, place + i)
                for i in range(4)
                for weight, values in ((own, theirs), (beyond, mine))
            ]
            terms += [(own[:, 4:5], others, place + line), (beyond[:, 4:5], ends, 2 * side + which)]
            added = sum(weight * values[row : row + 1, :width] for weight, values, row in terms)
            work[pl.ds(pl.multiple_of(start + first, 8), 8), :] += added
        for x in range(1, size_x - 1):
            row, weight = x * size_y + y, side * size_x + x
            work[row : row + 1, :] += (
                inner[weight : weight + 1, 0:1] * over_near[place + line : place + line + 1, :]
                + inner[weight : weight + 1, 1:2] * over_far[place + line : place + line + 1, :]
            )
    for start in (near, far):
        place = pl.ds(pl.multiple_of(start, size_y), size_y)
        work[place, :] = base[place, :] - hyper[...] * (masses[place, 1:2] * work[place, :])
    for x in range(1, size_x - 1):
        for first in (0, size_y - 8):
            rows = slice(x * size_y + first, x * size_y + first + 8)
            work[rows, :] = base[rows, :] - hyper[...] * (masses[rows, 1:2] * work[rows, :])
        rows = slice(x * size_y + 8, (x + 1) * size_y - 8)
        work[rows, :] = base[rows, :]
    pitch, half = levels + 1, levels // 2
    scale, carry, gain, keep, flow, cloud = (
        factors.at[i * levels : (i + 1) * levels] for i in range(6)
    )
    groups = [(first, min(8, variables - first)) for first in range(0, variables, 8)]
    buffers = list(zip(groups, (turned, turned_rest), (values, values_rest)))

    def turn(group, turned):
        first, count = group
        start, stop = first * levels, (first + count) * levels
        tile = start // 128 * 128
        rows = work[:, tile:stop].T
        for i in range(count):
            row = start - tile + i * levels
            turned[i * pitch : i * pitch + levels, :] = rows[row : row + levels]

    def forward(group, turned, values):
        count = group[1]
        known = [jnp.zeros((count, columns), jnp.float32)] * 2
        for i in range(half):
            for side, k in enumerate((i, levels - 1 - i)):
                scaled = turned[pl.ds(k, count, stride=pitch), :] * scale[k : k + 1, :]
                known[side] = scaled + carry[k : k + 1, :] * known[side]
                values[k, :count, :] = known[side]
        return known

    def back(group, turned, values, known):
        count = group[1]
        meet = factors[6 * levels + half : 6 * levels + half + 1, :]
        first = (known[0] + gain[half - 1 : half, :] * known[1]) * meet
        solved = [first, known[1] + gain[half : half + 1, :] * first]
        for i in reversed(range(half)):
            for side, k in enumerate((i, levels - 1 - i)):
                if i < half - 1:
                    solved[side] = values[k, :count, :] + gain[k : k + 1, :] * solved[side]
                turned[pl.ds(k, count, stride=pitch), :] = solved[side]

    def leave(i):
        lanes = slice(i * 128, min((i + 1) * 128, width))
        parts = []
        for (start, count), source, _ in buffers:
            for j in range(start, start + count):
                first, last = max(lanes.start, j * levels), min(lanes.stop, (j + 1) * levels)
                if first < last:
                    offset = (j - start) * pitch - j * levels
                    parts.append(source[first + offset : last + offset, :])
        rows = jnp.concatenate(parts, axis=0)
        staged[:, :, lanes] = rows.T.reshape(size_x, size_y, -1)
        copy = pltpu.make_async_copy(staged.at[:, :, lanes], out.at[:, :, lanes], sems.at[i])
        copy.start()
        return copy

    (main, main_turned, main_values), (rest, rest_turned, rest_values) = buffers
    turn(main, main_turned)
    main_known = forward(main, main_turned, main_values)
    turn(rest, rest_turned)
    rest_known = forward(rest, rest_turned, rest_values)
    back(main, main_turned, main_values, main_known)
    tiles = -(-width // 128)
    settled_tiles, main_tiles = -(-3 * levels // 128), main[1] * levels // 128
    copies = [leave(i) for i in range(settled_tiles, main_tiles)]
    heat, vapour, liquid = (turned.at[i * pitch : i * pitch + levels] for i in range(3))
    condensed = cloud[...] * 0.5 * jnp.maximum(vapour[...] - 0.3 * heat[...], 0.0)
    vapour[...] = vapour[...] - condensed
    heat[...] = heat[...] + 2.0 * condensed
    liquid[...] = (liquid[...] + condensed) * keep[...]
    settled = [jnp.zeros((1, columns), jnp.float32)] * 2
    for i in range(half):
        for side, k in enumerate((i, half + i)):
            settled[side] = liquid[k : k + 1, :] + flow[k : k + 1, :] * settled[side]
            liquid[k : k + 1, :] = settled[side]
    through = factors[6 * levels : 6 * levels + half, :]
    liquid[half:, :] = liquid[half:, :] + through * settled[0]
    back(rest, rest_turned, rest_values, rest_known)
    copies += [leave(i) for i in range(settled_tiles)]
    copies += [leave(i) for i in range(main_tiles, tiles)]
    for copy in copies:
        copy.wait()


def base_kernel(state, hyper, total, masses, base):
    columns, width = total.shape
    twice = masses[:, 1:2] * total[...]
    base[...] = state[...].reshape(columns, width) - hyper[...] * twice


def pick(slots, pieces):
    size_x, size_y = slots.shape
    columns = size_x * size_y
    wanted = jnp.concatenate([slots[x : x + 1, :] for x in range(size_x)], axis=1)
    picked = 0.0
    for owner, rest in pieces:
        span = rest.shape[1]
        entry = lax.broadcasted_iota(jnp.int32, (span, columns), 0) + owner * span
        choice = (entry == wanted).astype(jnp.float32).astype(jnp.bfloat16)
        for _ in range(3):
            part = rest.astype(jnp.bfloat16)
            rest = rest - part.astype(jnp.float32)
            picked = picked + jnp.dot(part, choice, preferred_element_type=jnp.float32)
    return picked


def factor_kernel(levels, slots, *refs):
    factors = refs[-1]
    if len(refs) == 5:
        here = lax.axis_index("gx")
        owners = (here, here ^ 3, here ^ 1, here ^ 2)
        pieces = [(owner, message[...]) for owner, message in zip(owners, refs)]
    else:
        pieces = [(peer, refs[0][peer]) for peer in range(refs[0].shape[0])]
    columns = factors.shape[1]
    picked = pick(slots, pieces)
    mixing, falling, covered = (picked[i * levels : (i + 1) * levels] for i in range(3))
    scale, carry, gain, keep, flow, cover = (
        factors.at[i * levels : (i + 1) * levels] for i in range(6)
    )
    zero = jnp.zeros((1, columns), jnp.float32)
    kept = 1.0 / (1.0 + falling)
    keep[...] = kept
    flow[:1, :] = zero
    flow[1:, :] = falling[:-1] * kept[1:]
    cover[...] = covered
    half = levels // 2
    gains = [zero, zero]
    through = jnp.ones((1, columns), jnp.float32)
    for i in range(half):
        for side, k in enumerate((i, levels - 1 - i)):
            above = mixing[k : k + 1] if k else zero
            below = mixing[k + 1 : k + 2] if k + 1 < levels else zero
            centre = 1.0 + above + (below if k + 1 < levels else mixing[:1])
            behind, ahead = (above, below) if side == 0 else (below, above)
            inverse = 1.0 / (centre - behind * gains[side])
            gains[side] = ahead * inverse
            scale[k : k + 1, :] = inverse
            carry[k : k + 1, :] = behind * inverse
            gain[k : k + 1, :] = gains[side]
        k = half + i
        through = through * falling[k - 1 : k] * kept[k : k + 1]
        factors[6 * levels + i : 6 * levels + i + 1, :] = through
    last = 6 * levels + half
    factors[last : last + 1, :] = 1.0 / (1.0 - gains[0] * gains[1])


def swapped(value, axis, partner):
    return lax.ppermute(value, axis, [(i, partner(i)) for i in range(lax.axis_size(axis))])


def exchanged(near, far, axis):
    size = lax.axis_size(axis)
    from_far = swapped(far, axis, lambda i: (i + (1 if i % 2 else -1)) % size)
    from_near = swapped(near, axis, lambda i: i ^ 1)
    return from_far, from_near


def shifted(value, axis, step):
    size = lax.axis_size(axis)
    return lax.ppermute(value, axis, [(i, (i + step) % size) for i in range(size)])


def local(
    model_state, hyper_coef, point_mass, inverse_mass, span_slot, vert_diff, fall_rate, cloud_frac
):
    size_x, size_y, width = model_state.shape
    levels, span = vert_diff.shape[1:]
    columns = size_x * size_y
    hyper = hyper_coef.reshape(1, width)
    padded = -(-(width + 5) // 128) * 128

    def array(*shape):
        return jax.ShapeDtypeStruct(shape, jnp.float32)

    def scratch(*shape):
        return pltpu.VMEM(shape, jnp.float32)

    def call(kernel, name, outs, scratches, *operands, spec=VMEM, out=VMEM, cost=None):
        return pl.pallas_call(
            kernel,
            out_shape=outs,
            in_specs=[spec] * len(operands),
            out_specs=[out] * len(outs),
            scratch_shapes=scratches,
            compiler_params=PARAMS,
            cost_estimate=cost,
            name=name,
        )(*operands)

    riding = lax.axis_size("gx") == 4
    whole = array(columns, width)
    edge = array(4 * size_x, padded)
    extra = 3 * levels if riding else 0
    rest = width // 256 * size_y
    first_rows, last_rows = packed_rows(size_y, width), packed_rows(size_y + 8, width)
    here, total, x_near, x_near_rest, x_far, y_low, y_high, operator, masses, coefs = call(
        start_kernel,
        "start",
        [
            array(size_x, size_y, width),
            whole,
            array(first_rows - rest, 128),
            array(rest, 128),
            array(first_rows + extra, 128),
            edge,
            edge,
            array(columns, columns),
            array(columns, 128),
            array(3 * levels, span),
        ],
        [
            scratch(size_x, size_y),
            scratch(size_x, size_y),
            scratch(first_rows, 128),
            pltpu.SemaphoreType.DMA((size_x + 5,)),
        ],
        *(
            pltpu.with_memory_space_constraint(value, pltpu.HBM)
            for value in (
                model_state,
                point_mass,
                inverse_mass,
                vert_diff,
                fall_rate,
                cloud_frac,
            )
        ),
        spec=pl.BlockSpec(memory_space=pltpu.HBM),
    )
    low = shifted(y_high, "gy", 1)
    from_far, from_near = exchanged(x_near, x_far, "gx")
    from_near_rest = swapped(x_near_rest, "gx", lambda i: i ^ 1)
    high = shifted(y_low, "gy", -1)
    (low_weights,) = call(
        functools.partial(weights_kernel, size_x, size_y, width),
        "weights",
        [array(24, 128)],
        [],
        masses,
        low,
        cost=LONG,
    )
    total, x_near, x_far, line_ends, inner, own_coefs, far_coefs = call(
        functools.partial(second_kernel, size_x),
        "second",
        [
            whole,
            array(last_rows, 128),
            array(last_rows + 8, 128),
            array(4, width),
            array(2 * size_x, 128),
            array(3 * levels, span),
            array(3 * levels, span),
        ],
        [
            scratch(columns, width),
            scratch(size_y + 8, width),
            scratch(size_y + 8, width),
            scratch(first_rows, 128),
        ],
        total,
        masses,
        operator,
        coefs,
        low_weights,
        low,
        from_far,
        from_near,
        from_near_rest,
        high,
    )
    last_x = exchanged(x_near, x_far, "gx")
    peers = lax.axis_size("gx")
    ends_near = swapped(line_ends, "gx", lambda i: (i + (2 if i % 2 else -2)) % peers)
    ends_far = ends_near
    if peers != 4:
        ends_far = swapped(line_ends, "gx", lambda i: (i - (2 if i % 2 else -2)) % peers)
    if riding:
        pieces = [own_coefs, far_coefs]
        pieces += [swapped(piece, "gx", lambda i: i ^ 1) for piece in pieces]
    else:
        pieces = [lax.all_gather(coefs, "gx")]
    (factors,) = call(
        functools.partial(factor_kernel, levels),
        "factors",
        [array(6 * levels + levels // 2 + 8, columns)],
        [],
        span_slot,
        *pieces,
    )
    (base,) = call(base_kernel, "base", [whole], [], here, hyper, total, masses)
    (result,) = call(
        functools.partial(third_kernel, levels),
        "third",
        [array(size_x, size_y, width)],
        [
            scratch(columns, width),
            scratch(8 * (levels + 1), columns),
            scratch((width // levels - 8) * (levels + 1), columns),
            scratch(levels, 8, columns),
            scratch(levels, 8, columns),
            scratch(size_x, size_y, width),
            pltpu.SemaphoreType.DMA((-(-width // 128),)),
        ]
        + [scratch(8, width)] * 4,
        hyper,
        base,
        masses,
        inner,
        factors,
        x_near,
        x_far,
        *last_x,
        ends_near,
        ends_far,
        out=pl.BlockSpec(memory_space=pltpu.HBM),
    )
    return result


def solution(mesh):
    placed = (
        P("gx", "gy", None),
        P(),
        P("gx", "gy"),
        P("gx", "gy"),
        P("gx", "gy"),
        P("gy", None, "gx"),
        P("gy", None, "gx"),
        P("gy", None, "gx"),
    )
    return jax.shard_map(
        local, mesh=mesh, in_specs=placed, out_specs=P("gx", "gy", None), check_vma=False
    )
```

```python
import functools

import jax
import jax.numpy as jnp
import numpy as np
from jax import lax
from jax.experimental import pallas as pl
from jax.experimental.pallas import tpu as pltpu
from jax.sharding import PartitionSpec as P

VMEM = pl.BlockSpec(memory_space=pltpu.VMEM)
LONG = pl.CostEstimate(flops=100_000_000_000, bytes_accessed=30_000_000, transcendentals=0)
PARAMS = pltpu.CompilerParams(vmem_limit_bytes=16 * 1024 * 1024)


def second_table():
    nodes = np.array([-1.0, -1.0 / np.sqrt(5.0), 1.0 / np.sqrt(5.0), 1.0])
    deriv = np.zeros((4, 4))
    for i in range(4):
        for j in range(4):
            if i == j:
                deriv[i, j] = sum(1.0 / (nodes[i] - nodes[k]) for k in range(4) if k != i)
            else:
                upper = np.prod([nodes[i] - nodes[k] for k in range(4) if k != i])
                lower = np.prod([nodes[j] - nodes[k] for k in range(4) if k != j])
                deriv[i, j] = upper / (lower * (nodes[i] - nodes[j]))
    return deriv @ deriv


def split(value):
    high = value.astype(jnp.bfloat16)
    return high, (value - high.astype(jnp.float32)).astype(jnp.bfloat16)


def product(left, right):
    left = jnp.concatenate([left[0], left[1], left[0]], axis=1)
    right = jnp.concatenate([right[0], right[0], right[1]], axis=0)
    return jnp.dot(left, right, preferred_element_type=jnp.float32)


def lookup(row, lane):
    second = second_table()
    row, lane = lax.rem(row, 4), lax.rem(lane, 4)
    result = jnp.zeros(row.shape, jnp.float32)
    for j in range(4):
        column = jnp.full(row.shape, float(second[3, j]), jnp.float32)
        for i in range(3):
            column = jnp.where(row == i, float(second[i, j]), column)
        result = jnp.where(lane == j, column, result)
    return result


def laplacian(size_x, size_y):
    count = size_x * size_y
    row, lane = (lax.broadcasted_iota(jnp.int32, (count, count), i) for i in range(2))
    row_x, lane_x = lax.div(row, size_y), lax.div(lane, size_y)
    row_y, lane_y = lax.rem(row, size_y), lax.rem(lane, size_y)
    same_x = (row_y == lane_y) & (lax.div(row_x, 4) == lax.div(lane_x, 4))
    same_y = (row_x == lane_x) & (lax.div(row_y, 4) == lax.div(lane_y, 4))
    along_x = jnp.where(same_x, lookup(row_x, lane_x), 0.0)
    return along_x + jnp.where(same_y, lookup(row_y, lane_y), 0.0)


def of_partner(values, size_y):
    count = values.shape[0]
    row_y = lax.rem(lax.broadcasted_iota(jnp.int32, values.shape, 0), size_y)
    phase = lax.rem(row_y, 4)
    before = jnp.where((phase == 0) & (row_y > 0), pltpu.roll(values, 1, 0), 0.0)
    after = (phase == 3) & (row_y < size_y - 1)
    return jnp.where(after, pltpu.roll(values, count - 1, 0), before)


def to_column(plane):
    size_x, size_y = plane.shape
    row = lax.broadcasted_iota(jnp.int32, (size_y, size_y), 0)
    lane = lax.broadcasted_iota(jnp.int32, (size_y, size_y), 1)
    parts = [
        jnp.sum(jnp.where(row == lane, plane[x : x + 1, :], 0.0), axis=1, keepdims=True)
        for x in range(size_x)
    ]
    return jnp.concatenate(parts, axis=0)


def even(axis):
    return lax.rem(lax.axis_index(axis), 2) == 0


def x_starts(count, size_y):
    near = jnp.where(even("gx"), count - size_y, 0)
    return near, count - size_y - near


def x_rows(count, size_y):
    starts = x_starts(count, size_y)
    return tuple(pl.ds(pl.multiple_of(start, size_y), size_y) for start in starts)


def add_packed(work, start, message, rows):
    def write(first, count, lanes, value):
        work[pl.ds(pl.multiple_of(start + first, 8), count), lanes] += value

    unpack(message, rows, work.shape[1], write)


def packed_rows(rows, width):
    return rows * (width // 128) + 8


def pack(value, message):
    rows, width = value.shape
    full, left = width // 128, width % 128
    for i in range(full):
        message[i * rows : (i + 1) * rows, :] = value[:, i * 128 : (i + 1) * 128]
    for i in range(rows // 8):
        lanes = slice(i * left, (i + 1) * left)
        message[full * rows : full * rows + 8, lanes] = value[i * 8 : (i + 1) * 8, full * 128 :]


def unpack(message, rows, width, write):
    full, left = width // 128, width % 128
    for i in range(full):
        write(0, rows, slice(i * 128, (i + 1) * 128), message[i * rows : (i + 1) * rows, :])
    for i in range(rows // 8):
        value = message[full * rows : full * rows + 8, i * left : (i + 1) * left]
        write(i * 8, 8, slice(full * 128, width), value)


def edge_rows(ref, y, size_x, size_y):
    return jnp.concatenate(
        [ref[x * size_y + y : x * size_y + y + 1, :] for x in range(size_x)], axis=0
    )


def start_kernel(
    state,
    mass,
    inverse,
    diff,
    fall,
    cloud,
    here,
    total,
    x_near,
    x_near_rest,
    x_far,
    low,
    high,
    operator,
    columns,
    coefs,
    mass_here,
    inverse_here,
    near_rows,
    sems,
):
    size_x, size_y, width = state.shape
    levels = diff.shape[1]
    pairs = [(mass, mass_here), (inverse, inverse_here)]
    pairs += [(state.at[x], here.at[x]) for x in range(size_x)]
    for i, source in enumerate((diff, fall, cloud)):
        pairs.append((source.at[0], coefs.at[i * levels : (i + 1) * levels]))
        start = near_rows.shape[0] + i * levels
        if x_far.shape[0] > start:
            pairs.append((source.at[0], x_far.at[start : start + levels]))
    copies = [
        pltpu.make_async_copy(source, target, sems.at[i])
        for i, (source, target) in enumerate(pairs)
    ]
    for copy in copies:
        copy.start()
    count = size_x * size_y
    matrix = laplacian(size_x, size_y)
    for copy in copies[:2]:
        copy.wait()
    own = jnp.broadcast_to(to_column(mass_here[...]), (count, count))
    matrix = own * matrix
    matrix = matrix + of_partner(matrix, size_y)
    operator[...] = matrix
    partner = of_partner(own, size_y)
    inverses = to_column(inverse_here[...])
    lane = lax.broadcasted_iota(jnp.int32, columns.shape, 1)
    columns[...] = jnp.where(lane == 0, own, jnp.where(lane == 1, inverses, partner))
    for copy in copies[2 : 2 + size_x]:
        copy.wait()
    total[...] = product(split(matrix), split(here[...].reshape(count, width)))
    near, far = x_rows(count, size_y)
    pack(total[near], near_rows)
    rest = x_near_rest.shape[0]
    x_near_rest[...] = near_rows[:rest, :]
    x_near[...] = near_rows[rest:, :]
    pack(total[far], x_far)
    for first, message in ((0, low), (size_y - 4, high)):
        for i in range(4):
            rows = slice(i * size_x, (i + 1) * size_x)
            message[rows, :width] = edge_rows(total, first + i, size_x, size_y)
            message[rows, width : width + 2] = edge_rows(columns, first + i, size_x, size_y)[:, :2]
    for copy in copies[2 + size_x :]:
        copy.wait()


def node_column(values, start, count):
    row = lax.broadcasted_iota(jnp.int32, (count, 1), 0)
    result = jnp.zeros((count, 1), jnp.float32)
    for i, value in enumerate(values):
        result = jnp.where(row == start + i, float(value), result)
    return result


def edge_weights(columns, message, size_x, size_y, width, edge, line):
    second = second_table()
    other = size_x - 1 - edge
    low = line == 3
    y, first = (0, 0) if low else (size_y - 1, size_y - 8)
    rows = slice(edge * size_y + first, edge * size_y + first + 8)
    here, there = (slice(x * size_y + y, x * size_y + y + 1) for x in (edge, other))
    mass, inverse = columns[here, 0:1], columns[here, 1:2]
    beyond = slice(line * size_x + edge, line * size_x + edge + 1)
    beyond_mass = message[beyond, width : width + 1]

    def beyond_inverse(i, x):
        return message[i * size_x + x : i * size_x + x + 1, width + 1 : width + 2]

    if low:
        own, partner = node_column(second[:, 0], 0, 8), node_column(second[3:, 0], 4, 8)
    else:
        own, partner = node_column(second[:, 3], 4, 8), node_column(second[:1, 3], 3, 8)
    along = inverse * (own * columns[rows, 0:1] + partner * columns[rows, 2:3])
    lane = lax.broadcasted_iota(jnp.int32, (8, 128), 1)
    place = lax.broadcasted_iota(jnp.int32, (8, 128), 0)
    tile = jnp.where(lane == line, along, 0.0)
    for i in range(4):
        value = float(second[line, i]) * beyond_mass * beyond_inverse(i, edge)
        if i == line:
            across = beyond_mass * beyond_inverse(line, edge) + mass * inverse
            value = value + float(second[edge, edge]) * across
        tile = tile + jnp.where((place == y - first) & (lane == i), value, 0.0)
    across = beyond_mass * beyond_inverse(line, other) + mass * columns[there, 1:2]
    value = float(second[edge, other]) * across
    return tile + jnp.where((place == y - first) & (lane == 4), value, 0.0)


def side_weights(columns, message, size_x, size_y, width, line):
    second = second_table()
    first, last = 0, size_x - 1
    tiles = [
        edge_weights(columns, message, size_x, size_y, width, edge, line) for edge in (first, last)
    ]
    mass = message[line * size_x : (line + 1) * size_x, width : width + 1]
    own = edge_rows(columns, 0 if line == 3 else size_y - 1, size_x, size_y)
    inner = []
    for edge in (first, last):
        inverse = message[line * size_x + edge : line * size_x + edge + 1, width + 1 : width + 2]
        across = mass * inverse + own[:, 0:1] * own[edge : edge + 1, 1:2]
        inner.append(node_column(second[:, edge], 0, size_x) * across)
    lane = lax.broadcasted_iota(jnp.int32, (size_x, 128), 1)
    from_last = jnp.where(even("gx"), 0, 1)
    return (
        jnp.where(even("gx"), tiles[1], tiles[0]),
        jnp.where(even("gx"), tiles[0], tiles[1]),
        jnp.where(lane == from_last, inner[1], inner[0]),
    )


def weights_kernel(size_x, size_y, width, columns, message, out):
    near, far, inner = side_weights(columns, message, size_x, size_y, width, 3)
    out[0:8, :] = near
    out[8:16, :] = far
    out[16 : 16 + size_x, :] = inner


def second_kernel(
    size_x,
    total,
    columns,
    operator,
    coefs,
    low_weights,
    low,
    from_far,
    from_near,
    from_near_rest,
    high,
    out,
    x_near,
    x_far,
    line_ends,
    inner,
    work,
    at_near,
    at_far,
    near_rows,
):
    size_y, width = total.shape[0] // size_x, total.shape[1]
    depth = size_y + 8
    second = second_table()
    near, far = x_starts(size_x * size_y, size_y)
    work[...] = total[...]
    rest = from_near_rest.shape[0]
    near_rows[:rest, :] = from_near_rest[...]
    near_rows[rest:, :] = from_near[...]
    add_packed(work, near, near_rows, size_y)
    add_packed(work, far, from_far, size_y)
    sides = ((low, 0, 3, 0), (high, size_y - 1, 0, size_y - 8))
    beyond = []
    for message, y, line, _ in sides:
        lines = [message[i * size_x : (i + 1) * size_x, :width] for i in range(4)]
        lines[line] = lines[line] + edge_rows(work, y, size_x, size_y)
        for x in range(size_x):
            work[x * size_y + y : x * size_y + y + 1, :] = lines[line][x : x + 1]
        for i in range(4):
            inverse = message[i * size_x : (i + 1) * size_x, width + 1 : width + 2]
            lines[i] = inverse * lines[i]
        value = sum(float(second[line, i]) * lines[i] for i in range(4))
        for x in range(size_x):
            value = value + node_column(second[:, x], 0, size_x) * lines[line][x : x + 1]
        mass = message[line * size_x : (line + 1) * size_x, width : width + 1]
        beyond.append(mass * value)
    out[...] = product(split(operator[...]), split(columns[:, 1:2] * work[...]))
    for (_, y, _, _), rows in zip(sides, beyond):
        for x in range(size_x):
            out[x * size_y + y : x * size_y + y + 1, :] += rows[x : x + 1]

    near, far = x_rows(size_x * size_y, size_y)
    at_near[:size_y, :] = out[near]
    at_far[:size_y, :] = out[far]
    last = depth * (width // 128)
    lanes = depth // 8 * (width % 128)
    high_weights = side_weights(columns, high, size_x, size_y, width, 0)
    for side, (message, _, line, _) in enumerate(sides):
        weights = high_weights if side else [low_weights[i : i + 8] for i in (0, 8, 16)]
        inner[side * size_x : (side + 1) * size_x, :] = weights[2][:size_x]
        place = slice(lanes + 8 * side, lanes + 8 * side + 5)
        x_near[last : last + 8, place] = weights[0][:, :5]
        x_far[last : last + 8, place] = weights[1][:, :5]
        for i in range(4):
            first, final = (
                message[i * size_x + x : i * size_x + x + 1, :width] for x in (0, size_x - 1)
            )
            row_near = jnp.where(even("gx"), final, first)
            row_far = jnp.where(even("gx"), first, final)
            place = size_y + 4 * side + i
            at_near[place : place + 1, :] = row_near
            at_far[place : place + 1, :] = row_far
            if i == line:
                line_ends[2 * side : 2 * side + 1, :] = row_far
                line_ends[2 * side + 1 : 2 * side + 2, :] = row_near
    pack(at_near[...], x_near)
    pack(at_far[...], x_far)
    if x_near.shape[0] > x_far.shape[0]:
        count = coefs.shape[0]
        start = last + 8
        x_near[start : start + count, :] = coefs[...]
        x_near[start + count :, :] = from_far[packed_rows(size_y, width) :, :]


def third_kernel(
    levels,
    hyper,
    base,
    masses,
    inner,
    factors,
    to_near,
    to_far,
    from_far,
    from_near,
    ends_near,
    ends_far,
    out,
    work,
    turned,
    turned_rest,
    values,
    values_rest,
    staged,
    sems,
    *beyond_rows,
):
    columns, width = base.shape
    size_x, size_y, _ = out.shape
    variables = width // levels
    rows = size_y + 8
    last, lanes = rows * (width // 128), rows // 8 * (width % 128)
    messages = (to_near, to_far, from_near, from_far)
    for message, target in zip(messages, beyond_rows):
        for i in range(width // 128):
            target[:, i * 128 : (i + 1) * 128] = message[i * rows + size_y : (i + 1) * rows, :]
        left = width % 128
        lanes_before = size_y // 8 * left
        target[:, width - left :] = message[last : last + 8, lanes_before : lanes_before + left]
    at_near, at_far, over_near, over_far = beyond_rows
    near, far = x_starts(columns, size_y)
    sides = ((0, 0, 3, 0), (1, size_y - 1, 0, size_y - 8))
    partners = (
        (near, at_near, over_near, over_far, ends_near),
        (far, at_far, over_far, over_near, ends_far),
    )
    for x in range(1, size_x - 1):
        for first in (0, size_y - 8):
            work[x * size_y + first : x * size_y + first + 8, :] = jnp.zeros((8, width), jnp.float32)
    for start, message in ((near, from_near), (far, from_far)):
        for i in range(width // 128):
            place = pl.ds(pl.multiple_of(start, size_y), size_y)
            work[place, i * 128 : (i + 1) * 128] = message[i * rows : i * rows + size_y, :]
        for i in range(size_y // 8):
            place = pl.ds(pl.multiple_of(start + i * 8, 8), 8)
            left = width % 128
            work[place, width - left :] = message[last : last + 8, i * left : (i + 1) * left]
    for side, y, line, first in sides:
        place = 4 * side
        weights = [
            message[last : last + 8, lanes + 8 * side : lanes + 8 * side + 5] for message in messages
        ]
        for which, (start, mine, theirs, others, ends) in enumerate(partners):
            own, beyond = weights[which], weights[2 + which]
            terms = [
                (weight[:, i : i + 1], values, place + i)
                for i in range(4)
                for weight, values in ((own, theirs), (beyond, mine))
            ]
            terms += [(own[:, 4:5], others, place + line), (beyond[:, 4:5], ends, 2 * side + which)]
            added = sum(weight * values[row : row + 1, :width] for weight, values, row in terms)
            work[pl.ds(pl.multiple_of(start + first, 8), 8), :] += added
        for x in range(1, size_x - 1):
            row, weight = x * size_y + y, side * size_x + x
            work[row : row + 1, :] += (
                inner[weight : weight + 1, 0:1] * over_near[place + line : place + line + 1, :]
                + inner[weight : weight + 1, 1:2] * over_far[place + line : place + line + 1, :]
            )
    for start in (near, far):
        place = pl.ds(pl.multiple_of(start, size_y), size_y)
        work[place, :] = base[place, :] - hyper[...] * (masses[place, 1:2] * work[place, :])
    for x in range(1, size_x - 1):
        for first in (0, size_y - 8):
            rows = slice(x * size_y + first, x * size_y + first + 8)
            work[rows, :] = base[rows, :] - hyper[...] * (masses[rows, 1:2] * work[rows, :])
        rows = slice(x * size_y + 8, (x + 1) * size_y - 8)
        work[rows, :] = base[rows, :]
    pitch, half = levels + 1, levels // 2
    scale, carry, gain, keep, flow, cloud = (
        factors.at[i * levels : (i + 1) * levels] for i in range(6)
    )
    groups = [(first, min(8, variables - first)) for first in range(0, variables, 8)]
    buffers = list(zip(groups, (turned, turned_rest), (values, values_rest)))

    def turn(group, turned):
        first, count = group
        start, stop = first * levels, (first + count) * levels
        tile = start // 128 * 128
        rows = work[:, tile:stop].T
        for i in range(count):
            row = start - tile + i * levels
            turned[i * pitch : i * pitch + levels, :] = rows[row : row + levels]

    def forward(group, turned, values):
        count = group[1]
        known = [jnp.zeros((count, columns), jnp.float32)] * 2
        for i in range(half):
            for side, k in enumerate((i, levels - 1 - i)):
                scaled = turned[pl.ds(k, count, stride=pitch), :] * scale[k : k + 1, :]
                known[side] = scaled + carry[k : k + 1, :] * known[side]
                values[k, :count, :] = known[side]
        return known

    def back(group, turned, values, known):
        count = group[1]
        meet = factors[6 * levels + half : 6 * levels + half + 1, :]
        first = (known[0] + gain[half - 1 : half, :] * known[1]) * meet
        solved = [first, known[1] + gain[half : half + 1, :] * first]
        for i in reversed(range(half)):
            for side, k in enumerate((i, levels - 1 - i)):
                if i < half - 1:
                    solved[side] = values[k, :count, :] + gain[k : k + 1, :] * solved[side]
                turned[pl.ds(k, count, stride=pitch), :] = solved[side]

    def leave(i):
        lanes = slice(i * 128, min((i + 1) * 128, width))
        parts = []
        for (start, count), source, _ in buffers:
            for j in range(start, start + count):
                first, last = max(lanes.start, j * levels), min(lanes.stop, (j + 1) * levels)
                if first < last:
                    offset = (j - start) * pitch - j * levels
                    parts.append(source[first + offset : last + offset, :])
        rows = jnp.concatenate(parts, axis=0)
        staged[:, :, lanes] = rows.T.reshape(size_x, size_y, -1)
        copy = pltpu.make_async_copy(staged.at[:, :, lanes], out.at[:, :, lanes], sems.at[i])
        copy.start()
        return copy

    (main, main_turned, main_values), (rest, rest_turned, rest_values) = buffers
    turn(main, main_turned)
    main_known = forward(main, main_turned, main_values)
    turn(rest, rest_turned)
    rest_known = forward(rest, rest_turned, rest_values)
    back(main, main_turned, main_values, main_known)
    tiles = -(-width // 128)
    settled_tiles = -(-3 * levels // 128)
    back(rest, rest_turned, rest_values, rest_known)
    copies = [leave(i) for i in range(settled_tiles, tiles)]
    heat, vapour, liquid = (turned.at[i * pitch : i * pitch + levels] for i in range(3))
    condensed = cloud[...] * 0.5 * jnp.maximum(vapour[...] - 0.3 * heat[...], 0.0)
    vapour[...] = vapour[...] - condensed
    heat[...] = heat[...] + 2.0 * condensed
    liquid[...] = (liquid[...] + condensed) * keep[...]
    settled = [jnp.zeros((1, columns), jnp.float32)] * 2
    for i in range(half):
        for side, k in enumerate((i, half + i)):
            settled[side] = liquid[k : k + 1, :] + flow[k : k + 1, :] * settled[side]
            liquid[k : k + 1, :] = settled[side]
    through = factors[6 * levels : 6 * levels + half, :]
    liquid[half:, :] = liquid[half:, :] + through * settled[0]
    copies += [leave(i) for i in range(settled_tiles)]
    for copy in copies:
        copy.wait()


def base_kernel(state, hyper, total, masses, base):
    columns, width = total.shape
    twice = masses[:, 1:2] * total[...]
    base[...] = state[...].reshape(columns, width) - hyper[...] * twice


def pick(slots, pieces):
    size_x, size_y = slots.shape
    columns = size_x * size_y
    wanted = jnp.concatenate([slots[x : x + 1, :] for x in range(size_x)], axis=1)
    picked = 0.0
    for owner, rest in pieces:
        span = rest.shape[1]
        entry = lax.broadcasted_iota(jnp.int32, (span, columns), 0) + owner * span
        choice = (entry == wanted).astype(jnp.float32).astype(jnp.bfloat16)
        for _ in range(3):
            part = rest.astype(jnp.bfloat16)
            rest = rest - part.astype(jnp.float32)
            picked = picked + jnp.dot(part, choice, preferred_element_type=jnp.float32)
    return picked


def factor_kernel(levels, slots, *refs):
    factors = refs[-1]
    if len(refs) == 3:
        here = lax.axis_index("gx")
        pieces = []
        for message, owner in zip(refs, (here, here ^ 1)):
            start = message.shape[0] - 6 * levels
            pieces.append((owner, message[start : start + 3 * levels, :]))
            pieces.append((owner ^ 3, message[start + 3 * levels :, :]))
    else:
        pieces = [(peer, refs[0][peer]) for peer in range(refs[0].shape[0])]
    columns = factors.shape[1]
    picked = pick(slots, pieces)
    mixing, falling, covered = (picked[i * levels : (i + 1) * levels] for i in range(3))
    scale, carry, gain, keep, flow, cover = (
        factors.at[i * levels : (i + 1) * levels] for i in range(6)
    )
    zero = jnp.zeros((1, columns), jnp.float32)
    kept = 1.0 / (1.0 + falling)
    keep[...] = kept
    flow[:1, :] = zero
    flow[1:, :] = falling[:-1] * kept[1:]
    cover[...] = covered
    half = levels // 2
    gains = [zero, zero]
    through = jnp.ones((1, columns), jnp.float32)
    for i in range(half):
        for side, k in enumerate((i, levels - 1 - i)):
            above = mixing[k : k + 1] if k else zero
            below = mixing[k + 1 : k + 2] if k + 1 < levels else zero
            centre = 1.0 + above + (below if k + 1 < levels else mixing[:1])
            behind, ahead = (above, below) if side == 0 else (below, above)
            inverse = 1.0 / (centre - behind * gains[side])
            gains[side] = ahead * inverse
            scale[k : k + 1, :] = inverse
            carry[k : k + 1, :] = behind * inverse
            gain[k : k + 1, :] = gains[side]
        k = half + i
        through = through * falling[k - 1 : k] * kept[k : k + 1]
        factors[6 * levels + i : 6 * levels + i + 1, :] = through
    last = 6 * levels + half
    factors[last : last + 1, :] = 1.0 / (1.0 - gains[0] * gains[1])


def swapped(value, axis, partner):
    return lax.ppermute(value, axis, [(i, partner(i)) for i in range(lax.axis_size(axis))])


def exchanged(near, far, axis):
    size = lax.axis_size(axis)
    from_far = swapped(far, axis, lambda i: (i + (1 if i % 2 else -1)) % size)
    from_near = swapped(near, axis, lambda i: i ^ 1)
    return from_far, from_near


def shifted(value, axis, step):
    size = lax.axis_size(axis)
    return lax.ppermute(value, axis, [(i, (i + step) % size) for i in range(size)])


def local(
    model_state, hyper_coef, point_mass, inverse_mass, span_slot, vert_diff, fall_rate, cloud_frac
):
    size_x, size_y, width = model_state.shape
    levels, span = vert_diff.shape[1:]
    columns = size_x * size_y
    hyper = hyper_coef.reshape(1, width)
    padded = -(-(width + 5) // 128) * 128

    def array(*shape):
        return jax.ShapeDtypeStruct(shape, jnp.float32)

    def scratch(*shape):
        return pltpu.VMEM(shape, jnp.float32)

    def call(kernel, name, outs, scratches, *operands, spec=VMEM, out=VMEM, cost=None):
        return pl.pallas_call(
            kernel,
            out_shape=outs,
            in_specs=[spec] * len(operands),
            out_specs=[out] * len(outs),
            scratch_shapes=scratches,
            compiler_params=PARAMS,
            cost_estimate=cost,
            name=name,
        )(*operands)

    riding = lax.axis_size("gx") == 4
    whole = array(columns, width)
    edge = array(4 * size_x, padded)
    extra = 3 * levels if riding else 0
    rest = width // 256 * size_y
    first_rows, last_rows = packed_rows(size_y, width), packed_rows(size_y + 8, width)
    here, total, x_near, x_near_rest, x_far, y_low, y_high, operator, masses, coefs = call(
        start_kernel,
        "start",
        [
            array(size_x, size_y, width),
            whole,
            array(first_rows - rest, 128),
            array(rest, 128),
            array(first_rows + extra, 128),
            edge,
            edge,
            array(columns, columns),
            array(columns, 128),
            array(3 * levels, span),
        ],
        [
            scratch(size_x, size_y),
            scratch(size_x, size_y),
            scratch(first_rows, 128),
            pltpu.SemaphoreType.DMA((size_x + 8,)),
        ],
        *(
            pltpu.with_memory_space_constraint(value, pltpu.HBM)
            for value in (
                model_state,
                point_mass,
                inverse_mass,
                vert_diff,
                fall_rate,
                cloud_frac,
            )
        ),
        spec=pl.BlockSpec(memory_space=pltpu.HBM),
    )
    low = shifted(y_high, "gy", 1)
    from_far, from_near = exchanged(x_near, x_far, "gx")
    from_near_rest = swapped(x_near_rest, "gx", lambda i: i ^ 1)
    high = shifted(y_low, "gy", -1)
    (low_weights,) = call(
        functools.partial(weights_kernel, size_x, size_y, width),
        "weights",
        [array(24, 128)],
        [],
        masses,
        low,
        cost=LONG,
    )
    total, x_near, x_far, line_ends, inner = call(
        functools.partial(second_kernel, size_x),
        "second",
        [
            whole,
            array(last_rows + 2 * extra, 128),
            array(last_rows, 128),
            array(4, width),
            array(2 * size_x, 128),
        ],
        [
            scratch(columns, width),
            scratch(size_y + 8, width),
            scratch(size_y + 8, width),
            scratch(first_rows, 128),
        ],
        total,
        masses,
        operator,
        coefs,
        low_weights,
        low,
        from_far,
        from_near,
        from_near_rest,
        high,
    )
    last_x = exchanged(x_near, x_far, "gx")
    peers = lax.axis_size("gx")
    ends_near = swapped(line_ends, "gx", lambda i: (i + (2 if i % 2 else -2)) % peers)
    ends_far = ends_near
    if peers != 4:
        ends_far = swapped(line_ends, "gx", lambda i: (i - (2 if i % 2 else -2)) % peers)
    if riding:
        pieces = [x_near, last_x[1]]
    else:
        pieces = [lax.all_gather(coefs, "gx")]
    (factors,) = call(
        functools.partial(factor_kernel, levels),
        "factors",
        [array(6 * levels + levels // 2 + 8, columns)],
        [],
        span_slot,
        *pieces,
    )
    (base,) = call(base_kernel, "base", [whole], [], here, hyper, total, masses)
    (result,) = call(
        functools.partial(third_kernel, levels),
        "third",
        [array(size_x, size_y, width)],
        [
            scratch(columns, width),
            scratch(8 * (levels + 1), columns),
            scratch((width // levels - 8) * (levels + 1), columns),
            scratch(levels, 8, columns),
            scratch(levels, 8, columns),
            scratch(size_x, size_y, width),
            pltpu.SemaphoreType.DMA((-(-width // 128),)),
        ]
        + [scratch(8, width)] * 4,
        hyper,
        base,
        masses,
        inner,
        factors,
        x_near,
        x_far,
        *last_x,
        ends_near,
        ends_far,
        out=pl.BlockSpec(memory_space=pltpu.HBM),
    )
    return result


def solution(mesh):
    placed = (
        P("gx", "gy", None),
        P(),
        P("gx", "gy"),
        P("gx", "gy"),
        P("gx", "gy"),
        P("gy", None, "gx"),
        P("gy", None, "gx"),
        P("gy", None, "gx"),
    )
    return jax.shard_map(
        local, mesh=mesh, in_specs=placed, out_specs=P("gx", "gy", None), check_vma=False
    )
```

```python
import functools

import jax
import jax.numpy as jnp
import numpy as np
from jax import lax
from jax.experimental import pallas as pl
from jax.experimental.pallas import tpu as pltpu
from jax.sharding import PartitionSpec as P

VMEM = pl.BlockSpec(memory_space=pltpu.VMEM)
LONG = pl.CostEstimate(flops=100_000_000_000, bytes_accessed=30_000_000, transcendentals=0)
PARAMS = pltpu.CompilerParams(vmem_limit_bytes=16 * 1024 * 1024)


def second_table():
    nodes = np.array([-1.0, -1.0 / np.sqrt(5.0), 1.0 / np.sqrt(5.0), 1.0])
    deriv = np.zeros((4, 4))
    for i in range(4):
        for j in range(4):
            if i == j:
                deriv[i, j] = sum(1.0 / (nodes[i] - nodes[k]) for k in range(4) if k != i)
            else:
                upper = np.prod([nodes[i] - nodes[k] for k in range(4) if k != i])
                lower = np.prod([nodes[j] - nodes[k] for k in range(4) if k != j])
                deriv[i, j] = upper / (lower * (nodes[i] - nodes[j]))
    return deriv @ deriv


def split(value):
    high = value.astype(jnp.bfloat16)
    return high, (value - high.astype(jnp.float32)).astype(jnp.bfloat16)


def product(left, right):
    left = jnp.concatenate([left[0], left[1], left[0]], axis=1)
    right = jnp.concatenate([right[0], right[0], right[1]], axis=0)
    return jnp.dot(left, right, preferred_element_type=jnp.float32)


def lookup(row, lane):
    second = second_table()
    row, lane = lax.rem(row, 4), lax.rem(lane, 4)
    result = jnp.zeros(row.shape, jnp.float32)
    for j in range(4):
        column = jnp.full(row.shape, float(second[3, j]), jnp.float32)
        for i in range(3):
            column = jnp.where(row == i, float(second[i, j]), column)
        result = jnp.where(lane == j, column, result)
    return result


def laplacian(size_x, size_y):
    count = size_x * size_y
    row, lane = (lax.broadcasted_iota(jnp.int32, (count, count), i) for i in range(2))
    row_x, lane_x = lax.div(row, size_y), lax.div(lane, size_y)
    row_y, lane_y = lax.rem(row, size_y), lax.rem(lane, size_y)
    same_x = (row_y == lane_y) & (lax.div(row_x, 4) == lax.div(lane_x, 4))
    same_y = (row_x == lane_x) & (lax.div(row_y, 4) == lax.div(lane_y, 4))
    along_x = jnp.where(same_x, lookup(row_x, lane_x), 0.0)
    return along_x + jnp.where(same_y, lookup(row_y, lane_y), 0.0)


def of_partner(values, size_y):
    count = values.shape[0]
    row_y = lax.rem(lax.broadcasted_iota(jnp.int32, values.shape, 0), size_y)
    phase = lax.rem(row_y, 4)
    before = jnp.where((phase == 0) & (row_y > 0), pltpu.roll(values, 1, 0), 0.0)
    after = (phase == 3) & (row_y < size_y - 1)
    return jnp.where(after, pltpu.roll(values, count - 1, 0), before)


def to_column(plane):
    size_x, size_y = plane.shape
    row = lax.broadcasted_iota(jnp.int32, (size_y, size_y), 0)
    lane = lax.broadcasted_iota(jnp.int32, (size_y, size_y), 1)
    parts = [
        jnp.sum(jnp.where(row == lane, plane[x : x + 1, :], 0.0), axis=1, keepdims=True)
        for x in range(size_x)
    ]
    return jnp.concatenate(parts, axis=0)


def even(axis):
    return lax.rem(lax.axis_index(axis), 2) == 0


def x_starts(count, size_y):
    near = jnp.where(even("gx"), count - size_y, 0)
    return near, count - size_y - near


def x_rows(count, size_y):
    starts = x_starts(count, size_y)
    return tuple(pl.ds(pl.multiple_of(start, size_y), size_y) for start in starts)


def add_packed(work, start, message, rows):
    def write(first, count, lanes, value):
        work[pl.ds(pl.multiple_of(start + first, 8), count), lanes] += value

    unpack(message, rows, work.shape[1], write)


def packed_rows(rows, width):
    return rows * (width // 128) + 8


def pack(value, message):
    rows, width = value.shape
    full, left = width // 128, width % 128
    for i in range(full):
        message[i * rows : (i + 1) * rows, :] = value[:, i * 128 : (i + 1) * 128]
    for i in range(rows // 8):
        lanes = slice(i * left, (i + 1) * left)
        message[full * rows : full * rows + 8, lanes] = value[i * 8 : (i + 1) * 8, full * 128 :]


def unpack(message, rows, width, write):
    full, left = width // 128, width % 128
    for i in range(full):
        write(0, rows, slice(i * 128, (i + 1) * 128), message[i * rows : (i + 1) * rows, :])
    for i in range(rows // 8):
        value = message[full * rows : full * rows + 8, i * left : (i + 1) * left]
        write(i * 8, 8, slice(full * 128, width), value)


def edge_rows(ref, y, size_x, size_y):
    return jnp.concatenate(
        [ref[x * size_y + y : x * size_y + y + 1, :] for x in range(size_x)], axis=0
    )


def start_kernel(
    state,
    mass,
    inverse,
    diff,
    fall,
    cloud,
    here,
    total,
    x_near,
    x_near_rest,
    x_far,
    low,
    high,
    operator,
    columns,
    coefs,
    mass_here,
    inverse_here,
    near_rows,
    sems,
):
    size_x, size_y, width = state.shape
    levels = diff.shape[1]
    pairs = [(mass, mass_here), (inverse, inverse_here)]
    pairs.append((state, here))
    for i, source in enumerate((diff, fall, cloud)):
        pairs.append((source.at[0], coefs.at[i * levels : (i + 1) * levels]))
    copies = [
        pltpu.make_async_copy(source, target, sems.at[i])
        for i, (source, target) in enumerate(pairs)
    ]
    for copy in copies:
        copy.start()
    count = size_x * size_y
    matrix = laplacian(size_x, size_y)
    for copy in copies[:2]:
        copy.wait()
    own = jnp.broadcast_to(to_column(mass_here[...]), (count, count))
    matrix = own * matrix
    matrix = matrix + of_partner(matrix, size_y)
    operator[...] = matrix
    partner = of_partner(own, size_y)
    inverses = to_column(inverse_here[...])
    lane = lax.broadcasted_iota(jnp.int32, columns.shape, 1)
    columns[...] = jnp.where(lane == 0, own, jnp.where(lane == 1, inverses, partner))
    copies[2].wait()
    total[...] = product(split(matrix), split(here[...].reshape(count, width)))
    near, far = x_rows(count, size_y)
    pack(total[near], near_rows)
    rest = x_near_rest.shape[0]
    x_near_rest[...] = near_rows[:rest, :]
    x_near[...] = near_rows[rest:, :]
    pack(total[far], x_far)
    for first, message in ((0, low), (size_y - 4, high)):
        for i in range(4):
            rows = slice(i * size_x, (i + 1) * size_x)
            message[rows, :width] = edge_rows(total, first + i, size_x, size_y)
            message[rows, width : width + 2] = edge_rows(columns, first + i, size_x, size_y)[:, :2]
    for copy in copies[3:]:
        copy.wait()
    if x_far.shape[0] > near_rows.shape[0]:
        x_far[near_rows.shape[0] :, :] = coefs[...]


def node_column(values, start, count):
    row = lax.broadcasted_iota(jnp.int32, (count, 1), 0)
    result = jnp.zeros((count, 1), jnp.float32)
    for i, value in enumerate(values):
        result = jnp.where(row == start + i, float(value), result)
    return result


def edge_weights(columns, message, size_x, size_y, width, edge, line):
    second = second_table()
    other = size_x - 1 - edge
    low = line == 3
    y, first = (0, 0) if low else (size_y - 1, size_y - 8)
    rows = slice(edge * size_y + first, edge * size_y + first + 8)
    here, there = (slice(x * size_y + y, x * size_y + y + 1) for x in (edge, other))
    mass, inverse = columns[here, 0:1], columns[here, 1:2]
    beyond = slice(line * size_x + edge, line * size_x + edge + 1)
    beyond_mass = message[beyond, width : width + 1]

    def beyond_inverse(i, x):
        return message[i * size_x + x : i * size_x + x + 1, width + 1 : width + 2]

    if low:
        own, partner = node_column(second[:, 0], 0, 8), node_column(second[3:, 0], 4, 8)
    else:
        own, partner = node_column(second[:, 3], 4, 8), node_column(second[:1, 3], 3, 8)
    along = inverse * (own * columns[rows, 0:1] + partner * columns[rows, 2:3])
    lane = lax.broadcasted_iota(jnp.int32, (8, 128), 1)
    place = lax.broadcasted_iota(jnp.int32, (8, 128), 0)
    tile = jnp.where(lane == line, along, 0.0)
    for i in range(4):
        value = float(second[line, i]) * beyond_mass * beyond_inverse(i, edge)
        if i == line:
            across = beyond_mass * beyond_inverse(line, edge) + mass * inverse
            value = value + float(second[edge, edge]) * across
        tile = tile + jnp.where((place == y - first) & (lane == i), value, 0.0)
    across = beyond_mass * beyond_inverse(line, other) + mass * columns[there, 1:2]
    value = float(second[edge, other]) * across
    return tile + jnp.where((place == y - first) & (lane == 4), value, 0.0)


def side_weights(columns, message, size_x, size_y, width, line):
    second = second_table()
    first, last = 0, size_x - 1
    tiles = [
        edge_weights(columns, message, size_x, size_y, width, edge, line) for edge in (first, last)
    ]
    mass = message[line * size_x : (line + 1) * size_x, width : width + 1]
    own = edge_rows(columns, 0 if line == 3 else size_y - 1, size_x, size_y)
    inner = []
    for edge in (first, last):
        inverse = message[line * size_x + edge : line * size_x + edge + 1, width + 1 : width + 2]
        across = mass * inverse + own[:, 0:1] * own[edge : edge + 1, 1:2]
        inner.append(node_column(second[:, edge], 0, size_x) * across)
    lane = lax.broadcasted_iota(jnp.int32, (size_x, 128), 1)
    from_last = jnp.where(even("gx"), 0, 1)
    return (
        jnp.where(even("gx"), tiles[1], tiles[0]),
        jnp.where(even("gx"), tiles[0], tiles[1]),
        jnp.where(lane == from_last, inner[1], inner[0]),
    )


def weights_kernel(size_x, size_y, width, columns, message, out):
    near, far, inner = side_weights(columns, message, size_x, size_y, width, 3)
    out[0:8, :] = near
    out[8:16, :] = far
    out[16 : 16 + size_x, :] = inner


def second_kernel(
    size_x,
    total,
    columns,
    operator,
    coefs,
    low_weights,
    low,
    from_far,
    from_near,
    from_near_rest,
    high,
    out,
    x_near,
    x_far,
    line_ends,
    inner,
    work,
    at_near,
    at_far,
    near_rows,
):
    size_y, width = total.shape[0] // size_x, total.shape[1]
    depth = size_y + 8
    second = second_table()
    near, far = x_starts(size_x * size_y, size_y)
    work[...] = total[...]
    rest = from_near_rest.shape[0]
    near_rows[:rest, :] = from_near_rest[...]
    near_rows[rest:, :] = from_near[...]
    add_packed(work, near, near_rows, size_y)
    add_packed(work, far, from_far, size_y)
    sides = ((low, 0, 3, 0), (high, size_y - 1, 0, size_y - 8))
    beyond = []
    for message, y, line, _ in sides:
        lines = [message[i * size_x : (i + 1) * size_x, :width] for i in range(4)]
        lines[line] = lines[line] + edge_rows(work, y, size_x, size_y)
        for x in range(size_x):
            work[x * size_y + y : x * size_y + y + 1, :] = lines[line][x : x + 1]
        for i in range(4):
            inverse = message[i * size_x : (i + 1) * size_x, width + 1 : width + 2]
            lines[i] = inverse * lines[i]
        value = sum(float(second[line, i]) * lines[i] for i in range(4))
        for x in range(size_x):
            value = value + node_column(second[:, x], 0, size_x) * lines[line][x : x + 1]
        mass = message[line * size_x : (line + 1) * size_x, width : width + 1]
        beyond.append(mass * value)
    out[...] = product(split(operator[...]), split(columns[:, 1:2] * work[...]))
    for (_, y, _, _), rows in zip(sides, beyond):
        for x in range(size_x):
            out[x * size_y + y : x * size_y + y + 1, :] += rows[x : x + 1]

    near, far = x_rows(size_x * size_y, size_y)
    at_near[:size_y, :] = out[near]
    at_far[:size_y, :] = out[far]
    last = depth * (width // 128)
    lanes = depth // 8 * (width % 128)
    high_weights = side_weights(columns, high, size_x, size_y, width, 0)
    for side, (message, _, line, _) in enumerate(sides):
        weights = high_weights if side else [low_weights[i : i + 8] for i in (0, 8, 16)]
        inner[side * size_x : (side + 1) * size_x, :] = weights[2][:size_x]
        place = slice(lanes + 8 * side, lanes + 8 * side + 5)
        x_near[last : last + 8, place] = weights[0][:, :5]
        x_far[last : last + 8, place] = weights[1][:, :5]
        for i in range(4):
            first, final = (
                message[i * size_x + x : i * size_x + x + 1, :width] for x in (0, size_x - 1)
            )
            row_near = jnp.where(even("gx"), final, first)
            row_far = jnp.where(even("gx"), first, final)
            place = size_y + 4 * side + i
            at_near[place : place + 1, :] = row_near
            at_far[place : place + 1, :] = row_far
            if i == line:
                line_ends[2 * side : 2 * side + 1, :] = row_far
                line_ends[2 * side + 1 : 2 * side + 2, :] = row_near
    pack(at_near[...], x_near)
    pack(at_far[...], x_far)
    if x_near.shape[0] > x_far.shape[0]:
        count = coefs.shape[0]
        start = last + 8
        x_near[start : start + count, :] = coefs[...]
        x_near[start + count :, :] = from_far[packed_rows(size_y, width) :, :]


def third_kernel(
    levels,
    hyper,
    base,
    masses,
    inner,
    factors,
    to_near,
    to_far,
    from_far,
    from_near,
    ends_near,
    ends_far,
    out,
    work,
    turned,
    turned_rest,
    values,
    values_rest,
    staged,
    sems,
    *beyond_rows,
):
    columns, width = base.shape
    size_x, size_y, _ = out.shape
    variables = width // levels
    rows = size_y + 8
    last, lanes = rows * (width // 128), rows // 8 * (width % 128)
    messages = (to_near, to_far, from_near, from_far)
    for message, target in zip(messages, beyond_rows):
        for i in range(width // 128):
            target[:, i * 128 : (i + 1) * 128] = message[i * rows + size_y : (i + 1) * rows, :]
        left = width % 128
        lanes_before = size_y // 8 * left
        target[:, width - left :] = message[last : last + 8, lanes_before : lanes_before + left]
    at_near, at_far, over_near, over_far = beyond_rows
    near, far = x_starts(columns, size_y)
    sides = ((0, 0, 3, 0), (1, size_y - 1, 0, size_y - 8))
    partners = (
        (near, at_near, over_near, over_far, ends_near),
        (far, at_far, over_far, over_near, ends_far),
    )
    for x in range(1, size_x - 1):
        for first in (0, size_y - 8):
            work[x * size_y + first : x * size_y + first + 8, :] = jnp.zeros((8, width), jnp.float32)
    for start, message in ((near, from_near), (far, from_far)):
        for i in range(width // 128):
            place = pl.ds(pl.multiple_of(start, size_y), size_y)
            work[place, i * 128 : (i + 1) * 128] = message[i * rows : i * rows + size_y, :]
        for i in range(size_y // 8):
            place = pl.ds(pl.multiple_of(start + i * 8, 8), 8)
            left = width % 128
            work[place, width - left :] = message[last : last + 8, i * left : (i + 1) * left]
    for side, y, line, first in sides:
        place = 4 * side
        weights = [
            message[last : last + 8, lanes + 8 * side : lanes + 8 * side + 5] for message in messages
        ]
        for which, (start, mine, theirs, others, ends) in enumerate(partners):
            own, beyond = weights[which], weights[2 + which]
            terms = [
                (weight[:, i : i + 1], values, place + i)
                for i in range(4)
                for weight, values in ((own, theirs), (beyond, mine))
            ]
            terms += [(own[:, 4:5], others, place + line), (beyond[:, 4:5], ends, 2 * side + which)]
            added = sum(weight * values[row : row + 1, :width] for weight, values, row in terms)
            work[pl.ds(pl.multiple_of(start + first, 8), 8), :] += added
        for x in range(1, size_x - 1):
            row, weight = x * size_y + y, side * size_x + x
            work[row : row + 1, :] += (
                inner[weight : weight + 1, 0:1] * over_near[place + line : place + line + 1, :]
                + inner[weight : weight + 1, 1:2] * over_far[place + line : place + line + 1, :]
            )
    for start in (near, far):
        place = pl.ds(pl.multiple_of(start, size_y), size_y)
        work[place, :] = base[place, :] - hyper[...] * (masses[place, 1:2] * work[place, :])
    for x in range(1, size_x - 1):
        for first in (0, size_y - 8):
            rows = slice(x * size_y + first, x * size_y + first + 8)
            work[rows, :] = base[rows, :] - hyper[...] * (masses[rows, 1:2] * work[rows, :])
        rows = slice(x * size_y + 8, (x + 1) * size_y - 8)
        work[rows, :] = base[rows, :]
    pitch, half = levels + 1, levels // 2
    scale, carry, gain, keep, flow, cloud = (
        factors.at[i * levels : (i + 1) * levels] for i in range(6)
    )
    groups = [(first, min(8, variables - first)) for first in range(0, variables, 8)]
    buffers = list(zip(groups, (turned, turned_rest), (values, values_rest)))

    def turn(group, turned):
        first, count = group
        start, stop = first * levels, (first + count) * levels
        tile = start // 128 * 128
        rows = work[:, tile:stop].T
        for i in range(count):
            row = start - tile + i * levels
            turned[i * pitch : i * pitch + levels, :] = rows[row : row + levels]

    def forward(group, turned, values):
        count = group[1]
        known = [jnp.zeros((count, columns), jnp.float32)] * 2
        for i in range(half):
            for side, k in enumerate((i, levels - 1 - i)):
                scaled = turned[pl.ds(k, count, stride=pitch), :] * scale[k : k + 1, :]
                known[side] = scaled + carry[k : k + 1, :] * known[side]
                values[k, :count, :] = known[side]
        return known

    def back(group, turned, values, known):
        count = group[1]
        meet = factors[6 * levels + half : 6 * levels + half + 1, :]
        first = (known[0] + gain[half - 1 : half, :] * known[1]) * meet
        solved = [first, known[1] + gain[half : half + 1, :] * first]
        for i in reversed(range(half)):
            for side, k in enumerate((i, levels - 1 - i)):
                if i < half - 1:
                    solved[side] = values[k, :count, :] + gain[k : k + 1, :] * solved[side]
                turned[pl.ds(k, count, stride=pitch), :] = solved[side]

    def place(i):
        lanes = slice(i * 128, min((i + 1) * 128, width))
        parts = []
        for (start, count), source, _ in buffers:
            for j in range(start, start + count):
                first, last = max(lanes.start, j * levels), min(lanes.stop, (j + 1) * levels)
                if first < last:
                    offset = (j - start) * pitch - j * levels
                    parts.append(source[first + offset : last + offset, :])
        rows = jnp.concatenate(parts, axis=0)
        staged[:, :, lanes] = rows.T.reshape(size_x, size_y, -1)

    def leave(which, first, last):
        for i in range(first, last):
            place(i)
        lanes = slice(first * 128, min(last * 128, width))
        copy = pltpu.make_async_copy(staged.at[:, :, lanes], out.at[:, :, lanes], sems.at[which])
        copy.start()
        return copy

    (main, main_turned, main_values), (rest, rest_turned, rest_values) = buffers
    turn(main, main_turned)
    main_known = forward(main, main_turned, main_values)
    turn(rest, rest_turned)
    rest_known = forward(rest, rest_turned, rest_values)
    back(main, main_turned, main_values, main_known)
    tiles = -(-width // 128)
    settled_tiles, main_tiles = -(-3 * levels // 128), main[1] * levels // 128
    copies = [leave(0, settled_tiles, main_tiles)]
    heat, vapour, liquid = (turned.at[i * pitch : i * pitch + levels] for i in range(3))
    condensed = cloud[...] * 0.5 * jnp.maximum(vapour[...] - 0.3 * heat[...], 0.0)
    vapour[...] = vapour[...] - condensed
    heat[...] = heat[...] + 2.0 * condensed
    liquid[...] = (liquid[...] + condensed) * keep[...]
    settled = [jnp.zeros((1, columns), jnp.float32)] * 2
    for i in range(half):
        for side, k in enumerate((i, half + i)):
            settled[side] = liquid[k : k + 1, :] + flow[k : k + 1, :] * settled[side]
            liquid[k : k + 1, :] = settled[side]
    through = factors[6 * levels : 6 * levels + half, :]
    liquid[half:, :] = liquid[half:, :] + through * settled[0]
    back(rest, rest_turned, rest_values, rest_known)
    copies.append(leave(1, 0, settled_tiles))
    copies.append(leave(2, main_tiles, tiles))
    for copy in copies:
        copy.wait()


def base_kernel(state, hyper, total, masses, base):
    columns, width = total.shape
    twice = masses[:, 1:2] * total[...]
    base[...] = state[...].reshape(columns, width) - hyper[...] * twice


def pick(slots, pieces):
    size_x, size_y = slots.shape
    columns = size_x * size_y
    wanted = jnp.concatenate([slots[x : x + 1, :] for x in range(size_x)], axis=1)
    picked = 0.0
    for owner, rest in pieces:
        span = rest.shape[1]
        entry = lax.broadcasted_iota(jnp.int32, (span, columns), 0) + owner * span
        choice = (entry == wanted).astype(jnp.float32).astype(jnp.bfloat16)
        for _ in range(3):
            part = rest.astype(jnp.bfloat16)
            rest = rest - part.astype(jnp.float32)
            picked = picked + jnp.dot(part, choice, preferred_element_type=jnp.float32)
    return picked


def factor_kernel(levels, slots, *refs):
    factors = refs[-1]
    if len(refs) == 3:
        here = lax.axis_index("gx")
        pieces = []
        for message, owner in zip(refs, (here, here ^ 1)):
            start = message.shape[0] - 6 * levels
            pieces.append((owner, message[start : start + 3 * levels, :]))
            pieces.append((owner ^ 3, message[start + 3 * levels :, :]))
    else:
        pieces = [(peer, refs[0][peer]) for peer in range(refs[0].shape[0])]
    columns = factors.shape[1]
    picked = pick(slots, pieces)
    mixing, falling, covered = (picked[i * levels : (i + 1) * levels] for i in range(3))
    scale, carry, gain, keep, flow, cover = (
        factors.at[i * levels : (i + 1) * levels] for i in range(6)
    )
    zero = jnp.zeros((1, columns), jnp.float32)
    kept = 1.0 / (1.0 + falling)
    keep[...] = kept
    flow[:1, :] = zero
    flow[1:, :] = falling[:-1] * kept[1:]
    cover[...] = covered
    half = levels // 2
    gains = [zero, zero]
    through = jnp.ones((1, columns), jnp.float32)
    for i in range(half):
        for side, k in enumerate((i, levels - 1 - i)):
            above = mixing[k : k + 1] if k else zero
            below = mixing[k + 1 : k + 2] if k + 1 < levels else zero
            centre = 1.0 + above + (below if k + 1 < levels else mixing[:1])
            behind, ahead = (above, below) if side == 0 else (below, above)
            inverse = 1.0 / (centre - behind * gains[side])
            gains[side] = ahead * inverse
            scale[k : k + 1, :] = inverse
            carry[k : k + 1, :] = behind * inverse
            gain[k : k + 1, :] = gains[side]
        k = half + i
        through = through * falling[k - 1 : k] * kept[k : k + 1]
        factors[6 * levels + i : 6 * levels + i + 1, :] = through
    last = 6 * levels + half
    factors[last : last + 1, :] = 1.0 / (1.0 - gains[0] * gains[1])


def swapped(value, axis, partner):
    return lax.ppermute(value, axis, [(i, partner(i)) for i in range(lax.axis_size(axis))])


def exchanged(near, far, axis):
    size = lax.axis_size(axis)
    from_far = swapped(far, axis, lambda i: (i + (1 if i % 2 else -1)) % size)
    from_near = swapped(near, axis, lambda i: i ^ 1)
    return from_far, from_near


def shifted(value, axis, step):
    size = lax.axis_size(axis)
    return lax.ppermute(value, axis, [(i, (i + step) % size) for i in range(size)])


def local(
    model_state, hyper_coef, point_mass, inverse_mass, span_slot, vert_diff, fall_rate, cloud_frac
):
    size_x, size_y, width = model_state.shape
    levels, span = vert_diff.shape[1:]
    columns = size_x * size_y
    hyper = hyper_coef.reshape(1, width)
    padded = -(-(width + 5) // 128) * 128

    def array(*shape):
        return jax.ShapeDtypeStruct(shape, jnp.float32)

    def scratch(*shape):
        return pltpu.VMEM(shape, jnp.float32)

    def call(kernel, name, outs, scratches, *operands, spec=VMEM, out=VMEM, cost=None):
        return pl.pallas_call(
            kernel,
            out_shape=outs,
            in_specs=[spec] * len(operands),
            out_specs=[out] * len(outs),
            scratch_shapes=scratches,
            compiler_params=PARAMS,
            cost_estimate=cost,
            name=name,
        )(*operands)

    riding = lax.axis_size("gx") == 4
    whole = array(columns, width)
    edge = array(4 * size_x, padded)
    extra = 3 * levels if riding else 0
    rest = width // 256 * size_y
    first_rows, last_rows = packed_rows(size_y, width), packed_rows(size_y + 8, width)
    here, total, x_near, x_near_rest, x_far, y_low, y_high, operator, masses, coefs = call(
        start_kernel,
        "start",
        [
            array(size_x, size_y, width),
            whole,
            array(first_rows - rest, 128),
            array(rest, 128),
            array(first_rows + extra, 128),
            edge,
            edge,
            array(columns, columns),
            array(columns, 128),
            array(3 * levels, span),
        ],
        [
            scratch(size_x, size_y),
            scratch(size_x, size_y),
            scratch(first_rows, 128),
            pltpu.SemaphoreType.DMA((6,)),
        ],
        *(
            pltpu.with_memory_space_constraint(value, pltpu.HBM)
            for value in (
                model_state,
                point_mass,
                inverse_mass,
                vert_diff,
                fall_rate,
                cloud_frac,
            )
        ),
        spec=pl.BlockSpec(memory_space=pltpu.HBM),
    )
    low = shifted(y_high, "gy", 1)
    from_far, from_near = exchanged(x_near, x_far, "gx")
    from_near_rest = swapped(x_near_rest, "gx", lambda i: i ^ 1)
    high = shifted(y_low, "gy", -1)
    (low_weights,) = call(
        functools.partial(weights_kernel, size_x, size_y, width),
        "weights",
        [array(24, 128)],
        [],
        masses,
        low,
        cost=LONG,
    )
    total, x_near, x_far, line_ends, inner = call(
        functools.partial(second_kernel, size_x),
        "second",
        [
            whole,
            array(last_rows + 2 * extra, 128),
            array(last_rows, 128),
            array(4, width),
            array(2 * size_x, 128),
        ],
        [
            scratch(columns, width),
            scratch(size_y + 8, width),
            scratch(size_y + 8, width),
            scratch(first_rows, 128),
        ],
        total,
        masses,
        operator,
        coefs,
        low_weights,
        low,
        from_far,
        from_near,
        from_near_rest,
        high,
    )
    last_x = exchanged(x_near, x_far, "gx")
    peers = lax.axis_size("gx")
    ends_near = swapped(line_ends, "gx", lambda i: (i + (2 if i % 2 else -2)) % peers)
    ends_far = ends_near
    if peers != 4:
        ends_far = swapped(line_ends, "gx", lambda i: (i - (2 if i % 2 else -2)) % peers)
    if riding:
        pieces = [x_near, last_x[1]]
    else:
        pieces = [lax.all_gather(coefs, "gx")]
    (factors,) = call(
        functools.partial(factor_kernel, levels),
        "factors",
        [array(6 * levels + levels // 2 + 8, columns)],
        [],
        span_slot,
        *pieces,
    )
    (base,) = call(base_kernel, "base", [whole], [], here, hyper, total, masses)
    (result,) = call(
        functools.partial(third_kernel, levels),
        "third",
        [array(size_x, size_y, width)],
        [
            scratch(columns, width),
            scratch(8 * (levels + 1), columns),
            scratch((width // levels - 8) * (levels + 1), columns),
            scratch(levels, 8, columns),
            scratch(levels, 8, columns),
            scratch(size_x, size_y, width),
            pltpu.SemaphoreType.DMA((3,)),
        ]
        + [scratch(8, width)] * 4,
        hyper,
        base,
        masses,
        inner,
        factors,
        x_near,
        x_far,
        *last_x,
        ends_near,
        ends_far,
        out=pl.BlockSpec(memory_space=pltpu.HBM),
    )
    return result


def solution(mesh):
    placed = (
        P("gx", "gy", None),
        P(),
        P("gx", "gy"),
        P("gx", "gy"),
        P("gx", "gy"),
        P("gy", None, "gx"),
        P("gy", None, "gx"),
        P("gy", None, "gx"),
    )
    return jax.shard_map(
        local, mesh=mesh, in_specs=placed, out_specs=P("gx", "gy", None), check_vma=False
    )
```

```python
import functools

import jax
import jax.numpy as jnp
import numpy as np
from jax import lax
from jax.experimental import pallas as pl
from jax.experimental.pallas import tpu as pltpu
from jax.sharding import PartitionSpec as P

VMEM = pl.BlockSpec(memory_space=pltpu.VMEM)
LONG = pl.CostEstimate(flops=100_000_000_000, bytes_accessed=30_000_000, transcendentals=0)
PARAMS = pltpu.CompilerParams(vmem_limit_bytes=16 * 1024 * 1024)


def second_table():
    nodes = np.array([-1.0, -1.0 / np.sqrt(5.0), 1.0 / np.sqrt(5.0), 1.0])
    deriv = np.zeros((4, 4))
    for i in range(4):
        for j in range(4):
            if i == j:
                deriv[i, j] = sum(1.0 / (nodes[i] - nodes[k]) for k in range(4) if k != i)
            else:
                upper = np.prod([nodes[i] - nodes[k] for k in range(4) if k != i])
                lower = np.prod([nodes[j] - nodes[k] for k in range(4) if k != j])
                deriv[i, j] = upper / (lower * (nodes[i] - nodes[j]))
    return deriv @ deriv


def split(value):
    high = value.astype(jnp.bfloat16)
    return high, (value - high.astype(jnp.float32)).astype(jnp.bfloat16)


def product(left, right):
    left = jnp.concatenate([left[0], left[1], left[0]], axis=1)
    right = jnp.concatenate([right[0], right[0], right[1]], axis=0)
    return jnp.dot(left, right, preferred_element_type=jnp.float32)


def lookup(row, lane):
    second = second_table()
    row, lane = lax.rem(row, 4), lax.rem(lane, 4)
    result = jnp.zeros(row.shape, jnp.float32)
    for j in range(4):
        column = jnp.full(row.shape, float(second[3, j]), jnp.float32)
        for i in range(3):
            column = jnp.where(row == i, float(second[i, j]), column)
        result = jnp.where(lane == j, column, result)
    return result


def laplacian(size_x, size_y):
    count = size_x * size_y
    row, lane = (lax.broadcasted_iota(jnp.int32, (count, count), i) for i in range(2))
    row_x, lane_x = lax.div(row, size_y), lax.div(lane, size_y)
    row_y, lane_y = lax.rem(row, size_y), lax.rem(lane, size_y)
    same_x = (row_y == lane_y) & (lax.div(row_x, 4) == lax.div(lane_x, 4))
    same_y = (row_x == lane_x) & (lax.div(row_y, 4) == lax.div(lane_y, 4))
    along_x = jnp.where(same_x, lookup(row_x, lane_x), 0.0)
    return along_x + jnp.where(same_y, lookup(row_y, lane_y), 0.0)


def of_partner(values, size_y):
    count = values.shape[0]
    row_y = lax.rem(lax.broadcasted_iota(jnp.int32, values.shape, 0), size_y)
    phase = lax.rem(row_y, 4)
    before = jnp.where((phase == 0) & (row_y > 0), pltpu.roll(values, 1, 0), 0.0)
    after = (phase == 3) & (row_y < size_y - 1)
    return jnp.where(after, pltpu.roll(values, count - 1, 0), before)


def to_column(plane):
    size_x, size_y = plane.shape
    row = lax.broadcasted_iota(jnp.int32, (size_y, size_y), 0)
    lane = lax.broadcasted_iota(jnp.int32, (size_y, size_y), 1)
    parts = [
        jnp.sum(jnp.where(row == lane, plane[x : x + 1, :], 0.0), axis=1, keepdims=True)
        for x in range(size_x)
    ]
    return jnp.concatenate(parts, axis=0)


def even(axis):
    return lax.rem(lax.axis_index(axis), 2) == 0


def x_starts(count, size_y):
    near = jnp.where(even("gx"), count - size_y, 0)
    return near, count - size_y - near


def x_rows(count, size_y):
    starts = x_starts(count, size_y)
    return tuple(pl.ds(pl.multiple_of(start, size_y), size_y) for start in starts)


def add_packed(work, start, message, rows):
    def write(first, count, lanes, value):
        work[pl.ds(pl.multiple_of(start + first, 8), count), lanes] += value

    unpack(message, rows, work.shape[1], write)


def packed_rows(rows, width):
    return rows * (width // 128) + 8


def pack(value, message):
    rows, width = value.shape
    full, left = width // 128, width % 128
    for i in range(full):
        message[i * rows : (i + 1) * rows, :] = value[:, i * 128 : (i + 1) * 128]
    for i in range(rows // 8):
        lanes = slice(i * left, (i + 1) * left)
        message[full * rows : full * rows + 8, lanes] = value[i * 8 : (i + 1) * 8, full * 128 :]


def unpack(message, rows, width, write):
    full, left = width // 128, width % 128
    for i in range(full):
        write(0, rows, slice(i * 128, (i + 1) * 128), message[i * rows : (i + 1) * rows, :])
    for i in range(rows // 8):
        value = message[full * rows : full * rows + 8, i * left : (i + 1) * left]
        write(i * 8, 8, slice(full * 128, width), value)


def edge_rows(ref, y, size_x, size_y):
    return jnp.concatenate(
        [ref[x * size_y + y : x * size_y + y + 1, :] for x in range(size_x)], axis=0
    )


def start_kernel(
    state,
    mass,
    inverse,
    diff,
    fall,
    cloud,
    here,
    total,
    x_near,
    x_near_rest,
    x_far,
    low,
    high,
    operator,
    columns,
    coefs,
    mass_here,
    inverse_here,
    near_rows,
    sems,
):
    size_x, size_y, width = state.shape
    levels = diff.shape[1]
    pairs = [(mass, mass_here), (inverse, inverse_here)]
    pairs.append((state, here))
    for i, source in enumerate((diff, fall, cloud)):
        pairs.append((source.at[0], coefs.at[i * levels : (i + 1) * levels]))
    copies = [
        pltpu.make_async_copy(source, target, sems.at[i])
        for i, (source, target) in enumerate(pairs)
    ]
    for copy in copies:
        copy.start()
    count = size_x * size_y
    matrix = laplacian(size_x, size_y)
    for copy in copies[:2]:
        copy.wait()
    own = jnp.broadcast_to(to_column(mass_here[...]), (count, count))
    matrix = own * matrix
    matrix = matrix + of_partner(matrix, size_y)
    operator[...] = matrix
    partner = of_partner(own, size_y)
    inverses = to_column(inverse_here[...])
    lane = lax.broadcasted_iota(jnp.int32, columns.shape, 1)
    columns[...] = jnp.where(lane == 0, own, jnp.where(lane == 1, inverses, partner))
    copies[2].wait()
    total[...] = product(split(matrix), split(here[...].reshape(count, width)))
    near, far = x_rows(count, size_y)
    pack(total[near], near_rows)
    rest = x_near_rest.shape[0]
    x_near_rest[...] = near_rows[:rest, :]
    x_near[...] = near_rows[rest:, :]
    pack(total[far], x_far)
    for first, message in ((0, low), (size_y - 4, high)):
        for i in range(4):
            rows = slice(i * size_x, (i + 1) * size_x)
            message[rows, :width] = edge_rows(total, first + i, size_x, size_y)
            message[rows, width : width + 2] = edge_rows(columns, first + i, size_x, size_y)[:, :2]
    for copy in copies[3:]:
        copy.wait()
    if x_far.shape[0] > near_rows.shape[0]:
        x_far[near_rows.shape[0] :, :] = coefs[...]


def node_column(values, start, count):
    row = lax.broadcasted_iota(jnp.int32, (count, 1), 0)
    result = jnp.zeros((count, 1), jnp.float32)
    for i, value in enumerate(values):
        result = jnp.where(row == start + i, float(value), result)
    return result


def edge_weights(columns, message, size_x, size_y, width, edge, line):
    second = second_table()
    other = size_x - 1 - edge
    low = line == 3
    y, first = (0, 0) if low else (size_y - 1, size_y - 8)
    rows = slice(edge * size_y + first, edge * size_y + first + 8)
    here, there = (slice(x * size_y + y, x * size_y + y + 1) for x in (edge, other))
    mass, inverse = columns[here, 0:1], columns[here, 1:2]
    beyond = slice(line * size_x + edge, line * size_x + edge + 1)
    beyond_mass = message[beyond, width : width + 1]

    def beyond_inverse(i, x):
        return message[i * size_x + x : i * size_x + x + 1, width + 1 : width + 2]

    if low:
        own, partner = node_column(second[:, 0], 0, 8), node_column(second[3:, 0], 4, 8)
    else:
        own, partner = node_column(second[:, 3], 4, 8), node_column(second[:1, 3], 3, 8)
    along = inverse * (own * columns[rows, 0:1] + partner * columns[rows, 2:3])
    lane = lax.broadcasted_iota(jnp.int32, (8, 128), 1)
    place = lax.broadcasted_iota(jnp.int32, (8, 128), 0)
    tile = jnp.where(lane == line, along, 0.0)
    for i in range(4):
        value = float(second[line, i]) * beyond_mass * beyond_inverse(i, edge)
        if i == line:
            across = beyond_mass * beyond_inverse(line, edge) + mass * inverse
            value = value + float(second[edge, edge]) * across
        tile = tile + jnp.where((place == y - first) & (lane == i), value, 0.0)
    across = beyond_mass * beyond_inverse(line, other) + mass * columns[there, 1:2]
    value = float(second[edge, other]) * across
    return tile + jnp.where((place == y - first) & (lane == 4), value, 0.0)


def side_weights(columns, message, size_x, size_y, width, line):
    second = second_table()
    first, last = 0, size_x - 1
    tiles = [
        edge_weights(columns, message, size_x, size_y, width, edge, line) for edge in (first, last)
    ]
    mass = message[line * size_x : (line + 1) * size_x, width : width + 1]
    own = edge_rows(columns, 0 if line == 3 else size_y - 1, size_x, size_y)
    inner = []
    for edge in (first, last):
        inverse = message[line * size_x + edge : line * size_x + edge + 1, width + 1 : width + 2]
        across = mass * inverse + own[:, 0:1] * own[edge : edge + 1, 1:2]
        inner.append(node_column(second[:, edge], 0, size_x) * across)
    lane = lax.broadcasted_iota(jnp.int32, (size_x, 128), 1)
    from_last = jnp.where(even("gx"), 0, 1)
    return (
        jnp.where(even("gx"), tiles[1], tiles[0]),
        jnp.where(even("gx"), tiles[0], tiles[1]),
        jnp.where(lane == from_last, inner[1], inner[0]),
    )


def weights_kernel(size_x, size_y, width, columns, message, out):
    near, far, inner = side_weights(columns, message, size_x, size_y, width, 3)
    out[0:8, :] = near
    out[8:16, :] = far
    out[16 : 16 + size_x, :] = inner


def second_kernel(
    size_x,
    total,
    columns,
    operator,
    coefs,
    low_weights,
    low,
    from_far,
    from_near,
    from_near_rest,
    high,
    out,
    x_near,
    x_far,
    line_ends,
    inner,
    work,
    at_near,
    at_far,
):
    size_y, width = total.shape[0] // size_x, total.shape[1]
    depth = size_y + 8
    second = second_table()
    near, far = x_starts(size_x * size_y, size_y)
    work[...] = total[...]
    half, left = from_near_rest.shape[0] // size_y, width % 128
    for message, first in ((from_near_rest, 0), (from_near, half)):
        for i in range(half):
            lanes = slice((first + i) * 128, (first + i + 1) * 128)
            rows = pl.ds(pl.multiple_of(near, size_y), size_y)
            work[rows, lanes] += message[i * size_y : (i + 1) * size_y, :]
    for i in range(size_y // 8):
        rows = pl.ds(pl.multiple_of(near + i * 8, 8), 8)
        value = from_near[half * size_y :, i * left : (i + 1) * left]
        work[rows, width - left :] += value
    add_packed(work, far, from_far, size_y)
    sides = ((low, 0, 3, 0), (high, size_y - 1, 0, size_y - 8))
    beyond = []
    for message, y, line, _ in sides:
        lines = [message[i * size_x : (i + 1) * size_x, :width] for i in range(4)]
        lines[line] = lines[line] + edge_rows(work, y, size_x, size_y)
        for x in range(size_x):
            work[x * size_y + y : x * size_y + y + 1, :] = lines[line][x : x + 1]
        for i in range(4):
            inverse = message[i * size_x : (i + 1) * size_x, width + 1 : width + 2]
            lines[i] = inverse * lines[i]
        value = sum(float(second[line, i]) * lines[i] for i in range(4))
        for x in range(size_x):
            value = value + node_column(second[:, x], 0, size_x) * lines[line][x : x + 1]
        mass = message[line * size_x : (line + 1) * size_x, width : width + 1]
        beyond.append(mass * value)
    out[...] = product(split(operator[...]), split(columns[:, 1:2] * work[...]))
    for (_, y, _, _), rows in zip(sides, beyond):
        for x in range(size_x):
            out[x * size_y + y : x * size_y + y + 1, :] += rows[x : x + 1]

    near, far = x_rows(size_x * size_y, size_y)
    at_near[:size_y, :] = out[near]
    at_far[:size_y, :] = out[far]
    last = depth * (width // 128)
    lanes = depth // 8 * (width % 128)
    high_weights = side_weights(columns, high, size_x, size_y, width, 0)
    for side, (message, _, line, _) in enumerate(sides):
        weights = high_weights if side else [low_weights[i : i + 8] for i in (0, 8, 16)]
        inner[side * size_x : (side + 1) * size_x, :] = weights[2][:size_x]
        place = slice(lanes + 8 * side, lanes + 8 * side + 5)
        x_near[last : last + 8, place] = weights[0][:, :5]
        x_far[last : last + 8, place] = weights[1][:, :5]
        for i in range(4):
            first, final = (
                message[i * size_x + x : i * size_x + x + 1, :width] for x in (0, size_x - 1)
            )
            row_near = jnp.where(even("gx"), final, first)
            row_far = jnp.where(even("gx"), first, final)
            place = size_y + 4 * side + i
            at_near[place : place + 1, :] = row_near
            at_far[place : place + 1, :] = row_far
            if i == line:
                line_ends[2 * side : 2 * side + 1, :] = row_far
                line_ends[2 * side + 1 : 2 * side + 2, :] = row_near
    pack(at_near[...], x_near)
    pack(at_far[...], x_far)
    if x_near.shape[0] > x_far.shape[0]:
        count = coefs.shape[0]
        start = last + 8
        x_near[start : start + count, :] = coefs[...]
        x_near[start + count :, :] = from_far[packed_rows(size_y, width) :, :]


def third_kernel(
    levels,
    hyper,
    base,
    masses,
    inner,
    factors,
    to_near,
    to_far,
    from_far,
    from_near,
    ends_near,
    ends_far,
    out,
    work,
    turned,
    turned_rest,
    values,
    values_rest,
    staged,
    sems,
    *beyond_rows,
):
    columns, width = base.shape
    size_x, size_y, _ = out.shape
    variables = width // levels
    rows = size_y + 8
    last, lanes = rows * (width // 128), rows // 8 * (width % 128)
    messages = (to_near, to_far, from_near, from_far)
    for message, target in zip(messages, beyond_rows):
        for i in range(width // 128):
            target[:, i * 128 : (i + 1) * 128] = message[i * rows + size_y : (i + 1) * rows, :]
        left = width % 128
        lanes_before = size_y // 8 * left
        target[:, width - left :] = message[last : last + 8, lanes_before : lanes_before + left]
    at_near, at_far, over_near, over_far = beyond_rows
    near, far = x_starts(columns, size_y)
    sides = ((0, 0, 3, 0), (1, size_y - 1, 0, size_y - 8))
    partners = (
        (near, at_near, over_near, over_far, ends_near),
        (far, at_far, over_far, over_near, ends_far),
    )
    for x in range(1, size_x - 1):
        for first in (0, size_y - 8):
            work[x * size_y + first : x * size_y + first + 8, :] = jnp.zeros((8, width), jnp.float32)
    for start, message in ((near, from_near), (far, from_far)):
        for i in range(width // 128):
            place = pl.ds(pl.multiple_of(start, size_y), size_y)
            work[place, i * 128 : (i + 1) * 128] = message[i * rows : i * rows + size_y, :]
        for i in range(size_y // 8):
            place = pl.ds(pl.multiple_of(start + i * 8, 8), 8)
            left = width % 128
            work[place, width - left :] = message[last : last + 8, i * left : (i + 1) * left]
    for side, y, line, first in sides:
        place = 4 * side
        weights = [
            message[last : last + 8, lanes + 8 * side : lanes + 8 * side + 5] for message in messages
        ]
        for which, (start, mine, theirs, others, ends) in enumerate(partners):
            own, beyond = weights[which], weights[2 + which]
            terms = [
                (weight[:, i : i + 1], values, place + i)
                for i in range(4)
                for weight, values in ((own, theirs), (beyond, mine))
            ]
            terms += [(own[:, 4:5], others, place + line), (beyond[:, 4:5], ends, 2 * side + which)]
            added = sum(weight * values[row : row + 1, :width] for weight, values, row in terms)
            work[pl.ds(pl.multiple_of(start + first, 8), 8), :] += added
        for x in range(1, size_x - 1):
            row, weight = x * size_y + y, side * size_x + x
            work[row : row + 1, :] += (
                inner[weight : weight + 1, 0:1] * over_near[place + line : place + line + 1, :]
                + inner[weight : weight + 1, 1:2] * over_far[place + line : place + line + 1, :]
            )
    for start in (near, far):
        place = pl.ds(pl.multiple_of(start, size_y), size_y)
        work[place, :] = base[place, :] - hyper[...] * (masses[place, 1:2] * work[place, :])
    for x in range(1, size_x - 1):
        for first in (0, size_y - 8):
            rows = slice(x * size_y + first, x * size_y + first + 8)
            work[rows, :] = base[rows, :] - hyper[...] * (masses[rows, 1:2] * work[rows, :])
        rows = slice(x * size_y + 8, (x + 1) * size_y - 8)
        work[rows, :] = base[rows, :]
    pitch, half = levels + 1, levels // 2
    scale, carry, gain, keep, flow, cloud = (
        factors.at[i * levels : (i + 1) * levels] for i in range(6)
    )
    groups = [(first, min(8, variables - first)) for first in range(0, variables, 8)]
    buffers = list(zip(groups, (turned, turned_rest), (values, values_rest)))

    def turn(group, turned):
        first, count = group
        start, stop = first * levels, (first + count) * levels
        tile = start // 128 * 128
        rows = work[:, tile:stop].T
        for i in range(count):
            row = start - tile + i * levels
            turned[i * pitch : i * pitch + levels, :] = rows[row : row + levels]

    def forward(group, turned, values):
        count = group[1]
        known = [jnp.zeros((count, columns), jnp.float32)] * 2
        for i in range(half):
            for side, k in enumerate((i, levels - 1 - i)):
                scaled = turned[pl.ds(k, count, stride=pitch), :] * scale[k : k + 1, :]
                known[side] = scaled + carry[k : k + 1, :] * known[side]
                values[k, :count, :] = known[side]
        return known

    def back(group, turned, values, known):
        count = group[1]
        meet = factors[6 * levels + half : 6 * levels + half + 1, :]
        first = (known[0] + gain[half - 1 : half, :] * known[1]) * meet
        solved = [first, known[1] + gain[half : half + 1, :] * first]
        for i in reversed(range(half)):
            for side, k in enumerate((i, levels - 1 - i)):
                if i < half - 1:
                    solved[side] = values[k, :count, :] + gain[k : k + 1, :] * solved[side]
                turned[pl.ds(k, count, stride=pitch), :] = solved[side]

    def place(i):
        lanes = slice(i * 128, min((i + 1) * 128, width))
        parts = []
        for (start, count), source, _ in buffers:
            for j in range(start, start + count):
                first, last = max(lanes.start, j * levels), min(lanes.stop, (j + 1) * levels)
                if first < last:
                    offset = (j - start) * pitch - j * levels
                    parts.append(source[first + offset : last + offset, :])
        rows = jnp.concatenate(parts, axis=0)
        staged[:, :, lanes] = rows.T.reshape(size_x, size_y, -1)

    def leave(which, first, last):
        for i in range(first, last):
            place(i)
        lanes = slice(first * 128, min(last * 128, width))
        copy = pltpu.make_async_copy(staged.at[:, :, lanes], out.at[:, :, lanes], sems.at[which])
        copy.start()
        return copy

    (main, main_turned, main_values), (rest, rest_turned, rest_values) = buffers
    turn(main, main_turned)
    main_known = forward(main, main_turned, main_values)
    turn(rest, rest_turned)
    rest_known = forward(rest, rest_turned, rest_values)
    back(main, main_turned, main_values, main_known)
    tiles = -(-width // 128)
    settled_tiles, main_tiles = -(-3 * levels // 128), main[1] * levels // 128
    copies = [leave(0, settled_tiles, main_tiles)]
    heat, vapour, liquid = (turned.at[i * pitch : i * pitch + levels] for i in range(3))
    condensed = cloud[...] * 0.5 * jnp.maximum(vapour[...] - 0.3 * heat[...], 0.0)
    vapour[...] = vapour[...] - condensed
    heat[...] = heat[...] + 2.0 * condensed
    liquid[...] = (liquid[...] + condensed) * keep[...]
    settled = [jnp.zeros((1, columns), jnp.float32)] * 2
    for i in range(half):
        for side, k in enumerate((i, half + i)):
            settled[side] = liquid[k : k + 1, :] + flow[k : k + 1, :] * settled[side]
            liquid[k : k + 1, :] = settled[side]
    through = factors[6 * levels : 6 * levels + half, :]
    liquid[half:, :] = liquid[half:, :] + through * settled[0]
    back(rest, rest_turned, rest_values, rest_known)
    copies.append(leave(1, 0, settled_tiles))
    copies.append(leave(2, main_tiles, tiles))
    for copy in copies:
        copy.wait()


def base_kernel(state, hyper, total, masses, base):
    columns, width = total.shape
    twice = masses[:, 1:2] * total[...]
    base[...] = state[...].reshape(columns, width) - hyper[...] * twice


def pick(slots, pieces):
    size_x, size_y = slots.shape
    columns = size_x * size_y
    wanted = jnp.concatenate([slots[x : x + 1, :] for x in range(size_x)], axis=1)
    picked = 0.0
    for owner, rest in pieces:
        span = rest.shape[1]
        entry = lax.broadcasted_iota(jnp.int32, (span, columns), 0) + owner * span
        choice = (entry == wanted).astype(jnp.float32).astype(jnp.bfloat16)
        for _ in range(3):
            part = rest.astype(jnp.bfloat16)
            rest = rest - part.astype(jnp.float32)
            picked = picked + jnp.dot(part, choice, preferred_element_type=jnp.float32)
    return picked


def factor_kernel(levels, slots, *refs):
    factors = refs[-1]
    if len(refs) == 3:
        here = lax.axis_index("gx")
        pieces = []
        for message, owner in zip(refs, (here, here ^ 1)):
            start = message.shape[0] - 6 * levels
            pieces.append((owner, message[start : start + 3 * levels, :]))
            pieces.append((owner ^ 3, message[start + 3 * levels :, :]))
    else:
        pieces = [(peer, refs[0][peer]) for peer in range(refs[0].shape[0])]
    columns = factors.shape[1]
    picked = pick(slots, pieces)
    mixing, falling, covered = (picked[i * levels : (i + 1) * levels] for i in range(3))
    scale, carry, gain, keep, flow, cover = (
        factors.at[i * levels : (i + 1) * levels] for i in range(6)
    )
    zero = jnp.zeros((1, columns), jnp.float32)
    kept = 1.0 / (1.0 + falling)
    keep[...] = kept
    flow[:1, :] = zero
    flow[1:, :] = falling[:-1] * kept[1:]
    cover[...] = covered
    half = levels // 2
    gains = [zero, zero]
    through = jnp.ones((1, columns), jnp.float32)
    for i in range(half):
        for side, k in enumerate((i, levels - 1 - i)):
            above = mixing[k : k + 1] if k else zero
            below = mixing[k + 1 : k + 2] if k + 1 < levels else zero
            centre = 1.0 + above + (below if k + 1 < levels else mixing[:1])
            behind, ahead = (above, below) if side == 0 else (below, above)
            inverse = 1.0 / (centre - behind * gains[side])
            gains[side] = ahead * inverse
            scale[k : k + 1, :] = inverse
            carry[k : k + 1, :] = behind * inverse
            gain[k : k + 1, :] = gains[side]
        k = half + i
        through = through * falling[k - 1 : k] * kept[k : k + 1]
        factors[6 * levels + i : 6 * levels + i + 1, :] = through
    last = 6 * levels + half
    factors[last : last + 1, :] = 1.0 / (1.0 - gains[0] * gains[1])


def swapped(value, axis, partner):
    return lax.ppermute(value, axis, [(i, partner(i)) for i in range(lax.axis_size(axis))])


def exchanged(near, far, axis):
    size = lax.axis_size(axis)
    from_far = swapped(far, axis, lambda i: (i + (1 if i % 2 else -1)) % size)
    from_near = swapped(near, axis, lambda i: i ^ 1)
    return from_far, from_near


def shifted(value, axis, step):
    size = lax.axis_size(axis)
    return lax.ppermute(value, axis, [(i, (i + step) % size) for i in range(size)])


def local(
    model_state, hyper_coef, point_mass, inverse_mass, span_slot, vert_diff, fall_rate, cloud_frac
):
    size_x, size_y, width = model_state.shape
    levels, span = vert_diff.shape[1:]
    columns = size_x * size_y
    hyper = hyper_coef.reshape(1, width)
    padded = -(-(width + 5) // 128) * 128

    def array(*shape):
        return jax.ShapeDtypeStruct(shape, jnp.float32)

    def scratch(*shape):
        return pltpu.VMEM(shape, jnp.float32)

    def call(kernel, name, outs, scratches, *operands, spec=VMEM, out=VMEM, cost=None):
        return pl.pallas_call(
            kernel,
            out_shape=outs,
            in_specs=[spec] * len(operands),
            out_specs=[out] * len(outs),
            scratch_shapes=scratches,
            compiler_params=PARAMS,
            cost_estimate=cost,
            name=name,
        )(*operands)

    riding = lax.axis_size("gx") == 4
    whole = array(columns, width)
    edge = array(4 * size_x, padded)
    extra = 3 * levels if riding else 0
    rest = width // 256 * size_y
    first_rows, last_rows = packed_rows(size_y, width), packed_rows(size_y + 8, width)
    here, total, x_near, x_near_rest, x_far, y_low, y_high, operator, masses, coefs = call(
        start_kernel,
        "start",
        [
            array(size_x, size_y, width),
            whole,
            array(first_rows - rest, 128),
            array(rest, 128),
            array(first_rows + extra, 128),
            edge,
            edge,
            array(columns, columns),
            array(columns, 128),
            array(3 * levels, span),
        ],
        [
            scratch(size_x, size_y),
            scratch(size_x, size_y),
            scratch(first_rows, 128),
            pltpu.SemaphoreType.DMA((6,)),
        ],
        *(
            pltpu.with_memory_space_constraint(value, pltpu.HBM)
            for value in (
                model_state,
                point_mass,
                inverse_mass,
                vert_diff,
                fall_rate,
                cloud_frac,
            )
        ),
        spec=pl.BlockSpec(memory_space=pltpu.HBM),
    )
    low = shifted(y_high, "gy", 1)
    from_far, from_near = exchanged(x_near, x_far, "gx")
    from_near_rest = swapped(x_near_rest, "gx", lambda i: i ^ 1)
    high = shifted(y_low, "gy", -1)
    (low_weights,) = call(
        functools.partial(weights_kernel, size_x, size_y, width),
        "weights",
        [array(24, 128)],
        [],
        masses,
        low,
        cost=LONG,
    )
    total, x_near, x_far, line_ends, inner = call(
        functools.partial(second_kernel, size_x),
        "second",
        [
            whole,
            array(last_rows + 2 * extra, 128),
            array(last_rows, 128),
            array(4, width),
            array(2 * size_x, 128),
        ],
        [
            scratch(columns, width),
            scratch(size_y + 8, width),
            scratch(size_y + 8, width),
        ],
        total,
        masses,
        operator,
        coefs,
        low_weights,
        low,
        from_far,
        from_near,
        from_near_rest,
        high,
    )
    last_x = exchanged(x_near, x_far, "gx")
    peers = lax.axis_size("gx")
    ends_near = swapped(line_ends, "gx", lambda i: (i + (2 if i % 2 else -2)) % peers)
    ends_far = ends_near
    if peers != 4:
        ends_far = swapped(line_ends, "gx", lambda i: (i - (2 if i % 2 else -2)) % peers)
    if riding:
        pieces = [x_near, last_x[1]]
    else:
        pieces = [lax.all_gather(coefs, "gx")]
    (factors,) = call(
        functools.partial(factor_kernel, levels),
        "factors",
        [array(6 * levels + levels // 2 + 8, columns)],
        [],
        span_slot,
        *pieces,
    )
    (base,) = call(base_kernel, "base", [whole], [], here, hyper, total, masses)
    (result,) = call(
        functools.partial(third_kernel, levels),
        "third",
        [array(size_x, size_y, width)],
        [
            scratch(columns, width),
            scratch(8 * (levels + 1), columns),
            scratch((width // levels - 8) * (levels + 1), columns),
            scratch(levels, 8, columns),
            scratch(levels, 8, columns),
            scratch(size_x, size_y, width),
            pltpu.SemaphoreType.DMA((3,)),
        ]
        + [scratch(8, width)] * 4,
        hyper,
        base,
        masses,
        inner,
        factors,
        x_near,
        x_far,
        *last_x,
        ends_near,
        ends_far,
        out=pl.BlockSpec(memory_space=pltpu.HBM),
    )
    return result


def solution(mesh):
    placed = (
        P("gx", "gy", None),
        P(),
        P("gx", "gy"),
        P("gx", "gy"),
        P("gx", "gy"),
        P("gy", None, "gx"),
        P("gy", None, "gx"),
        P("gy", None, "gx"),
    )
    return jax.shard_map(
        local, mesh=mesh, in_specs=placed, out_specs=P("gx", "gy", None), check_vma=False
    )
```
